32 devices in a mesh: tm: 4 (over y, core), height: 2 (over x), width: 4 (over z).
Axes of the slice: x: 2, y: 2, z: 4, core: 2. Of those that a mesh axis runs over, the one named last changes fastest.
Arguments:
- latents: bfloat16 [16, 16, 32, 512], P('tm', 'height', 'width'), may hold values from -6 to 6
- spatial_taps: float32 [3, 3, 512], replicated, may hold values from -2 to 2
- kernel_taps: bfloat16 [16, 512], replicated, may hold values from -0.4 to 0.4
- skip_gain: float32 [512], replicated, may hold values from 0.5 to 1.5
- gate_weight: bfloat16 [512, 512], replicated, may hold values from -0.25 to 0.25
- value_weight: bfloat16 [512, 512], replicated, may hold values from -0.25 to 0.25
- out_weight: bfloat16 [512, 512], replicated, may hold values from -0.25 to 0.25
Outputs:
- mixed_out: bfloat16 [16, 16, 32, 512], P('tm', 'height', 'width')
The draws below stay inside these ranges and needn't reach their ends.
All inputs are finite; a program needn't handle non-finite values.
Results may differ from the reference program's by a relative error of at most 0.0064.
Values may be sent and summed in bfloat16 or wider, within the bound.
No kernel may reach another device: no remote copies, remote signals or barrier semaphores. Data moves between devices by JAX's collectives and lax.ppermute only.
A program may use at most 64 MiB of HBM per device.

```python
import math
import jax
import jax.numpy as jnp
from jax import lax

FEATURE_WIDTH = 512
F_DEV = 4
MOVIE_LENGTH = 16
H = 16
W = 32
N_TM = 4


def draw_kernel_taps(key, part):
    key = jax.random.fold_in(key, 11)
    keys = jax.random.split(key, 6)
    lagging_images = jnp.arange(MOVIE_LENGTH, dtype=jnp.float32)[:, None]
    low = math.log(30.0)
    high = math.log(4.0 * MOVIE_LENGTH)
    support_radius = jnp.exp(jax.random.uniform(keys[0], (1, FEATURE_WIDTH), jnp.float32, low, high))
    jump_increment = jax.random.uniform(keys[1], (1, FEATURE_WIDTH), jnp.float32, 0.0, 0.3)
    cycle_shift = jax.random.uniform(keys[2], (1, FEATURE_WIDTH), jnp.float32, -math.pi, math.pi)
    rough_guess = jax.random.uniform(keys[3], (MOVIE_LENGTH, FEATURE_WIDTH), jnp.float32, 0.5, 1.5)
    pixel_locations = jax.random.randint(keys[4], (3,), 1, MOVIE_LENGTH).astype(jnp.float32)
    discarded_entries = jax.random.uniform(keys[5], (3, FEATURE_WIDTH), jnp.float32, 0.5, 0.8)
    packet_bundles = jnp.ones((MOVIE_LENGTH, FEATURE_WIDTH), jnp.float32)
    for chosen_position in range(3):
        packet_bundles = packet_bundles * jnp.where(lagging_images >= pixel_locations[chosen_position], discarded_entries[chosen_position][None, :], 1.0)
    magnitude_multiplier = jnp.sqrt(2.0 / support_radius)
    response_weights = magnitude_multiplier * jnp.exp(-lagging_images / support_radius) * jnp.cos(jump_increment * lagging_images + cycle_shift) * rough_guess * packet_bundles
    return jnp.clip(response_weights, -0.3984375, 0.3984375).astype(jnp.bfloat16)


def levels(stream_key, shape, pieces, low, largest):
    def one(dim, blocks):
        steps = jax.random.uniform(jax.random.fold_in(jax.random.fold_in(stream_key, 6), dim), (blocks,), jnp.float32, low / len(pieces), largest / len(pieces))
        return jnp.repeat(jnp.exp(steps), shape[dim] // blocks).reshape((-1,) + (1,) * (len(shape) - dim - 1))

    gain = one(*pieces[0])
    for cut in pieces[1:]:
        gain = gain * one(*cut)
    return gain


def centred(rng, extent, deviation, most, cuts=(), kind=jnp.bfloat16):
    loudness = levels(rng, extent, cuts, -0.22, 0.18) if cuts else 1.0
    values = jax.random.normal(rng, extent, jnp.float32) * deviation * loudness
    return jnp.minimum(jnp.maximum(values, -most), most).astype(kind)


def setup_inputs(seed: int = 0) -> dict:
    splits = jax.random.split(jax.random.key(seed), 8)
    latents = centred(splits[0], (MOVIE_LENGTH, H, W, FEATURE_WIDTH), 1.0, 6.0, ((0, 4), (1, 2), (2, 4)))
    spatial_taps = centred(splits[1], (3, 3, FEATURE_WIDTH), 9 ** -0.5, 2.0, (), jnp.float32)
    kernel_taps = draw_kernel_taps(jax.random.fold_in(splits[7], 71), 0)
    skip_gain = jnp.clip(jax.random.uniform(splits[3], (FEATURE_WIDTH,), jnp.float32, 0.5, 1.5), 0.5, 1.5)
    gate_weight = centred(splits[4], (FEATURE_WIDTH, FEATURE_WIDTH), FEATURE_WIDTH ** -0.5, 0.25)
    value_weight = centred(splits[5], (FEATURE_WIDTH, FEATURE_WIDTH), FEATURE_WIDTH ** -0.5, 0.25)
    out_weight = centred(splits[6], (FEATURE_WIDTH, FEATURE_WIDTH), FEATURE_WIDTH ** -0.5, 0.25)
    return {"latents": latents, "spatial_taps": spatial_taps, "kernel_taps": kernel_taps, "skip_gain": skip_gain, "gate_weight": gate_weight, "value_weight": value_weight, "out_weight": out_weight}


def spatial_mix(padded, spatial_taps):
    rows = padded.shape[1] - 2
    cols = padded.shape[2] - 2
    total = jnp.zeros((padded.shape[0], rows, cols, padded.shape[3]), jnp.float32)
    for first in range(3):
        for second in range(3):
            window = padded[:, first:first + rows, second:second + cols, :].astype(jnp.float32)
            total = total + window * spatial_taps[first, second]
    return total.astype(jnp.bfloat16)


def reference(latents, spatial_taps, kernel_taps, skip_gain, gate_weight, value_weight, out_weight):
    frames, rows, cols, chans = latents.shape
    blocks = latents.reshape(N_TM, F_DEV, rows, cols, chans)

    def filter_block(block):
        padded = jnp.pad(block, ((0, 0), (1, 1), (1, 1), (0, 0)))
        return spatial_mix(padded, spatial_taps)

    spatial = lax.map(filter_block, blocks).reshape(frames, rows, cols, chans)
    groups = chans // 32
    lag = jnp.arange(frames, dtype=jnp.int32)[:, None] - jnp.arange(frames, dtype=jnp.int32)[None, :]
    index = jnp.clip(lag, 0, frames - 1).astype(jnp.int32)
    columns = spatial.reshape(frames, rows * cols, groups, 32).transpose(2, 0, 1, 3)
    grouped_taps = kernel_taps.reshape(frames, groups, 32).transpose(1, 2, 0)

    def convolve(inputs):
        column_block, tap_block = inputs
        toeplitz = jnp.where(lag[None, :, :] >= 0, jnp.take(tap_block, index, axis=1).astype(jnp.float32), jnp.float32(0.0))
        return jnp.einsum("cts,sxc->txc", toeplitz, column_block.astype(jnp.float32), precision=lax.Precision.HIGHEST)

    causal = lax.map(convolve, (columns, grouped_taps))
    causal = causal.transpose(1, 2, 0, 3).reshape(frames, rows, cols, chans)
    mixed = (causal + skip_gain * spatial.astype(jnp.float32)).astype(jnp.bfloat16)

    def project(inputs):
        frame_in, frame_mixed = inputs
        flat_in = frame_in.reshape(rows * cols, chans)
        flat_mixed = frame_mixed.reshape(rows * cols, chans)
        gate = jax.nn.silu(jnp.dot(flat_in, gate_weight, preferred_element_type=jnp.float32))
        value = jnp.dot(flat_mixed, value_weight, preferred_element_type=jnp.float32)
        hidden = (value * gate).astype(jnp.bfloat16)
        result = jnp.dot(hidden, out_weight, preferred_element_type=jnp.float32).astype(jnp.bfloat16)
        return result.reshape(rows, cols, chans)

    return lax.map(project, (latents, mixed))
```

```python
import functools

import jax
import jax.numpy as jnp
from jax import lax
from jax.experimental import pallas as pl
from jax.experimental.pallas import tpu as pltpu
from jax.sharding import PartitionSpec as P

LANES = 128
VMEM = pl.BlockSpec(memory_space=pltpu.VMEM)
SMEM = pl.BlockSpec(memory_space=pltpu.SMEM)
PARAMS = pltpu.CompilerParams(vmem_limit_bytes=16 * 1024 * 1024)


def gate_kernel(x_ref, w_ref, gate_ref):
    v = jnp.dot(x_ref[...], w_ref[...], preferred_element_type=jnp.float32)
    gate_ref[...] = v / (1.0 + jnp.exp(-v))


def mix_kernel(frames, cols, me_ref, clip_ref, taps_ref, skip_ref, u_ref, left_ref, right_ref, table, held):
    me = me_ref[0]
    lags, chans = taps_ref.shape
    sites = u_ref.shape[0] // frames
    taps = taps_ref[...].astype(jnp.float32)
    table[0:lags] = jnp.zeros((lags, cols, chans), jnp.float32)
    for lag in range(lags):
        tap = taps[lag : lag + 1] + (skip_ref[...] if lag == 0 else 0.0)
        table[lags + lag] = jnp.broadcast_to(tap, (cols, chans))
    for lane in range(0, chans, LANES):
        span = slice(lane, lane + LANES)

        def step(block, totals):
            totals = list(totals)
            for s in range(frames):
                start = pl.multiple_of((block * frames + s) * sites, sites)
                x = clip_ref[pl.ds(start, sites), span].astype(jnp.float32).reshape(sites // cols, cols, LANES)
                for t in range(frames):
                    tap = table[lags + (me - block) * frames + t - s, :, span]
                    totals[t] = totals[t] + tap * x
            return tuple(totals)

        zero = jnp.zeros((sites // cols, cols, LANES), jnp.float32)
        totals = lax.fori_loop(0, me + 1, step, (zero,) * frames)
        for t in range(frames):
            held[t * sites : (t + 1) * sites, :] = totals[t].reshape(sites, LANES)
        u_ref[:, span] = held[...].astype(jnp.bfloat16)
        lines = frames * sites // cols
        left_ref[:, span] = held[pl.ds(0, lines, stride=cols), :].astype(jnp.bfloat16)
        right_ref[:, span] = held[pl.ds(cols - 1, lines, stride=cols), :].astype(jnp.bfloat16)


def finish_kernel(
    frames, rows, cols, at_ref, u_ref, left_ref, right_ref, above_ref, below_ref, taps_ref, gate_ref, wv_ref, wo_ref,
    out_ref, mixed,
):
    first = at_ref[0].astype(jnp.float32)
    last = at_ref[1].astype(jnp.float32)
    chans = u_ref.shape[1]
    place = lax.broadcasted_iota(jnp.int32, (cols, LANES), 0)
    for lane in range(0, chans, LANES):
        span = slice(lane, lane + LANES)
        taps = [[taps_ref[3 * a + b : 3 * a + b + 1, span] for b in range(3)] for a in range(3)]
        left = left_ref[:, span].astype(jnp.float32)
        right = right_ref[:, span].astype(jnp.float32)
        above = above_ref[:, span].astype(jnp.float32) * first
        below = below_ref[:, span].astype(jnp.float32) * last
        corner = frames * cols
        for t in range(frames):
            tile = u_ref[t * rows * cols : (t + 1) * rows * cols, span].astype(jnp.float32)
            lines = [above[t * cols : (t + 1) * cols]]
            lefts = [above[corner + t : corner + t + 1]]
            rights = [above[corner + frames + t : corner + frames + t + 1]]
            for r in range(rows):
                lines.append(tile[r * cols : (r + 1) * cols])
                lefts.append(left[t * rows + r : t * rows + r + 1])
                rights.append(right[t * rows + r : t * rows + r + 1])
            lines.append(below[t * cols : (t + 1) * cols])
            lefts.append(below[corner + t : corner + t + 1])
            rights.append(below[corner + frames + t : corner + frames + t + 1])
            totals = [None] * rows
            for r in range(rows + 2):
                before = jnp.where(place == 0, lefts[r], pltpu.roll(lines[r], 1, 0))
                after = jnp.where(place == cols - 1, rights[r], pltpu.roll(lines[r], cols - 1, 0))
                for a in range(3):
                    to = r - a
                    if 0 <= to < rows:
                        term = before * taps[a][0] + lines[r] * taps[a][1] + after * taps[a][2]
                        totals[to] = term if totals[to] is None else totals[to] + term
            mixed[t * rows * cols : (t + 1) * rows * cols, span] = jnp.concatenate(totals, axis=0).astype(jnp.bfloat16)
    value = jnp.dot(mixed[...], wv_ref[...], preferred_element_type=jnp.float32)
    hidden = (value * gate_ref[...]).astype(jnp.bfloat16)
    out_ref[...] = jnp.dot(hidden, wo_ref[...], preferred_element_type=jnp.float32).astype(jnp.bfloat16)


def body(latents, spatial_taps, kernel_taps, skip_gain, gate_weight, value_weight, out_weight):
    frames, rows, cols, chans = latents.shape
    lags = kernel_taps.shape[0]
    n_h, n_w = lax.axis_size("height"), lax.axis_size("width")
    sites = rows * cols
    lines = frames * rows
    bf16, f32 = jnp.bfloat16, jnp.float32
    x = latents.reshape(frames * sites, chans)

    clip = lax.all_gather(x, "tm", axis=0, tiled=True)
    gate = pl.pallas_call(
        gate_kernel,
        out_shape=jax.ShapeDtypeStruct(x.shape, f32),
        in_specs=[VMEM] * 2,
        out_specs=VMEM,
        compiler_params=PARAMS,
        cost_estimate=pl.CostEstimate(flops=2 * x.size * chans, bytes_accessed=2 * x.size * 4, transcendentals=x.size),
        name="gate",
    )(x, gate_weight)
    me = lax.axis_index("tm").astype(jnp.int32).reshape(1)
    u, left, right = pl.pallas_call(
        functools.partial(mix_kernel, frames, cols),
        out_shape=(
            jax.ShapeDtypeStruct(x.shape, bf16),
            jax.ShapeDtypeStruct((lines, chans), bf16),
            jax.ShapeDtypeStruct((lines, chans), bf16),
        ),
        in_specs=[SMEM, VMEM, VMEM, VMEM],
        out_specs=(VMEM, VMEM, VMEM),
        scratch_shapes=[pltpu.VMEM((2 * lags, cols, chans), f32), pltpu.VMEM((frames * sites, LANES), f32)],
        compiler_params=PARAMS,
        name="mix",
    )(me, clip, kernel_taps, skip_gain.reshape(1, chans))

    from_left = lax.ppermute(right, "width", [(i, i + 1) for i in range(n_w - 1)])
    from_right = lax.ppermute(left, "width", [(i + 1, i) for i in range(n_w - 1)])

    def border(row):
        pick = slice(row, row + 1)
        line = u.reshape(frames, rows, cols, chans)[:, row].reshape(frames * cols, chans)
        lhs = from_left.reshape(frames, rows, chans)[:, row]
        rhs = from_right.reshape(frames, rows, chans)[:, row]
        fill = jnp.zeros((-(frames * cols + 2 * frames) % 16, chans), bf16)
        return jnp.concatenate([line, lhs, rhs, fill], axis=0)

    h = lax.axis_index("height")
    top, bottom = border(0), border(rows - 1)
    if n_h == 2:
        above = below = lax.ppermute(jnp.where(h == 0, bottom, top), "height", [(0, 1), (1, 0)])
    else:
        above = lax.ppermute(bottom, "height", [(i, i + 1) for i in range(n_h - 1)])
        below = lax.ppermute(top, "height", [(i + 1, i) for i in range(n_h - 1)])
    at = jnp.stack([h > 0, h < n_h - 1]).astype(jnp.int32)

    out = pl.pallas_call(
        functools.partial(finish_kernel, frames, rows, cols),
        out_shape=jax.ShapeDtypeStruct(x.shape, bf16),
        in_specs=[SMEM] + [VMEM] * 9,
        out_specs=VMEM,
        scratch_shapes=[pltpu.VMEM(x.shape, bf16)],
        compiler_params=PARAMS,
        name="finish",
    )(at, u, from_left, from_right, above, below, spatial_taps.reshape(9, chans), gate, value_weight, out_weight)
    return out.reshape(latents.shape)


def solution(mesh):
    in_specs = (P("tm", "height", "width", None), P(), P(), P(), P(), P(), P())
    out_specs = P("tm", "height", "width", None)
    return jax.shard_map(body, mesh=mesh, in_specs=in_specs, out_specs=out_specs, check_vma=False)
```

```python
import functools

import jax
import jax.numpy as jnp
from jax import lax
from jax.experimental import pallas as pl
from jax.experimental.pallas import tpu as pltpu
from jax.sharding import PartitionSpec as P

LANES = 128
F32, BF16 = jnp.float32, jnp.bfloat16
VMEM = pl.BlockSpec(memory_space=pltpu.VMEM)


def call(kernel, name, outs, scratch, operands, flops=0, exps=0):
    moved = sum(a.size * a.dtype.itemsize for a in operands) + sum(a.size * a.dtype.itemsize for a in outs)
    return pl.pallas_call(
        kernel,
        out_shape=tuple(outs),
        in_specs=[VMEM] * len(operands),
        out_specs=(VMEM,) * len(outs),
        scratch_shapes=scratch,
        compiler_params=pltpu.CompilerParams(vmem_limit_bytes=24 * 1024 * 1024),
        cost_estimate=pl.CostEstimate(flops=flops, bytes_accessed=moved, transcendentals=exps),
        name=name,
    )(*operands)


def swaps(axis):
    n = lax.axis_size(axis)
    rounds = []
    for first in range(2 if n > 2 else 1):
        to = list(range(n))
        for i in range(first, n - 1, 2):
            to[i], to[i + 1] = i + 1, i
        rounds.append(list(enumerate(to)))
    return rounds


def position(axis):
    i, n = lax.axis_index(axis), lax.axis_size(axis)
    return lax.rem(i, 2) == 1, i > 0, i < n - 1


def received(axis, arrived):
    odd, lower, upper = position(axis)
    even_low, even_high = arrived[-1], arrived[0]
    low = jnp.where(odd, arrived[0], even_low)
    high = jnp.where(odd, arrived[-1], even_high)
    zero = jnp.zeros_like(low)
    return jnp.where(lower, low, zero), jnp.where(upper, high, zero)


def gate_kernel(x_ref, w_ref, gate_ref):
    v = jnp.dot(x_ref[...], w_ref[...], preferred_element_type=F32)
    gate_ref[...] = v / (1.0 + jnp.exp(-v))


def mix_kernel(frames, rows, cols, own_ref, partner_ref, taps_ref, skip_ref, fields_ref, lines_ref, *refs):
    *sides, table, held = refs
    lags, chans = taps_ref.shape
    block = rows * cols * frames
    pad = 2 * frames
    shift = jnp.where(lax.rem(lax.axis_index("tm"), 2) == 1, frames, -frames)
    odd, _, _ = position("width")
    taps = taps_ref[...].astype(F32)
    table[0:pad] = jnp.zeros((pad, cols, chans), F32)
    for lag in range(lags):
        tap = taps[lag : lag + 1] + (skip_ref[...] if lag == 0 else 0.0)
        table[pad + lag] = jnp.broadcast_to(tap, (cols, chans))
    sites = rows * cols
    for lane in range(0, chans, LANES):
        span = slice(lane, lane + LANES)
        for d in range(fields_ref.shape[0] // block):
            totals = [jnp.zeros((rows, cols, LANES), F32)] * frames
            for source, offset in ((own_ref, 0), (partner_ref, shift)):
                for s in range(frames):
                    x = source[s * sites : (s + 1) * sites, span].astype(F32).reshape(rows, cols, LANES)
                    for t in range(frames):
                        if source is own_ref and d == 0 and t < s:
                            continue
                        totals[t] = totals[t] + table[pad + 2 * d * frames + offset + t - s, :, span] * x
            for t in range(frames):
                held[t * sites : (t + 1) * sites, :] = totals[t].reshape(sites, LANES)
            fields_ref[d * block : (d + 1) * block, span] = held[...]
            first = held[pl.ds(0, frames * rows, stride=cols), :].astype(BF16)
            last = held[pl.ds(cols - 1, frames * rows, stride=cols), :].astype(BF16)
            out = slice(d * frames * rows, (d + 1) * frames * rows)
            sides[0][out, span] = jnp.where(odd, first, last)
            if len(sides) > 1:
                sides[1][out, span] = jnp.where(odd, last, first)
            for k, r in enumerate((0, rows - 1)):
                line = jnp.concatenate([t[r] for t in totals], axis=0).astype(BF16)
                at = (2 * d + k) * frames * cols
                lines_ref[at : at + frames * cols, span] = line


def border_kernel(frames, rows, cols, rounds_w, lines_ref, *refs):
    sides, outs = refs[:rounds_w], refs[rounds_w:]
    odd, _, _ = position("height")
    low, high = received("width", [s[...].astype(F32) for s in sides])
    size = outs[0].shape[0] * frames * rows // low.shape[0]
    fill = jnp.zeros((size - frames * cols - 2 * frames, low.shape[1]), F32)
    for d in range(low.shape[0] // (frames * rows)):
        ends = []
        for k, r in enumerate((0, rows - 1)):
            at = (2 * d + k) * frames * cols
            line = lines_ref[at : at + frames * cols].astype(F32)
            base = d * frames * rows + r
            lefts = [low[base + t * rows : base + t * rows + 1] for t in range(frames)]
            rights = [high[base + t * rows : base + t * rows + 1] for t in range(frames)]
            ends.append(jnp.concatenate([line] + lefts + rights + [fill], axis=0).astype(BF16))
        out = slice(d * size, (d + 1) * size)
        outs[0][out] = jnp.where(odd, ends[0], ends[1])
        if len(outs) > 1:
            outs[1][out] = jnp.where(odd, ends[1], ends[0])


def filter_kernel(frames, rows, cols, rounds_w, fields_ref, taps_ref, *refs):
    sides, ends, (mine_ref, *others) = refs[:rounds_w], refs[rounds_w : -2], refs[-2:]
    chans = fields_ref.shape[1]
    sites = rows * cols
    block = frames * sites
    count = fields_ref.shape[0] // block
    size = ends[0].shape[0] // count
    place = lax.broadcasted_iota(jnp.int32, (cols, LANES), 0)
    for lane in range(0, chans, LANES):
        span = slice(lane, lane + LANES)
        taps = [[taps_ref[3 * a + b : 3 * a + b + 1, span] for b in range(3)] for a in range(3)]
        low, high = received("width", [s[:, span].astype(F32) for s in sides])
        above, below = received("height", [e[:, span].astype(F32) for e in ends])
        for d in range(count):
            for t in range(frames):
                at = d * block + t * sites
                tile = fields_ref[at : at + sites, span]
                lines = [tile[r * cols : (r + 1) * cols] for r in range(rows)]
                side = (d * frames + t) * rows
                lefts = [low[side + r : side + r + 1] for r in range(rows)]
                rights = [high[side + r : side + r + 1] for r in range(rows)]
                for end, where in ((above, 0), (below, rows + 1)):
                    row = d * size + t * cols
                    corner = d * size + frames * cols + t
                    lines.insert(where, end[row : row + cols])
                    lefts.insert(where, end[corner : corner + 1])
                    rights.insert(where, end[corner + frames : corner + frames + 1])
                totals = [None] * rows
                for r in range(rows + 2):
                    before = jnp.where(place == 0, lefts[r], pltpu.roll(lines[r], 1, 0))
                    after = jnp.where(place == cols - 1, rights[r], pltpu.roll(lines[r], cols - 1, 0))
                    for a in range(3):
                        to = r - a
                        if 0 <= to < rows:
                            term = before * taps[a][0] + lines[r] * taps[a][1] + after * taps[a][2]
                            totals[to] = term if totals[to] is None else totals[to] + term
                total = jnp.concatenate(totals, axis=0)
                if d == 0:
                    mine_ref[at : at + sites, span] = total
                else:
                    others[0][at - block : at - block + sites, span] = total.astype(BF16)


def finish_kernel(mine_ref, gate_ref, wv_ref, wo_ref, *refs):
    *arrived, out_ref = refs
    chip = lax.div(lax.axis_index("tm"), 2)
    mixed = mine_ref[...]
    for d, ref in enumerate(arrived, 1):
        mixed = mixed + jnp.where(chip >= d, ref[...].astype(F32), 0.0)
    value = jnp.dot(mixed.astype(BF16), wv_ref[...], preferred_element_type=F32)
    hidden = (value * gate_ref[...]).astype(BF16)
    out_ref[...] = jnp.dot(hidden, wo_ref[...], preferred_element_type=F32).astype(BF16)


def body(latents, spatial_taps, kernel_taps, skip_gain, gate_weight, value_weight, out_weight):
    frames, rows, cols, chans = latents.shape
    lags = kernel_taps.shape[0]
    n_t = lax.axis_size("tm")
    chips = n_t // 2
    sites = rows * cols
    block = frames * sites
    shape = jax.ShapeDtypeStruct
    x = latents.reshape(block, chans)

    partner = lax.ppermute(x, "tm", [(i, i ^ 1) for i in range(n_t)])
    (gate,) = call(gate_kernel, "gate", [shape((block, chans), F32)], [], [x, gate_weight], 2 * block * chans * chans, x.size)

    w_rounds, h_rounds = swaps("width"), swaps("height")
    side = shape((chips * frames * rows, chans), BF16)
    fields, lines, *sides = call(
        functools.partial(mix_kernel, frames, rows, cols),
        "mix",
        [shape((chips * block, chans), F32), shape((chips * 2 * frames * cols, chans), BF16)] + [side] * len(w_rounds),
        [pltpu.VMEM((lags + 2 * frames, cols, chans), F32), pltpu.VMEM((block, LANES), F32)],
        [x, partner, kernel_taps, skip_gain.reshape(1, chans)],
        4 * chips * frames * x.size,
    )
    sides = [lax.ppermute(s, "width", pairs) for s, pairs in zip(sides, w_rounds)]

    size = -(-(frames * cols + 2 * frames) // 16) * 16
    ends = call(
        functools.partial(border_kernel, frames, rows, cols, len(w_rounds)),
        "border",
        [shape((chips * size, chans), BF16)] * len(h_rounds),
        [],
        [lines] + sides,
    )
    ends = [lax.ppermute(e, "height", pairs) for e, pairs in zip(ends, h_rounds)]

    mine, others = call(
        functools.partial(filter_kernel, frames, rows, cols, len(w_rounds)),
        "filter",
        [shape((block, chans), F32), shape(((chips - 1) * block, chans), BF16)],
        [],
        [fields, spatial_taps.reshape(9, chans)] + sides + ends,
        18 * chips * x.size,
    )
    arrived = [
        lax.ppermute(others[(d - 1) * block : d * block], "tm", [(i, (i + 2 * d) % n_t) for i in range(n_t)])
        for d in range(1, chips)
    ]
    (out,) = call(
        finish_kernel,
        "finish",
        [shape((block, chans), BF16)],
        [],
        [mine, gate, value_weight, out_weight] + arrived,
        4 * block * chans * chans,
    )
    return out.reshape(latents.shape)


def solution(mesh):
    in_specs = (P("tm", "height", "width", None), P(), P(), P(), P(), P(), P())
    out_specs = P("tm", "height", "width", None)
    return jax.shard_map(body, mesh=mesh, in_specs=in_specs, out_specs=out_specs, check_vma=False)
```

```python
import functools

import jax
import jax.numpy as jnp
from jax import lax
from jax.experimental import pallas as pl
from jax.experimental.pallas import tpu as pltpu
from jax.sharding import PartitionSpec as P

LANES = 128
F32, BF16 = jnp.float32, jnp.bfloat16
VMEM = pl.BlockSpec(memory_space=pltpu.VMEM)
HBM = pl.BlockSpec(memory_space=pltpu.HBM)


def call(kernel, name, outs, scratch, operands, flops=0, exps=0, far=0):
    operands = [pltpu.with_memory_space_constraint(a, pltpu.HBM) for a in operands[:far]] + list(operands[far:])
    moved = sum(a.size * a.dtype.itemsize for a in operands) + sum(a.size * a.dtype.itemsize for a in outs)
    return pl.pallas_call(
        kernel,
        out_shape=tuple(outs),
        in_specs=[HBM] * far + [VMEM] * (len(operands) - far),
        out_specs=(VMEM,) * len(outs),
        scratch_shapes=scratch,
        compiler_params=pltpu.CompilerParams(vmem_limit_bytes=24 * 1024 * 1024),
        cost_estimate=pl.CostEstimate(flops=flops, bytes_accessed=moved, transcendentals=exps),
        name=name,
    )(*operands)


def swaps(axis):
    n = lax.axis_size(axis)
    rounds = []
    for first in range(2 if n > 2 else 1):
        to = list(range(n))
        for i in range(first, n - 1, 2):
            to[i], to[i + 1] = i + 1, i
        rounds.append(list(enumerate(to)))
    return rounds


def position(axis):
    i, n = lax.axis_index(axis), lax.axis_size(axis)
    return lax.rem(i, 2) == 1, i > 0, i < n - 1


def received(axis, arrived):
    odd, lower, upper = position(axis)
    even_low, even_high = arrived[-1], arrived[0]
    low = jnp.where(odd, arrived[0], even_low)
    high = jnp.where(odd, arrived[-1], even_high)
    zero = jnp.zeros_like(low)
    return jnp.where(lower, low, zero), jnp.where(upper, high, zero)


def early_kernel(frames, rows, cols, *refs):
    far, (gate_ref, fields_ref, table_ref), near, arrived = refs[:4], refs[4:7], refs[7:11], refs[11]
    copies = [pltpu.make_async_copy(a, b, arrived.at[i]) for i, (a, b) in enumerate(zip(far, near))]
    for copy in copies:
        copy.start()
    taps_ref, skip_ref, x_ref, w_ref = near
    lags, chans = taps_ref.shape
    copies[0].wait()
    copies[1].wait()
    pad = 2 * frames
    taps = taps_ref[...].astype(F32)
    table_ref[0:pad] = jnp.zeros((pad, cols, chans), F32)
    for lag in range(lags):
        tap = taps[lag : lag + 1] + (skip_ref[...] if lag == 0 else 0.0)
        table_ref[pad + lag] = jnp.broadcast_to(tap, (cols, chans))
    sites = rows * cols
    block = frames * sites
    copies[2].wait()
    for lane in range(0, chans, LANES):
        span = slice(lane, lane + LANES)
        for d in range(fields_ref.shape[0] // block):
            totals = [None] * frames
            for s in range(frames):
                x = x_ref[s * sites : (s + 1) * sites, span].astype(F32).reshape(rows, cols, LANES)
                for t in range(s if d == 0 else 0, frames):
                    term = table_ref[pad + 2 * d * frames + t - s, :, span] * x
                    totals[t] = term if totals[t] is None else totals[t] + term
            for t in range(frames):
                at = d * block + t * sites
                fields_ref[at : at + sites, span] = totals[t].reshape(sites, LANES)
    copies[3].wait()
    v = jnp.dot(x_ref[...], w_ref[...], preferred_element_type=F32)
    gate_ref[...] = v / (1.0 + jnp.exp(-v))


def mix_kernel(frames, rows, cols, rounds_w, rounds_h, partner_ref, fields_ref, table_ref, mine_ref, *refs):
    *outs, held = refs
    sites = rows * cols
    block = frames * sites
    pad = 2 * frames
    shift = jnp.where(lax.rem(lax.axis_index("tm"), 2) == 1, frames, -frames)
    odd_w, odd_h = position("width")[0], position("height")[0]
    for lane in range(0, mine_ref.shape[1], LANES):
        span = slice(lane, lane + LANES)
        outs_left = list(outs)
        for d in range(fields_ref.shape[0] // block):
            totals = []
            for t in range(frames):
                at = d * block + t * sites
                totals.append(fields_ref[at : at + sites, span].reshape(rows, cols, LANES))
            for s in range(frames):
                x = partner_ref[s * sites : (s + 1) * sites, span].astype(F32).reshape(rows, cols, LANES)
                for t in range(frames):
                    totals[t] = totals[t] + table_ref[pad + 2 * d * frames + shift + t - s, :, span] * x
            for t in range(frames):
                held[t * sites : (t + 1) * sites, :] = totals[t].reshape(sites, LANES)
            first = held[pl.ds(0, frames * rows, stride=cols), :].astype(BF16)
            last = held[pl.ds(cols - 1, frames * rows, stride=cols), :].astype(BF16)
            for k in range(rounds_w):
                outs_left.pop(0)[:, span] = jnp.where(odd_w, last, first) if k else jnp.where(odd_w, first, last)
            if d == 0:
                mine_ref[:, span] = held[...]
                continue
            top = jnp.concatenate([t[0] for t in totals], axis=0).astype(BF16)
            bottom = jnp.concatenate([t[rows - 1] for t in totals], axis=0).astype(BF16)
            lines_ref = outs_left.pop(0)
            for k in range(rounds_h):
                line = jnp.where(odd_h, bottom, top) if k else jnp.where(odd_h, top, bottom)
                lines_ref[k * frames * cols : (k + 1) * frames * cols, span] = line
            outs_left.pop(0)[:, span] = held[...]


def round_kernel(x_ref, out_ref):
    out_ref[...] = x_ref[...].astype(BF16)


def later(d, value):
    return jnp.where(lax.div(lax.axis_index("tm"), 2) >= d, value, jnp.zeros_like(value))


def border_kernel(frames, rows, cols, rounds_w, chips, mine_ref, *refs):
    ins, (low_ref, high_ref, *outs) = refs[: chips * rounds_w + chips - 1], refs[chips * rounds_w + chips - 1 :]
    sites = rows * cols
    odd, _, _ = position("height")
    low = high = None
    lines = []
    for d in range(chips):
        sides, ins = ins[:rounds_w], ins[rounds_w:]
        arrived = received("width", [s[...].astype(F32) for s in sides])
        if d == 0:
            low, high = arrived
        else:
            low, high = low + later(d, arrived[0]), high + later(d, arrived[1])
            lines.append(ins[0])
            ins = ins[1:]
    low_ref[...] = low
    high_ref[...] = high
    size = frames * cols
    fill = jnp.zeros((outs[0].shape[0] - size - 2 * frames, low.shape[1]), F32)
    for k, out in enumerate(outs):
        ends = []
        for r in (0, rows - 1):
            line = [mine_ref[t * sites + r * cols : t * sites + (r + 1) * cols] for t in range(frames)]
            lefts = [low[t * rows + r : t * rows + r + 1] for t in range(frames)]
            rights = [high[t * rows + r : t * rows + r + 1] for t in range(frames)]
            ends.append((jnp.concatenate(line, axis=0), jnp.concatenate(lefts + rights + [fill], axis=0)))
        pick = lambda j: jnp.where(odd, ends[1][j], ends[0][j]) if k else jnp.where(odd, ends[0][j], ends[1][j])
        line = pick(0)
        for d, ref in enumerate(lines, 1):
            line = line + later(d, ref[k * size : (k + 1) * size].astype(F32))
        out[...] = jnp.concatenate([line, pick(1)], axis=0).astype(BF16)


def finish_kernel(frames, rows, cols, rounds_h, mine_ref, low_ref, high_ref, taps_ref, gate_ref, wv_ref, wo_ref, *refs):
    ends, wholes, (out_ref, mixed) = refs[:rounds_h], refs[rounds_h:-2], refs[-2:]
    chans = mine_ref.shape[1]
    sites = rows * cols
    place = lax.broadcasted_iota(jnp.int32, (cols, LANES), 0)
    corner = frames * cols
    for lane in range(0, chans, LANES):
        span = slice(lane, lane + LANES)
        taps = [[taps_ref[3 * a + b : 3 * a + b + 1, span] for b in range(3)] for a in range(3)]
        low, high = low_ref[:, span], high_ref[:, span]
        above, below = received("height", [e[:, span].astype(F32) for e in ends])
        for t in range(frames):
            at = t * sites
            tile = mine_ref[at : at + sites, span]
            for d, ref in enumerate(wholes, 1):
                tile = tile + later(d, ref[at : at + sites, span].astype(F32))
            lines = [tile[r * cols : (r + 1) * cols] for r in range(rows)]
            lefts = [low[t * rows + r : t * rows + r + 1] for r in range(rows)]
            rights = [high[t * rows + r : t * rows + r + 1] for r in range(rows)]
            for end, where in ((above, 0), (below, rows + 1)):
                lines.insert(where, end[t * cols : (t + 1) * cols])
                lefts.insert(where, end[corner + t : corner + t + 1])
                rights.insert(where, end[corner + frames + t : corner + frames + t + 1])
            totals = [None] * rows
            for r in range(rows + 2):
                before = jnp.where(place == 0, lefts[r], pltpu.roll(lines[r], 1, 0))
                after = jnp.where(place == cols - 1, rights[r], pltpu.roll(lines[r], cols - 1, 0))
                for a in range(3):
                    to = r - a
                    if 0 <= to < rows:
                        term = before * taps[a][0] + lines[r] * taps[a][1] + after * taps[a][2]
                        totals[to] = term if totals[to] is None else totals[to] + term
            mixed[at : at + sites, span] = jnp.concatenate(totals, axis=0).astype(BF16)
    value = jnp.dot(mixed[...], wv_ref[...], preferred_element_type=F32)
    hidden = (value * gate_ref[...]).astype(BF16)
    out_ref[...] = jnp.dot(hidden, wo_ref[...], preferred_element_type=F32).astype(BF16)


def body(latents, spatial_taps, kernel_taps, skip_gain, gate_weight, value_weight, out_weight):
    frames, rows, cols, chans = latents.shape
    lags = kernel_taps.shape[0]
    n_t, n_w = lax.axis_size("tm"), lax.axis_size("width")
    chips = n_t // 2
    block = frames * rows * cols
    shape = jax.ShapeDtypeStruct
    x = latents.reshape(block, chans)

    partner = lax.ppermute(x, "tm", [(i, i ^ 1) for i in range(n_t)])
    inputs = [kernel_taps, skip_gain.reshape(1, chans), x, gate_weight]
    gate, fields, table = call(
        functools.partial(early_kernel, frames, rows, cols),
        "early",
        [
            shape((block, chans), F32),
            shape((chips * block, chans), F32),
            shape((lags + 2 * frames, cols, chans), F32),
        ],
        [pltpu.VMEM(a.shape, a.dtype) for a in inputs] + [pltpu.SemaphoreType.DMA((len(inputs),))],
        inputs,
        2 * block * chans * chans,
        x.size,
        far=len(inputs),
    )

    w_rounds, h_rounds = swaps("width"), swaps("height")
    sides = [shape((frames * rows, chans), BF16)] * len(w_rounds)
    lines = shape((len(h_rounds) * frames * cols, chans), BF16)
    mine, *sent = call(
        functools.partial(mix_kernel, frames, rows, cols, len(w_rounds), len(h_rounds)),
        "mix",
        [shape((block, chans), F32)] + sides + (sides + [lines, shape((block, chans), F32)]) * (chips - 1),
        [pltpu.VMEM((block, LANES), F32)],
        [partner, fields, table],
        2 * chips * frames * x.size,
    )
    borders, wholes = [], []
    for d in range(chips):
        for pairs in w_rounds:
            route = [(i * n_w + a, (i + 2 * d) % n_t * n_w + b) for i in range(n_t) for a, b in pairs]
            borders.append(lax.ppermute(sent.pop(0), ("tm", "width"), route))
        if d:
            route = [(i, (i + 2 * d) % n_t) for i in range(n_t)]
            borders.append(lax.ppermute(sent.pop(0), "tm", route))
            (whole,) = call(round_kernel, "round", [shape((block, chans), BF16)], [], [sent.pop(0)])
            wholes.append(lax.ppermute(whole, "tm", route))

    size = -(-(frames * cols + 2 * frames) // 16) * 16
    low, high, *ends = call(
        functools.partial(border_kernel, frames, rows, cols, len(w_rounds), chips),
        "border",
        [shape((frames * rows, chans), F32)] * 2 + [shape((size, chans), BF16)] * len(h_rounds),
        [],
        [mine] + borders,
    )
    ends = [lax.ppermute(e, "height", pairs) for e, pairs in zip(ends, h_rounds)]

    (out,) = call(
        functools.partial(finish_kernel, frames, rows, cols, len(h_rounds)),
        "finish",
        [shape((block, chans), BF16)],
        [pltpu.VMEM((block, chans), BF16)],
        [mine, low, high, spatial_taps.reshape(9, chans), gate, value_weight, out_weight] + ends + wholes,
        4 * block * chans * chans,
    )
    return out.reshape(latents.shape)


def solution(mesh):
    in_specs = (P("tm", "height", "width", None), P(), P(), P(), P(), P(), P())
    out_specs = P("tm", "height", "width", None)
    return jax.shard_map(body, mesh=mesh, in_specs=in_specs, out_specs=out_specs, check_vma=False)
```

```python
import functools

import jax
import jax.numpy as jnp
from jax import lax
from jax.experimental import pallas as pl
from jax.experimental.pallas import tpu as pltpu
from jax.sharding import PartitionSpec as P

LANES = 128
F32, BF16 = jnp.float32, jnp.bfloat16
VMEM = pl.BlockSpec(memory_space=pltpu.VMEM)
HBM = pl.BlockSpec(memory_space=pltpu.HBM)


def call(kernel, name, outs, scratch, operands, flops=0, exps=0, far=0):
    operands = [pltpu.with_memory_space_constraint(a, pltpu.HBM) for a in operands[:far]] + list(operands[far:])
    moved = sum(a.size * a.dtype.itemsize for a in operands) + sum(a.size * a.dtype.itemsize for a in outs)
    return pl.pallas_call(
        kernel,
        out_shape=tuple(outs),
        in_specs=[HBM] * far + [VMEM] * (len(operands) - far),
        out_specs=(VMEM,) * len(outs),
        scratch_shapes=scratch,
        compiler_params=pltpu.CompilerParams(vmem_limit_bytes=24 * 1024 * 1024),
        cost_estimate=pl.CostEstimate(flops=flops, bytes_accessed=moved, transcendentals=exps),
        name=name,
    )(*operands)


def swaps(axis):
    n = lax.axis_size(axis)
    rounds = []
    for first in range(2 if n > 2 else 1):
        to = list(range(n))
        for i in range(first, n - 1, 2):
            to[i], to[i + 1] = i + 1, i
        rounds.append(list(enumerate(to)))
    return rounds


def position(axis):
    i, n = lax.axis_index(axis), lax.axis_size(axis)
    return lax.rem(i, 2) == 1, i > 0, i < n - 1


def received(axis, arrived):
    odd, lower, upper = position(axis)
    even_low, even_high = arrived[-1], arrived[0]
    low = jnp.where(odd, arrived[0], even_low)
    high = jnp.where(odd, arrived[-1], even_high)
    zero = jnp.zeros_like(low)
    return jnp.where(lower, low, zero), jnp.where(upper, high, zero)


def early_kernel(frames, rows, cols, *refs):
    far, (gate_ref, fields_ref, table_ref), near, arrived = refs[:4], refs[4:7], refs[7:11], refs[11]
    copies = [pltpu.make_async_copy(a, b, arrived.at[i]) for i, (a, b) in enumerate(zip(far, near))]
    for copy in copies:
        copy.start()
    taps_ref, skip_ref, x_ref, w_ref = near
    lags, chans = taps_ref.shape
    copies[0].wait()
    copies[1].wait()
    pad = 2 * frames
    taps = taps_ref[...].astype(F32)
    table_ref[0:pad] = jnp.zeros((pad, cols, chans), F32)
    for lag in range(lags):
        tap = taps[lag : lag + 1] + (skip_ref[...] if lag == 0 else 0.0)
        table_ref[pad + lag] = jnp.broadcast_to(tap, (cols, chans))
    sites = rows * cols
    block = frames * sites
    copies[2].wait()
    for lane in range(0, chans, LANES):
        span = slice(lane, lane + LANES)
        for d in range(fields_ref.shape[0] // block):
            totals = [None] * frames
            for s in range(frames):
                x = x_ref[s * sites : (s + 1) * sites, span].astype(F32).reshape(rows, cols, LANES)
                for t in range(s if d == 0 else 0, frames):
                    term = table_ref[pad + 2 * d * frames + t - s, :, span] * x
                    totals[t] = term if totals[t] is None else totals[t] + term
            for t in range(frames):
                at = d * block + t * sites
                fields_ref[at : at + sites, span] = totals[t].reshape(sites, LANES)
    copies[3].wait()
    v = jnp.dot(x_ref[...], w_ref[...], preferred_element_type=F32)
    gate_ref[...] = v / (1.0 + jnp.exp(-v))


def mix_kernel(frames, rows, cols, rounds_w, partner_ref, fields_ref, table_ref, mine_ref, *refs):
    *outs, held = refs
    sites = rows * cols
    block = frames * sites
    pad = 2 * frames
    shift = jnp.where(lax.rem(lax.axis_index("tm"), 2) == 1, frames, -frames)
    odd = position("width")[0]
    for lane in range(0, mine_ref.shape[1], LANES):
        span = slice(lane, lane + LANES)
        outs_left = list(outs)
        for d in range(fields_ref.shape[0] // block):
            totals = []
            for t in range(frames):
                at = d * block + t * sites
                totals.append(fields_ref[at : at + sites, span].reshape(rows, cols, LANES))
            for s in range(frames):
                x = partner_ref[s * sites : (s + 1) * sites, span].astype(F32).reshape(rows, cols, LANES)
                for t in range(frames):
                    totals[t] = totals[t] + table_ref[pad + 2 * d * frames + shift + t - s, :, span] * x
            for t in range(frames):
                held[t * sites : (t + 1) * sites, :] = totals[t].reshape(sites, LANES)
            first = held[pl.ds(0, frames * rows, stride=cols), :].astype(BF16)
            last = held[pl.ds(cols - 1, frames * rows, stride=cols), :].astype(BF16)
            for k in range(rounds_w):
                outs_left.pop(0)[:, span] = jnp.where(odd, last, first) if k else jnp.where(odd, first, last)
            if d == 0:
                mine_ref[:, span] = held[...]
                continue
            outs_left.pop(0)[:, span] = held[...].astype(BF16)


def later(d, value):
    return jnp.where(lax.div(lax.axis_index("tm"), 2) >= d, value, jnp.zeros_like(value))


def border_kernel(frames, rows, cols, rounds_w, chips, mine_ref, *refs):
    sides, wholes = refs[: chips * rounds_w], refs[chips * rounds_w : chips * rounds_w + chips - 1]
    low_ref, high_ref, *outs = refs[chips * rounds_w + chips - 1 :]
    sites = rows * cols
    odd, _, _ = position("height")
    low = high = None
    for d in range(chips):
        arrived = received("width", [s[...].astype(F32) for s in sides[d * rounds_w : (d + 1) * rounds_w]])
        if d == 0:
            low, high = arrived
        else:
            low, high = low + later(d, arrived[0]), high + later(d, arrived[1])
    low_ref[...] = low
    high_ref[...] = high
    fill = jnp.zeros((outs[0].shape[0] - frames * cols - 2 * frames, low.shape[1]), F32)
    ends = []
    for r in (0, rows - 1):
        lines = []
        for t in range(frames):
            at = t * sites + r * cols
            line = mine_ref[at : at + cols]
            for d, ref in enumerate(wholes, 1):
                line = line + later(d, ref[at : at + cols].astype(F32))
            lines.append(line)
        lefts = [low[t * rows + r : t * rows + r + 1] for t in range(frames)]
        rights = [high[t * rows + r : t * rows + r + 1] for t in range(frames)]
        ends.append(jnp.concatenate(lines + lefts + rights + [fill], axis=0))
    for k, out in enumerate(outs):
        out[...] = (jnp.where(odd, ends[1], ends[0]) if k else jnp.where(odd, ends[0], ends[1])).astype(BF16)


def shifted(line, left, right):
    cols = line.shape[0]
    place = lax.broadcasted_iota(jnp.int32, line.shape, 0)
    before = jnp.where(place == 0, left, pltpu.roll(line, 1, 0))
    after = jnp.where(place == cols - 1, right, pltpu.roll(line, cols - 1, 0))
    return before, line, after


def projected(mixed, gate, wv_ref, wo_ref):
    value = jnp.dot(mixed, wv_ref[...], preferred_element_type=F32)
    hidden = (value * gate).astype(BF16)
    return jnp.dot(hidden, wo_ref[...], preferred_element_type=F32).astype(BF16)


def inner_kernel(frames, rows, cols, mine_ref, low_ref, high_ref, taps_ref, gate_ref, wv_ref, wo_ref, *refs):
    *wholes, out_ref, edges_ref, mixed = refs
    chans = mine_ref.shape[1]
    sites = rows * cols
    for lane in range(0, chans, LANES):
        span = slice(lane, lane + LANES)
        taps = [[taps_ref[3 * a + b : 3 * a + b + 1, span] for b in range(3)] for a in range(3)]
        low, high = low_ref[:, span], high_ref[:, span]
        for t in range(frames):
            at = t * sites
            tile = mine_ref[at : at + sites, span]
            for d, ref in enumerate(wholes, 1):
                tile = tile + later(d, ref[at : at + sites, span].astype(F32))
            totals = [None] * rows
            for r in range(rows):
                row = t * rows + r
                near = shifted(tile[r * cols : (r + 1) * cols], low[row : row + 1], high[row : row + 1])
                for a in range(3):
                    to = r + 1 - a
                    if 0 <= to < rows:
                        term = near[0] * taps[a][0] + near[1] * taps[a][1] + near[2] * taps[a][2]
                        totals[to] = term if totals[to] is None else totals[to] + term
            mixed[at : at + sites, span] = jnp.concatenate(totals, axis=0).astype(BF16)
            edges_ref[t * cols : (t + 1) * cols, span] = totals[0]
            edges_ref[(frames + t) * cols : (frames + t + 1) * cols, span] = totals[rows - 1]
    out_ref[...] = projected(mixed[...], gate_ref[...], wv_ref, wo_ref)


def edge_kernel(frames, rows, cols, rounds_h, edges_ref, taps_ref, gate_ref, wv_ref, wo_ref, inner_ref, *refs):
    ends, out_ref = refs[:rounds_h], refs[rounds_h]
    sites = rows * cols
    size = frames * cols
    odd, _, _ = position("height")
    out_ref[...] = inner_ref[...]
    taps = taps_ref[...]
    mixed, gate = [], []
    for k, end in enumerate(ends):
        end = end[...].astype(F32)
        first = jnp.logical_not(odd) if k else odd
        lefts, rights = end[size : size + frames], end[size + frames : size + 2 * frames]
        lower, upper = position("height")[1:]
        exists = jnp.where(first, lower, upper)
        tap = jnp.where(first, taps[0:3], taps[6:9])
        total = jnp.where(first, edges_ref[0:size], edges_ref[size : 2 * size])
        for t in range(frames):
            near = shifted(end[t * cols : (t + 1) * cols], lefts[t : t + 1], rights[t : t + 1])
            more = near[0] * tap[0:1] + near[1] * tap[1:2] + near[2] * tap[2:3]
            mixed.append(total[t * cols : (t + 1) * cols] + jnp.where(exists, more, jnp.zeros_like(more)))
            at = t * sites
            gate.append(jnp.where(first, gate_ref[at : at + cols], gate_ref[at + sites - cols : at + sites]))
    out = projected(jnp.concatenate(mixed, axis=0).astype(BF16), jnp.concatenate(gate, axis=0), wv_ref, wo_ref)
    for t in range(frames):
        new = [out[k * size + t * cols : k * size + (t + 1) * cols] for k in range(rounds_h)]
        for at, other in ((t * sites, False), (t * sites + sites - cols, True)):
            kept = new[1] if rounds_h > 1 else inner_ref[at : at + cols]
            out_ref[at : at + cols] = jnp.where(odd, kept, new[0]) if other else jnp.where(odd, new[0], kept)


def body(latents, spatial_taps, kernel_taps, skip_gain, gate_weight, value_weight, out_weight):
    frames, rows, cols, chans = latents.shape
    lags = kernel_taps.shape[0]
    n_t, n_w = lax.axis_size("tm"), lax.axis_size("width")
    chips = n_t // 2
    block = frames * rows * cols
    shape = jax.ShapeDtypeStruct
    x = latents.reshape(block, chans)

    partner = lax.ppermute(x, "tm", [(i, i ^ 1) for i in range(n_t)])
    inputs = [kernel_taps, skip_gain.reshape(1, chans), x, gate_weight]
    gate, fields, table = call(
        functools.partial(early_kernel, frames, rows, cols),
        "early",
        [
            shape((block, chans), F32),
            shape((chips * block, chans), F32),
            shape((lags + 2 * frames, cols, chans), F32),
        ],
        [pltpu.VMEM(a.shape, a.dtype) for a in inputs] + [pltpu.SemaphoreType.DMA((len(inputs),))],
        inputs,
        2 * block * chans * chans,
        x.size,
        far=len(inputs),
    )

    w_rounds, h_rounds = swaps("width"), swaps("height")
    sides = [shape((frames * rows, chans), BF16)] * len(w_rounds)
    mine, *sent = call(
        functools.partial(mix_kernel, frames, rows, cols, len(w_rounds)),
        "mix",
        [shape((block, chans), F32)] + sides + (sides + [shape((block, chans), BF16)]) * (chips - 1),
        [pltpu.VMEM((block, LANES), F32)],
        [partner, fields, table],
        2 * chips * frames * x.size,
    )
    borders, wholes = [], []
    for d in range(chips):
        for pairs in w_rounds:
            route = [(i * n_w + a, (i + 2 * d) % n_t * n_w + b) for i in range(n_t) for a, b in pairs]
            borders.append(lax.ppermute(sent.pop(0), ("tm", "width"), route))
        if d:
            wholes.append(lax.ppermute(sent.pop(0), "tm", [(i, (i + 2 * d) % n_t) for i in range(n_t)]))

    size = -(-(frames * cols + 2 * frames) // 16) * 16
    low, high, *ends = call(
        functools.partial(border_kernel, frames, rows, cols, len(w_rounds), chips),
        "border",
        [shape((frames * rows, chans), F32)] * 2 + [shape((size, chans), BF16)] * len(h_rounds),
        [],
        [mine] + borders + wholes,
    )
    ends = [lax.ppermute(e, "height", pairs) for e, pairs in zip(ends, h_rounds)]

    taps = spatial_taps.reshape(9, chans)
    inner, edges = call(
        functools.partial(inner_kernel, frames, rows, cols),
        "inner",
        [shape((block, chans), BF16), shape((2 * frames * cols, chans), F32)],
        [pltpu.VMEM((block, chans), BF16)],
        [mine, low, high, taps, gate, value_weight, out_weight] + wholes,
        4 * block * chans * chans,
    )
    (out,) = call(
        functools.partial(edge_kernel, frames, rows, cols, len(h_rounds)),
        "edge",
        [shape((block, chans), BF16)],
        [],
        [edges, taps, gate, value_weight, out_weight, inner] + ends,
        4 * frames * cols * chans * chans,
    )
    return out.reshape(latents.shape)


def solution(mesh):
    in_specs = (P("tm", "height", "width", None), P(), P(), P(), P(), P(), P())
    out_specs = P("tm", "height", "width", None)
    return jax.shard_map(body, mesh=mesh, in_specs=in_specs, out_specs=out_specs, check_vma=False)
```

```python
import functools

import jax
import jax.numpy as jnp
from jax import lax
from jax.experimental import pallas as pl
from jax.experimental.pallas import tpu as pltpu
from jax.sharding import PartitionSpec as P

LANES = 128
F32, BF16 = jnp.float32, jnp.bfloat16
VMEM = pl.BlockSpec(memory_space=pltpu.VMEM)
HBM = pl.BlockSpec(memory_space=pltpu.HBM)


def call(kernel, name, outs, scratch, operands, flops=0, exps=0, far=0):
    operands = [pltpu.with_memory_space_constraint(a, pltpu.HBM) for a in operands[:far]] + list(operands[far:])
    moved = sum(a.size * a.dtype.itemsize for a in operands) + sum(a.size * a.dtype.itemsize for a in outs)
    return pl.pallas_call(
        kernel,
        out_shape=tuple(outs),
        in_specs=[HBM] * far + [VMEM] * (len(operands) - far),
        out_specs=(VMEM,) * len(outs),
        scratch_shapes=scratch,
        compiler_params=pltpu.CompilerParams(vmem_limit_bytes=24 * 1024 * 1024),
        cost_estimate=pl.CostEstimate(flops=flops, bytes_accessed=moved, transcendentals=exps),
        name=name,
    )(*operands)


def swaps(axis):
    n = lax.axis_size(axis)
    rounds = []
    for first in range(2 if n > 2 else 1):
        to = list(range(n))
        for i in range(first, n - 1, 2):
            to[i], to[i + 1] = i + 1, i
        rounds.append(list(enumerate(to)))
    return rounds


def position(axis):
    i, n = lax.axis_index(axis), lax.axis_size(axis)
    return lax.rem(i, 2) == 1, i > 0, i < n - 1


def right_core():
    return lax.rem(lax.axis_index("tm"), 2) == 1


def outer_column(ref, lines, cols):
    return jnp.where(right_core(), ref[pl.ds(cols - 1, lines, stride=cols), :], ref[pl.ds(0, lines, stride=cols), :])


def early_kernel(frames, rows, cols, *refs):
    far, (gate_ref, fields_ref, table_ref, side_ref), near, (arrived, held) = refs[:4], refs[4:8], refs[8:12], refs[12:]
    copies = [pltpu.make_async_copy(a, b, arrived.at[i]) for i, (a, b) in enumerate(zip(far, near))]
    for copy in copies:
        copy.start()
    taps_ref, skip_ref, x_ref, w_ref = near
    lags, chans = taps_ref.shape
    copies[0].wait()
    copies[1].wait()
    pad = 2 * frames
    taps = taps_ref[...].astype(F32)
    table_ref[0:pad] = jnp.zeros((pad, cols, chans), F32)
    for lag in range(lags):
        tap = taps[lag : lag + 1] + (skip_ref[...] if lag == 0 else 0.0)
        table_ref[pad + lag] = jnp.broadcast_to(tap, (cols, chans))
    sites = rows * cols
    block = frames * sites
    copies[2].wait()
    for lane in range(0, chans, LANES):
        span = slice(lane, lane + LANES)
        held[...] = x_ref[:, span].astype(F32)
        side_ref[:, span] = outer_column(held, frames * rows, cols)
        for d in range(fields_ref.shape[0] // block):
            totals = [None] * frames
            for s in range(frames):
                x = x_ref[s * sites : (s + 1) * sites, span].astype(F32).reshape(rows, cols, LANES)
                for t in range(s if d == 0 else 0, frames):
                    term = table_ref[pad + 2 * d * frames + t - s, :, span] * x
                    totals[t] = term if totals[t] is None else totals[t] + term
            for t in range(frames):
                at = d * block + t * sites
                fields_ref[at : at + sites, span] = totals[t].reshape(sites, LANES)
    copies[3].wait()
    v = jnp.dot(x_ref[...], w_ref[...], preferred_element_type=F32)
    gate_ref[...] = v / (1.0 + jnp.exp(-v))


def mix_kernel(frames, rows, cols, partner_ref, fields_ref, table_ref, side_ref, mine_ref, *refs):
    *outs, held = refs
    sites = rows * cols
    lines = frames * rows
    block = frames * sites
    pad = 2 * frames
    shift = jnp.where(right_core(), frames, -frames)
    for lane in range(0, mine_ref.shape[1], LANES):
        span = slice(lane, lane + LANES)
        held[...] = partner_ref[:, span].astype(F32)
        near = [side_ref[s * rows : (s + 1) * rows, span] for s in range(frames)]
        far = outer_column(held, lines, cols)
        for d in range(fields_ref.shape[0] // block):
            totals = []
            for t in range(frames):
                at = d * block + t * sites
                totals.append(fields_ref[at : at + sites, span].reshape(rows, cols, LANES))
            base = pad + 2 * d * frames
            for s in range(frames):
                x = partner_ref[s * sites : (s + 1) * sites, span].astype(F32).reshape(rows, cols, LANES)
                for t in range(frames):
                    totals[t] = totals[t] + table_ref[base + shift + t - s, :, span] * x
            for t in range(frames):
                held[t * sites : (t + 1) * sites, :] = totals[t].reshape(sites, LANES)
            if d:
                outs[2 * d][:, span] = held[...].astype(BF16)
            else:
                mine_ref[:, span] = held[...]
            ends = []
            for t in range(frames):
                end = jnp.zeros((rows, LANES), F32)
                for s in range(frames):
                    end = end + table_ref[base - shift + t - s, :, span] * near[s]
                    if d or t >= s:
                        end = end + table_ref[base + t - s, :, span] * far[s * rows : (s + 1) * rows]
                ends.append(end)
            column = jnp.concatenate([outer_column(held, lines, cols)] + ends, axis=0)
            outs[2 * d - 1 if d else 0][:, span] = column.astype(BF16)


def later(d, value):
    return jnp.where(lax.div(lax.axis_index("tm"), 2) >= d, value, jnp.zeros_like(value))


def side_kernel(lines, *refs):
    *arrived, own_ref, other_ref = refs
    _, lower, upper = position("width")
    exists = jnp.where(right_core(), upper, lower)
    total = 0.0
    for d, ref in enumerate(arrived):
        total = total + later(d, ref[...].astype(F32))
    total = jnp.where(exists, total, jnp.zeros_like(total))
    other_ref[...] = total[:lines].astype(BF16)
    own_ref[...] = total[lines:]


def border_kernel(frames, rows, cols, mine_ref, own_ref, other_ref, *refs):
    n = sum(ref.shape == mine_ref.shape for ref in refs)
    wholes, (low_ref, high_ref, *outs) = refs[:n], refs[n:]
    sites = rows * cols
    odd, _, _ = position("height")
    right, own, other = right_core(), own_ref[...], other_ref[...].astype(F32)
    low, high = jnp.where(right, other, own), jnp.where(right, own, other)
    low_ref[...] = low
    high_ref[...] = high
    fill = jnp.zeros((outs[0].shape[0] - frames * cols - 2 * frames, low.shape[1]), F32)
    ends = []
    for r in (0, rows - 1):
        lines = []
        for t in range(frames):
            at = t * sites + r * cols
            line = mine_ref[at : at + cols]
            for d, ref in enumerate(wholes, 1):
                line = line + later(d, ref[at : at + cols].astype(F32))
            lines.append(line)
        lefts = [low[t * rows + r : t * rows + r + 1] for t in range(frames)]
        rights = [high[t * rows + r : t * rows + r + 1] for t in range(frames)]
        ends.append(jnp.concatenate(lines + lefts + rights + [fill], axis=0))
    for k, out in enumerate(outs):
        out[...] = (jnp.where(odd, ends[1], ends[0]) if k else jnp.where(odd, ends[0], ends[1])).astype(BF16)


def shifted(line, left, right):
    cols = line.shape[0]
    place = lax.broadcasted_iota(jnp.int32, line.shape, 0)
    before = jnp.where(place == 0, left, pltpu.roll(line, 1, 0))
    after = jnp.where(place == cols - 1, right, pltpu.roll(line, cols - 1, 0))
    return before, line, after


def projected(mixed, gate, wv_ref, wo_ref):
    value = jnp.dot(mixed, wv_ref[...], preferred_element_type=F32)
    hidden = (value * gate).astype(BF16)
    return jnp.dot(hidden, wo_ref[...], preferred_element_type=F32).astype(BF16)


def inner_kernel(frames, rows, cols, mine_ref, low_ref, high_ref, taps_ref, gate_ref, wv_ref, wo_ref, *refs):
    *wholes, out_ref, edges_ref, mixed = refs
    chans = mine_ref.shape[1]
    sites = rows * cols
    for lane in range(0, chans, LANES):
        span = slice(lane, lane + LANES)
        taps = [[taps_ref[3 * a + b : 3 * a + b + 1, span] for b in range(3)] for a in range(3)]
        low, high = low_ref[:, span], high_ref[:, span]
        for t in range(frames):
            at = t * sites
            tile = mine_ref[at : at + sites, span]
            for d, ref in enumerate(wholes, 1):
                tile = tile + later(d, ref[at : at + sites, span].astype(F32))
            totals = [None] * rows
            for r in range(rows):
                row = t * rows + r
                near = shifted(tile[r * cols : (r + 1) * cols], low[row : row + 1], high[row : row + 1])
                for a in range(3):
                    to = r + 1 - a
                    if 0 <= to < rows:
                        term = near[0] * taps[a][0] + near[1] * taps[a][1] + near[2] * taps[a][2]
                        totals[to] = term if totals[to] is None else totals[to] + term
            mixed[at : at + sites, span] = jnp.concatenate(totals, axis=0).astype(BF16)
            edges_ref[t * cols : (t + 1) * cols, span] = totals[0]
            edges_ref[(frames + t) * cols : (frames + t + 1) * cols, span] = totals[rows - 1]
    out_ref[...] = projected(mixed[...], gate_ref[...], wv_ref, wo_ref)


def edge_kernel(frames, rows, cols, rounds_h, edges_ref, taps_ref, gate_ref, wv_ref, wo_ref, inner_ref, *refs):
    ends, out_ref = refs[:rounds_h], refs[rounds_h]
    sites = rows * cols
    size = frames * cols
    odd, _, _ = position("height")
    out_ref[...] = inner_ref[...]
    taps = taps_ref[...]
    mixed, gate = [], []
    for k, end in enumerate(ends):
        end = end[...].astype(F32)
        first = jnp.logical_not(odd) if k else odd
        lefts, rights = end[size : size + frames], end[size + frames : size + 2 * frames]
        lower, upper = position("height")[1:]
        exists = jnp.where(first, lower, upper)
        tap = jnp.where(first, taps[0:3], taps[6:9])
        total = jnp.where(first, edges_ref[0:size], edges_ref[size : 2 * size])
        for t in range(frames):
            near = shifted(end[t * cols : (t + 1) * cols], lefts[t : t + 1], rights[t : t + 1])
            more = near[0] * tap[0:1] + near[1] * tap[1:2] + near[2] * tap[2:3]
            mixed.append(total[t * cols : (t + 1) * cols] + jnp.where(exists, more, jnp.zeros_like(more)))
            at = t * sites
            gate.append(jnp.where(first, gate_ref[at : at + cols], gate_ref[at + sites - cols : at + sites]))
    out = projected(jnp.concatenate(mixed, axis=0).astype(BF16), jnp.concatenate(gate, axis=0), wv_ref, wo_ref)
    for t in range(frames):
        new = [out[k * size + t * cols : k * size + (t + 1) * cols] for k in range(rounds_h)]
        for at, other in ((t * sites, False), (t * sites + sites - cols, True)):
            kept = new[1] if rounds_h > 1 else inner_ref[at : at + cols]
            out_ref[at : at + cols] = jnp.where(odd, kept, new[0]) if other else jnp.where(odd, new[0], kept)


def body(latents, spatial_taps, kernel_taps, skip_gain, gate_weight, value_weight, out_weight):
    frames, rows, cols, chans = latents.shape
    lags = kernel_taps.shape[0]
    n_t, n_w = lax.axis_size("tm"), lax.axis_size("width")
    chips = n_t // 2
    block = frames * rows * cols
    shape = jax.ShapeDtypeStruct
    x = latents.reshape(block, chans)

    partner = lax.ppermute(x, "tm", [(i, i ^ 1) for i in range(n_t)])
    inputs = [kernel_taps, skip_gain.reshape(1, chans), x, gate_weight]
    lines = frames * rows
    gate, fields, table, side = call(
        functools.partial(early_kernel, frames, rows, cols),
        "early",
        [
            shape((block, chans), F32),
            shape((chips * block, chans), F32),
            shape((lags + 2 * frames, cols, chans), F32),
            shape((lines, chans), F32),
        ],
        [pltpu.VMEM(a.shape, a.dtype) for a in inputs]
        + [pltpu.SemaphoreType.DMA((len(inputs),)), pltpu.VMEM((block, LANES), F32)],
        inputs,
        2 * block * chans * chans,
        x.size,
        far=len(inputs),
    )

    h_rounds = swaps("height")
    column = shape((2 * lines, chans), BF16)
    mine, *sent = call(
        functools.partial(mix_kernel, frames, rows, cols),
        "mix",
        [shape((block, chans), F32), column] + [column, shape((block, chans), BF16)] * (chips - 1),
        [pltpu.VMEM((block, LANES), F32)],
        [partner, fields, table, side],
        2 * chips * frames * x.size,
    )
    columns, wholes = [], []
    for d in range(chips):
        route = []
        for i in range(n_t):
            for j in range(n_w):
                to = j + (1 if i % 2 else -1)
                core, to = (1 - i % 2, to) if 0 <= to < n_w else (i % 2, j)
                route.append((i * n_w + j, ((i // 2 + d) % chips * 2 + core) * n_w + to))
        columns.append(lax.ppermute(sent.pop(0), ("tm", "width"), route))
        if d:
            wholes.append(lax.ppermute(sent.pop(0), "tm", [(i, (i + 2 * d) % n_t) for i in range(n_t)]))

    own, other = call(
        functools.partial(side_kernel, lines),
        "side",
        [shape((lines, chans), F32), shape((lines, chans), BF16)],
        [],
        columns,
    )
    other = lax.ppermute(other, "tm", [(i, i ^ 1) for i in range(n_t)])
    size = -(-(frames * cols + 2 * frames) // 16) * 16
    low, high, *ends = call(
        functools.partial(border_kernel, frames, rows, cols),
        "border",
        [shape((lines, chans), F32)] * 2 + [shape((size, chans), BF16)] * len(h_rounds),
        [],
        [mine, own, other] + wholes,
    )
    ends = [lax.ppermute(e, "height", pairs) for e, pairs in zip(ends, h_rounds)]

    taps = spatial_taps.reshape(9, chans)
    inner, edges = call(
        functools.partial(inner_kernel, frames, rows, cols),
        "inner",
        [shape((block, chans), BF16), shape((2 * frames * cols, chans), F32)],
        [pltpu.VMEM((block, chans), BF16)],
        [mine, low, high, taps, gate, value_weight, out_weight] + wholes,
        4 * block * chans * chans,
    )
    (out,) = call(
        functools.partial(edge_kernel, frames, rows, cols, len(h_rounds)),
        "edge",
        [shape((block, chans), BF16)],
        [],
        [edges, taps, gate, value_weight, out_weight, inner] + ends,
        4 * frames * cols * chans * chans,
    )
    return out.reshape(latents.shape)


def solution(mesh):
    in_specs = (P("tm", "height", "width", None), P(), P(), P(), P(), P(), P())
    out_specs = P("tm", "height", "width", None)
    return jax.shard_map(body, mesh=mesh, in_specs=in_specs, out_specs=out_specs, check_vma=False)
```

```python
import functools

import jax
import jax.numpy as jnp
from jax import lax
from jax.experimental import pallas as pl
from jax.experimental.pallas import tpu as pltpu
from jax.sharding import PartitionSpec as P

LANES = 128
F32, BF16 = jnp.float32, jnp.bfloat16
VMEM = pl.BlockSpec(memory_space=pltpu.VMEM)
HBM = pl.BlockSpec(memory_space=pltpu.HBM)


def call(kernel, name, outs, scratch, operands, flops=0, exps=0, far=0):
    operands = [pltpu.with_memory_space_constraint(a, pltpu.HBM) for a in operands[:far]] + list(operands[far:])
    moved = sum(a.size * a.dtype.itemsize for a in operands) + sum(a.size * a.dtype.itemsize for a in outs)
    return pl.pallas_call(
        kernel,
        out_shape=tuple(outs),
        in_specs=[HBM] * far + [VMEM] * (len(operands) - far),
        out_specs=(VMEM,) * len(outs),
        scratch_shapes=scratch,
        compiler_params=pltpu.CompilerParams(vmem_limit_bytes=24 * 1024 * 1024),
        cost_estimate=pl.CostEstimate(flops=flops, bytes_accessed=moved, transcendentals=exps),
        name=name,
    )(*operands)


def swaps(axis):
    n = lax.axis_size(axis)
    rounds = []
    for first in range(2 if n > 2 else 1):
        to = list(range(n))
        for i in range(first, n - 1, 2):
            to[i], to[i + 1] = i + 1, i
        rounds.append(list(enumerate(to)))
    return rounds


def position(axis):
    i, n = lax.axis_index(axis), lax.axis_size(axis)
    return lax.rem(i, 2) == 1, i > 0, i < n - 1


def second():
    return lax.rem(lax.axis_index("tm"), 2) == 1


def on_right():
    return lax.rem(lax.axis_index("tm") + lax.axis_index("width"), 2) == 0


def facing(core, column, columns):
    to = column + (1 if (core + column) % 2 == 0 else -1)
    return to if 0 <= to < columns else column


def outer_column(ref, lines, cols):
    return jnp.where(on_right(), ref[pl.ds(cols - 1, lines, stride=cols), :], ref[pl.ds(0, lines, stride=cols), :])


def early_kernel(frames, rows, cols, *refs):
    far, (gate_ref, fields_ref, table_ref, side_ref), near, (arrived, held) = refs[:4], refs[4:8], refs[8:12], refs[12:]
    copies = [pltpu.make_async_copy(a, b, arrived.at[i]) for i, (a, b) in enumerate(zip(far, near))]
    for copy in copies:
        copy.start()
    taps_ref, skip_ref, x_ref, w_ref = near
    lags, chans = taps_ref.shape
    copies[0].wait()
    copies[1].wait()
    pad = 2 * frames
    taps = taps_ref[...].astype(F32)
    table_ref[0:pad] = jnp.zeros((pad, cols, chans), F32)
    for lag in range(lags):
        tap = taps[lag : lag + 1] + (skip_ref[...] if lag == 0 else 0.0)
        table_ref[pad + lag] = jnp.broadcast_to(tap, (cols, chans))
    sites = rows * cols
    block = frames * sites
    copies[2].wait()
    for lane in range(0, chans, LANES):
        span = slice(lane, lane + LANES)
        held[...] = x_ref[:, span].astype(F32)
        side_ref[:, span] = outer_column(held, frames * rows, cols)
        for d in range(fields_ref.shape[0] // block):
            totals = [None] * frames
            for s in range(frames):
                x = x_ref[s * sites : (s + 1) * sites, span].astype(F32).reshape(rows, cols, LANES)
                for t in range(s if d == 0 else 0, frames):
                    term = table_ref[pad + 2 * d * frames + t - s, :, span] * x
                    totals[t] = term if totals[t] is None else totals[t] + term
            for t in range(frames):
                at = d * block + t * sites
                fields_ref[at : at + sites, span] = totals[t].reshape(sites, LANES)
    copies[3].wait()
    v = jnp.dot(x_ref[...], w_ref[...], preferred_element_type=F32)
    gate_ref[...] = v / (1.0 + jnp.exp(-v))


def mix_kernel(frames, rows, cols, partner_ref, fields_ref, table_ref, side_ref, mine_ref, *refs):
    *outs, held = refs
    sites = rows * cols
    lines = frames * rows
    block = frames * sites
    pad = 2 * frames
    shift = jnp.where(second(), frames, -frames)
    for lane in range(0, mine_ref.shape[1], LANES):
        span = slice(lane, lane + LANES)
        held[...] = partner_ref[:, span].astype(F32)
        near = [side_ref[s * rows : (s + 1) * rows, span] for s in range(frames)]
        far = outer_column(held, lines, cols)
        for d in range(fields_ref.shape[0] // block):
            totals = []
            for t in range(frames):
                at = d * block + t * sites
                totals.append(fields_ref[at : at + sites, span].reshape(rows, cols, LANES))
            base = pad + 2 * d * frames
            for s in range(frames):
                x = partner_ref[s * sites : (s + 1) * sites, span].astype(F32).reshape(rows, cols, LANES)
                for t in range(frames):
                    totals[t] = totals[t] + table_ref[base + shift + t - s, :, span] * x
            for t in range(frames):
                held[t * sites : (t + 1) * sites, :] = totals[t].reshape(sites, LANES)
            if d:
                outs[2 * d][:, span] = held[...].astype(BF16)
            else:
                mine_ref[:, span] = held[...]
            ends = []
            for t in range(frames):
                end = jnp.zeros((rows, LANES), F32)
                for s in range(frames):
                    end = end + table_ref[base - shift + t - s, :, span] * near[s]
                    if d or t >= s:
                        end = end + table_ref[base + t - s, :, span] * far[s * rows : (s + 1) * rows]
                ends.append(end)
            column = jnp.concatenate([outer_column(held, lines, cols)] + ends, axis=0)
            outs[2 * d - 1 if d else 0][:, span] = column.astype(BF16)


def later(d, value):
    return jnp.where(lax.div(lax.axis_index("tm"), 2) >= d, value, jnp.zeros_like(value))


def side_kernel(lines, *refs):
    *arrived, own_ref, other_ref = refs
    _, lower, upper = position("width")
    exists = jnp.where(on_right(), upper, lower)
    total = 0.0
    for d, ref in enumerate(arrived):
        total = total + later(d, ref[...].astype(F32))
    total = jnp.where(exists, total, jnp.zeros_like(total))
    own_ref[...] = total[:lines]
    other_ref[...] = total[lines:].astype(BF16)


def border_kernel(frames, rows, cols, mine_ref, own_ref, other_ref, *refs):
    n = sum(ref.shape == mine_ref.shape for ref in refs)
    wholes, (low_ref, high_ref, *outs) = refs[:n], refs[n:]
    sites = rows * cols
    odd, _, _ = position("height")
    right, own, other = on_right(), own_ref[...], other_ref[...].astype(F32)
    low, high = jnp.where(right, other, own), jnp.where(right, own, other)
    low_ref[...] = low
    high_ref[...] = high
    fill = jnp.zeros((outs[0].shape[0] - frames * cols - 2 * frames, low.shape[1]), F32)
    ends = []
    for r in (0, rows - 1):
        lines = []
        for t in range(frames):
            at = t * sites + r * cols
            line = mine_ref[at : at + cols]
            for d, ref in enumerate(wholes, 1):
                line = line + later(d, ref[at : at + cols].astype(F32))
            lines.append(line)
        lefts = [low[t * rows + r : t * rows + r + 1] for t in range(frames)]
        rights = [high[t * rows + r : t * rows + r + 1] for t in range(frames)]
        ends.append(jnp.concatenate(lines + lefts + rights + [fill], axis=0))
    for k, out in enumerate(outs):
        out[...] = (jnp.where(odd, ends[1], ends[0]) if k else jnp.where(odd, ends[0], ends[1])).astype(BF16)


def shifted(line, left, right):
    cols = line.shape[0]
    place = lax.broadcasted_iota(jnp.int32, line.shape, 0)
    before = jnp.where(place == 0, left, pltpu.roll(line, 1, 0))
    after = jnp.where(place == cols - 1, right, pltpu.roll(line, cols - 1, 0))
    return before, line, after


def projected(mixed, gate, wv_ref, wo_ref):
    value = jnp.dot(mixed, wv_ref[...], preferred_element_type=F32)
    hidden = (value * gate).astype(BF16)
    return jnp.dot(hidden, wo_ref[...], preferred_element_type=F32).astype(BF16)


def inner_kernel(frames, rows, cols, mine_ref, low_ref, high_ref, taps_ref, gate_ref, wv_ref, wo_ref, *refs):
    *wholes, out_ref, edges_ref, mixed = refs
    chans = mine_ref.shape[1]
    sites = rows * cols
    for lane in range(0, chans, LANES):
        span = slice(lane, lane + LANES)
        taps = [[taps_ref[3 * a + b : 3 * a + b + 1, span] for b in range(3)] for a in range(3)]
        low, high = low_ref[:, span], high_ref[:, span]
        for t in range(frames):
            at = t * sites
            tile = mine_ref[at : at + sites, span]
            for d, ref in enumerate(wholes, 1):
                tile = tile + later(d, ref[at : at + sites, span].astype(F32))
            totals = [None] * rows
            for r in range(rows):
                row = t * rows + r
                near = shifted(tile[r * cols : (r + 1) * cols], low[row : row + 1], high[row : row + 1])
                for a in range(3):
                    to = r + 1 - a
                    if 0 <= to < rows:
                        term = near[0] * taps[a][0] + near[1] * taps[a][1] + near[2] * taps[a][2]
                        totals[to] = term if totals[to] is None else totals[to] + term
            mixed[at : at + sites, span] = jnp.concatenate(totals, axis=0).astype(BF16)
            edges_ref[t * cols : (t + 1) * cols, span] = totals[0]
            edges_ref[(frames + t) * cols : (frames + t + 1) * cols, span] = totals[rows - 1]
    out_ref[...] = projected(mixed[...], gate_ref[...], wv_ref, wo_ref)


def edge_kernel(frames, rows, cols, rounds_h, edges_ref, taps_ref, gate_ref, wv_ref, wo_ref, inner_ref, *refs):
    ends, out_ref = refs[:rounds_h], refs[rounds_h]
    sites = rows * cols
    size = frames * cols
    odd, _, _ = position("height")
    out_ref[...] = inner_ref[...]
    taps = taps_ref[...]
    mixed, gate = [], []
    for k, end in enumerate(ends):
        end = end[...].astype(F32)
        first = jnp.logical_not(odd) if k else odd
        lefts, rights = end[size : size + frames], end[size + frames : size + 2 * frames]
        lower, upper = position("height")[1:]
        exists = jnp.where(first, lower, upper)
        tap = jnp.where(first, taps[0:3], taps[6:9])
        total = jnp.where(first, edges_ref[0:size], edges_ref[size : 2 * size])
        for t in range(frames):
            near = shifted(end[t * cols : (t + 1) * cols], lefts[t : t + 1], rights[t : t + 1])
            more = near[0] * tap[0:1] + near[1] * tap[1:2] + near[2] * tap[2:3]
            mixed.append(total[t * cols : (t + 1) * cols] + jnp.where(exists, more, jnp.zeros_like(more)))
            at = t * sites
            gate.append(jnp.where(first, gate_ref[at : at + cols], gate_ref[at + sites - cols : at + sites]))
    out = projected(jnp.concatenate(mixed, axis=0).astype(BF16), jnp.concatenate(gate, axis=0), wv_ref, wo_ref)
    for t in range(frames):
        new = [out[k * size + t * cols : k * size + (t + 1) * cols] for k in range(rounds_h)]
        for at, other in ((t * sites, False), (t * sites + sites - cols, True)):
            kept = new[1] if rounds_h > 1 else inner_ref[at : at + cols]
            out_ref[at : at + cols] = jnp.where(odd, kept, new[0]) if other else jnp.where(odd, new[0], kept)


def body(latents, spatial_taps, kernel_taps, skip_gain, gate_weight, value_weight, out_weight):
    frames, rows, cols, chans = latents.shape
    lags = kernel_taps.shape[0]
    n_t, n_w = lax.axis_size("tm"), lax.axis_size("width")
    chips = n_t // 2
    block = frames * rows * cols
    shape = jax.ShapeDtypeStruct
    x = latents.reshape(block, chans)

    partner = lax.ppermute(x, "tm", [(i, i ^ 1) for i in range(n_t)])
    inputs = [kernel_taps, skip_gain.reshape(1, chans), x, gate_weight]
    lines = frames * rows
    gate, fields, table, side = call(
        functools.partial(early_kernel, frames, rows, cols),
        "early",
        [
            shape((block, chans), F32),
            shape((chips * block, chans), F32),
            shape((lags + 2 * frames, cols, chans), F32),
            shape((lines, chans), F32),
        ],
        [pltpu.VMEM(a.shape, a.dtype) for a in inputs]
        + [pltpu.SemaphoreType.DMA((len(inputs),)), pltpu.VMEM((block, LANES), F32)],
        inputs,
        2 * block * chans * chans,
        x.size,
        far=len(inputs),
    )

    h_rounds = swaps("height")
    column = shape((2 * lines, chans), BF16)
    mine, *sent = call(
        functools.partial(mix_kernel, frames, rows, cols),
        "mix",
        [shape((block, chans), F32), column] + [column, shape((block, chans), BF16)] * (chips - 1),
        [pltpu.VMEM((block, LANES), F32)],
        [partner, fields, table, side],
        2 * chips * frames * x.size,
    )
    columns, wholes = [], []
    for d in range(chips):
        route = [
            (i * n_w + j, (i + 2 * d) % n_t * n_w + facing(i % 2, j, n_w)) for i in range(n_t) for j in range(n_w)
        ]
        columns.append(lax.ppermute(sent.pop(0), ("tm", "width"), route))
        if d:
            wholes.append(lax.ppermute(sent.pop(0), "tm", [(i, (i + 2 * d) % n_t) for i in range(n_t)]))

    own, other = call(
        functools.partial(side_kernel, lines),
        "side",
        [shape((lines, chans), F32), shape((lines, chans), BF16)],
        [],
        columns,
    )
    other = lax.ppermute(other, "tm", [(i, i ^ 1) for i in range(n_t)])
    size = -(-(frames * cols + 2 * frames) // 16) * 16
    low, high, *ends = call(
        functools.partial(border_kernel, frames, rows, cols),
        "border",
        [shape((lines, chans), F32)] * 2 + [shape((size, chans), BF16)] * len(h_rounds),
        [],
        [mine, own, other] + wholes,
    )
    ends = [lax.ppermute(e, "height", pairs) for e, pairs in zip(ends, h_rounds)]

    taps = spatial_taps.reshape(9, chans)
    inner, edges = call(
        functools.partial(inner_kernel, frames, rows, cols),
        "inner",
        [shape((block, chans), BF16), shape((2 * frames * cols, chans), F32)],
        [pltpu.VMEM((block, chans), BF16)],
        [mine, low, high, taps, gate, value_weight, out_weight] + wholes,
        4 * block * chans * chans,
    )
    (out,) = call(
        functools.partial(edge_kernel, frames, rows, cols, len(h_rounds)),
        "edge",
        [shape((block, chans), BF16)],
        [],
        [edges, taps, gate, value_weight, out_weight, inner] + ends,
        4 * frames * cols * chans * chans,
    )
    return out.reshape(latents.shape)


def solution(mesh):
    in_specs = (P("tm", "height", "width", None), P(), P(), P(), P(), P(), P())
    out_specs = P("tm", "height", "width", None)
    return jax.shard_map(body, mesh=mesh, in_specs=in_specs, out_specs=out_specs, check_vma=False)
```

```python
import functools

import jax
import jax.numpy as jnp
from jax import lax
from jax.experimental import pallas as pl
from jax.experimental.pallas import tpu as pltpu
from jax.sharding import PartitionSpec as P

LANES = 128
F32, BF16 = jnp.float32, jnp.bfloat16
VMEM = pl.BlockSpec(memory_space=pltpu.VMEM)
HBM = pl.BlockSpec(memory_space=pltpu.HBM)


def call(kernel, name, outs, scratch, operands, flops=0, exps=0, far=0):
    operands = [pltpu.with_memory_space_constraint(a, pltpu.HBM) for a in operands[:far]] + list(operands[far:])
    moved = sum(a.size * a.dtype.itemsize for a in operands) + sum(a.size * a.dtype.itemsize for a in outs)
    return pl.pallas_call(
        kernel,
        out_shape=tuple(outs),
        in_specs=[HBM] * far + [VMEM] * (len(operands) - far),
        out_specs=(VMEM,) * len(outs),
        scratch_shapes=scratch,
        compiler_params=pltpu.CompilerParams(vmem_limit_bytes=24 * 1024 * 1024),
        cost_estimate=pl.CostEstimate(flops=flops, bytes_accessed=moved, transcendentals=exps),
        name=name,
    )(*operands)


def swaps(axis):
    n = lax.axis_size(axis)
    rounds = []
    for first in range(2 if n > 2 else 1):
        to = list(range(n))
        for i in range(first, n - 1, 2):
            to[i], to[i + 1] = i + 1, i
        rounds.append(list(enumerate(to)))
    return rounds


def position(axis):
    i, n = lax.axis_index(axis), lax.axis_size(axis)
    return lax.rem(i, 2) == 1, i > 0, i < n - 1


def second():
    return lax.rem(lax.axis_index("tm"), 2) == 1


def on_right():
    return lax.rem(lax.axis_index("tm") + lax.axis_index("width"), 2) == 0


def facing(core, column, columns):
    to = column + (1 if (core + column) % 2 == 0 else -1)
    return to if 0 <= to < columns else column


def outer_column(ref, lines, cols):
    return jnp.where(on_right(), ref[pl.ds(cols - 1, lines, stride=cols), :], ref[pl.ds(0, lines, stride=cols), :])


def early_kernel(frames, rows, cols, *refs):
    far, (gate_ref, fields_ref, table_ref, side_ref), near, (arrived, held) = refs[:4], refs[4:8], refs[8:12], refs[12:]
    copies = [pltpu.make_async_copy(a, b, arrived.at[i]) for i, (a, b) in enumerate(zip(far, near))]
    for copy in copies:
        copy.start()
    taps_ref, skip_ref, x_ref, w_ref = near
    lags, chans = taps_ref.shape
    copies[0].wait()
    copies[1].wait()
    pad = 2 * frames
    taps = taps_ref[...].astype(F32)
    table_ref[0:pad] = jnp.zeros((pad, cols, chans), F32)
    for lag in range(lags):
        tap = taps[lag : lag + 1] + (skip_ref[...] if lag == 0 else 0.0)
        table_ref[pad + lag] = jnp.broadcast_to(tap, (cols, chans))
    sites = rows * cols
    block = frames * sites
    copies[2].wait()
    for lane in range(0, chans, LANES):
        span = slice(lane, lane + LANES)
        held[...] = x_ref[:, span].astype(F32)
        side_ref[:, span] = outer_column(held, frames * rows, cols)
        for d in range(fields_ref.shape[0] // block):
            totals = [None] * frames
            for s in range(frames):
                x = x_ref[s * sites : (s + 1) * sites, span].astype(F32).reshape(rows, cols, LANES)
                for t in range(s if d == 0 else 0, frames):
                    term = table_ref[pad + 2 * d * frames + t - s, :, span] * x
                    totals[t] = term if totals[t] is None else totals[t] + term
            for t in range(frames):
                at = d * block + t * sites
                fields_ref[at : at + sites, span] = totals[t].reshape(sites, LANES)
    copies[3].wait()
    v = jnp.dot(x_ref[...], w_ref[...], preferred_element_type=F32)
    gate_ref[...] = v / (1.0 + jnp.exp(-v))


def mix_kernel(frames, rows, cols, partner_ref, fields_ref, table_ref, side_ref, mine_ref, *refs):
    *outs, held = refs
    sites = rows * cols
    lines = frames * rows
    block = frames * sites
    pad = 2 * frames
    shift = jnp.where(second(), frames, -frames)
    for lane in range(0, mine_ref.shape[1], LANES):
        span = slice(lane, lane + LANES)
        held[...] = partner_ref[:, span].astype(F32)
        near = [side_ref[s * rows : (s + 1) * rows, span] for s in range(frames)]
        far = outer_column(held, lines, cols)
        for d in range(fields_ref.shape[0] // block):
            totals = []
            for t in range(frames):
                at = d * block + t * sites
                totals.append(fields_ref[at : at + sites, span].reshape(rows, cols, LANES))
            base = pad + 2 * d * frames
            for s in range(frames):
                x = partner_ref[s * sites : (s + 1) * sites, span].astype(F32).reshape(rows, cols, LANES)
                for t in range(frames):
                    totals[t] = totals[t] + table_ref[base + shift + t - s, :, span] * x
            for t in range(frames):
                held[t * sites : (t + 1) * sites, :] = totals[t].reshape(sites, LANES)
            if d:
                outs[2 * d][:, span] = held[...].astype(BF16)
            else:
                mine_ref[:, span] = held[...]
            ends = []
            for t in range(frames):
                end = jnp.zeros((rows, LANES), F32)
                for s in range(frames):
                    end = end + table_ref[base - shift + t - s, :, span] * near[s]
                    if d or t >= s:
                        end = end + table_ref[base + t - s, :, span] * far[s * rows : (s + 1) * rows]
                ends.append(end)
            column = jnp.concatenate([outer_column(held, lines, cols)] + ends, axis=0)
            outs[2 * d - 1 if d else 0][:, span] = column.astype(BF16)


def later(d, value):
    return jnp.where(lax.div(lax.axis_index("tm"), 2) >= d, value, jnp.zeros_like(value))


def side_kernel(lines, *refs):
    *arrived, own_ref, other_ref = refs
    _, lower, upper = position("width")
    exists = jnp.where(on_right(), upper, lower)
    total = 0.0
    for d, ref in enumerate(arrived):
        total = total + later(d, ref[...].astype(F32))
    total = jnp.where(exists, total, jnp.zeros_like(total))
    own_ref[...] = total[:lines]
    other_ref[...] = total[lines:].astype(BF16)


def border_kernel(frames, rows, cols, mine_ref, own_ref, other_ref, *refs):
    n = sum(ref.shape == mine_ref.shape for ref in refs)
    wholes, (low_ref, high_ref, *outs) = refs[:n], refs[n:]
    sites = rows * cols
    odd, _, _ = position("height")
    right, own, other = on_right(), own_ref[...], other_ref[...].astype(F32)
    low, high = jnp.where(right, other, own), jnp.where(right, own, other)
    low_ref[...] = low
    high_ref[...] = high
    fill = jnp.zeros((outs[0].shape[0] - frames * cols - 2 * frames, low.shape[1]), F32)
    ends = []
    for r in (0, rows - 1):
        lines = []
        for t in range(frames):
            at = t * sites + r * cols
            line = mine_ref[at : at + cols]
            for d, ref in enumerate(wholes, 1):
                line = line + later(d, ref[at : at + cols].astype(F32))
            lines.append(line)
        lefts = [low[t * rows + r : t * rows + r + 1] for t in range(frames)]
        rights = [high[t * rows + r : t * rows + r + 1] for t in range(frames)]
        ends.append(jnp.concatenate(lines + lefts + rights + [fill], axis=0))
    for k, out in enumerate(outs):
        out[...] = (jnp.where(odd, ends[1], ends[0]) if k else jnp.where(odd, ends[0], ends[1])).astype(BF16)


def shifted(line, left, right):
    cols = line.shape[0]
    place = lax.broadcasted_iota(jnp.int32, line.shape, 0)
    before = jnp.where(place == 0, left, pltpu.roll(line, 1, 0))
    after = jnp.where(place == cols - 1, right, pltpu.roll(line, cols - 1, 0))
    return before, line, after


def projected(mixed, gate, wv_ref, wo_ref):
    value = jnp.dot(mixed, wv_ref[...], preferred_element_type=F32)
    hidden = (value * gate).astype(BF16)
    return jnp.dot(hidden, wo_ref[...], preferred_element_type=F32).astype(BF16)


def inner_kernel(frames, rows, cols, mine_ref, low_ref, high_ref, taps_ref, gate_ref, wv_ref, wo_ref, *refs):
    *wholes, out_ref, edges_ref, mixed = refs
    chans = mine_ref.shape[1]
    sites = rows * cols
    for lane in range(0, chans, LANES):
        span = slice(lane, lane + LANES)
        taps = [[taps_ref[3 * a + b : 3 * a + b + 1, span] for b in range(3)] for a in range(3)]
        low, high = low_ref[:, span], high_ref[:, span]
        for t in range(frames):
            at = t * sites
            tile = mine_ref[at : at + sites, span]
            for d, ref in enumerate(wholes, 1):
                tile = tile + later(d, ref[at : at + sites, span].astype(F32))
            totals = [None] * rows
            for r in range(rows):
                row = t * rows + r
                near = shifted(tile[r * cols : (r + 1) * cols], low[row : row + 1], high[row : row + 1])
                for a in range(3):
                    to = r + 1 - a
                    if 0 <= to < rows:
                        term = near[0] * taps[a][0] + near[1] * taps[a][1] + near[2] * taps[a][2]
                        totals[to] = term if totals[to] is None else totals[to] + term
            mixed[at : at + sites, span] = jnp.concatenate(totals, axis=0).astype(BF16)
            edges_ref[t * cols : (t + 1) * cols, span] = totals[0]
            edges_ref[(frames + t) * cols : (frames + t + 1) * cols, span] = totals[rows - 1]
    out_ref[...] = projected(mixed[...], gate_ref[...], wv_ref, wo_ref)


def edge_kernel(frames, rows, cols, rounds_h, edges_ref, taps_ref, gate_ref, wv_ref, wo_ref, inner_ref, *refs):
    ends, out_ref = refs[:rounds_h], refs[rounds_h]
    sites = rows * cols
    size = frames * cols
    odd, _, _ = position("height")
    out_ref[...] = inner_ref[...]
    taps = taps_ref[...]
    mixed, gate = [], []
    for k, end in enumerate(ends):
        end = end[...].astype(F32)
        first = jnp.logical_not(odd) if k else odd
        lefts, rights = end[size : size + frames], end[size + frames : size + 2 * frames]
        lower, upper = position("height")[1:]
        exists = jnp.where(first, lower, upper)
        tap = jnp.where(first, taps[0:3], taps[6:9])
        total = jnp.where(first, edges_ref[0:size], edges_ref[size : 2 * size])
        for t in range(frames):
            near = shifted(end[t * cols : (t + 1) * cols], lefts[t : t + 1], rights[t : t + 1])
            more = near[0] * tap[0:1] + near[1] * tap[1:2] + near[2] * tap[2:3]
            mixed.append(total[t * cols : (t + 1) * cols] + jnp.where(exists, more, jnp.zeros_like(more)))
            at = t * sites
            gate.append(jnp.where(first, gate_ref[at : at + cols], gate_ref[at + sites - cols : at + sites]))
    out = projected(jnp.concatenate(mixed, axis=0).astype(BF16), jnp.concatenate(gate, axis=0), wv_ref, wo_ref)
    for t in range(frames):
        new = [out[k * size + t * cols : k * size + (t + 1) * cols] for k in range(rounds_h)]
        for at, other in ((t * sites, False), (t * sites + sites - cols, True)):
            kept = new[1] if rounds_h > 1 else inner_ref[at : at + cols]
            out_ref[at : at + cols] = jnp.where(odd, kept, new[0]) if other else jnp.where(odd, new[0], kept)


def body(latents, spatial_taps, kernel_taps, skip_gain, gate_weight, value_weight, out_weight):
    frames, rows, cols, chans = latents.shape
    lags = kernel_taps.shape[0]
    n_t, n_h, n_w = lax.axis_size("tm"), lax.axis_size("height"), lax.axis_size("width")
    chips = n_t // 2
    block = frames * rows * cols
    shape = jax.ShapeDtypeStruct
    x = latents.reshape(block, chans)

    partner = lax.ppermute(x, "tm", [(i, i ^ 1) for i in range(n_t)])
    inputs = [kernel_taps, skip_gain.reshape(1, chans), x, gate_weight]
    lines = frames * rows
    gate, fields, table, side = call(
        functools.partial(early_kernel, frames, rows, cols),
        "early",
        [
            shape((block, chans), F32),
            shape((chips * block, chans), F32),
            shape((lags + 2 * frames, cols, chans), F32),
            shape((lines, chans), F32),
        ],
        [pltpu.VMEM(a.shape, a.dtype) for a in inputs]
        + [pltpu.SemaphoreType.DMA((len(inputs),)), pltpu.VMEM((block, LANES), F32)],
        inputs,
        2 * block * chans * chans,
        x.size,
        far=len(inputs),
    )

    h_rounds = swaps("height")
    column = shape((2 * lines, chans), BF16)
    mine, *sent = call(
        functools.partial(mix_kernel, frames, rows, cols),
        "mix",
        [shape((block, chans), F32), column] + [column, shape((block, chans), BF16)] * (chips - 1),
        [pltpu.VMEM((block, LANES), F32)],
        [partner, fields, table, side],
        2 * chips * frames * x.size,
    )
    columns, wholes = [], []
    for d in range(chips):
        route = []
        for i in range(n_t):
            for h in range(n_h):
                for j in range(n_w):
                    to = facing(i % 2, j, n_w)
                    row = h ^ 1 if to == j and n_h % 2 == 0 else h
                    source = (i * n_h + h) * n_w + j
                    route.append((source, ((i + 2 * d) % n_t * n_h + row) * n_w + to))
        columns.append(lax.ppermute(sent.pop(0), ("tm", "height", "width"), route))
        if d:
            wholes.append(lax.ppermute(sent.pop(0), "tm", [(i, (i + 2 * d) % n_t) for i in range(n_t)]))

    own, other = call(
        functools.partial(side_kernel, lines),
        "side",
        [shape((lines, chans), F32), shape((lines, chans), BF16)],
        [],
        columns,
    )
    other = lax.ppermute(other, "tm", [(i, i ^ 1) for i in range(n_t)])
    size = -(-(frames * cols + 2 * frames) // 16) * 16
    low, high, *ends = call(
        functools.partial(border_kernel, frames, rows, cols),
        "border",
        [shape((lines, chans), F32)] * 2 + [shape((size, chans), BF16)] * len(h_rounds),
        [],
        [mine, own, other] + wholes,
    )
    ends = [lax.ppermute(e, "height", pairs) for e, pairs in zip(ends, h_rounds)]

    taps = spatial_taps.reshape(9, chans)
    inner, edges = call(
        functools.partial(inner_kernel, frames, rows, cols),
        "inner",
        [shape((block, chans), BF16), shape((2 * frames * cols, chans), F32)],
        [pltpu.VMEM((block, chans), BF16)],
        [mine, low, high, taps, gate, value_weight, out_weight] + wholes,
        4 * block * chans * chans,
    )
    (out,) = call(
        functools.partial(edge_kernel, frames, rows, cols, len(h_rounds)),
        "edge",
        [shape((block, chans), BF16)],
        [],
        [edges, taps, gate, value_weight, out_weight, inner] + ends,
        4 * frames * cols * chans * chans,
    )
    return out.reshape(latents.shape)


def solution(mesh):
    in_specs = (P("tm", "height", "width", None), P(), P(), P(), P(), P(), P())
    out_specs = P("tm", "height", "width", None)
    return jax.shard_map(body, mesh=mesh, in_specs=in_specs, out_specs=out_specs, check_vma=False)
```

```python
import functools

import jax
import jax.numpy as jnp
from jax import lax
from jax.experimental import pallas as pl
from jax.experimental.pallas import tpu as pltpu
from jax.sharding import PartitionSpec as P

LANES = 128
LATER = 8 * 10**9
F32, BF16 = jnp.float32, jnp.bfloat16
VMEM = pl.BlockSpec(memory_space=pltpu.VMEM)
HBM = pl.BlockSpec(memory_space=pltpu.HBM)


def call(kernel, name, outs, scratch, operands, flops=0, exps=0, far=0):
    operands = [pltpu.with_memory_space_constraint(a, pltpu.HBM) for a in operands[:far]] + list(operands[far:])
    moved = sum(a.size * a.dtype.itemsize for a in operands) + sum(a.size * a.dtype.itemsize for a in outs)
    return pl.pallas_call(
        kernel,
        out_shape=tuple(outs),
        in_specs=[HBM] * far + [VMEM] * (len(operands) - far),
        out_specs=(VMEM,) * len(outs),
        scratch_shapes=scratch,
        compiler_params=pltpu.CompilerParams(vmem_limit_bytes=24 * 1024 * 1024),
        cost_estimate=pl.CostEstimate(flops=flops, bytes_accessed=moved, transcendentals=exps),
        name=name,
    )(*operands)


def swaps(axis):
    n = lax.axis_size(axis)
    rounds = []
    for first in range(2 if n > 2 else 1):
        to = list(range(n))
        for i in range(first, n - 1, 2):
            to[i], to[i + 1] = i + 1, i
        rounds.append(list(enumerate(to)))
    return rounds


def position(axis):
    i, n = lax.axis_index(axis), lax.axis_size(axis)
    return lax.rem(i, 2) == 1, i > 0, i < n - 1


def second():
    return lax.rem(lax.axis_index("tm"), 2) == 1


def on_right():
    return lax.rem(lax.axis_index("tm") + lax.axis_index("width"), 2) == 0


def facing(core, column, columns):
    to = column + (1 if (core + column) % 2 == 0 else -1)
    return to if 0 <= to < columns else column


def outer_column(ref, lines, cols):
    return jnp.where(on_right(), ref[pl.ds(cols - 1, lines, stride=cols), :], ref[pl.ds(0, lines, stride=cols), :])


def early_kernel(frames, rows, cols, *refs):
    far, (gate_ref, fields_ref, table_ref, side_ref), near, (arrived, held) = refs[:4], refs[4:8], refs[8:12], refs[12:]
    copies = [pltpu.make_async_copy(a, b, arrived.at[i]) for i, (a, b) in enumerate(zip(far, near))]
    for copy in copies:
        copy.start()
    taps_ref, skip_ref, x_ref, w_ref = near
    lags, chans = taps_ref.shape
    copies[0].wait()
    copies[1].wait()
    pad = 2 * frames
    taps = taps_ref[...].astype(F32)
    table_ref[0:pad] = jnp.zeros((pad, cols, chans), F32)
    for lag in range(lags):
        tap = taps[lag : lag + 1] + (skip_ref[...] if lag == 0 else 0.0)
        table_ref[pad + lag] = jnp.broadcast_to(tap, (cols, chans))
    sites = rows * cols
    block = frames * sites
    copies[2].wait()
    for lane in range(0, chans, LANES):
        span = slice(lane, lane + LANES)
        held[...] = x_ref[:, span].astype(F32)
        side_ref[:, span] = outer_column(held, frames * rows, cols)
        for d in range(fields_ref.shape[0] // block):
            totals = [None] * frames
            for s in range(frames):
                x = x_ref[s * sites : (s + 1) * sites, span].astype(F32).reshape(rows, cols, LANES)
                for t in range(s if d == 0 else 0, frames):
                    term = table_ref[pad + 2 * d * frames + t - s, :, span] * x
                    totals[t] = term if totals[t] is None else totals[t] + term
            for t in range(frames):
                at = d * block + t * sites
                fields_ref[at : at + sites, span] = totals[t].reshape(sites, LANES)
    copies[3].wait()
    v = jnp.dot(x_ref[...], w_ref[...], preferred_element_type=F32)
    gate_ref[...] = v / (1.0 + jnp.exp(-v))


def mix_kernel(frames, rows, cols, rounds_h, partner_ref, fields_ref, table_ref, side_ref, mine_ref, *refs):
    *outs, held = refs
    sites = rows * cols
    lines = frames * rows
    block = frames * sites
    pad = 2 * frames
    shift = jnp.where(second(), frames, -frames)
    odd = position("height")[0]
    for lane in range(0, mine_ref.shape[1], LANES):
        span = slice(lane, lane + LANES)
        held[...] = partner_ref[:, span].astype(F32)
        near = [side_ref[s * rows : (s + 1) * rows, span] for s in range(frames)]
        far = outer_column(held, lines, cols)
        for d in range(fields_ref.shape[0] // block):
            totals = []
            for t in range(frames):
                at = d * block + t * sites
                totals.append(fields_ref[at : at + sites, span].reshape(rows, cols, LANES))
            base = pad + 2 * d * frames
            for s in range(frames):
                x = partner_ref[s * sites : (s + 1) * sites, span].astype(F32).reshape(rows, cols, LANES)
                for t in range(frames):
                    totals[t] = totals[t] + table_ref[base + shift + t - s, :, span] * x
            for t in range(frames):
                held[t * sites : (t + 1) * sites, :] = totals[t].reshape(sites, LANES)
            if d:
                outs[3 * d][:, span] = held[...].astype(BF16)
                ends = [jnp.concatenate([t[r] for t in totals], axis=0) for r in (0, rows - 1)]
                line = [jnp.where(odd, *(ends[::-1] if k else ends)) for k in range(rounds_h)]
                outs[3 * d - 1][:, span] = jnp.concatenate(line, axis=0).astype(BF16)
            else:
                mine_ref[:, span] = held[...]
            ends = []
            for t in range(frames):
                end = jnp.zeros((rows, LANES), F32)
                for s in range(frames):
                    end = end + table_ref[base - shift + t - s, :, span] * near[s]
                    if d or t >= s:
                        end = end + table_ref[base + t - s, :, span] * far[s * rows : (s + 1) * rows]
                ends.append(end)
            column = jnp.concatenate([outer_column(held, lines, cols)] + ends, axis=0)
            outs[3 * d - 2 if d else 0][:, span] = column.astype(BF16)


def later(d, value):
    return jnp.where(lax.div(lax.axis_index("tm"), 2) >= d, value, jnp.zeros_like(value))


def side_kernel(lines, *refs):
    *arrived, own_ref, other_ref = refs
    _, lower, upper = position("width")
    exists = jnp.where(on_right(), upper, lower)
    total = 0.0
    for d, ref in enumerate(arrived):
        total = total + later(d, ref[...].astype(F32))
    total = jnp.where(exists, total, jnp.zeros_like(total))
    own_ref[...] = total[:lines]
    other_ref[...] = total[lines:].astype(BF16)


def border_kernel(frames, rows, cols, chips, mine_ref, own_ref, other_ref, *refs):
    arrived, (low_ref, high_ref, *outs) = refs[: chips - 1], refs[chips - 1 :]
    sites = rows * cols
    odd, _, _ = position("height")
    right, own, other = on_right(), own_ref[...], other_ref[...].astype(F32)
    low, high = jnp.where(right, other, own), jnp.where(right, own, other)
    low_ref[...] = low
    high_ref[...] = high
    size = frames * cols
    fill = jnp.zeros((outs[0].shape[0] - size - 2 * frames, low.shape[1]), F32)
    lines, corners = [], []
    for r in (0, rows - 1):
        lines.append(jnp.concatenate([mine_ref[t * sites + r * cols : t * sites + (r + 1) * cols] for t in range(frames)]))
        ends = [side[t * rows + r : t * rows + r + 1] for side in (low, high) for t in range(frames)]
        corners.append(jnp.concatenate(ends + [fill]))
    for k, out in enumerate(outs):
        line = jnp.where(odd, *(lines[::-1] if k else lines))
        for d, ref in enumerate(arrived, 1):
            line = line + later(d, ref[k * size : (k + 1) * size].astype(F32))
        out[...] = jnp.concatenate([line, jnp.where(odd, *(corners[::-1] if k else corners))]).astype(BF16)


def shifted(line, left, right):
    cols = line.shape[0]
    place = lax.broadcasted_iota(jnp.int32, line.shape, 0)
    before = jnp.where(place == 0, left, pltpu.roll(line, 1, 0))
    after = jnp.where(place == cols - 1, right, pltpu.roll(line, cols - 1, 0))
    return before, line, after


def projected(mixed, gate, wv_ref, wo_ref):
    value = jnp.dot(mixed, wv_ref[...], preferred_element_type=F32)
    hidden = (value * gate).astype(BF16)
    return jnp.dot(hidden, wo_ref[...], preferred_element_type=F32).astype(BF16)


def inner_kernel(frames, rows, cols, mine_ref, low_ref, high_ref, taps_ref, gate_ref, wv_ref, wo_ref, *refs):
    *wholes, out_ref, edges_ref, mixed = refs
    chans = mine_ref.shape[1]
    sites = rows * cols
    for lane in range(0, chans, LANES):
        span = slice(lane, lane + LANES)
        taps = [[taps_ref[3 * a + b : 3 * a + b + 1, span] for b in range(3)] for a in range(3)]
        low, high = low_ref[:, span], high_ref[:, span]
        for t in range(frames):
            at = t * sites
            tile = mine_ref[at : at + sites, span]
            for d, ref in enumerate(wholes, 1):
                tile = tile + later(d, ref[at : at + sites, span].astype(F32))
            totals = [None] * rows
            for r in range(rows):
                row = t * rows + r
                near = shifted(tile[r * cols : (r + 1) * cols], low[row : row + 1], high[row : row + 1])
                for a in range(3):
                    to = r + 1 - a
                    if 0 <= to < rows:
                        term = near[0] * taps[a][0] + near[1] * taps[a][1] + near[2] * taps[a][2]
                        totals[to] = term if totals[to] is None else totals[to] + term
            mixed[at : at + sites, span] = jnp.concatenate(totals, axis=0).astype(BF16)
            edges_ref[t * cols : (t + 1) * cols, span] = totals[0]
            edges_ref[(frames + t) * cols : (frames + t + 1) * cols, span] = totals[rows - 1]
    out_ref[...] = projected(mixed[...], gate_ref[...], wv_ref, wo_ref)


def edge_kernel(frames, rows, cols, rounds_h, edges_ref, taps_ref, gate_ref, wv_ref, wo_ref, inner_ref, *refs):
    ends, out_ref = refs[:rounds_h], refs[rounds_h]
    sites = rows * cols
    size = frames * cols
    odd, _, _ = position("height")
    out_ref[...] = inner_ref[...]
    taps = taps_ref[...]
    mixed, gate = [], []
    for k, end in enumerate(ends):
        end = end[...].astype(F32)
        first = jnp.logical_not(odd) if k else odd
        lefts, rights = end[size : size + frames], end[size + frames : size + 2 * frames]
        lower, upper = position("height")[1:]
        exists = jnp.where(first, lower, upper)
        tap = jnp.where(first, taps[0:3], taps[6:9])
        total = jnp.where(first, edges_ref[0:size], edges_ref[size : 2 * size])
        for t in range(frames):
            near = shifted(end[t * cols : (t + 1) * cols], lefts[t : t + 1], rights[t : t + 1])
            more = near[0] * tap[0:1] + near[1] * tap[1:2] + near[2] * tap[2:3]
            mixed.append(total[t * cols : (t + 1) * cols] + jnp.where(exists, more, jnp.zeros_like(more)))
            at = t * sites
            gate.append(jnp.where(first, gate_ref[at : at + cols], gate_ref[at + sites - cols : at + sites]))
    out = projected(jnp.concatenate(mixed, axis=0).astype(BF16), jnp.concatenate(gate, axis=0), wv_ref, wo_ref)
    for t in range(frames):
        new = [out[k * size + t * cols : k * size + (t + 1) * cols] for k in range(rounds_h)]
        for at, other in ((t * sites, False), (t * sites + sites - cols, True)):
            kept = new[1] if rounds_h > 1 else inner_ref[at : at + cols]
            out_ref[at : at + cols] = jnp.where(odd, kept, new[0]) if other else jnp.where(odd, new[0], kept)


def body(latents, spatial_taps, kernel_taps, skip_gain, gate_weight, value_weight, out_weight):
    frames, rows, cols, chans = latents.shape
    lags = kernel_taps.shape[0]
    n_t, n_h, n_w = lax.axis_size("tm"), lax.axis_size("height"), lax.axis_size("width")
    chips = n_t // 2
    block = frames * rows * cols
    shape = jax.ShapeDtypeStruct
    x = latents.reshape(block, chans)

    partner = lax.ppermute(x, "tm", [(i, i ^ 1) for i in range(n_t)])
    inputs = [kernel_taps, skip_gain.reshape(1, chans), x, gate_weight]
    lines = frames * rows
    gate, fields, table, side = call(
        functools.partial(early_kernel, frames, rows, cols),
        "early",
        [
            shape((block, chans), F32),
            shape((chips * block, chans), F32),
            shape((lags + 2 * frames, cols, chans), F32),
            shape((lines, chans), F32),
        ],
        [pltpu.VMEM(a.shape, a.dtype) for a in inputs]
        + [pltpu.SemaphoreType.DMA((len(inputs),)), pltpu.VMEM((block, LANES), F32)],
        inputs,
        2 * block * chans * chans,
        x.size,
        far=len(inputs),
    )

    h_rounds = swaps("height")
    column = shape((2 * lines, chans), BF16)
    row = shape((len(h_rounds) * frames * cols, chans), BF16)
    mine, *sent = call(
        functools.partial(mix_kernel, frames, rows, cols, len(h_rounds)),
        "mix",
        [shape((block, chans), F32), column] + [column, row, shape((block, chans), BF16)] * (chips - 1),
        [pltpu.VMEM((block, LANES), F32)],
        [partner, fields, table, side],
        2 * chips * frames * x.size,
    )
    columns, arrived, wholes = [], [], []
    for d in range(chips):
        route = []
        for i in range(n_t):
            for h in range(n_h):
                for j in range(n_w):
                    to = facing(i % 2, j, n_w)
                    beside = h ^ 1 if to == j and n_h % 2 == 0 else h
                    source = (i * n_h + h) * n_w + j
                    route.append((source, ((i + 2 * d) % n_t * n_h + beside) * n_w + to))
        columns.append(lax.ppermute(sent.pop(0), ("tm", "height", "width"), route))
        if d:
            for kept in (arrived, wholes):
                kept.append(lax.ppermute(sent.pop(0), "tm", [(i, (i + 2 * d) % n_t) for i in range(n_t)]))

    own, other = call(
        functools.partial(side_kernel, lines),
        "side",
        [shape((lines, chans), F32), shape((lines, chans), BF16)],
        [],
        columns,
        LATER,
    )
    other = lax.ppermute(other, "tm", [(i, i ^ 1) for i in range(n_t)])
    size = -(-(frames * cols + 2 * frames) // 16) * 16
    low, high, *ends = call(
        functools.partial(border_kernel, frames, rows, cols, chips),
        "border",
        [shape((lines, chans), F32)] * 2 + [shape((size, chans), BF16)] * len(h_rounds),
        [],
        [mine, own, other] + arrived,
    )
    ends = [lax.ppermute(e, "height", pairs) for e, pairs in zip(ends, h_rounds)]

    taps = spatial_taps.reshape(9, chans)
    inner, edges = call(
        functools.partial(inner_kernel, frames, rows, cols),
        "inner",
        [shape((block, chans), BF16), shape((2 * frames * cols, chans), F32)],
        [pltpu.VMEM((block, chans), BF16)],
        [mine, low, high, taps, gate, value_weight, out_weight] + wholes,
        4 * block * chans * chans,
    )
    (out,) = call(
        functools.partial(edge_kernel, frames, rows, cols, len(h_rounds)),
        "edge",
        [shape((block, chans), BF16)],
        [],
        [edges, taps, gate, value_weight, out_weight, inner] + ends,
        4 * frames * cols * chans * chans,
    )
    return out.reshape(latents.shape)


def solution(mesh):
    in_specs = (P("tm", "height", "width", None), P(), P(), P(), P(), P(), P())
    out_specs = P("tm", "height", "width", None)
    return jax.shard_map(body, mesh=mesh, in_specs=in_specs, out_specs=out_specs, check_vma=False)
```

```python
import functools

import jax
import jax.numpy as jnp
from jax import lax
from jax.experimental import pallas as pl
from jax.experimental.pallas import tpu as pltpu
from jax.sharding import PartitionSpec as P

LANES = 128
LATER = 8 * 10**9
F32, BF16 = jnp.float32, jnp.bfloat16
VMEM = pl.BlockSpec(memory_space=pltpu.VMEM)
HBM = pl.BlockSpec(memory_space=pltpu.HBM)


def call(kernel, name, outs, scratch, operands, flops=0, exps=0, far=0):
    operands = [pltpu.with_memory_space_constraint(a, pltpu.HBM) for a in operands[:far]] + list(operands[far:])
    moved = sum(a.size * a.dtype.itemsize for a in operands) + sum(a.size * a.dtype.itemsize for a in outs)
    return pl.pallas_call(
        kernel,
        out_shape=tuple(outs),
        in_specs=[HBM] * far + [VMEM] * (len(operands) - far),
        out_specs=(VMEM,) * len(outs),
        scratch_shapes=scratch,
        compiler_params=pltpu.CompilerParams(vmem_limit_bytes=24 * 1024 * 1024),
        cost_estimate=pl.CostEstimate(flops=flops, bytes_accessed=moved, transcendentals=exps),
        name=name,
    )(*operands)


def swaps(axis):
    n = lax.axis_size(axis)
    rounds = []
    for first in range(2 if n > 2 else 1):
        to = list(range(n))
        for i in range(first, n - 1, 2):
            to[i], to[i + 1] = i + 1, i
        rounds.append(list(enumerate(to)))
    return rounds


def position(axis):
    i, n = lax.axis_index(axis), lax.axis_size(axis)
    return lax.rem(i, 2) == 1, i > 0, i < n - 1


def second():
    return lax.rem(lax.axis_index("tm"), 2) == 1


def on_right():
    return lax.rem(lax.axis_index("tm") + lax.axis_index("width"), 2) == 0


def facing(core, column, columns):
    to = column + (1 if (core + column) % 2 == 0 else -1)
    return to if 0 <= to < columns else column


def outer_column(ref, lines, cols):
    return jnp.where(on_right(), ref[pl.ds(cols - 1, lines, stride=cols), :], ref[pl.ds(0, lines, stride=cols), :])


def gate_kernel(x_ref, w_ref, gate_ref):
    v = jnp.dot(x_ref[...], w_ref[...], preferred_element_type=F32)
    gate_ref[...] = v / (1.0 + jnp.exp(-v))


def early_kernel(frames, rows, cols, *refs):
    far, (fields_ref, table_ref, side_ref), near, (arrived, held) = refs[:3], refs[3:6], refs[6:9], refs[9:]
    copies = [pltpu.make_async_copy(a, b, arrived.at[i]) for i, (a, b) in enumerate(zip(far, near))]
    for copy in copies:
        copy.start()
    taps_ref, skip_ref, x_ref = near
    lags, chans = taps_ref.shape
    copies[0].wait()
    copies[1].wait()
    pad = 2 * frames
    taps = taps_ref[...].astype(F32)
    table_ref[0:pad] = jnp.zeros((pad, cols, chans), F32)
    for lag in range(lags):
        tap = taps[lag : lag + 1] + (skip_ref[...] if lag == 0 else 0.0)
        table_ref[pad + lag] = jnp.broadcast_to(tap, (cols, chans))
    sites = rows * cols
    block = frames * sites
    copies[2].wait()
    for lane in range(0, chans, LANES):
        span = slice(lane, lane + LANES)
        held[...] = x_ref[:, span].astype(F32)
        side_ref[:, span] = outer_column(held, frames * rows, cols)
        for d in range(fields_ref.shape[0] // block):
            totals = [None] * frames
            for s in range(frames):
                x = x_ref[s * sites : (s + 1) * sites, span].astype(F32).reshape(rows, cols, LANES)
                for t in range(s if d == 0 else 0, frames):
                    term = table_ref[pad + 2 * d * frames + t - s, :, span] * x
                    totals[t] = term if totals[t] is None else totals[t] + term
            for t in range(frames):
                at = d * block + t * sites
                fields_ref[at : at + sites, span] = totals[t].reshape(sites, LANES)


def reordered(lines, rounds_h, back=False):
    if rounds_h > 1:
        return lines[:1] + lines[2:] + lines[1:2] if back else lines[:1] + lines[-1:] + lines[1:-1]
    odd = position("height")[0]
    return [jnp.where(odd, a, b) for a, b in zip(lines, lines[::-1])]


def mix_kernel(frames, rows, cols, rounds_h, partner_ref, fields_ref, table_ref, side_ref, mine_ref, *refs):
    *outs, held = refs
    sites = rows * cols
    lines = frames * rows
    block = frames * sites
    pad = 2 * frames
    shift = jnp.where(second(), frames, -frames)
    for lane in range(0, mine_ref.shape[1], LANES):
        span = slice(lane, lane + LANES)
        held[...] = partner_ref[:, span].astype(F32)
        near = [side_ref[s * rows : (s + 1) * rows, span] for s in range(frames)]
        far = outer_column(held, lines, cols)
        for d in range(fields_ref.shape[0] // block):
            totals = []
            for t in range(frames):
                at = d * block + t * sites
                totals.append(fields_ref[at : at + sites, span].reshape(rows, cols, LANES))
            base = pad + 2 * d * frames
            for s in range(frames):
                x = partner_ref[s * sites : (s + 1) * sites, span].astype(F32).reshape(rows, cols, LANES)
                for t in range(frames):
                    totals[t] = totals[t] + table_ref[base + shift + t - s, :, span] * x
            for t in range(frames):
                held[t * sites : (t + 1) * sites, :] = totals[t].reshape(sites, LANES)
            if d:
                tiles = [jnp.concatenate([t[r] for t in totals]) for r in range(rows)]
                tiles = reordered(tiles, rounds_h)
                outs[3 * d - 1][:, span] = jnp.concatenate(tiles[:2]).astype(BF16)
                outs[3 * d][:, span] = jnp.concatenate(tiles[2:]).astype(BF16)
            else:
                mine_ref[:, span] = held[...]
            ends = []
            for t in range(frames):
                end = jnp.zeros((rows, LANES), F32)
                for s in range(frames):
                    end = end + table_ref[base - shift + t - s, :, span] * near[s]
                    if d or t >= s:
                        end = end + table_ref[base + t - s, :, span] * far[s * rows : (s + 1) * rows]
                ends.append(end)
            column = jnp.concatenate([outer_column(held, lines, cols)] + ends, axis=0)
            outs[3 * d - 2 if d else 0][:, span] = column.astype(BF16)


def later(d, value):
    return jnp.where(lax.div(lax.axis_index("tm"), 2) >= d, value, jnp.zeros_like(value))


def side_kernel(lines, *refs):
    *arrived, own_ref, other_ref = refs
    _, lower, upper = position("width")
    exists = jnp.where(on_right(), upper, lower)
    total = 0.0
    for d, ref in enumerate(arrived[::-1]):
        total = total + later(d, ref[...].astype(F32))
    total = jnp.where(exists, total, jnp.zeros_like(total))
    own_ref[...] = total[:lines]
    other_ref[...] = total[lines:].astype(BF16)


def border_kernel(frames, rows, cols, chips, mine_ref, own_ref, other_ref, *refs):
    arrived, (low_ref, high_ref, *outs) = refs[: chips - 1], refs[chips - 1 :]
    sites = rows * cols
    odd, _, _ = position("height")
    right, own, other = on_right(), own_ref[...], other_ref[...].astype(F32)
    low, high = jnp.where(right, other, own), jnp.where(right, own, other)
    low_ref[...] = low
    high_ref[...] = high
    size = frames * cols
    lines, corners = [], []
    for r in (0, rows - 1):
        lines.append(jnp.concatenate([mine_ref[t * sites + r * cols : t * sites + (r + 1) * cols] for t in range(frames)]))
        ends = [side[t * rows + r : t * rows + r + 1] for side in (low, high) for t in range(frames)]
        corners.append(jnp.concatenate(ends))
    for k, out in enumerate(outs):
        line = jnp.where(odd, *(lines[::-1] if k else lines))
        for d, ref in enumerate(arrived, 1):
            if len(outs) > 1:
                ends = [ref[i * size : (i + 1) * size].astype(F32) for i in range(2)]
                more = jnp.where(odd, *(ends[::-1] if k else ends))
            else:
                more = ref[:size].astype(F32)
            line = line + later(d, more)
        out[...] = jnp.concatenate([line, jnp.where(odd, *(corners[::-1] if k else corners))]).astype(BF16)


def shifted(line, left, right):
    cols = line.shape[0]
    place = lax.broadcasted_iota(jnp.int32, line.shape, 0)
    before = jnp.where(place == 0, left, pltpu.roll(line, 1, 0))
    after = jnp.where(place == cols - 1, right, pltpu.roll(line, cols - 1, 0))
    return before, line, after


def projected(mixed, gate, wv_ref, wo_ref):
    value = jnp.dot(mixed, wv_ref[...], preferred_element_type=F32)
    hidden = (value * gate).astype(BF16)
    return jnp.dot(hidden, wo_ref[...], preferred_element_type=F32).astype(BF16)


def inner_kernel(
    frames, rows, cols, rounds_h, mine_ref, low_ref, high_ref, taps_ref, gate_ref, wv_ref, wo_ref, *refs
):
    *parts, out_ref, edges_ref, mixed = refs
    firsts, rests = parts[: len(parts) // 2], parts[len(parts) // 2 :]
    chans = mine_ref.shape[1]
    sites = rows * cols
    size = frames * cols
    for lane in range(0, chans, LANES):
        span = slice(lane, lane + LANES)
        taps = [[taps_ref[3 * a + b : 3 * a + b + 1, span] for b in range(3)] for a in range(3)]
        low, high = low_ref[:, span], high_ref[:, span]
        lines = [
            jnp.concatenate([mine_ref[t * sites + r * cols : t * sites + (r + 1) * cols, span] for t in range(frames)])
            for r in range(rows)
        ]
        for d, (first, rest) in enumerate(zip(firsts, rests), 1):
            more = [first[i * size : (i + 1) * size, span].astype(F32) for i in range(2)]
            more += [rest[i * size : (i + 1) * size, span].astype(F32) for i in range(rows - 2)]
            more = reordered(more, rounds_h, back=True)
            lines = [line + later(d, other) for line, other in zip(lines, more)]
        for t in range(frames):
            at = t * sites
            totals = [None] * rows
            for r in range(rows):
                row = t * rows + r
                near = shifted(lines[r][t * cols : (t + 1) * cols], low[row : row + 1], high[row : row + 1])
                for a in range(3):
                    to = r + 1 - a
                    if 0 <= to < rows:
                        term = near[0] * taps[a][0] + near[1] * taps[a][1] + near[2] * taps[a][2]
                        totals[to] = term if totals[to] is None else totals[to] + term
            mixed[at : at + sites, span] = jnp.concatenate(totals, axis=0).astype(BF16)
            edges_ref[t * cols : (t + 1) * cols, span] = totals[0]
            edges_ref[(frames + t) * cols : (frames + t + 1) * cols, span] = totals[rows - 1]
    out_ref[...] = projected(mixed[...], gate_ref[...], wv_ref, wo_ref)


def edge_kernel(frames, rows, cols, rounds_h, edges_ref, taps_ref, gate_ref, wv_ref, wo_ref, inner_ref, *refs):
    ends, out_ref = refs[:rounds_h], refs[rounds_h]
    sites = rows * cols
    size = frames * cols
    odd, _, _ = position("height")
    out_ref[...] = inner_ref[...]
    taps = taps_ref[...]
    mixed, gate = [], []
    for k, end in enumerate(ends):
        end = end[...].astype(F32)
        first = jnp.logical_not(odd) if k else odd
        lefts, rights = end[size : size + frames], end[size + frames : size + 2 * frames]
        lower, upper = position("height")[1:]
        exists = jnp.where(first, lower, upper)
        tap = jnp.where(first, taps[0:3], taps[6:9])
        total = jnp.where(first, edges_ref[0:size], edges_ref[size : 2 * size])
        for t in range(frames):
            near = shifted(end[t * cols : (t + 1) * cols], lefts[t : t + 1], rights[t : t + 1])
            more = near[0] * tap[0:1] + near[1] * tap[1:2] + near[2] * tap[2:3]
            mixed.append(total[t * cols : (t + 1) * cols] + jnp.where(exists, more, jnp.zeros_like(more)))
            at = t * sites
            gate.append(jnp.where(first, gate_ref[at : at + cols], gate_ref[at + sites - cols : at + sites]))
    out = projected(jnp.concatenate(mixed, axis=0).astype(BF16), jnp.concatenate(gate, axis=0), wv_ref, wo_ref)
    for t in range(frames):
        new = [out[k * size + t * cols : k * size + (t + 1) * cols] for k in range(rounds_h)]
        for at, other in ((t * sites, False), (t * sites + sites - cols, True)):
            kept = new[1] if rounds_h > 1 else inner_ref[at : at + cols]
            out_ref[at : at + cols] = jnp.where(odd, kept, new[0]) if other else jnp.where(odd, new[0], kept)


def body(latents, spatial_taps, kernel_taps, skip_gain, gate_weight, value_weight, out_weight):
    frames, rows, cols, chans = latents.shape
    lags = kernel_taps.shape[0]
    n_t, n_h, n_w = lax.axis_size("tm"), lax.axis_size("height"), lax.axis_size("width")
    chips = n_t // 2
    block = frames * rows * cols
    shape = jax.ShapeDtypeStruct
    x = latents.reshape(block, chans)

    partner = lax.ppermute(x, "tm", [(i, i ^ 1) for i in range(n_t)])
    inputs = [kernel_taps, skip_gain.reshape(1, chans), x]
    lines = frames * rows
    fields, table, side = call(
        functools.partial(early_kernel, frames, rows, cols),
        "early",
        [
            shape((chips * block, chans), F32),
            shape((lags + 2 * frames, cols, chans), F32),
            shape((lines, chans), F32),
        ],
        [pltpu.VMEM(a.shape, a.dtype) for a in inputs]
        + [pltpu.SemaphoreType.DMA((len(inputs),)), pltpu.VMEM((block, LANES), F32)],
        inputs,
        2 * chips * frames * x.size,
        far=len(inputs),
    )
    (gate,) = call(
        gate_kernel, "gate", [shape((block, chans), F32)], [], [x, gate_weight], 2 * block * chans * chans, x.size
    )

    h_rounds = swaps("height")
    column = shape((2 * lines, chans), BF16)
    parts = [shape((n * frames * cols, chans), BF16) for n in (2, rows - 2)]
    mine, *sent = call(
        functools.partial(mix_kernel, frames, rows, cols, len(h_rounds)),
        "mix",
        [shape((block, chans), F32), column] + ([column] + parts) * (chips - 1),
        [pltpu.VMEM((block, LANES), F32)],
        [partner, fields, table, side],
        2 * chips * frames * x.size,
    )
    columns, firsts, rests = [], [], []
    sent = [sent[0:1]] + [sent[i : i + 3] for i in range(1, len(sent), 3)]
    for d in reversed(range(chips)):
        route = []
        for i in range(n_t):
            for h in range(n_h):
                for j in range(n_w):
                    to = facing(i % 2, j, n_w)
                    beside = h ^ 1 if to == j and n_h % 2 == 0 else h
                    source = (i * n_h + h) * n_w + j
                    route.append((source, ((i + 2 * d) % n_t * n_h + beside) * n_w + to))
        columns.append(lax.ppermute(sent[d].pop(0), ("tm", "height", "width"), route))
    for d in range(1, chips):
        for kept in (firsts, rests):
            kept.append(lax.ppermute(sent[d].pop(0), "tm", [(i, (i + 2 * d) % n_t) for i in range(n_t)]))

    own, other = call(
        functools.partial(side_kernel, lines),
        "side",
        [shape((lines, chans), F32), shape((lines, chans), BF16)],
        [],
        columns,
        LATER,
    )
    other = lax.ppermute(other, "tm", [(i, i ^ 1) for i in range(n_t)])
    size = frames * cols + 2 * frames
    low, high, *ends = call(
        functools.partial(border_kernel, frames, rows, cols, chips),
        "border",
        [shape((lines, chans), F32)] * 2 + [shape((size, chans), BF16)] * len(h_rounds),
        [],
        [mine, own, other] + firsts,
    )
    ends = [lax.ppermute(e, "height", pairs) for e, pairs in zip(ends, h_rounds)]

    taps = spatial_taps.reshape(9, chans)
    inner, edges = call(
        functools.partial(inner_kernel, frames, rows, cols, len(h_rounds)),
        "inner",
        [shape((block, chans), BF16), shape((2 * frames * cols, chans), F32)],
        [pltpu.VMEM((block, chans), BF16)],
        [mine, low, high, taps, gate, value_weight, out_weight] + firsts + rests,
        4 * block * chans * chans,
    )
    (out,) = call(
        functools.partial(edge_kernel, frames, rows, cols, len(h_rounds)),
        "edge",
        [shape((block, chans), BF16)],
        [],
        [edges, taps, gate, value_weight, out_weight, inner] + ends,
        4 * frames * cols * chans * chans,
    )
    return out.reshape(latents.shape)


def solution(mesh):
    in_specs = (P("tm", "height", "width", None), P(), P(), P(), P(), P(), P())
    out_specs = P("tm", "height", "width", None)
    return jax.shard_map(body, mesh=mesh, in_specs=in_specs, out_specs=out_specs, check_vma=False)
```

```python
import functools

import jax
import jax.numpy as jnp
from jax import lax
from jax.experimental import pallas as pl
from jax.experimental.pallas import tpu as pltpu
from jax.sharding import PartitionSpec as P

LANES = 128
LATER = 8 * 10**9
F32, BF16 = jnp.float32, jnp.bfloat16
VMEM = pl.BlockSpec(memory_space=pltpu.VMEM)
HBM = pl.BlockSpec(memory_space=pltpu.HBM)


def call(kernel, name, outs, scratch, operands, flops=0, exps=0, far=0, far_outs=0, aliases={}):
    operands = [pltpu.with_memory_space_constraint(a, pltpu.HBM) for a in operands[:far]] + list(operands[far:])
    moved = sum(a.size * a.dtype.itemsize for a in operands) + sum(a.size * a.dtype.itemsize for a in outs)
    return pl.pallas_call(
        kernel,
        out_shape=tuple(outs),
        in_specs=[HBM] * far + [VMEM] * (len(operands) - far),
        out_specs=(HBM,) * far_outs + (VMEM,) * (len(outs) - far_outs),
        scratch_shapes=scratch,
        input_output_aliases=aliases,
        compiler_params=pltpu.CompilerParams(vmem_limit_bytes=24 * 1024 * 1024),
        cost_estimate=pl.CostEstimate(flops=flops, bytes_accessed=moved, transcendentals=exps),
        name=name,
    )(*operands)


def swaps(axis):
    n = lax.axis_size(axis)
    rounds = []
    for first in range(2 if n > 2 else 1):
        to = list(range(n))
        for i in range(first, n - 1, 2):
            to[i], to[i + 1] = i + 1, i
        rounds.append(list(enumerate(to)))
    return rounds


def position(axis):
    i, n = lax.axis_index(axis), lax.axis_size(axis)
    return lax.rem(i, 2) == 1, i > 0, i < n - 1


def second():
    return lax.rem(lax.axis_index("tm"), 2) == 1


def on_right():
    return lax.rem(lax.axis_index("tm") + lax.axis_index("width"), 2) == 0


def facing(core, column, columns):
    to = column + (1 if (core + column) % 2 == 0 else -1)
    return to if 0 <= to < columns else column


def outer_column(ref, lines, cols):
    return jnp.where(on_right(), ref[pl.ds(cols - 1, lines, stride=cols), :], ref[pl.ds(0, lines, stride=cols), :])


def gate_kernel(x_ref, w_ref, gate_ref):
    v = jnp.dot(x_ref[...], w_ref[...], preferred_element_type=F32)
    gate_ref[...] = v / (1.0 + jnp.exp(-v))


def early_kernel(frames, rows, cols, *refs):
    far, (table_ref, side_ref, *fields), near, (arrived, held) = refs[:3], refs[3:-5], refs[-5:-2], refs[-2:]
    copies = [pltpu.make_async_copy(a, b, arrived.at[i]) for i, (a, b) in enumerate(zip(far, near))]
    for copy in copies:
        copy.start()
    taps_ref, skip_ref, x_ref = near
    lags, chans = taps_ref.shape
    copies[0].wait()
    copies[1].wait()
    pad = 2 * frames
    taps = taps_ref[...].astype(F32)
    table_ref[0:pad] = jnp.zeros((pad, cols, chans), F32)
    for lag in range(lags):
        tap = taps[lag : lag + 1] + (skip_ref[...] if lag == 0 else 0.0)
        table_ref[pad + lag] = jnp.broadcast_to(tap, (cols, chans))
    sites = rows * cols
    copies[2].wait()
    for lane in range(0, chans, LANES):
        span = slice(lane, lane + LANES)
        held[...] = x_ref[:, span].astype(F32)
        side_ref[:, span] = outer_column(held, frames * rows, cols)
        for d, field in enumerate(fields):
            totals = [None] * frames
            for s in range(frames):
                x = x_ref[s * sites : (s + 1) * sites, span].astype(F32).reshape(rows, cols, LANES)
                for t in range(s if d == 0 else 0, frames):
                    term = table_ref[pad + 2 * d * frames + t - s, :, span] * x
                    totals[t] = term if totals[t] is None else totals[t] + term
            for t in range(frames):
                field[t * sites : (t + 1) * sites, span] = totals[t].reshape(sites, LANES)


def reordered(lines, rounds_h, back=False):
    if rounds_h > 1:
        return lines[:1] + lines[2:] + lines[1:2] if back else lines[:1] + lines[-1:] + lines[1:-1]
    odd = position("height")[0]
    return [jnp.where(odd, a, b) for a, b in zip(lines, lines[::-1])]


def column_kernel(frames, rows, cols, partner_ref, side_ref, out_ref, held):
    lines = frames * rows
    for lane in range(0, out_ref.shape[1], LANES):
        span = slice(lane, lane + LANES)
        held[...] = partner_ref[:, span].astype(F32)
        out_ref[:, span] = jnp.concatenate([side_ref[:, span], outer_column(held, lines, cols)]).astype(BF16)


def shift(frames):
    return jnp.where(second(), frames, -frames)


def with_partner(frames, rows, cols, d, field_ref, partner_ref, table_ref, span):
    sites = rows * cols
    base = 2 * frames + 2 * d * frames + shift(frames)
    totals = [field_ref[t * sites : (t + 1) * sites, span].reshape(rows, cols, LANES) for t in range(frames)]
    for s in range(frames):
        x = partner_ref[s * sites : (s + 1) * sites, span].astype(F32).reshape(rows, cols, LANES)
        for t in range(frames):
            totals[t] = totals[t] + table_ref[base + t - s, :, span] * x
    return totals


def later_kernel(frames, rows, cols, rounds_h, partner_ref, table_ref, *refs):
    fields, outs = refs[: len(refs) // 3], refs[len(refs) // 3 :]
    for d, field in enumerate(fields, 1):
        for lane in range(0, field.shape[1], LANES):
            span = slice(lane, lane + LANES)
            totals = with_partner(frames, rows, cols, d, field, partner_ref, table_ref, span)
            tiles = reordered([jnp.concatenate([t[r] for t in totals]) for r in range(rows)], rounds_h)
            outs[2 * d - 2][:, span] = jnp.concatenate(tiles[:2]).astype(BF16)
            outs[2 * d - 1][:, span] = jnp.concatenate(tiles[2:]).astype(BF16)


def own_kernel(frames, rows, cols, partner_ref, table_ref, field_ref, mine_ref):
    for lane in range(0, mine_ref.shape[1], LANES):
        span = slice(lane, lane + LANES)
        totals = with_partner(frames, rows, cols, 0, field_ref, partner_ref, table_ref, span)
        mine_ref[:, span] = jnp.concatenate(totals).reshape(mine_ref.shape[0], LANES)


def later(d, value):
    return jnp.where(lax.div(lax.axis_index("tm"), 2) >= d, value, jnp.zeros_like(value))


def side_kernel(frames, rows, table_ref, *refs):
    *arrived, own_ref, other_ref = refs
    _, lower, upper = position("width")
    exists = jnp.where(on_right(), upper, lower)
    for lane in range(0, own_ref.shape[1], LANES):
        span = slice(lane, lane + LANES)
        totals = [jnp.zeros((rows, LANES), F32)] * (2 * frames)
        for d, ref in enumerate(arrived[::-1]):
            column = later(d, ref[:, span].astype(F32))
            base = 2 * frames + 2 * d * frames
            for t in range(2 * frames):
                for s in range(2 * frames):
                    lag = t % frames - s % frames
                    if t // frames == s // frames:
                        if d == 0 and lag < 0:
                            continue
                    else:
                        lag = lag + (shift(frames) if t < frames else -shift(frames))
                    totals[t] = totals[t] + table_ref[base + lag, :, span] * column[s * rows : (s + 1) * rows]
        totals = [jnp.where(exists, total, jnp.zeros_like(total)) for total in totals]
        own_ref[:, span] = jnp.concatenate(totals[:frames])
        other_ref[:, span] = jnp.concatenate(totals[frames:]).astype(BF16)


def border_kernel(frames, rows, cols, chips, mine_ref, own_ref, other_ref, *refs):
    arrived, (low_ref, high_ref, *outs) = refs[: chips - 1], refs[chips - 1 :]
    sites = rows * cols
    odd, _, _ = position("height")
    right, own, other = on_right(), own_ref[...], other_ref[...].astype(F32)
    low, high = jnp.where(right, other, own), jnp.where(right, own, other)
    low_ref[...] = low
    high_ref[...] = high
    size = frames * cols
    lines, corners = [], []
    for r in (0, rows - 1):
        lines.append(jnp.concatenate([mine_ref[t * sites + r * cols : t * sites + (r + 1) * cols] for t in range(frames)]))
        ends = [side[t * rows + r : t * rows + r + 1] for side in (low, high) for t in range(frames)]
        corners.append(jnp.concatenate(ends))
    for k, out in enumerate(outs):
        line = jnp.where(odd, *(lines[::-1] if k else lines))
        for d, ref in enumerate(arrived, 1):
            if len(outs) > 1:
                ends = [ref[i * size : (i + 1) * size].astype(F32) for i in range(2)]
                more = jnp.where(odd, *(ends[::-1] if k else ends))
            else:
                more = ref[:size].astype(F32)
            line = line + later(d, more)
        out[...] = jnp.concatenate([line, jnp.where(odd, *(corners[::-1] if k else corners))]).astype(BF16)


def shifted(line, left, right):
    cols = line.shape[0]
    place = lax.broadcasted_iota(jnp.int32, line.shape, 0)
    before = jnp.where(place == 0, left, pltpu.roll(line, 1, 0))
    after = jnp.where(place == cols - 1, right, pltpu.roll(line, cols - 1, 0))
    return before, line, after


def projected(mixed, gate, wv_ref, wo_ref):
    value = jnp.dot(mixed, wv_ref[...], preferred_element_type=F32)
    hidden = (value * gate).astype(BF16)
    return jnp.dot(hidden, wo_ref[...], preferred_element_type=F32).astype(BF16)


def inner_kernel(
    frames, rows, cols, rounds_h, mine_ref, low_ref, high_ref, taps_ref, gate_ref, wv_ref, wo_ref, *refs
):
    *parts, out_ref, edges_ref, mixed, held, done = refs
    firsts, rests = parts[: len(parts) // 2], parts[len(parts) // 2 :]
    chans = mine_ref.shape[1]
    sites = rows * cols
    size = frames * cols
    for lane in range(0, chans, LANES):
        span = slice(lane, lane + LANES)
        taps = [[taps_ref[3 * a + b : 3 * a + b + 1, span] for b in range(3)] for a in range(3)]
        low, high = low_ref[:, span], high_ref[:, span]
        lines = [
            jnp.concatenate([mine_ref[t * sites + r * cols : t * sites + (r + 1) * cols, span] for t in range(frames)])
            for r in range(rows)
        ]
        for d, (first, rest) in enumerate(zip(firsts, rests), 1):
            more = [first[i * size : (i + 1) * size, span].astype(F32) for i in range(2)]
            more += [rest[i * size : (i + 1) * size, span].astype(F32) for i in range(rows - 2)]
            more = reordered(more, rounds_h, back=True)
            lines = [line + later(d, other) for line, other in zip(lines, more)]
        for t in range(frames):
            at = t * sites
            totals = [None] * rows
            for r in range(rows):
                row = t * rows + r
                near = shifted(lines[r][t * cols : (t + 1) * cols], low[row : row + 1], high[row : row + 1])
                for a in range(3):
                    to = r + 1 - a
                    if 0 <= to < rows:
                        term = near[0] * taps[a][0] + near[1] * taps[a][1] + near[2] * taps[a][2]
                        totals[to] = term if totals[to] is None else totals[to] + term
            mixed[at : at + sites, span] = jnp.concatenate(totals, axis=0).astype(BF16)
            for k, edge in enumerate((totals[:2], totals[-2:])):
                edges_ref[2 * (k * size + t * cols) : 2 * (k * size + (t + 1) * cols), span] = jnp.concatenate(edge)
    held[...] = projected(mixed[...], gate_ref[...], wv_ref, wo_ref)
    copy = pltpu.make_async_copy(held, out_ref, done)
    copy.start()
    copy.wait()


def edge_kernel(frames, rows, cols, rounds_h, inner_ref, edges_ref, taps_ref, gate_ref, wv_ref, wo_ref, *refs):
    ends, (out_ref, held, done) = refs[:rounds_h], refs[rounds_h:]
    sites = rows * cols
    size = frames * cols
    odd, lower, upper = position("height")
    taps = taps_ref[...]
    mixed, gate, starts = [], [], []
    for k, end in enumerate(ends):
        end = end[...].astype(F32)
        first = jnp.logical_not(odd) if k else odd
        lefts, rights = end[size : size + frames], end[size + frames : size + 2 * frames]
        exists = jnp.where(first, lower, upper)
        tap = jnp.where(first, taps[0:3], taps[6:9])
        total = jnp.where(first, edges_ref[: 2 * size], edges_ref[2 * size :])
        for t in range(frames):
            near = shifted(end[t * cols : (t + 1) * cols], lefts[t : t + 1], rights[t : t + 1])
            more = near[0] * tap[0:1] + near[1] * tap[1:2] + near[2] * tap[2:3]
            more = jnp.where(exists, more, jnp.zeros_like(more))
            none = jnp.zeros_like(more)
            mixed.append(total[2 * t * cols : (2 * t + 1) * cols] + jnp.where(first, more, none))
            mixed.append(total[(2 * t + 1) * cols : (2 * t + 2) * cols] + jnp.where(first, none, more))
            at = t * sites
            gate.append(jnp.where(first, gate_ref[at : at + 2 * cols], gate_ref[at + sites - 2 * cols : at + sites]))
            starts.append(pl.multiple_of(at + jnp.where(first, 0, sites - 2 * cols), 2 * cols))
    held[...] = projected(jnp.concatenate(mixed).astype(BF16), jnp.concatenate(gate), wv_ref, wo_ref)
    copies = [
        pltpu.make_async_copy(held.at[pl.ds(2 * i * cols, 2 * cols)], out_ref.at[pl.ds(at, 2 * cols)], done.at[i])
        for i, at in enumerate(starts)
    ]
    for copy in copies:
        copy.start()
    for copy in copies:
        copy.wait()


def body(latents, spatial_taps, kernel_taps, skip_gain, gate_weight, value_weight, out_weight):
    frames, rows, cols, chans = latents.shape
    lags = kernel_taps.shape[0]
    n_t, n_h, n_w = lax.axis_size("tm"), lax.axis_size("height"), lax.axis_size("width")
    chips = n_t // 2
    block = frames * rows * cols
    shape = jax.ShapeDtypeStruct
    x = latents.reshape(block, chans)

    partner = lax.ppermute(x, "tm", [(i, i ^ 1) for i in range(n_t)])
    inputs = [kernel_taps, skip_gain.reshape(1, chans), x]
    lines = frames * rows
    field = shape((block, chans), F32)
    table, side, *fields = call(
        functools.partial(early_kernel, frames, rows, cols),
        "early",
        [shape((lags + 2 * frames, cols, chans), F32), shape((lines, chans), F32)] + [field] * chips,
        [pltpu.VMEM(a.shape, a.dtype) for a in inputs]
        + [pltpu.SemaphoreType.DMA((len(inputs),)), pltpu.VMEM((block, LANES), F32)],
        inputs,
        2 * chips * frames * x.size,
        far=len(inputs),
    )
    (gate,) = call(
        gate_kernel, "gate", [shape((block, chans), F32)], [], [x, gate_weight], 2 * block * chans * chans, x.size
    )

    h_rounds = swaps("height")
    (column,) = call(
        functools.partial(column_kernel, frames, rows, cols),
        "column",
        [shape((2 * lines, chans), BF16)],
        [pltpu.VMEM((block, LANES), F32)],
        [partner, side],
    )
    parts = [shape((n * frames * cols, chans), BF16) for n in (2, rows - 2)]
    sent = call(
        functools.partial(later_kernel, frames, rows, cols, len(h_rounds)),
        "later",
        parts * (chips - 1),
        [],
        [partner, table] + fields[1:],
        2 * (chips - 1) * frames * x.size,
    )
    (mine,) = call(
        functools.partial(own_kernel, frames, rows, cols),
        "own",
        [field],
        [],
        [partner, table, fields[0]],
        2 * frames * x.size,
    )
    columns, firsts, rests = [], [], []
    for d in reversed(range(chips)):
        route = []
        for i in range(n_t):
            for h in range(n_h):
                for j in range(n_w):
                    to = facing(i % 2, j, n_w)
                    beside = h ^ 1 if to == j and n_h % 2 == 0 else h
                    source = (i * n_h + h) * n_w + j
                    route.append((source, ((i + 2 * d) % n_t * n_h + beside) * n_w + to))
        columns.append(lax.ppermute(column, ("tm", "height", "width"), route))
    for d in range(1, chips):
        route = [(i, (i + 2 * d) % n_t) for i in range(n_t)]
        firsts.append(lax.ppermute(sent[2 * d - 2], "tm", route))
        rests.append(lax.ppermute(sent[2 * d - 1], "tm", route))

    own, other = call(
        functools.partial(side_kernel, frames, rows),
        "side",
        [shape((lines, chans), F32), shape((lines, chans), BF16)],
        [],
        [table] + columns,
        LATER,
    )
    other = lax.ppermute(other, "tm", [(i, i ^ 1) for i in range(n_t)])
    size = frames * cols + 2 * frames
    low, high, *ends = call(
        functools.partial(border_kernel, frames, rows, cols, chips),
        "border",
        [shape((lines, chans), F32)] * 2 + [shape((size, chans), BF16)] * len(h_rounds),
        [],
        [mine, own, other] + firsts,
    )
    ends = [lax.ppermute(e, "height", pairs) for e, pairs in zip(ends, h_rounds)]

    taps = spatial_taps.reshape(9, chans)
    inner, edges = call(
        functools.partial(inner_kernel, frames, rows, cols, len(h_rounds)),
        "inner",
        [shape((block, chans), BF16), shape((4 * frames * cols, chans), F32)],
        [pltpu.VMEM((block, chans), BF16)] * 2 + [pltpu.SemaphoreType.DMA],
        [mine, low, high, taps, gate, value_weight, out_weight] + firsts + rests,
        4 * block * chans * chans,
        far_outs=1,
    )
    (out,) = call(
        functools.partial(edge_kernel, frames, rows, cols, len(h_rounds)),
        "edge",
        [shape((block, chans), BF16)],
        [
            pltpu.VMEM((len(h_rounds) * 2 * frames * cols, chans), BF16),
            pltpu.SemaphoreType.DMA((len(h_rounds) * frames,)),
        ],
        [inner, edges, taps, gate, value_weight, out_weight] + ends,
        8 * frames * cols * chans * chans,
        far=1,
        far_outs=1,
        aliases={0: 0},
    )
    return out.reshape(latents.shape)


def solution(mesh):
    in_specs = (P("tm", "height", "width", None), P(), P(), P(), P(), P(), P())
    out_specs = P("tm", "height", "width", None)
    return jax.shard_map(body, mesh=mesh, in_specs=in_specs, out_specs=out_specs, check_vma=False)
```

```python
import functools

import jax
import jax.numpy as jnp
from jax import lax
from jax.experimental import pallas as pl
from jax.experimental.pallas import tpu as pltpu
from jax.sharding import PartitionSpec as P

LANES = 128
LATER = 8 * 10**9
F32, BF16 = jnp.float32, jnp.bfloat16
VMEM = pl.BlockSpec(memory_space=pltpu.VMEM)
HBM = pl.BlockSpec(memory_space=pltpu.HBM)


def call(kernel, name, outs, scratch, operands, flops=0, exps=0, far=0):
    operands = [pltpu.with_memory_space_constraint(a, pltpu.HBM) for a in operands[:far]] + list(operands[far:])
    moved = sum(a.size * a.dtype.itemsize for a in operands) + sum(a.size * a.dtype.itemsize for a in outs)
    return pl.pallas_call(
        kernel,
        out_shape=tuple(outs),
        in_specs=[HBM] * far + [VMEM] * (len(operands) - far),
        out_specs=(VMEM,) * len(outs),
        scratch_shapes=scratch,
        compiler_params=pltpu.CompilerParams(vmem_limit_bytes=24 * 1024 * 1024),
        cost_estimate=pl.CostEstimate(flops=flops, bytes_accessed=moved, transcendentals=exps),
        name=name,
    )(*operands)


def swaps(axis):
    n = lax.axis_size(axis)
    rounds = []
    for first in range(2 if n > 2 else 1):
        to = list(range(n))
        for i in range(first, n - 1, 2):
            to[i], to[i + 1] = i + 1, i
        rounds.append(list(enumerate(to)))
    return rounds


def position(axis):
    i, n = lax.axis_index(axis), lax.axis_size(axis)
    return lax.rem(i, 2) == 1, i > 0, i < n - 1


def second():
    return lax.rem(lax.axis_index("tm"), 2) == 1


def on_right():
    return lax.rem(lax.axis_index("tm") + lax.axis_index("width"), 2) == 0


def facing(core, column, columns):
    to = column + (1 if (core + column) % 2 == 0 else -1)
    return to if 0 <= to < columns else column


def outer_column(ref, lines, cols):
    return jnp.where(on_right(), ref[pl.ds(cols - 1, lines, stride=cols), :], ref[pl.ds(0, lines, stride=cols), :])


def gate_kernel(x_ref, w_ref, gate_ref):
    v = jnp.dot(x_ref[...], w_ref[...], preferred_element_type=F32)
    gate_ref[...] = v / (1.0 + jnp.exp(-v))


def early_kernel(frames, rows, cols, *refs):
    far, (table_ref, side_ref, *fields), near, (arrived, held) = refs[:3], refs[3:-5], refs[-5:-2], refs[-2:]
    copies = [pltpu.make_async_copy(a, b, arrived.at[i]) for i, (a, b) in enumerate(zip(far, near))]
    for copy in copies:
        copy.start()
    taps_ref, skip_ref, x_ref = near
    lags, chans = taps_ref.shape
    copies[0].wait()
    copies[1].wait()
    pad = 2 * frames
    taps = taps_ref[...].astype(F32)
    table_ref[0:pad] = jnp.zeros((pad, cols, chans), F32)
    for lag in range(lags):
        tap = taps[lag : lag + 1] + (skip_ref[...] if lag == 0 else 0.0)
        table_ref[pad + lag] = jnp.broadcast_to(tap, (cols, chans))
    sites = rows * cols
    copies[2].wait()
    for lane in range(0, chans, LANES):
        span = slice(lane, lane + LANES)
        held[...] = x_ref[:, span].astype(F32)
        side_ref[:, span] = outer_column(held, frames * rows, cols)
        for d, field in enumerate(fields):
            totals = [None] * frames
            for s in range(frames):
                x = x_ref[s * sites : (s + 1) * sites, span].astype(F32).reshape(rows, cols, LANES)
                for t in range(s if d == 0 else 0, frames):
                    term = table_ref[pad + 2 * d * frames + t - s, :, span] * x
                    totals[t] = term if totals[t] is None else totals[t] + term
            for t in range(frames):
                field[t * sites : (t + 1) * sites, span] = totals[t].reshape(sites, LANES)


def reordered(lines, rounds_h, back=False):
    if rounds_h > 1:
        return lines[:1] + lines[2:] + lines[1:2] if back else lines[:1] + lines[-1:] + lines[1:-1]
    odd = position("height")[0]
    return [jnp.where(odd, a, b) for a, b in zip(lines, lines[::-1])]


def column_kernel(frames, rows, cols, partner_ref, side_ref, out_ref, held):
    lines = frames * rows
    for lane in range(0, out_ref.shape[1], LANES):
        span = slice(lane, lane + LANES)
        held[...] = partner_ref[:, span].astype(F32)
        out_ref[:, span] = jnp.concatenate([side_ref[:, span], outer_column(held, lines, cols)]).astype(BF16)


def shift(frames):
    return jnp.where(second(), frames, -frames)


def with_partner(frames, rows, cols, d, field_ref, partner_ref, table_ref, span):
    sites = rows * cols
    base = 2 * frames + 2 * d * frames + shift(frames)
    totals = [field_ref[t * sites : (t + 1) * sites, span].reshape(rows, cols, LANES) for t in range(frames)]
    for s in range(frames):
        x = partner_ref[s * sites : (s + 1) * sites, span].astype(F32).reshape(rows, cols, LANES)
        for t in range(frames):
            totals[t] = totals[t] + table_ref[base + t - s, :, span] * x
    return totals


def later_kernel(frames, rows, cols, rounds_h, partner_ref, table_ref, *refs):
    fields, outs = refs[: len(refs) // 3], refs[len(refs) // 3 :]
    for d, field in enumerate(fields, 1):
        for lane in range(0, field.shape[1], LANES):
            span = slice(lane, lane + LANES)
            totals = with_partner(frames, rows, cols, d, field, partner_ref, table_ref, span)
            tiles = reordered([jnp.concatenate([t[r] for t in totals]) for r in range(rows)], rounds_h)
            outs[2 * d - 2][:, span] = jnp.concatenate(tiles[:rounds_h]).astype(BF16)
            outs[2 * d - 1][:, span] = jnp.concatenate(tiles[rounds_h:]).astype(BF16)


def own_kernel(frames, rows, cols, partner_ref, table_ref, field_ref, mine_ref):
    for lane in range(0, mine_ref.shape[1], LANES):
        span = slice(lane, lane + LANES)
        totals = with_partner(frames, rows, cols, 0, field_ref, partner_ref, table_ref, span)
        mine_ref[:, span] = jnp.concatenate(totals).reshape(mine_ref.shape[0], LANES)


def later(d, value):
    return jnp.where(lax.div(lax.axis_index("tm"), 2) >= d, value, jnp.zeros_like(value))


def side_kernel(frames, rows, table_ref, *refs):
    *arrived, own_ref, other_ref = refs
    _, lower, upper = position("width")
    exists = jnp.where(on_right(), upper, lower)
    for lane in range(0, own_ref.shape[1], LANES):
        span = slice(lane, lane + LANES)
        totals = [jnp.zeros((rows, LANES), F32)] * (2 * frames)
        for d, ref in enumerate(arrived[::-1]):
            column = later(d, ref[:, span].astype(F32))
            base = 2 * frames + 2 * d * frames
            for t in range(2 * frames):
                for s in range(2 * frames):
                    lag = t % frames - s % frames
                    if t // frames == s // frames:
                        if d == 0 and lag < 0:
                            continue
                    else:
                        lag = lag + (shift(frames) if t < frames else -shift(frames))
                    totals[t] = totals[t] + table_ref[base + lag, :, span] * column[s * rows : (s + 1) * rows]
        totals = [jnp.where(exists, total, jnp.zeros_like(total)) for total in totals]
        own_ref[:, span] = jnp.concatenate(totals[:frames])
        other_ref[:, span] = jnp.concatenate(totals[frames:]).astype(BF16)


def border_kernel(frames, rows, cols, chips, mine_ref, own_ref, other_ref, *refs):
    arrived, (low_ref, high_ref, *outs) = refs[: chips - 1], refs[chips - 1 :]
    sites = rows * cols
    odd, _, _ = position("height")
    right, own, other = on_right(), own_ref[...], other_ref[...].astype(F32)
    low, high = jnp.where(right, other, own), jnp.where(right, own, other)
    low_ref[...] = low
    high_ref[...] = high
    size = frames * cols
    lines, corners = [], []
    for r in (0, rows - 1):
        lines.append(jnp.concatenate([mine_ref[t * sites + r * cols : t * sites + (r + 1) * cols] for t in range(frames)]))
        ends = [side[t * rows + r : t * rows + r + 1] for side in (low, high) for t in range(frames)]
        corners.append(jnp.concatenate(ends))
    for k, out in enumerate(outs):
        line = jnp.where(odd, *(lines[::-1] if k else lines))
        for d, ref in enumerate(arrived, 1):
            if len(outs) > 1:
                ends = [ref[i * size : (i + 1) * size].astype(F32) for i in range(2)]
                more = jnp.where(odd, *(ends[::-1] if k else ends))
            else:
                more = ref[:size].astype(F32)
            line = line + later(d, more)
        out[...] = jnp.concatenate([line, jnp.where(odd, *(corners[::-1] if k else corners))]).astype(BF16)


def shifted(line, left, right):
    cols = line.shape[0]
    place = lax.broadcasted_iota(jnp.int32, line.shape, 0)
    before = jnp.where(place == 0, left, pltpu.roll(line, 1, 0))
    after = jnp.where(place == cols - 1, right, pltpu.roll(line, cols - 1, 0))
    return before, line, after


def projected(mixed, gate, wv_ref, wo_ref):
    value = jnp.dot(mixed, wv_ref[...], preferred_element_type=F32)
    hidden = (value * gate).astype(BF16)
    return jnp.dot(hidden, wo_ref[...], preferred_element_type=F32).astype(BF16)


def inner_kernel(
    frames, rows, cols, rounds_h, mine_ref, low_ref, high_ref, taps_ref, gate_ref, wv_ref, wo_ref, *refs
):
    *parts, out_ref, edges_ref, mixed = refs
    firsts, rests = parts[: len(parts) // 2], parts[len(parts) // 2 :]
    chans = mine_ref.shape[1]
    sites = rows * cols
    size = frames * cols
    for lane in range(0, chans, LANES):
        span = slice(lane, lane + LANES)
        taps = [[taps_ref[3 * a + b : 3 * a + b + 1, span] for b in range(3)] for a in range(3)]
        low, high = low_ref[:, span], high_ref[:, span]
        lines = [
            jnp.concatenate([mine_ref[t * sites + r * cols : t * sites + (r + 1) * cols, span] for t in range(frames)])
            for r in range(rows)
        ]
        for d, (first, rest) in enumerate(zip(firsts, rests), 1):
            more = [first[i * size : (i + 1) * size, span].astype(F32) for i in range(rounds_h)]
            more += [rest[i * size : (i + 1) * size, span].astype(F32) for i in range(rows - rounds_h)]
            more = reordered(more, rounds_h, back=True)
            lines = [line + later(d, other) for line, other in zip(lines, more)]
        for t in range(frames):
            at = t * sites
            totals = [None] * rows
            for r in range(rows):
                row = t * rows + r
                near = shifted(lines[r][t * cols : (t + 1) * cols], low[row : row + 1], high[row : row + 1])
                for a in range(3):
                    to = r + 1 - a
                    if 0 <= to < rows:
                        term = near[0] * taps[a][0] + near[1] * taps[a][1] + near[2] * taps[a][2]
                        totals[to] = term if totals[to] is None else totals[to] + term
            mixed[at : at + sites, span] = jnp.concatenate(totals, axis=0).astype(BF16)
            edges_ref[t * cols : (t + 1) * cols, span] = totals[0]
            edges_ref[size + t * cols : size + (t + 1) * cols, span] = totals[rows - 1]
    out_ref[...] = projected(mixed[...], gate_ref[...], wv_ref, wo_ref)


def edge_kernel(frames, rows, cols, rounds_h, edges_ref, taps_ref, gate_ref, wv_ref, wo_ref, inner_ref, *refs):
    ends, out_ref = refs[:rounds_h], refs[rounds_h]
    sites = rows * cols
    size = frames * cols
    odd, _, _ = position("height")
    out_ref[...] = inner_ref[...]
    taps = taps_ref[...]
    mixed, gate = [], []
    for k, end in enumerate(ends):
        end = end[...].astype(F32)
        first = jnp.logical_not(odd) if k else odd
        lefts, rights = end[size : size + frames], end[size + frames : size + 2 * frames]
        lower, upper = position("height")[1:]
        exists = jnp.where(first, lower, upper)
        tap = jnp.where(first, taps[0:3], taps[6:9])
        total = jnp.where(first, edges_ref[0:size], edges_ref[size : 2 * size])
        for t in range(frames):
            near = shifted(end[t * cols : (t + 1) * cols], lefts[t : t + 1], rights[t : t + 1])
            more = near[0] * tap[0:1] + near[1] * tap[1:2] + near[2] * tap[2:3]
            mixed.append(total[t * cols : (t + 1) * cols] + jnp.where(exists, more, jnp.zeros_like(more)))
            at = t * sites
            gate.append(jnp.where(first, gate_ref[at : at + cols], gate_ref[at + sites - cols : at + sites]))
    out = projected(jnp.concatenate(mixed, axis=0).astype(BF16), jnp.concatenate(gate, axis=0), wv_ref, wo_ref)
    for t in range(frames):
        new = [out[k * size + t * cols : k * size + (t + 1) * cols] for k in range(rounds_h)]
        for at, other in ((t * sites, False), (t * sites + sites - cols, True)):
            kept = new[1] if rounds_h > 1 else inner_ref[at : at + cols]
            out_ref[at : at + cols] = jnp.where(odd, kept, new[0]) if other else jnp.where(odd, new[0], kept)


def body(latents, spatial_taps, kernel_taps, skip_gain, gate_weight, value_weight, out_weight):
    frames, rows, cols, chans = latents.shape
    lags = kernel_taps.shape[0]
    n_t, n_h, n_w = lax.axis_size("tm"), lax.axis_size("height"), lax.axis_size("width")
    chips = n_t // 2
    block = frames * rows * cols
    shape = jax.ShapeDtypeStruct
    x = latents.reshape(block, chans)

    partner = lax.ppermute(x, "tm", [(i, i ^ 1) for i in range(n_t)])
    inputs = [kernel_taps, skip_gain.reshape(1, chans), x]
    lines = frames * rows
    field = shape((block, chans), F32)
    table, side, *fields = call(
        functools.partial(early_kernel, frames, rows, cols),
        "early",
        [shape((lags + 2 * frames, cols, chans), F32), shape((lines, chans), F32)] + [field] * chips,
        [pltpu.VMEM(a.shape, a.dtype) for a in inputs]
        + [pltpu.SemaphoreType.DMA((len(inputs),)), pltpu.VMEM((block, LANES), F32)],
        inputs,
        2 * chips * frames * x.size,
        far=len(inputs),
    )
    (gate,) = call(
        gate_kernel, "gate", [shape((block, chans), F32)], [], [x, gate_weight], 2 * block * chans * chans, x.size
    )

    h_rounds = swaps("height")
    (column,) = call(
        functools.partial(column_kernel, frames, rows, cols),
        "column",
        [shape((2 * lines, chans), BF16)],
        [pltpu.VMEM((block, LANES), F32)],
        [partner, side],
    )
    parts = [shape((n * frames * cols, chans), BF16) for n in (len(h_rounds), rows - len(h_rounds))]
    sent = call(
        functools.partial(later_kernel, frames, rows, cols, len(h_rounds)),
        "later",
        parts * (chips - 1),
        [],
        [partner, table] + fields[1:],
        2 * (chips - 1) * frames * x.size,
    )
    (mine,) = call(
        functools.partial(own_kernel, frames, rows, cols),
        "own",
        [field],
        [],
        [partner, table, fields[0]],
        2 * frames * x.size,
    )
    columns, firsts, rests = [], [], []
    for d in reversed(range(chips)):
        route = []
        for i in range(n_t):
            for h in range(n_h):
                for j in range(n_w):
                    to = facing(i % 2, j, n_w)
                    beside = h ^ 1 if to == j and n_h % 2 == 0 else h
                    source = (i * n_h + h) * n_w + j
                    route.append((source, ((i + 2 * d) % n_t * n_h + beside) * n_w + to))
        columns.append(lax.ppermute(column, ("tm", "height", "width"), route))
    for d in range(1, chips):
        route = [(i, (i + 2 * d) % n_t) for i in range(n_t)]
        firsts.append(lax.ppermute(sent[2 * d - 2], "tm", route))
        rests.append(lax.ppermute(sent[2 * d - 1], "tm", route))

    own, other = call(
        functools.partial(side_kernel, frames, rows),
        "side",
        [shape((lines, chans), F32), shape((lines, chans), BF16)],
        [],
        [table] + columns,
        LATER,
    )
    other = lax.ppermute(other, "tm", [(i, i ^ 1) for i in range(n_t)])
    size = frames * cols + 2 * frames
    low, high, *ends = call(
        functools.partial(border_kernel, frames, rows, cols, chips),
        "border",
        [shape((lines, chans), F32)] * 2 + [shape((size, chans), BF16)] * len(h_rounds),
        [],
        [mine, own, other] + firsts,
    )
    ends = [lax.ppermute(e, "height", pairs) for e, pairs in zip(ends, h_rounds)]

    taps = spatial_taps.reshape(9, chans)
    inner, edges = call(
        functools.partial(inner_kernel, frames, rows, cols, len(h_rounds)),
        "inner",
        [shape((block, chans), BF16), shape((2 * frames * cols, chans), F32)],
        [pltpu.VMEM((block, chans), BF16)],
        [mine, low, high, taps, gate, value_weight, out_weight] + firsts + rests,
        4 * block * chans * chans,
    )
    (out,) = call(
        functools.partial(edge_kernel, frames, rows, cols, len(h_rounds)),
        "edge",
        [shape((block, chans), BF16)],
        [],
        [edges, taps, gate, value_weight, out_weight, inner] + ends,
        4 * frames * cols * chans * chans,
    )
    return out.reshape(latents.shape)


def solution(mesh):
    in_specs = (P("tm", "height", "width", None), P(), P(), P(), P(), P(), P())
    out_specs = P("tm", "height", "width", None)
    return jax.shard_map(body, mesh=mesh, in_specs=in_specs, out_specs=out_specs, check_vma=False)
```

```python
import functools

import jax
import jax.numpy as jnp
from jax import lax
from jax.experimental import pallas as pl
from jax.experimental.pallas import tpu as pltpu
from jax.sharding import PartitionSpec as P

LANES = 128
LATER = 8 * 10**9
F32, BF16 = jnp.float32, jnp.bfloat16
VMEM = pl.BlockSpec(memory_space=pltpu.VMEM)
HBM = pl.BlockSpec(memory_space=pltpu.HBM)


def call(kernel, name, outs, scratch, operands, flops=0, exps=0, far=0):
    operands = [pltpu.with_memory_space_constraint(a, pltpu.HBM) for a in operands[:far]] + list(operands[far:])
    moved = sum(a.size * a.dtype.itemsize for a in operands) + sum(a.size * a.dtype.itemsize for a in outs)
    return pl.pallas_call(
        kernel,
        out_shape=tuple(outs),
        in_specs=[HBM] * far + [VMEM] * (len(operands) - far),
        out_specs=(VMEM,) * len(outs),
        scratch_shapes=scratch,
        compiler_params=pltpu.CompilerParams(vmem_limit_bytes=24 * 1024 * 1024),
        cost_estimate=pl.CostEstimate(flops=flops, bytes_accessed=moved, transcendentals=exps),
        name=name,
    )(*operands)


def swaps(axis):
    n = lax.axis_size(axis)
    rounds = []
    for first in range(2 if n > 2 else 1):
        to = list(range(n))
        for i in range(first, n - 1, 2):
            to[i], to[i + 1] = i + 1, i
        rounds.append(list(enumerate(to)))
    return rounds


def position(axis):
    i, n = lax.axis_index(axis), lax.axis_size(axis)
    return lax.rem(i, 2) == 1, i > 0, i < n - 1


def second():
    return lax.rem(lax.axis_index("tm"), 2) == 1


def on_right():
    return lax.rem(lax.axis_index("tm") + lax.axis_index("width"), 2) == 0


def facing(core, column, columns):
    to = column + (1 if (core + column) % 2 == 0 else -1)
    return to if 0 <= to < columns else column


def outer_column(ref, lines, cols):
    return jnp.where(on_right(), ref[pl.ds(cols - 1, lines, stride=cols), :], ref[pl.ds(0, lines, stride=cols), :])


def gate_kernel(x_ref, w_ref, gate_ref):
    v = jnp.dot(x_ref[...], w_ref[...], preferred_element_type=F32)
    gate_ref[...] = v / (1.0 + jnp.exp(-v))


def early_kernel(frames, rows, cols, *refs):
    far, (table_ref, side_ref, *fields), near, (arrived, held) = refs[:3], refs[3:-5], refs[-5:-2], refs[-2:]
    copies = [pltpu.make_async_copy(a, b, arrived.at[i]) for i, (a, b) in enumerate(zip(far, near))]
    for copy in copies:
        copy.start()
    taps_ref, skip_ref, x_ref = near
    lags, chans = taps_ref.shape
    copies[0].wait()
    copies[1].wait()
    pad = 2 * frames
    taps = taps_ref[...].astype(F32)
    table_ref[0:pad] = jnp.zeros((pad, cols, chans), F32)
    for lag in range(lags):
        tap = taps[lag : lag + 1] + (skip_ref[...] if lag == 0 else 0.0)
        table_ref[pad + lag] = jnp.broadcast_to(tap, (cols, chans))
    sites = rows * cols
    copies[2].wait()
    for lane in range(0, chans, LANES):
        span = slice(lane, lane + LANES)
        held[...] = x_ref[:, span].astype(F32)
        side_ref[:, span] = outer_column(held, frames * rows, cols)
        for d, field in enumerate(fields):
            totals = [None] * frames
            for s in range(frames):
                x = x_ref[s * sites : (s + 1) * sites, span].astype(F32).reshape(rows, cols, LANES)
                for t in range(s if d == 0 else 0, frames):
                    term = table_ref[pad + 2 * d * frames + t - s, :, span] * x
                    totals[t] = term if totals[t] is None else totals[t] + term
            for t in range(frames):
                field[t * sites : (t + 1) * sites, span] = totals[t].reshape(sites, LANES)


def reordered(lines, rounds_h, back=False):
    if rounds_h > 1:
        return lines[:1] + lines[2:] + lines[1:2] if back else lines[:1] + lines[-1:] + lines[1:-1]
    odd = position("height")[0]
    return [jnp.where(odd, a, b) for a, b in zip(lines, lines[::-1])]


def column_kernel(frames, rows, cols, partner_ref, side_ref, out_ref, held):
    lines = frames * rows
    for lane in range(0, out_ref.shape[1], LANES):
        span = slice(lane, lane + LANES)
        held[...] = partner_ref[:, span].astype(F32)
        out_ref[:, span] = jnp.concatenate([side_ref[:, span], outer_column(held, lines, cols)]).astype(BF16)


def shift(frames):
    return jnp.where(second(), frames, -frames)


def with_partner(frames, rows, cols, d, field_ref, partner_ref, table_ref, span):
    sites = rows * cols
    base = 2 * frames + 2 * d * frames + shift(frames)
    totals = [field_ref[t * sites : (t + 1) * sites, span].reshape(rows, cols, LANES) for t in range(frames)]
    for s in range(frames):
        x = partner_ref[s * sites : (s + 1) * sites, span].astype(F32).reshape(rows, cols, LANES)
        for t in range(frames):
            totals[t] = totals[t] + table_ref[base + t - s, :, span] * x
    return totals


def later_kernel(frames, rows, cols, rounds_h, partner_ref, table_ref, *refs):
    fields, outs = refs[: len(refs) // 3], refs[len(refs) // 3 :]
    for d, field in enumerate(fields, 1):
        for lane in range(0, field.shape[1], LANES):
            span = slice(lane, lane + LANES)
            totals = with_partner(frames, rows, cols, d, field, partner_ref, table_ref, span)
            tiles = reordered([jnp.concatenate([t[r] for t in totals]) for r in range(rows)], rounds_h)
            outs[2 * d - 2][:, span] = jnp.concatenate(tiles[:rounds_h]).astype(BF16)
            outs[2 * d - 1][:, span] = jnp.concatenate(tiles[rounds_h:]).astype(BF16)


def own_kernel(frames, rows, cols, partner_ref, table_ref, field_ref, mine_ref):
    for lane in range(0, mine_ref.shape[1], LANES):
        span = slice(lane, lane + LANES)
        totals = with_partner(frames, rows, cols, 0, field_ref, partner_ref, table_ref, span)
        mine_ref[:, span] = jnp.concatenate(totals).reshape(mine_ref.shape[0], LANES)


def later(d, value):
    return jnp.where(lax.div(lax.axis_index("tm"), 2) >= d, value, jnp.zeros_like(value))


def side_kernel(frames, rows, table_ref, *refs):
    *arrived, own_ref, other_ref = refs
    _, lower, upper = position("width")
    exists = jnp.where(on_right(), upper, lower)
    for lane in range(0, own_ref.shape[1], LANES):
        span = slice(lane, lane + LANES)
        totals = [jnp.zeros((rows, LANES), F32)] * (2 * frames)
        for d, ref in enumerate(arrived):
            column = later(d, ref[:, span].astype(F32))
            base = 2 * frames + 2 * d * frames
            for t in range(2 * frames):
                for s in range(2 * frames):
                    lag = t % frames - s % frames
                    if t // frames == s // frames:
                        if d == 0 and lag < 0:
                            continue
                    else:
                        lag = lag + (shift(frames) if t < frames else -shift(frames))
                    totals[t] = totals[t] + table_ref[base + lag, :, span] * column[s * rows : (s + 1) * rows]
        totals = [jnp.where(exists, total, jnp.zeros_like(total)) for total in totals]
        own_ref[:, span] = jnp.concatenate(totals[:frames])
        other_ref[:, span] = jnp.concatenate(totals[frames:]).astype(BF16)


def border_kernel(frames, rows, cols, chips, mine_ref, own_ref, other_ref, *refs):
    arrived, (low_ref, high_ref, *outs) = refs[: chips - 1], refs[chips - 1 :]
    sites = rows * cols
    odd, _, _ = position("height")
    right, own, other = on_right(), own_ref[...], other_ref[...].astype(F32)
    low, high = jnp.where(right, other, own), jnp.where(right, own, other)
    low_ref[...] = low
    high_ref[...] = high
    size = frames * cols
    lines, corners = [], []
    for r in (0, rows - 1):
        lines.append(jnp.concatenate([mine_ref[t * sites + r * cols : t * sites + (r + 1) * cols] for t in range(frames)]))
        ends = [side[t * rows + r : t * rows + r + 1] for side in (low, high) for t in range(frames)]
        corners.append(jnp.concatenate(ends))
    for k, out in enumerate(outs):
        line = jnp.where(odd, *(lines[::-1] if k else lines))
        for d, ref in enumerate(arrived, 1):
            if len(outs) > 1:
                ends = [ref[i * size : (i + 1) * size].astype(F32) for i in range(2)]
                more = jnp.where(odd, *(ends[::-1] if k else ends))
            else:
                more = ref[:size].astype(F32)
            line = line + later(d, more)
        out[...] = jnp.concatenate([line, jnp.where(odd, *(corners[::-1] if k else corners))]).astype(BF16)


def shifted(line, left, right):
    cols = line.shape[0]
    place = lax.broadcasted_iota(jnp.int32, line.shape, 0)
    before = jnp.where(place == 0, left, pltpu.roll(line, 1, 0))
    after = jnp.where(place == cols - 1, right, pltpu.roll(line, cols - 1, 0))
    return before, line, after


def projected(mixed, gate, wv_ref, wo_ref):
    value = jnp.dot(mixed, wv_ref[...], preferred_element_type=F32)
    hidden = (value * gate).astype(BF16)
    return jnp.dot(hidden, wo_ref[...], preferred_element_type=F32).astype(BF16)


def inner_kernel(
    frames, rows, cols, rounds_h, mine_ref, low_ref, high_ref, taps_ref, gate_ref, wv_ref, wo_ref, *refs
):
    *parts, out_ref, edges_ref, mixed = refs
    value = 0.0
    firsts, rests = parts[: len(parts) // 2], parts[len(parts) // 2 :]
    chans = mine_ref.shape[1]
    sites = rows * cols
    size = frames * cols
    for lane in range(0, chans, LANES):
        span = slice(lane, lane + LANES)
        taps = [[taps_ref[3 * a + b : 3 * a + b + 1, span] for b in range(3)] for a in range(3)]
        low, high = low_ref[:, span], high_ref[:, span]
        lines = [
            jnp.concatenate([mine_ref[t * sites + r * cols : t * sites + (r + 1) * cols, span] for t in range(frames)])
            for r in range(rows)
        ]
        for d, (first, rest) in enumerate(zip(firsts, rests), 1):
            more = [first[i * size : (i + 1) * size, span].astype(F32) for i in range(rounds_h)]
            more += [rest[i * size : (i + 1) * size, span].astype(F32) for i in range(rows - rounds_h)]
            more = reordered(more, rounds_h, back=True)
            lines = [line + later(d, other) for line, other in zip(lines, more)]
        for t in range(frames):
            at = t * sites
            totals = [None] * rows
            for r in range(rows):
                row = t * rows + r
                near = shifted(lines[r][t * cols : (t + 1) * cols], low[row : row + 1], high[row : row + 1])
                for a in range(3):
                    to = r + 1 - a
                    if 0 <= to < rows:
                        term = near[0] * taps[a][0] + near[1] * taps[a][1] + near[2] * taps[a][2]
                        totals[to] = term if totals[to] is None else totals[to] + term
            mixed[at : at + sites, span] = jnp.concatenate(totals, axis=0).astype(BF16)
            edges_ref[t * cols : (t + 1) * cols, span] = totals[0]
            edges_ref[size + t * cols : size + (t + 1) * cols, span] = totals[rows - 1]
        if (lane + LANES) % (chans // 2) == 0:
            half = slice(lane + LANES - chans // 2, lane + LANES)
            value = value + jnp.dot(mixed[:, half], wv_ref[half], preferred_element_type=F32)
    hidden = (value * gate_ref[...]).astype(BF16)
    out_ref[...] = jnp.dot(hidden, wo_ref[...], preferred_element_type=F32).astype(BF16)


def edge_kernel(frames, rows, cols, rounds_h, edges_ref, taps_ref, gate_ref, wv_ref, wo_ref, inner_ref, *refs):
    ends, out_ref = refs[:rounds_h], refs[rounds_h]
    sites = rows * cols
    size = frames * cols
    odd, _, _ = position("height")
    out_ref[...] = inner_ref[...]
    taps = taps_ref[...]
    mixed, gate = [], []
    for k, end in enumerate(ends):
        end = end[...].astype(F32)
        first = jnp.logical_not(odd) if k else odd
        lefts, rights = end[size : size + frames], end[size + frames : size + 2 * frames]
        lower, upper = position("height")[1:]
        exists = jnp.where(first, lower, upper)
        tap = jnp.where(first, taps[0:3], taps[6:9])
        total = jnp.where(first, edges_ref[0:size], edges_ref[size : 2 * size])
        for t in range(frames):
            near = shifted(end[t * cols : (t + 1) * cols], lefts[t : t + 1], rights[t : t + 1])
            more = near[0] * tap[0:1] + near[1] * tap[1:2] + near[2] * tap[2:3]
            mixed.append(total[t * cols : (t + 1) * cols] + jnp.where(exists, more, jnp.zeros_like(more)))
            at = t * sites
            gate.append(jnp.where(first, gate_ref[at : at + cols], gate_ref[at + sites - cols : at + sites]))
    out = projected(jnp.concatenate(mixed, axis=0).astype(BF16), jnp.concatenate(gate, axis=0), wv_ref, wo_ref)
    for t in range(frames):
        new = [out[k * size + t * cols : k * size + (t + 1) * cols] for k in range(rounds_h)]
        for at, other in ((t * sites, False), (t * sites + sites - cols, True)):
            kept = new[1] if rounds_h > 1 else inner_ref[at : at + cols]
            out_ref[at : at + cols] = jnp.where(odd, kept, new[0]) if other else jnp.where(odd, new[0], kept)


def body(latents, spatial_taps, kernel_taps, skip_gain, gate_weight, value_weight, out_weight):
    frames, rows, cols, chans = latents.shape
    lags = kernel_taps.shape[0]
    n_t, n_h, n_w = lax.axis_size("tm"), lax.axis_size("height"), lax.axis_size("width")
    chips = n_t // 2
    block = frames * rows * cols
    shape = jax.ShapeDtypeStruct
    x = latents.reshape(block, chans)

    partner = lax.ppermute(x, "tm", [(i, i ^ 1) for i in range(n_t)])
    inputs = [kernel_taps, skip_gain.reshape(1, chans), x]
    lines = frames * rows
    field = shape((block, chans), F32)
    table, side, *fields = call(
        functools.partial(early_kernel, frames, rows, cols),
        "early",
        [shape((lags + 2 * frames, cols, chans), F32), shape((lines, chans), F32)] + [field] * chips,
        [pltpu.VMEM(a.shape, a.dtype) for a in inputs]
        + [pltpu.SemaphoreType.DMA((len(inputs),)), pltpu.VMEM((block, LANES), F32)],
        inputs,
        2 * chips * frames * x.size,
        far=len(inputs),
    )
    (gate,) = call(
        gate_kernel, "gate", [shape((block, chans), F32)], [], [x, gate_weight], 2 * block * chans * chans, x.size
    )

    h_rounds = swaps("height")
    (column,) = call(
        functools.partial(column_kernel, frames, rows, cols),
        "column",
        [shape((2 * lines, chans), BF16)],
        [pltpu.VMEM((block, LANES), F32)],
        [partner, side],
    )
    parts = [shape((n * frames * cols, chans), BF16) for n in (len(h_rounds), rows - len(h_rounds))]
    sent = call(
        functools.partial(later_kernel, frames, rows, cols, len(h_rounds)),
        "later",
        parts * (chips - 1),
        [],
        [partner, table] + fields[1:],
        2 * (chips - 1) * frames * x.size,
    )
    (mine,) = call(
        functools.partial(own_kernel, frames, rows, cols),
        "own",
        [field],
        [],
        [partner, table, fields[0]],
        2 * frames * x.size,
    )
    columns, firsts, rests = [], [], []
    for d in range(chips):
        route = []
        for i in range(n_t):
            for h in range(n_h):
                for j in range(n_w):
                    to = facing(i % 2, j, n_w)
                    beside = h ^ 1 if to == j and n_h % 2 == 0 else h
                    source = (i * n_h + h) * n_w + j
                    route.append((source, ((i + 2 * d) % n_t * n_h + beside) * n_w + to))
        columns.append(lax.ppermute(column, ("tm", "height", "width"), route))
    for d in range(1, chips):
        route = [(i, (i + 2 * d) % n_t) for i in range(n_t)]
        firsts.append(lax.ppermute(sent[2 * d - 2], "tm", route))
        rests.append(lax.ppermute(sent[2 * d - 1], "tm", route))

    own, other = call(
        functools.partial(side_kernel, frames, rows),
        "side",
        [shape((lines, chans), F32), shape((lines, chans), BF16)],
        [],
        [table] + columns,
        LATER,
    )
    other = lax.ppermute(other, "tm", [(i, i ^ 1) for i in range(n_t)])
    size = frames * cols + 2 * frames
    low, high, *ends = call(
        functools.partial(border_kernel, frames, rows, cols, chips),
        "border",
        [shape((lines, chans), F32)] * 2 + [shape((size, chans), BF16)] * len(h_rounds),
        [],
        [mine, own, other] + firsts,
    )
    ends = [lax.ppermute(e, "height", pairs) for e, pairs in zip(ends, h_rounds)]

    taps = spatial_taps.reshape(9, chans)
    inner, edges = call(
        functools.partial(inner_kernel, frames, rows, cols, len(h_rounds)),
        "inner",
        [shape((block, chans), BF16), shape((2 * frames * cols, chans), F32)],
        [pltpu.VMEM((block, chans), BF16)],
        [mine, low, high, taps, gate, value_weight, out_weight] + firsts + rests,
        4 * block * chans * chans,
    )
    (out,) = call(
        functools.partial(edge_kernel, frames, rows, cols, len(h_rounds)),
        "edge",
        [shape((block, chans), BF16)],
        [],
        [edges, taps, gate, value_weight, out_weight, inner] + ends,
        4 * frames * cols * chans * chans,
    )
    return out.reshape(latents.shape)


def solution(mesh):
    in_specs = (P("tm", "height", "width", None), P(), P(), P(), P(), P(), P())
    out_specs = P("tm", "height", "width", None)
    return jax.shard_map(body, mesh=mesh, in_specs=in_specs, out_specs=out_specs, check_vma=False)
```

```python
import functools

import jax
import jax.numpy as jnp
from jax import lax
from jax.experimental import pallas as pl
from jax.experimental.pallas import tpu as pltpu
from jax.sharding import PartitionSpec as P

LANES = 128
LATER = 8 * 10**9
F32, BF16 = jnp.float32, jnp.bfloat16
VMEM = pl.BlockSpec(memory_space=pltpu.VMEM)
HBM = pl.BlockSpec(memory_space=pltpu.HBM)


def call(kernel, name, outs, scratch, operands, flops=0, exps=0, far=0):
    operands = [pltpu.with_memory_space_constraint(a, pltpu.HBM) for a in operands[:far]] + list(operands[far:])
    moved = sum(a.size * a.dtype.itemsize for a in operands) + sum(a.size * a.dtype.itemsize for a in outs)
    return pl.pallas_call(
        kernel,
        out_shape=tuple(outs),
        in_specs=[HBM] * far + [VMEM] * (len(operands) - far),
        out_specs=(VMEM,) * len(outs),
        scratch_shapes=scratch,
        compiler_params=pltpu.CompilerParams(vmem_limit_bytes=24 * 1024 * 1024),
        cost_estimate=pl.CostEstimate(flops=flops, bytes_accessed=moved, transcendentals=exps),
        name=name,
    )(*operands)


def swaps(axis):
    n = lax.axis_size(axis)
    rounds = []
    for first in range(2 if n > 2 else 1):
        to = list(range(n))
        for i in range(first, n - 1, 2):
            to[i], to[i + 1] = i + 1, i
        rounds.append(list(enumerate(to)))
    return rounds


def position(axis):
    i, n = lax.axis_index(axis), lax.axis_size(axis)
    return lax.rem(i, 2) == 1, i > 0, i < n - 1


def second():
    return lax.rem(lax.axis_index("tm"), 2) == 1


def on_right():
    return lax.rem(lax.axis_index("tm") + lax.axis_index("width"), 2) == 0


def facing(core, column, columns):
    to = column + (1 if (core + column) % 2 == 0 else -1)
    return to if 0 <= to < columns else column


def outer_column(ref, lines, cols):
    return jnp.where(on_right(), ref[pl.ds(cols - 1, lines, stride=cols), :], ref[pl.ds(0, lines, stride=cols), :])


def gate_kernel(x_ref, w_ref, gate_ref):
    v = jnp.dot(x_ref[...], w_ref[...], preferred_element_type=F32)
    gate_ref[...] = v / (1.0 + jnp.exp(-v))


def early_kernel(frames, rows, cols, *refs):
    far, (table_ref, side_ref, *fields), near, (arrived, held) = refs[:3], refs[3:-5], refs[-5:-2], refs[-2:]
    copies = [pltpu.make_async_copy(a, b, arrived.at[i]) for i, (a, b) in enumerate(zip(far, near))]
    for copy in copies:
        copy.start()
    taps_ref, skip_ref, x_ref = near
    lags, chans = taps_ref.shape
    copies[0].wait()
    copies[1].wait()
    pad = 2 * frames
    taps = taps_ref[...].astype(F32)
    table_ref[0:pad] = jnp.zeros((pad, cols, chans), F32)
    for lag in range(lags):
        tap = taps[lag : lag + 1] + (skip_ref[...] if lag == 0 else 0.0)
        table_ref[pad + lag] = jnp.broadcast_to(tap, (cols, chans))
    sites = rows * cols
    copies[2].wait()
    for lane in range(0, chans, LANES):
        span = slice(lane, lane + LANES)
        held[...] = x_ref[:, span].astype(F32)
        side_ref[:, span] = outer_column(held, frames * rows, cols)
        for d, field in enumerate(fields):
            totals = [None] * frames
            for s in range(frames):
                x = x_ref[s * sites : (s + 1) * sites, span].astype(F32).reshape(rows, cols, LANES)
                for t in range(s if d == 0 else 0, frames):
                    term = table_ref[pad + 2 * d * frames + t - s, :, span] * x
                    totals[t] = term if totals[t] is None else totals[t] + term
            for t in range(frames):
                field[t * sites : (t + 1) * sites, span] = totals[t].reshape(sites, LANES)


def reordered(lines, rounds_h, back=False):
    if rounds_h > 1:
        return lines[:1] + lines[2:] + lines[1:2] if back else lines[:1] + lines[-1:] + lines[1:-1]
    odd = position("height")[0]
    return [jnp.where(odd, a, b) for a, b in zip(lines, lines[::-1])]


def column_kernel(frames, rows, cols, partner_ref, side_ref, out_ref, held):
    lines = frames * rows
    for lane in range(0, out_ref.shape[1], LANES):
        span = slice(lane, lane + LANES)
        held[...] = partner_ref[:, span].astype(F32)
        out_ref[:, span] = jnp.concatenate([side_ref[:, span], outer_column(held, lines, cols)]).astype(BF16)


def shift(frames):
    return jnp.where(second(), frames, -frames)


def with_partner(frames, rows, cols, d, field_ref, partner_ref, table_ref, span):
    sites = rows * cols
    base = 2 * frames + 2 * d * frames + shift(frames)
    totals = [field_ref[t * sites : (t + 1) * sites, span].reshape(rows, cols, LANES) for t in range(frames)]
    for s in range(frames):
        x = partner_ref[s * sites : (s + 1) * sites, span].astype(F32).reshape(rows, cols, LANES)
        for t in range(frames):
            totals[t] = totals[t] + table_ref[base + t - s, :, span] * x
    return totals


def later_kernel(frames, rows, cols, rounds_h, partner_ref, table_ref, *refs):
    fields, outs = refs[: len(refs) // 3], refs[len(refs) // 3 :]
    for d, field in enumerate(fields, 1):
        for lane in range(0, field.shape[1], LANES):
            span = slice(lane, lane + LANES)
            totals = with_partner(frames, rows, cols, d, field, partner_ref, table_ref, span)
            tiles = reordered([jnp.concatenate([t[r] for t in totals]) for r in range(rows)], rounds_h)
            outs[2 * d - 2][:, span] = jnp.concatenate(tiles[:rounds_h]).astype(BF16)
            outs[2 * d - 1][:, span] = jnp.concatenate(tiles[rounds_h:]).astype(BF16)


def own_kernel(frames, rows, cols, partner_ref, table_ref, field_ref, mine_ref):
    for lane in range(0, mine_ref.shape[1], LANES):
        span = slice(lane, lane + LANES)
        totals = with_partner(frames, rows, cols, 0, field_ref, partner_ref, table_ref, span)
        mine_ref[:, span] = jnp.concatenate(totals).reshape(mine_ref.shape[0], LANES)


def later(d, value):
    return jnp.where(lax.div(lax.axis_index("tm"), 2) >= d, value, jnp.zeros_like(value))


def side_kernel(frames, rows, table_ref, *refs):
    *arrived, own_ref, other_ref = refs
    _, lower, upper = position("width")
    exists = jnp.where(on_right(), upper, lower)
    for lane in range(0, own_ref.shape[1], LANES):
        span = slice(lane, lane + LANES)
        totals = [jnp.zeros((rows, LANES), F32)] * (2 * frames)
        for d, ref in enumerate(arrived[::-1]):
            column = later(d, ref[:, span].astype(F32))
            base = 2 * frames + 2 * d * frames
            for t in range(2 * frames):
                for s in range(2 * frames):
                    lag = t % frames - s % frames
                    if t // frames == s // frames:
                        if d == 0 and lag < 0:
                            continue
                    else:
                        lag = lag + (shift(frames) if t < frames else -shift(frames))
                    totals[t] = totals[t] + table_ref[base + lag, :, span] * column[s * rows : (s + 1) * rows]
        totals = [jnp.where(exists, total, jnp.zeros_like(total)) for total in totals]
        own_ref[:, span] = jnp.concatenate(totals[:frames])
        other_ref[:, span] = jnp.concatenate(totals[frames:]).astype(BF16)


def border_kernel(frames, rows, cols, chips, mine_ref, own_ref, other_ref, *refs):
    arrived, (low_ref, high_ref, *outs) = refs[: chips - 1], refs[chips - 1 :]
    sites = rows * cols
    odd, _, _ = position("height")
    right, own, other = on_right(), own_ref[...], other_ref[...].astype(F32)
    low, high = jnp.where(right, other, own), jnp.where(right, own, other)
    low_ref[...] = low
    high_ref[...] = high
    size = frames * cols
    lines, corners = [], []
    for r in (0, rows - 1):
        lines.append(jnp.concatenate([mine_ref[t * sites + r * cols : t * sites + (r + 1) * cols] for t in range(frames)]))
        ends = [side[t * rows + r : t * rows + r + 1] for side in (low, high) for t in range(frames)]
        corners.append(jnp.concatenate(ends))
    for k, out in enumerate(outs):
        line = jnp.where(odd, *(lines[::-1] if k else lines))
        for d, ref in enumerate(arrived, 1):
            if len(outs) > 1:
                ends = [ref[i * size : (i + 1) * size].astype(F32) for i in range(2)]
                more = jnp.where(odd, *(ends[::-1] if k else ends))
            else:
                more = ref[:size].astype(F32)
            line = line + later(d, more)
        out[...] = jnp.concatenate([line, jnp.where(odd, *(corners[::-1] if k else corners))]).astype(BF16)


def shifted(line, left, right):
    cols = line.shape[0]
    place = lax.broadcasted_iota(jnp.int32, line.shape, 0)
    before = jnp.where(place == 0, left, pltpu.roll(line, 1, 0))
    after = jnp.where(place == cols - 1, right, pltpu.roll(line, cols - 1, 0))
    return before, line, after


def projected(mixed, gate, wv_ref, wo_ref):
    value = jnp.dot(mixed, wv_ref[...], preferred_element_type=F32)
    hidden = (value * gate).astype(BF16)
    return jnp.dot(hidden, wo_ref[...], preferred_element_type=F32).astype(BF16)


def filtered(lines, lefts, rights, taps):
    totals = [None] * len(lines)
    for r, line in enumerate(lines):
        near = shifted(line, lefts[r], rights[r])
        for a in range(3):
            to = r + 1 - a
            if 0 <= to < len(lines):
                term = near[0] * taps[a][0] + near[1] * taps[a][1] + near[2] * taps[a][2]
                totals[to] = term if totals[to] is None else totals[to] + term
    return totals


def taps_of(taps_ref, span):
    return [[taps_ref[3 * a + b : 3 * a + b + 1, span] for b in range(3)] for a in range(3)]


def inner_kernel(
    frames, rows, cols, mine_ref, low_ref, high_ref, taps_ref, gate_ref, wv_ref, wo_ref, out_ref, totals_ref, mixed
):
    sites = rows * cols
    for lane in range(0, mine_ref.shape[1], LANES):
        span = slice(lane, lane + LANES)
        taps = taps_of(taps_ref, span)
        low, high = low_ref[:, span], high_ref[:, span]
        for t in range(frames):
            at = t * sites
            lines = [mine_ref[at + r * cols : at + (r + 1) * cols, span] for r in range(rows)]
            lefts = [low[t * rows + r : t * rows + r + 1] for r in range(rows)]
            rights = [high[t * rows + r : t * rows + r + 1] for r in range(rows)]
            total = jnp.concatenate(filtered(lines, lefts, rights, taps))
            totals_ref[at : at + sites, span] = total
            mixed[at : at + sites, span] = total.astype(BF16)
    out_ref[...] = projected(mixed[...], gate_ref[...], wv_ref, wo_ref)


def last_kernel(frames, rows, cols, chips, inner_ref, totals_ref, taps_ref, gate_ref, wv_ref, wo_ref, *refs):
    *parts, out_ref, mixed = refs
    firsts, rests, ends = parts[: chips - 1], parts[chips - 1 : 2 * chips - 2], parts[2 * chips - 2 :]
    rounds_h = len(ends)
    chans = out_ref.shape[1]
    sites = rows * cols
    size = frames * cols
    odd, lower, upper = position("height")
    earlier = lax.div(lax.axis_index("tm"), 2) > 0
    none = jnp.zeros((cols, chans), F32)
    above, below = [none] * frames, [none] * frames
    for k, end in enumerate(ends):
        end = end[...].astype(F32)
        first = jnp.logical_not(odd) if k else odd
        lefts, rights = end[size : size + frames], end[size + frames : size + 2 * frames]
        exists = jnp.where(first, lower, upper)
        tap = jnp.where(first, taps_ref[0:3], taps_ref[6:9])
        for t in range(frames):
            near = shifted(end[t * cols : (t + 1) * cols], lefts[t : t + 1], rights[t : t + 1])
            more = near[0] * tap[0:1] + near[1] * tap[1:2] + near[2] * tap[2:3]
            more = jnp.where(exists, more, none)
            above[t] = above[t] + jnp.where(first, more, none)
            below[t] = below[t] + jnp.where(first, none, more)

    @pl.when(jnp.logical_not(earlier))
    def _():
        out_ref[...] = inner_ref[...]
        rows_at = [t * sites for t in range(frames)], [(t + 1) * sites - cols for t in range(frames)]
        added = above, below
        if rounds_h > 1:
            change, gate = [], []
            for at, more in zip(rows_at, added):
                change += [totals_ref[i : i + cols] + m for i, m in zip(at, more)]
                gate += [gate_ref[i : i + cols] for i in at]
        else:
            change = [
                jnp.where(odd, totals_ref[i : i + cols] + m, totals_ref[j : j + cols] + n)
                for i, j, m, n in zip(*rows_at, *added)
            ]
            gate = [jnp.where(odd, gate_ref[i : i + cols], gate_ref[j : j + cols]) for i, j in zip(*rows_at)]
        new = projected(jnp.concatenate(change).astype(BF16), jnp.concatenate(gate), wv_ref, wo_ref)
        for t in range(frames):
            i, j = rows_at[0][t], rows_at[1][t]
            line = new[t * cols : (t + 1) * cols]
            if rounds_h > 1:
                out_ref[i : i + cols] = line
                out_ref[j : j + cols] = new[size + t * cols : size + (t + 1) * cols]
            else:
                out_ref[i : i + cols] = jnp.where(odd, line, inner_ref[i : i + cols])
                out_ref[j : j + cols] = jnp.where(odd, inner_ref[j : j + cols], line)

    @pl.when(earlier)
    def _():
        for lane in range(0, chans, LANES):
            span = slice(lane, lane + LANES)
            taps = taps_of(taps_ref, span)
            lines = [jnp.zeros((size, LANES), F32)] * rows
            for d, (first, rest) in enumerate(zip(firsts, rests), 1):
                more = [first[i * size : (i + 1) * size, span].astype(F32) for i in range(rounds_h)]
                more += [rest[i * size : (i + 1) * size, span].astype(F32) for i in range(rows - rounds_h)]
                more = reordered(more, rounds_h, back=True)
                lines = [line + later(d, other) for line, other in zip(lines, more)]
            zero = [jnp.zeros((1, LANES), F32)] * rows
            for t in range(frames):
                at = t * sites
                total = filtered([line[t * cols : (t + 1) * cols] for line in lines], zero, zero, taps)
                total[0] = total[0] + above[t][:, span]
                total[rows - 1] = total[rows - 1] + below[t][:, span]
                total = jnp.concatenate(total) + totals_ref[at : at + sites, span]
                mixed[at : at + sites, span] = total.astype(BF16)
        out_ref[...] = projected(mixed[...], gate_ref[...], wv_ref, wo_ref)


def body(latents, spatial_taps, kernel_taps, skip_gain, gate_weight, value_weight, out_weight):
    frames, rows, cols, chans = latents.shape
    lags = kernel_taps.shape[0]
    n_t, n_h, n_w = lax.axis_size("tm"), lax.axis_size("height"), lax.axis_size("width")
    chips = n_t // 2
    block = frames * rows * cols
    shape = jax.ShapeDtypeStruct
    x = latents.reshape(block, chans)

    partner = lax.ppermute(x, "tm", [(i, i ^ 1) for i in range(n_t)])
    inputs = [kernel_taps, skip_gain.reshape(1, chans), x]
    lines = frames * rows
    field = shape((block, chans), F32)
    table, side, *fields = call(
        functools.partial(early_kernel, frames, rows, cols),
        "early",
        [shape((lags + 2 * frames, cols, chans), F32), shape((lines, chans), F32)] + [field] * chips,
        [pltpu.VMEM(a.shape, a.dtype) for a in inputs]
        + [pltpu.SemaphoreType.DMA((len(inputs),)), pltpu.VMEM((block, LANES), F32)],
        inputs,
        2 * chips * frames * x.size,
        far=len(inputs),
    )
    (gate,) = call(
        gate_kernel, "gate", [shape((block, chans), F32)], [], [x, gate_weight], 2 * block * chans * chans, x.size
    )

    h_rounds = swaps("height")
    (column,) = call(
        functools.partial(column_kernel, frames, rows, cols),
        "column",
        [shape((2 * lines, chans), BF16)],
        [pltpu.VMEM((block, LANES), F32)],
        [partner, side],
    )
    parts = [shape((n * frames * cols, chans), BF16) for n in (len(h_rounds), rows - len(h_rounds))]
    sent = call(
        functools.partial(later_kernel, frames, rows, cols, len(h_rounds)),
        "later",
        parts * (chips - 1),
        [],
        [partner, table] + fields[1:],
        2 * (chips - 1) * frames * x.size,
    )
    (mine,) = call(
        functools.partial(own_kernel, frames, rows, cols),
        "own",
        [field],
        [],
        [partner, table, fields[0]],
        2 * frames * x.size,
    )
    columns, firsts, rests = [], [], []
    for d in reversed(range(chips)):
        route = []
        for i in range(n_t):
            for h in range(n_h):
                for j in range(n_w):
                    to, beside = facing(i % 2, j, n_w), h
                    if i // 2 + d >= chips:
                        to = j
                    elif to == j and n_h % 2 == 0:
                        beside = h ^ 1
                    source = (i * n_h + h) * n_w + j
                    route.append((source, ((i + 2 * d) % n_t * n_h + beside) * n_w + to))
        columns.append(lax.ppermute(column, ("tm", "height", "width"), route))
    for d in range(1, chips):
        route = [(i, (i + 2 * d) % n_t) for i in range(n_t)]
        firsts.append(lax.ppermute(sent[2 * d - 2], "tm", route))
        rests.append(lax.ppermute(sent[2 * d - 1], "tm", route))

    own, other = call(
        functools.partial(side_kernel, frames, rows),
        "side",
        [shape((lines, chans), F32), shape((lines, chans), BF16)],
        [],
        [table] + columns,
        LATER,
    )
    other = lax.ppermute(other, "tm", [(i, i ^ 1) for i in range(n_t)])
    size = frames * cols + 2 * frames
    low, high, *ends = call(
        functools.partial(border_kernel, frames, rows, cols, chips),
        "border",
        [shape((lines, chans), F32)] * 2 + [shape((size, chans), BF16)] * len(h_rounds),
        [],
        [mine, own, other] + firsts,
    )
    ends = [lax.ppermute(e, "height", pairs) for e, pairs in zip(ends, h_rounds)]

    taps = spatial_taps.reshape(9, chans)
    inner, totals = call(
        functools.partial(inner_kernel, frames, rows, cols),
        "inner",
        [shape((block, chans), BF16), field],
        [pltpu.VMEM((block, chans), BF16)],
        [mine, low, high, taps, gate, value_weight, out_weight],
        4 * block * chans * chans,
    )
    (out,) = call(
        functools.partial(last_kernel, frames, rows, cols, chips),
        "last",
        [shape((block, chans), BF16)],
        [pltpu.VMEM((block, chans), BF16)],
        [inner, totals, taps, gate, value_weight, out_weight] + firsts + rests + ends,
        4 * block * chans * chans,
    )
    return out.reshape(latents.shape)


def solution(mesh):
    in_specs = (P("tm", "height", "width", None), P(), P(), P(), P(), P(), P())
    out_specs = P("tm", "height", "width", None)
    return jax.shard_map(body, mesh=mesh, in_specs=in_specs, out_specs=out_specs, check_vma=False)
```

```python
import functools

import jax
import jax.numpy as jnp
from jax import lax
from jax.experimental import pallas as pl
from jax.experimental.pallas import tpu as pltpu
from jax.sharding import PartitionSpec as P

LANES = 128
F32, BF16 = jnp.float32, jnp.bfloat16
VMEM = pl.BlockSpec(memory_space=pltpu.VMEM)
HBM = pl.BlockSpec(memory_space=pltpu.HBM)


def call(kernel, name, outs, scratch, operands, flops=0, exps=0, far=0):
    operands = [pltpu.with_memory_space_constraint(a, pltpu.HBM) for a in operands[:far]] + list(operands[far:])
    moved = sum(a.size * a.dtype.itemsize for a in operands) + sum(a.size * a.dtype.itemsize for a in outs)
    return pl.pallas_call(
        kernel,
        out_shape=tuple(outs),
        in_specs=[HBM] * far + [VMEM] * (len(operands) - far),
        out_specs=(VMEM,) * len(outs),
        scratch_shapes=scratch,
        compiler_params=pltpu.CompilerParams(vmem_limit_bytes=24 * 1024 * 1024),
        cost_estimate=pl.CostEstimate(flops=flops, bytes_accessed=moved, transcendentals=exps),
        name=name,
    )(*operands)


def swaps(axis):
    n = lax.axis_size(axis)
    rounds = []
    for first in range(2 if n > 2 else 1):
        to = list(range(n))
        for i in range(first, n - 1, 2):
            to[i], to[i + 1] = i + 1, i
        rounds.append(list(enumerate(to)))
    return rounds


def position(axis):
    i, n = lax.axis_index(axis), lax.axis_size(axis)
    return lax.rem(i, 2) == 1, i > 0, i < n - 1


def second():
    return lax.rem(lax.axis_index("tm"), 2) == 1


def on_right():
    return lax.rem(lax.axis_index("tm") + lax.axis_index("width"), 2) == 0


def facing(core, column, columns):
    to = column + (1 if (core + column) % 2 == 0 else -1)
    return to if 0 <= to < columns else column


def outer_column(ref, lines, cols):
    return jnp.where(on_right(), ref[pl.ds(cols - 1, lines, stride=cols), :], ref[pl.ds(0, lines, stride=cols), :])


def gate_kernel(x_ref, w_ref, gate_ref):
    v = jnp.dot(x_ref[...], w_ref[...], preferred_element_type=F32)
    gate_ref[...] = v / (1.0 + jnp.exp(-v))


def early_kernel(frames, rows, cols, *refs):
    far, (table_ref, side_ref, *fields), near, (arrived, held) = refs[:3], refs[3:-5], refs[-5:-2], refs[-2:]
    copies = [pltpu.make_async_copy(a, b, arrived.at[i]) for i, (a, b) in enumerate(zip(far, near))]
    for copy in copies:
        copy.start()
    taps_ref, skip_ref, x_ref = near
    lags, chans = taps_ref.shape
    copies[0].wait()
    copies[1].wait()
    pad = 2 * frames
    taps = taps_ref[...].astype(F32)
    table_ref[0:pad] = jnp.zeros((pad, cols, chans), F32)
    for lag in range(lags):
        tap = taps[lag : lag + 1] + (skip_ref[...] if lag == 0 else 0.0)
        table_ref[pad + lag] = jnp.broadcast_to(tap, (cols, chans))
    sites = rows * cols
    copies[2].wait()
    for lane in range(0, chans, LANES):
        span = slice(lane, lane + LANES)
        held[...] = x_ref[:, span].astype(F32)
        side_ref[:, span] = outer_column(held, frames * rows, cols)
        for d, field in enumerate(fields):
            totals = [None] * frames
            for s in range(frames):
                x = x_ref[s * sites : (s + 1) * sites, span].astype(F32).reshape(rows, cols, LANES)
                for t in range(s if d == 0 else 0, frames):
                    term = table_ref[pad + 2 * d * frames + t - s, :, span] * x
                    totals[t] = term if totals[t] is None else totals[t] + term
            for t in range(frames):
                field[t * sites : (t + 1) * sites, span] = totals[t].reshape(sites, LANES)


def column_kernel(frames, rows, cols, partner_ref, side_ref, out_ref, *refs):
    *corners, held = refs
    odd = position("height")[0]
    for lane in range(0, out_ref.shape[1], LANES):
        span = slice(lane, lane + LANES)
        held[...] = partner_ref[:, span].astype(F32)
        column = jnp.concatenate([side_ref[:, span], outer_column(held, frames * rows, cols)])
        out_ref[:, span] = column.astype(BF16)
        ends = [jnp.concatenate([column[s + r : s + r + 1] for s in range(0, column.shape[0], rows)]) for r in (0, rows - 1)]
        for k, corner in enumerate(corners):
            corner[:, span] = jnp.where(odd, *(ends[::-1] if k else ends)).astype(BF16)


def shift(frames):
    return jnp.where(second(), frames, -frames)


def with_partner(frames, rows, cols, d, field_ref, partner_ref, table_ref, span):
    sites = rows * cols
    base = 2 * frames + 2 * d * frames + shift(frames)
    totals = [field_ref[t * sites : (t + 1) * sites, span].reshape(rows, cols, LANES) for t in range(frames)]
    for s in range(frames):
        x = partner_ref[s * sites : (s + 1) * sites, span].astype(F32).reshape(rows, cols, LANES)
        for t in range(frames):
            totals[t] = totals[t] + table_ref[base + t - s, :, span] * x
    return totals


def later_kernel(frames, rows, cols, rounds_h, partner_ref, table_ref, *refs):
    n = len(refs) // (2 + rounds_h)
    fields, outs = refs[:n], refs[n:]
    odd = position("height")[0]
    for d, field in enumerate(fields, 1):
        whole, *lines = outs[(d - 1) * (1 + rounds_h) : d * (1 + rounds_h)]
        for lane in range(0, field.shape[1], LANES):
            span = slice(lane, lane + LANES)
            totals = with_partner(frames, rows, cols, d, field, partner_ref, table_ref, span)
            whole[:, span] = jnp.concatenate(totals).reshape(whole.shape[0], LANES).astype(BF16)
            ends = [jnp.concatenate([t[r] for t in totals]) for r in (0, rows - 1)]
            for k, line in enumerate(lines):
                line[:, span] = jnp.where(odd, *(ends[::-1] if k else ends)).astype(BF16)


def own_kernel(frames, rows, cols, partner_ref, table_ref, field_ref, mine_ref):
    for lane in range(0, mine_ref.shape[1], LANES):
        span = slice(lane, lane + LANES)
        totals = with_partner(frames, rows, cols, 0, field_ref, partner_ref, table_ref, span)
        mine_ref[:, span] = jnp.concatenate(totals).reshape(mine_ref.shape[0], LANES)


def later(d, value):
    return jnp.where(lax.div(lax.axis_index("tm"), 2) >= d, value, jnp.zeros_like(value))


def mixed_columns(frames, rows, d, column, table_ref, span):
    base = 2 * frames + 2 * d * frames
    totals = [jnp.zeros((rows, column.shape[1]), F32)] * (2 * frames)
    for t in range(2 * frames):
        for s in range(2 * frames):
            lag = t % frames - s % frames
            if t // frames == s // frames:
                if d == 0 and lag < 0:
                    continue
            else:
                lag = lag + (shift(frames) if t < frames else -shift(frames))
            tap = table_ref[base + lag, :, span][:rows]
            totals[t] = totals[t] + tap * column[s * rows : (s + 1) * rows]
    return totals


def beside(totals):
    _, lower, upper = position("width")
    exists = jnp.where(on_right(), upper, lower)
    return [jnp.where(exists, total, jnp.zeros_like(total)) for total in totals]


def side_kernel(frames, rows, table_ref, arrived_ref, own_ref, other_ref):
    for lane in range(0, own_ref.shape[1], LANES):
        span = slice(lane, lane + LANES)
        totals = beside(mixed_columns(frames, rows, 0, arrived_ref[:, span].astype(F32), table_ref, span))
        own_ref[:, span] = jnp.concatenate(totals[:frames])
        other_ref[:, span] = jnp.concatenate(totals[frames:]).astype(BF16)


def before_kernel(frames, rows, rounds_h, table_ref, *refs):
    *arrived, own_ref, other_ref = refs
    per = 1 + rounds_h
    for lane in range(0, own_ref.shape[1], LANES):
        span = slice(lane, lane + LANES)
        parts = [0.0] * per
        for d in range(1, len(arrived) // per + 1):
            for i, ref in enumerate(arrived[(d - 1) * per : d * per]):
                pixels = rows if i == 0 else 1
                column = later(d, ref[:, span].astype(F32))
                totals = beside(mixed_columns(frames, pixels, d, column, table_ref, span))
                sums = jnp.concatenate(totals[:frames]), jnp.concatenate(totals[frames:])
                parts[i] = sums if d == 1 else tuple(a + b for a, b in zip(parts[i], sums))
        own_ref[:, span] = jnp.concatenate([a for a, _ in parts])
        other_ref[:, span] = jnp.concatenate([b for _, b in parts]).astype(BF16)


def both_sides(own, other):
    right = on_right()
    return jnp.where(right, other, own), jnp.where(right, own, other)


def border_kernel(frames, rows, cols, mine_ref, own_ref, other_ref, low_ref, high_ref, *outs):
    sites = rows * cols
    odd, _, _ = position("height")
    low, high = both_sides(own_ref[...], other_ref[...].astype(F32))
    low_ref[...] = low
    high_ref[...] = high
    ends = []
    for r in (0, rows - 1):
        line = [mine_ref[t * sites + r * cols : t * sites + (r + 1) * cols] for t in range(frames)]
        corners = [side[t * rows + r : t * rows + r + 1] for side in (low, high) for t in range(frames)]
        ends.append(jnp.concatenate(line + corners))
    for k, out in enumerate(outs):
        out[...] = jnp.where(odd, *(ends[::-1] if k else ends)).astype(BF16)


def shifted(line, left, right):
    cols = line.shape[0]
    place = lax.broadcasted_iota(jnp.int32, line.shape, 0)
    before = jnp.where(place == 0, left, pltpu.roll(line, 1, 0))
    after = jnp.where(place == cols - 1, right, pltpu.roll(line, cols - 1, 0))
    return before, line, after


def projected(mixed, gate, wv_ref, wo_ref):
    value = jnp.dot(mixed, wv_ref[...], preferred_element_type=F32)
    hidden = (value * gate).astype(BF16)
    return jnp.dot(hidden, wo_ref[...], preferred_element_type=F32).astype(BF16)


def filtered(lines, lefts, rights, taps):
    totals = [None] * len(lines)
    for r, line in enumerate(lines):
        near = shifted(line, lefts[r], rights[r])
        for a in range(3):
            to = r + 1 - a
            if 0 <= to < len(lines):
                term = near[0] * taps[a][0] + near[1] * taps[a][1] + near[2] * taps[a][2]
                totals[to] = term if totals[to] is None else totals[to] + term
    return totals


def taps_of(taps_ref, span):
    return [[taps_ref[3 * a + b : 3 * a + b + 1, span] for b in range(3)] for a in range(3)]


def inner_kernel(
    frames, rows, cols, mine_ref, low_ref, high_ref, taps_ref, gate_ref, wv_ref, wo_ref, out_ref, totals_ref, mixed
):
    sites = rows * cols
    for lane in range(0, mine_ref.shape[1], LANES):
        span = slice(lane, lane + LANES)
        taps = taps_of(taps_ref, span)
        low, high = low_ref[:, span], high_ref[:, span]
        for t in range(frames):
            at = t * sites
            lines = [mine_ref[at + r * cols : at + (r + 1) * cols, span] for r in range(rows)]
            lefts = [low[t * rows + r : t * rows + r + 1] for r in range(rows)]
            rights = [high[t * rows + r : t * rows + r + 1] for r in range(rows)]
            total = jnp.concatenate(filtered(lines, lefts, rights, taps))
            totals_ref[at : at + sites, span] = total
            mixed[at : at + sites, span] = total.astype(BF16)
    out_ref[...] = projected(mixed[...], gate_ref[...], wv_ref, wo_ref)


def last_kernel(frames, rows, cols, chips, inner_ref, totals_ref, taps_ref, gate_ref, wv_ref, wo_ref, *refs):
    *parts, out_ref, mixed = refs
    chans = out_ref.shape[1]
    sites = rows * cols
    size = frames * cols
    odd, lower, upper = position("height")
    earlier = lax.div(lax.axis_index("tm"), 2) > 0
    rounds_h = (len(parts) - (chips + 1 if chips > 1 else 0)) // chips
    ends, parts = parts[:rounds_h], parts[rounds_h:]
    lines_before, parts = parts[: rounds_h * (chips - 1)], parts[rounds_h * (chips - 1) :]
    wholes, sides = parts[: chips - 1], parts[chips - 1 :]
    none = jnp.zeros((cols, chans), F32)
    above, below = [none] * frames, [none] * frames
    low = high = None
    if sides:
        low, high = both_sides(sides[0][...], sides[1][...].astype(F32))
    for k, end in enumerate(ends):
        end = end[...].astype(F32)
        first = jnp.logical_not(odd) if k else odd
        line, lefts, rights = end[:size], end[size : size + frames], end[size + frames : size + 2 * frames]
        for d in range(1, chips):
            line = line + later(d, lines_before[(d - 1) * rounds_h + k][...].astype(F32))
        if sides:
            at = frames * rows + k * frames
            lefts, rights = lefts + low[at : at + frames], rights + high[at : at + frames]
        exists = jnp.where(first, lower, upper)
        tap = jnp.where(first, taps_ref[0:3], taps_ref[6:9])
        for t in range(frames):
            near = shifted(line[t * cols : (t + 1) * cols], lefts[t : t + 1], rights[t : t + 1])
            more = near[0] * tap[0:1] + near[1] * tap[1:2] + near[2] * tap[2:3]
            more = jnp.where(exists, more, none)
            above[t] = above[t] + jnp.where(first, more, none)
            below[t] = below[t] + jnp.where(first, none, more)

    @pl.when(jnp.logical_not(earlier))
    def _():
        out_ref[...] = inner_ref[...]
        rows_at = [t * sites for t in range(frames)], [(t + 1) * sites - cols for t in range(frames)]
        added = above, below
        if rounds_h > 1:
            change, gate = [], []
            for at, more in zip(rows_at, added):
                change += [totals_ref[i : i + cols] + m for i, m in zip(at, more)]
                gate += [gate_ref[i : i + cols] for i in at]
        else:
            change = [
                jnp.where(odd, totals_ref[i : i + cols] + m, totals_ref[j : j + cols] + n)
                for i, j, m, n in zip(*rows_at, *added)
            ]
            gate = [jnp.where(odd, gate_ref[i : i + cols], gate_ref[j : j + cols]) for i, j in zip(*rows_at)]
        new = projected(jnp.concatenate(change).astype(BF16), jnp.concatenate(gate), wv_ref, wo_ref)
        for t in range(frames):
            i, j = rows_at[0][t], rows_at[1][t]
            line = new[t * cols : (t + 1) * cols]
            if rounds_h > 1:
                out_ref[i : i + cols] = line
                out_ref[j : j + cols] = new[size + t * cols : size + (t + 1) * cols]
            else:
                out_ref[i : i + cols] = jnp.where(odd, line, inner_ref[i : i + cols])
                out_ref[j : j + cols] = jnp.where(odd, inner_ref[j : j + cols], line)

    if chips == 1:
        return

    @pl.when(earlier)
    def _():
        for lane in range(0, chans, LANES):
            span = slice(lane, lane + LANES)
            taps = taps_of(taps_ref, span)
            for t in range(frames):
                at = t * sites
                tile = 0.0
                for d, ref in enumerate(wholes, 1):
                    tile = tile + later(d, ref[at : at + sites, span].astype(F32))
                lines = [tile[r * cols : (r + 1) * cols] for r in range(rows)]
                lefts = [low[t * rows + r : t * rows + r + 1, span] for r in range(rows)]
                rights = [high[t * rows + r : t * rows + r + 1, span] for r in range(rows)]
                total = filtered(lines, lefts, rights, taps)
                total[0] = total[0] + above[t][:, span]
                total[rows - 1] = total[rows - 1] + below[t][:, span]
                total = jnp.concatenate(total) + totals_ref[at : at + sites, span]
                mixed[at : at + sites, span] = total.astype(BF16)
        out_ref[...] = projected(mixed[...], gate_ref[...], wv_ref, wo_ref)


def body(latents, spatial_taps, kernel_taps, skip_gain, gate_weight, value_weight, out_weight):
    frames, rows, cols, chans = latents.shape
    lags = kernel_taps.shape[0]
    n_t, n_h, n_w = lax.axis_size("tm"), lax.axis_size("height"), lax.axis_size("width")
    chips = n_t // 2
    block = frames * rows * cols
    shape = jax.ShapeDtypeStruct
    x = latents.reshape(block, chans)

    partner = lax.ppermute(x, "tm", [(i, i ^ 1) for i in range(n_t)])
    inputs = [kernel_taps, skip_gain.reshape(1, chans), x]
    lines = frames * rows
    field = shape((block, chans), F32)
    table, side, *fields = call(
        functools.partial(early_kernel, frames, rows, cols),
        "early",
        [shape((lags + 2 * frames, cols, chans), F32), shape((lines, chans), F32)] + [field] * chips,
        [pltpu.VMEM(a.shape, a.dtype) for a in inputs]
        + [pltpu.SemaphoreType.DMA((len(inputs),)), pltpu.VMEM((block, LANES), F32)],
        inputs,
        2 * chips * frames * x.size,
        far=len(inputs),
    )
    (gate,) = call(
        gate_kernel, "gate", [shape((block, chans), F32)], [], [x, gate_weight], 2 * block * chans * chans, x.size
    )

    h_rounds = swaps("height")
    rounds = len(h_rounds)
    column, *corners = call(
        functools.partial(column_kernel, frames, rows, cols),
        "column",
        [shape((2 * lines, chans), BF16)] + [shape((2 * frames, chans), BF16)] * rounds,
        [pltpu.VMEM((block, LANES), F32)],
        [partner, side],
    )
    sent = call(
        functools.partial(later_kernel, frames, rows, cols, rounds),
        "later",
        ([shape((block, chans), BF16)] + [shape((frames * cols, chans), BF16)] * rounds) * (chips - 1),
        [],
        [partner, table] + fields[1:],
        2 * (chips - 1) * frames * x.size,
    )
    (mine,) = call(
        functools.partial(own_kernel, frames, rows, cols),
        "own",
        [field],
        [],
        [partner, table, fields[0]],
        2 * frames * x.size,
    )

    def move(data, d, across_w, pairs=None):
        route = []
        for i in range(n_t):
            for h in range(n_h):
                for j in range(n_w):
                    real = i // 2 + d < chips
                    to = facing(i % 2, j, n_w) if across_w and real else j
                    at = pairs[h][1] if pairs and real else h
                    if d == 0 and to == j and n_h % 2 == 0:
                        at = h ^ 1
                    route.append(((i * n_h + h) * n_w + j, ((i + 2 * d) % n_t * n_h + at) * n_w + to))
        return lax.ppermute(data, ("tm", "height", "width"), route)

    wholes, before, rows_before = [], [], []
    for d in range(1, chips):
        whole, *edges = sent[(d - 1) * (1 + rounds) : d * (1 + rounds)]
        wholes.append(move(whole, d, False))
        before.append(move(column, d, True))
        rows_before += [move(edge, d, False, pairs) for edge, pairs in zip(edges, h_rounds)]
        before += [move(corner, d, True, pairs) for corner, pairs in zip(corners, h_rounds)]
    swap = [(i, i ^ 1) for i in range(n_t)]
    own, other = call(
        functools.partial(side_kernel, frames, rows),
        "side",
        [shape((lines, chans), F32), shape((lines, chans), BF16)],
        [],
        [table, move(column, 0, True)],
    )
    other = lax.ppermute(other, "tm", swap)
    sides = []
    if chips > 1:
        many = lines + rounds * frames
        mine_before, other_before = call(
            functools.partial(before_kernel, frames, rows, rounds),
            "before",
            [shape((many, chans), F32), shape((many, chans), BF16)],
            [],
            [table] + before,
        )
        sides = [mine_before, lax.ppermute(other_before, "tm", swap)]
    size = frames * cols + 2 * frames
    low, high, *ends = call(
        functools.partial(border_kernel, frames, rows, cols),
        "border",
        [shape((lines, chans), F32)] * 2 + [shape((size, chans), BF16)] * len(h_rounds),
        [],
        [mine, own, other],
    )
    ends = [lax.ppermute(e, "height", pairs) for e, pairs in zip(ends, h_rounds)]

    taps = spatial_taps.reshape(9, chans)
    inner, totals = call(
        functools.partial(inner_kernel, frames, rows, cols),
        "inner",
        [shape((block, chans), BF16), field],
        [pltpu.VMEM((block, chans), BF16)],
        [mine, low, high, taps, gate, value_weight, out_weight],
        4 * block * chans * chans,
    )
    (out,) = call(
        functools.partial(last_kernel, frames, rows, cols, chips),
        "last",
        [shape((block, chans), BF16)],
        [pltpu.VMEM((block, chans), BF16)],
        [inner, totals, taps, gate, value_weight, out_weight] + ends + rows_before + wholes + sides,
        4 * block * chans * chans,
    )
    return out.reshape(latents.shape)


def solution(mesh):
    in_specs = (P("tm", "height", "width", None), P(), P(), P(), P(), P(), P())
    out_specs = P("tm", "height", "width", None)
    return jax.shard_map(body, mesh=mesh, in_specs=in_specs, out_specs=out_specs, check_vma=False)
```

```python
import functools

import jax
import jax.numpy as jnp
from jax import lax
from jax.experimental import pallas as pl
from jax.experimental.pallas import tpu as pltpu
from jax.sharding import PartitionSpec as P

LANES = 128
F32, BF16 = jnp.float32, jnp.bfloat16
VMEM = pl.BlockSpec(memory_space=pltpu.VMEM)
HBM = pl.BlockSpec(memory_space=pltpu.HBM)


def call(kernel, name, outs, scratch, operands, far=0):
    operands = [pltpu.with_memory_space_constraint(a, pltpu.HBM) for a in operands[:far]] + list(operands[far:])
    return pl.pallas_call(
        kernel,
        out_shape=tuple(outs),
        in_specs=[HBM] * far + [VMEM] * (len(operands) - far),
        out_specs=(VMEM,) * len(outs),
        scratch_shapes=scratch,
        compiler_params=pltpu.CompilerParams(vmem_limit_bytes=24 * 1024 * 1024),
        cost_estimate=pl.CostEstimate(flops=0, bytes_accessed=0, transcendentals=0),
        name=name,
    )(*operands)


def swaps(axis):
    n = lax.axis_size(axis)
    rounds = []
    for first in range(2 if n > 2 else 1):
        to = list(range(n))
        for i in range(first, n - 1, 2):
            to[i], to[i + 1] = i + 1, i
        rounds.append(list(enumerate(to)))
    return rounds


def position(axis):
    i, n = lax.axis_index(axis), lax.axis_size(axis)
    return lax.rem(i, 2) == 1, i > 0, i < n - 1


def second():
    return lax.rem(lax.axis_index("tm"), 2) == 1


def on_right():
    return lax.rem(lax.axis_index("tm") + lax.axis_index("width"), 2) == 0


def facing(core, column, columns):
    to = column + (1 if (core + column) % 2 == 0 else -1)
    return to if 0 <= to < columns else column


def outer_column(ref, lines, cols):
    return jnp.where(on_right(), ref[pl.ds(cols - 1, lines, stride=cols), :], ref[pl.ds(0, lines, stride=cols), :])


def gate_kernel(x_ref, w_ref, gate_ref):
    v = jnp.dot(x_ref[...], w_ref[...], preferred_element_type=F32)
    gate_ref[...] = v / (1.0 + jnp.exp(-v))


def early_kernel(frames, rows, cols, count, *refs):
    far, kept, rest = refs[:count], refs[count : 2 * count - 2], refs[2 * count - 2 :]
    table_ref, side_ref, *fields, taps_ref, skip_ref, arrived, held = rest
    near = (taps_ref, skip_ref) + kept
    x_ref = near[2]
    copies = [pltpu.make_async_copy(a, b, arrived.at[i]) for i, (a, b) in enumerate(zip(far, near))]
    for copy in copies:
        copy.start()
    lags, chans = taps_ref.shape
    copies[0].wait()
    copies[1].wait()
    pad = 2 * frames
    taps = taps_ref[...].astype(F32)
    table_ref[0:pad] = jnp.zeros((pad, cols, chans), F32)
    for lag in range(lags):
        tap = taps[lag : lag + 1] + (skip_ref[...] if lag == 0 else 0.0)
        table_ref[pad + lag] = jnp.broadcast_to(tap, (cols, chans))
    sites = rows * cols
    copies[2].wait()
    for lane in range(0, chans, LANES):
        span = slice(lane, lane + LANES)
        held[...] = x_ref[:, span].astype(F32)
        side_ref[:, span] = outer_column(held, frames * rows, cols)
        for d, field in enumerate(fields):
            totals = [None] * frames
            for s in range(frames):
                x = x_ref[s * sites : (s + 1) * sites, span].astype(F32).reshape(rows, cols, LANES)
                for t in range(s if d == 0 else 0, frames):
                    term = table_ref[pad + 2 * d * frames + t - s, :, span] * x
                    totals[t] = term if totals[t] is None else totals[t] + term
            for t in range(frames):
                field[t * sites : (t + 1) * sites, span] = totals[t].reshape(sites, LANES)
    for copy in copies[3:]:
        copy.wait()


def column_kernel(frames, rows, cols, partner_ref, side_ref, out_ref, *refs):
    *corners, held = refs
    odd = position("height")[0]
    for lane in range(0, out_ref.shape[1], LANES):
        span = slice(lane, lane + LANES)
        held[...] = partner_ref[:, span].astype(F32)
        column = jnp.concatenate([side_ref[:, span], outer_column(held, frames * rows, cols)])
        out_ref[:, span] = column.astype(BF16)
        ends = [jnp.concatenate([column[s + r : s + r + 1] for s in range(0, column.shape[0], rows)]) for r in (0, rows - 1)]
        for k, corner in enumerate(corners):
            corner[:, span] = jnp.where(odd, *(ends[::-1] if k else ends)).astype(BF16)


def shift(frames):
    return jnp.where(second(), frames, -frames)


def with_partner(frames, rows, cols, d, field_ref, partner_ref, table_ref, span):
    sites = rows * cols
    base = 2 * frames + 2 * d * frames + shift(frames)
    totals = [field_ref[t * sites : (t + 1) * sites, span].reshape(rows, cols, LANES) for t in range(frames)]
    for s in range(frames):
        x = partner_ref[s * sites : (s + 1) * sites, span].astype(F32).reshape(rows, cols, LANES)
        for t in range(frames):
            totals[t] = totals[t] + table_ref[base + t - s, :, span] * x
    return totals


def later_kernel(frames, rows, cols, rounds_h, partner_ref, table_ref, *refs):
    n = len(refs) // (2 + rounds_h)
    fields, outs = refs[:n], refs[n:]
    odd = position("height")[0]
    for d, field in enumerate(fields, 1):
        whole, *lines = outs[(d - 1) * (1 + rounds_h) : d * (1 + rounds_h)]
        for lane in range(0, field.shape[1], LANES):
            span = slice(lane, lane + LANES)
            totals = with_partner(frames, rows, cols, d, field, partner_ref, table_ref, span)
            whole[:, span] = jnp.concatenate(totals).reshape(whole.shape[0], LANES).astype(BF16)
            ends = [jnp.concatenate([t[r] for t in totals]) for r in (0, rows - 1)]
            for k, line in enumerate(lines):
                line[:, span] = jnp.where(odd, *(ends[::-1] if k else ends)).astype(BF16)


def own_kernel(frames, rows, cols, partner_ref, table_ref, field_ref, mine_ref):
    for lane in range(0, mine_ref.shape[1], LANES):
        span = slice(lane, lane + LANES)
        totals = with_partner(frames, rows, cols, 0, field_ref, partner_ref, table_ref, span)
        mine_ref[:, span] = jnp.concatenate(totals).reshape(mine_ref.shape[0], LANES)


def later(d, value):
    return jnp.where(lax.div(lax.axis_index("tm"), 2) >= d, value, jnp.zeros_like(value))


def mixed_columns(frames, rows, d, column, table_ref, span):
    base = 2 * frames + 2 * d * frames
    totals = [jnp.zeros((rows, column.shape[1]), F32)] * (2 * frames)
    for t in range(2 * frames):
        for s in range(2 * frames):
            lag = t % frames - s % frames
            if t // frames == s // frames:
                if d == 0 and lag < 0:
                    continue
            else:
                lag = lag + (shift(frames) if t < frames else -shift(frames))
            tap = table_ref[base + lag, :, span][:rows]
            totals[t] = totals[t] + tap * column[s * rows : (s + 1) * rows]
    return totals


def beside(totals):
    _, lower, upper = position("width")
    exists = jnp.where(on_right(), upper, lower)
    return [jnp.where(exists, total, jnp.zeros_like(total)) for total in totals]


def side_kernel(frames, rows, table_ref, arrived_ref, own_ref, other_ref, *corners):
    odd = position("height")[0]
    for lane in range(0, own_ref.shape[1], LANES):
        span = slice(lane, lane + LANES)
        totals = beside(mixed_columns(frames, rows, 0, arrived_ref[:, span].astype(F32), table_ref, span))
        own_ref[:, span] = jnp.concatenate(totals[:frames])
        other_ref[:, span] = jnp.concatenate(totals[frames:]).astype(BF16)
        ends = [jnp.concatenate([total[r : r + 1] for total in totals]) for r in (0, rows - 1)]
        for k, corner in enumerate(corners):
            corner[:, span] = jnp.where(odd, *(ends[::-1] if k else ends)).astype(BF16)


def before_kernel(frames, rows, rounds_h, table_ref, *refs):
    *arrived, own_ref, other_ref, line_ref = refs
    per = 1 + rounds_h
    chips = len(arrived) // (per + rounds_h)
    arrived, lines = arrived[: chips * per], arrived[chips * per :]
    size = line_ref.shape[0] // rounds_h
    for k in range(rounds_h):
        line = 0.0
        for d in range(1, chips + 1):
            line = line + later(d, lines[(d - 1) * rounds_h + k][...].astype(F32))
        line_ref[k * size : (k + 1) * size] = line
    for lane in range(0, own_ref.shape[1], LANES):
        span = slice(lane, lane + LANES)
        parts = [0.0] * per
        for d in range(1, chips + 1):
            for i, ref in enumerate(arrived[(d - 1) * per : d * per]):
                pixels = rows if i == 0 else 1
                column = later(d, ref[:, span].astype(F32))
                totals = beside(mixed_columns(frames, pixels, d, column, table_ref, span))
                sums = jnp.concatenate(totals[:frames]), jnp.concatenate(totals[frames:])
                parts[i] = sums if d == 1 else tuple(a + b for a, b in zip(parts[i], sums))
        own_ref[:, span] = jnp.concatenate([a for a, _ in parts])
        other_ref[:, span] = jnp.concatenate([b for _, b in parts]).astype(BF16)


def both_sides(own, other):
    right = on_right()
    return jnp.where(right, other, own), jnp.where(right, own, other)


def border_kernel(frames, rows, cols, mine_ref, *refs):
    n = len(refs) // 3
    sites = rows * cols
    odd, _, _ = position("height")
    ends = []
    for r in (0, rows - 1):
        line = [mine_ref[t * sites + r * cols : t * sites + (r + 1) * cols] for t in range(frames)]
        ends.append(jnp.concatenate(line))
    for k, (own, other, out) in enumerate(zip(refs[:n], refs[n : 2 * n], refs[2 * n :])):
        corners = both_sides(own[...].astype(F32)[:frames], other[...].astype(F32)[frames:])
        out[...] = jnp.concatenate([jnp.where(odd, *(ends[::-1] if k else ends)), *corners]).astype(BF16)


def shifted(line, left, right):
    cols = line.shape[0]
    place = lax.broadcasted_iota(jnp.int32, line.shape, 0)
    before = jnp.where(place == 0, left, pltpu.roll(line, 1, 0))
    after = jnp.where(place == cols - 1, right, pltpu.roll(line, cols - 1, 0))
    return before, line, after


def projected(mixed, gate, wv_ref, wo_ref):
    value = jnp.dot(mixed, wv_ref[...], preferred_element_type=F32)
    hidden = (value * gate).astype(BF16)
    return jnp.dot(hidden, wo_ref[...], preferred_element_type=F32).astype(BF16)


def filtered(lines, lefts, rights, taps):
    totals = [None] * len(lines)
    for r, line in enumerate(lines):
        near = shifted(line, lefts[r], rights[r])
        for a in range(3):
            to = r + 1 - a
            if 0 <= to < len(lines):
                term = near[0] * taps[a][0] + near[1] * taps[a][1] + near[2] * taps[a][2]
                totals[to] = term if totals[to] is None else totals[to] + term
    return totals


def taps_of(taps_ref, span):
    return [[taps_ref[a, b : b + 1, span] for b in range(3)] for a in range(3)]


def inner_kernel(
    frames, rows, cols, mine_ref, own_ref, other_ref, taps_ref, gate_ref, wv_ref, wo_ref, out_ref, totals_ref, mixed
):
    sites = rows * cols
    for lane in range(0, mine_ref.shape[1], LANES):
        span = slice(lane, lane + LANES)
        taps = taps_of(taps_ref, span)
        low, high = both_sides(own_ref[:, span], other_ref[:, span].astype(F32))
        for t in range(frames):
            at = t * sites
            lines = [mine_ref[at + r * cols : at + (r + 1) * cols, span] for r in range(rows)]
            lefts = [low[t * rows + r : t * rows + r + 1] for r in range(rows)]
            rights = [high[t * rows + r : t * rows + r + 1] for r in range(rows)]
            total = jnp.concatenate(filtered(lines, lefts, rights, taps))
            totals_ref[at : at + sites, span] = total
            mixed[at : at + sites, span] = total.astype(BF16)
    out_ref[...] = projected(mixed[...], gate_ref[...], wv_ref, wo_ref)


def last_kernel(frames, rows, cols, chips, inner_ref, totals_ref, taps_ref, gate_ref, wv_ref, wo_ref, *refs):
    *parts, out_ref, mixed = refs
    chans = out_ref.shape[1]
    sites = rows * cols
    size = frames * cols
    odd, lower, upper = position("height")
    earlier = lax.div(lax.axis_index("tm"), 2) > 0
    rounds_h = len(parts) - (chips + 2 if chips > 1 else 0)
    ends, wholes, sides = parts[:rounds_h], parts[rounds_h : rounds_h + chips - 1], parts[rounds_h + chips - 1 :]
    none = jnp.zeros((cols, chans), F32)
    above, below = [none] * frames, [none] * frames
    low = high = None
    if sides:
        low, high = both_sides(sides[0][...], sides[1][...].astype(F32))
    for k, end in enumerate(ends):
        end = end[...].astype(F32)
        first = jnp.logical_not(odd) if k else odd
        line, lefts, rights = end[:size], end[size : size + frames], end[size + frames : size + 2 * frames]
        if sides:
            line = line + sides[2][k * size : (k + 1) * size]
            at = frames * rows + k * frames
            lefts, rights = lefts + low[at : at + frames], rights + high[at : at + frames]
        exists = jnp.where(first, lower, upper)
        tap = jnp.where(first, taps_ref[0], taps_ref[2])
        for t in range(frames):
            near = shifted(line[t * cols : (t + 1) * cols], lefts[t : t + 1], rights[t : t + 1])
            more = near[0] * tap[0:1] + near[1] * tap[1:2] + near[2] * tap[2:3]
            more = jnp.where(exists, more, none)
            above[t] = above[t] + jnp.where(first, more, none)
            below[t] = below[t] + jnp.where(first, none, more)

    @pl.when(jnp.logical_not(earlier))
    def _():
        out_ref[...] = inner_ref[...]
        rows_at = [t * sites for t in range(frames)], [(t + 1) * sites - cols for t in range(frames)]
        added = above, below
        if rounds_h > 1:
            change, gate = [], []
            for at, more in zip(rows_at, added):
                change += [totals_ref[i : i + cols] + m for i, m in zip(at, more)]
                gate += [gate_ref[i : i + cols] for i in at]
        else:
            change = [
                jnp.where(odd, totals_ref[i : i + cols] + m, totals_ref[j : j + cols] + n)
                for i, j, m, n in zip(*rows_at, *added)
            ]
            gate = [jnp.where(odd, gate_ref[i : i + cols], gate_ref[j : j + cols]) for i, j in zip(*rows_at)]
        new = projected(jnp.concatenate(change).astype(BF16), jnp.concatenate(gate), wv_ref, wo_ref)
        for t in range(frames):
            i, j = rows_at[0][t], rows_at[1][t]
            line = new[t * cols : (t + 1) * cols]
            if rounds_h > 1:
                out_ref[i : i + cols] = line
                out_ref[j : j + cols] = new[size + t * cols : size + (t + 1) * cols]
            else:
                out_ref[i : i + cols] = jnp.where(odd, line, inner_ref[i : i + cols])
                out_ref[j : j + cols] = jnp.where(odd, inner_ref[j : j + cols], line)

    if chips == 1:
        return

    @pl.when(earlier)
    def _():
        for lane in range(0, chans, LANES):
            span = slice(lane, lane + LANES)
            taps = taps_of(taps_ref, span)
            for t in range(frames):
                at = t * sites
                tile = 0.0
                for d, ref in enumerate(wholes, 1):
                    tile = tile + later(d, ref[at : at + sites, span].astype(F32))
                lines = [tile[r * cols : (r + 1) * cols] for r in range(rows)]
                lefts = [low[t * rows + r : t * rows + r + 1, span] for r in range(rows)]
                rights = [high[t * rows + r : t * rows + r + 1, span] for r in range(rows)]
                total = filtered(lines, lefts, rights, taps)
                total[0] = total[0] + above[t][:, span]
                total[rows - 1] = total[rows - 1] + below[t][:, span]
                total = jnp.concatenate(total) + totals_ref[at : at + sites, span]
                mixed[at : at + sites, span] = total.astype(BF16)
        out_ref[...] = projected(mixed[...], gate_ref[...], wv_ref, wo_ref)


def body(latents, spatial_taps, kernel_taps, skip_gain, gate_weight, value_weight, out_weight):
    frames, rows, cols, chans = latents.shape
    lags = kernel_taps.shape[0]
    n_t, n_h, n_w = lax.axis_size("tm"), lax.axis_size("height"), lax.axis_size("width")
    chips = n_t // 2
    block = frames * rows * cols
    shape = jax.ShapeDtypeStruct
    x = latents.reshape(block, chans)

    partner = lax.ppermute(x, "tm", [(i, i ^ 1) for i in range(n_t)])
    lines = frames * rows
    field = shape((block, chans), F32)
    inputs = [kernel_taps, skip_gain.reshape(1, chans), x, gate_weight, spatial_taps, value_weight, out_weight]
    near_x, near_gate, taps, value_weight, out_weight, table, side, *fields = call(
        functools.partial(early_kernel, frames, rows, cols, len(inputs)),
        "early",
        [shape(a.shape, a.dtype) for a in inputs[2:]]
        + [shape((lags + 2 * frames, cols, chans), F32), shape((lines, chans), F32)]
        + [field] * chips,
        [pltpu.VMEM(a.shape, a.dtype) for a in inputs[:2]]
        + [pltpu.SemaphoreType.DMA((len(inputs),)), pltpu.VMEM((block, LANES), F32)],
        inputs,
        far=len(inputs),
    )
    (gate,) = call(gate_kernel, "gate", [field], [], [near_x, near_gate])

    h_rounds = swaps("height")
    rounds = len(h_rounds)
    column, *corners = call(
        functools.partial(column_kernel, frames, rows, cols),
        "column",
        [shape((2 * lines, chans), BF16)] + [shape((2 * frames, chans), BF16)] * rounds,
        [pltpu.VMEM((block, LANES), F32)],
        [partner, side],
    )
    sent = call(
        functools.partial(later_kernel, frames, rows, cols, rounds),
        "later",
        ([shape((block, chans), BF16)] + [shape((frames * cols, chans), BF16)] * rounds) * (chips - 1),
        [],
        [partner, table] + fields[1:],
    )
    (mine,) = call(
        functools.partial(own_kernel, frames, rows, cols),
        "own",
        [field],
        [],
        [partner, table, fields[0]],
    )

    def move(data, d, across_w, pairs=None):
        route = []
        for i in range(n_t):
            for h in range(n_h):
                for j in range(n_w):
                    real = i // 2 + d < chips
                    to = facing(i % 2, j, n_w) if across_w and real else j
                    at = pairs[h][1] if pairs and real else h
                    if d == 0 and to == j and n_h % 2 == 0:
                        at = h ^ 1
                    route.append(((i * n_h + h) * n_w + j, ((i + 2 * d) % n_t * n_h + at) * n_w + to))
        return lax.ppermute(data, ("tm", "height", "width"), route)

    wholes, before, rows_before = [], [], []
    for d in range(1, chips):
        whole, *edges = sent[(d - 1) * (1 + rounds) : d * (1 + rounds)]
        wholes.append(move(whole, d, False))
        before.append(move(column, d, True))
        rows_before += [move(edge, d, False, pairs) for edge, pairs in zip(edges, h_rounds)]
        before += [move(corner, d, True, pairs) for corner, pairs in zip(corners, h_rounds)]
    swap = [(i, i ^ 1) for i in range(n_t)]
    own, other, *own_corners = call(
        functools.partial(side_kernel, frames, rows),
        "side",
        [shape((lines, chans), F32), shape((lines, chans), BF16)] + [shape((2 * frames, chans), BF16)] * rounds,
        [],
        [table, move(column, 0, True)],
    )
    other_corners = [lax.ppermute(corner, "tm", swap) for corner in own_corners]
    other = lax.ppermute(other, "tm", swap)
    sides = []
    if chips > 1:
        many = lines + rounds * frames
        mine_before, other_before, line = call(
            functools.partial(before_kernel, frames, rows, rounds),
            "before",
            [shape((many, chans), F32), shape((many, chans), BF16), shape((rounds * frames * cols, chans), F32)],
            [],
            [table] + before + rows_before,
        )
        sides = [mine_before, lax.ppermute(other_before, "tm", swap), line]
    size = frames * cols + 2 * frames
    ends = call(
        functools.partial(border_kernel, frames, rows, cols),
        "border",
        [shape((size, chans), BF16)] * rounds,
        [],
        [mine] + own_corners + other_corners,
    )
    ends = [lax.ppermute(e, "height", pairs) for e, pairs in zip(ends, h_rounds)]

    inner, totals = call(
        functools.partial(inner_kernel, frames, rows, cols),
        "inner",
        [shape((block, chans), BF16), field],
        [pltpu.VMEM((block, chans), BF16)],
        [mine, own, other, taps, gate, value_weight, out_weight],
    )
    (out,) = call(
        functools.partial(last_kernel, frames, rows, cols, chips),
        "last",
        [shape((block, chans), BF16)],
        [pltpu.VMEM((block, chans), BF16)],
        [inner, totals, taps, gate, value_weight, out_weight] + ends + wholes + sides,
    )
    return out.reshape(latents.shape)


def solution(mesh):
    in_specs = (P("tm", "height", "width", None), P(), P(), P(), P(), P(), P())
    out_specs = P("tm", "height", "width", None)
    return jax.shard_map(body, mesh=mesh, in_specs=in_specs, out_specs=out_specs, check_vma=False)
```

```python
import functools

import jax
import jax.numpy as jnp
from jax import lax
from jax.experimental import pallas as pl
from jax.experimental.pallas import tpu as pltpu
from jax.sharding import PartitionSpec as P

LANES = 128
LATER = 8 * 10**9
F32, BF16 = jnp.float32, jnp.bfloat16
VMEM = pl.BlockSpec(memory_space=pltpu.VMEM)
HBM = pl.BlockSpec(memory_space=pltpu.HBM)


def call(kernel, name, outs, scratch, operands, flops=0, exps=0, far=0):
    operands = [pltpu.with_memory_space_constraint(a, pltpu.HBM) for a in operands[:far]] + list(operands[far:])
    moved = sum(a.size * a.dtype.itemsize for a in operands) + sum(a.size * a.dtype.itemsize for a in outs)
    return pl.pallas_call(
        kernel,
        out_shape=tuple(outs),
        in_specs=[HBM] * far + [VMEM] * (len(operands) - far),
        out_specs=(VMEM,) * len(outs),
        scratch_shapes=scratch,
        compiler_params=pltpu.CompilerParams(vmem_limit_bytes=24 * 1024 * 1024),
        cost_estimate=pl.CostEstimate(flops=flops, bytes_accessed=moved, transcendentals=exps),
        name=name,
    )(*operands)


def swaps(axis):
    n = lax.axis_size(axis)
    rounds = []
    for first in range(2 if n > 2 else 1):
        to = list(range(n))
        for i in range(first, n - 1, 2):
            to[i], to[i + 1] = i + 1, i
        rounds.append(list(enumerate(to)))
    return rounds


def position(axis):
    i, n = lax.axis_index(axis), lax.axis_size(axis)
    return lax.rem(i, 2) == 1, i > 0, i < n - 1


def second():
    return lax.rem(lax.axis_index("tm"), 2) == 1


def on_right():
    return lax.rem(lax.axis_index("tm") + lax.axis_index("width"), 2) == 0


def facing(core, column, columns):
    to = column + (1 if (core + column) % 2 == 0 else -1)
    return to if 0 <= to < columns else column


def outer_column(ref, lines, cols):
    return jnp.where(on_right(), ref[pl.ds(cols - 1, lines, stride=cols), :], ref[pl.ds(0, lines, stride=cols), :])


def gate_kernel(x_ref, w_ref, gate_ref):
    v = jnp.dot(x_ref[...], w_ref[...], preferred_element_type=F32)
    gate_ref[...] = v / (1.0 + jnp.exp(-v))


def early_kernel(frames, rows, cols, count, *refs):
    far, kept, rest = refs[:count], refs[count : 2 * count - 2], refs[2 * count - 2 :]
    table_ref, side_ref, *fields, taps_ref, skip_ref, arrived, held = rest
    near = (taps_ref, skip_ref) + kept
    x_ref = near[2]
    copies = [pltpu.make_async_copy(a, b, arrived.at[i]) for i, (a, b) in enumerate(zip(far, near))]
    for copy in copies:
        copy.start()
    lags, chans = taps_ref.shape
    copies[0].wait()
    copies[1].wait()
    pad = 2 * frames
    taps = taps_ref[...].astype(F32)
    table_ref[0:pad] = jnp.zeros((pad, cols, chans), F32)
    for lag in range(lags):
        tap = taps[lag : lag + 1] + (skip_ref[...] if lag == 0 else 0.0)
        table_ref[pad + lag] = jnp.broadcast_to(tap, (cols, chans))
    sites = rows * cols
    copies[2].wait()
    for lane in range(0, chans, LANES):
        span = slice(lane, lane + LANES)
        held[...] = x_ref[:, span].astype(F32)
        side_ref[:, span] = outer_column(held, frames * rows, cols)
        for d, field in enumerate(fields):
            totals = [None] * frames
            for s in range(frames):
                x = x_ref[s * sites : (s + 1) * sites, span].astype(F32).reshape(rows, cols, LANES)
                for t in range(s if d == 0 else 0, frames):
                    term = table_ref[pad + 2 * d * frames + t - s, :, span] * x
                    totals[t] = term if totals[t] is None else totals[t] + term
            for t in range(frames):
                field[t * sites : (t + 1) * sites, span] = totals[t].reshape(sites, LANES)
    for copy in copies[3:]:
        copy.wait()


def reordered(lines, rounds_h, back=False):
    if rounds_h > 1:
        return lines[:1] + lines[2:] + lines[1:2] if back else lines[:1] + lines[-1:] + lines[1:-1]
    odd = position("height")[0]
    return [jnp.where(odd, a, b) for a, b in zip(lines, lines[::-1])]


def column_kernel(frames, rows, cols, partner_ref, side_ref, out_ref, held):
    lines = frames * rows
    for lane in range(0, out_ref.shape[1], LANES):
        span = slice(lane, lane + LANES)
        held[...] = partner_ref[:, span].astype(F32)
        out_ref[:, span] = jnp.concatenate([side_ref[:, span], outer_column(held, lines, cols)]).astype(BF16)


def shift(frames):
    return jnp.where(second(), frames, -frames)


def with_partner(frames, rows, cols, d, field_ref, partner_ref, table_ref, span):
    sites = rows * cols
    base = 2 * frames + 2 * d * frames + shift(frames)
    totals = [field_ref[t * sites : (t + 1) * sites, span].reshape(rows, cols, LANES) for t in range(frames)]
    for s in range(frames):
        x = partner_ref[s * sites : (s + 1) * sites, span].astype(F32).reshape(rows, cols, LANES)
        for t in range(frames):
            totals[t] = totals[t] + table_ref[base + t - s, :, span] * x
    return totals


def later_kernel(frames, rows, cols, rounds_h, partner_ref, table_ref, *refs):
    fields, outs = refs[: len(refs) // 3], refs[len(refs) // 3 :]
    for d, field in enumerate(fields, 1):
        for lane in range(0, field.shape[1], LANES):
            span = slice(lane, lane + LANES)
            totals = with_partner(frames, rows, cols, d, field, partner_ref, table_ref, span)
            tiles = reordered([jnp.concatenate([t[r] for t in totals]) for r in range(rows)], rounds_h)
            outs[2 * d - 2][:, span] = jnp.concatenate(tiles[:rounds_h]).astype(BF16)
            outs[2 * d - 1][:, span] = jnp.concatenate(tiles[rounds_h:]).astype(BF16)


def own_kernel(frames, rows, cols, partner_ref, table_ref, field_ref, mine_ref):
    for lane in range(0, mine_ref.shape[1], LANES):
        span = slice(lane, lane + LANES)
        totals = with_partner(frames, rows, cols, 0, field_ref, partner_ref, table_ref, span)
        mine_ref[:, span] = jnp.concatenate(totals).reshape(mine_ref.shape[0], LANES)


def later(d, value):
    return jnp.where(lax.div(lax.axis_index("tm"), 2) >= d, value, jnp.zeros_like(value))


def side_kernel(frames, rows, table_ref, *refs):
    *arrived, own_ref, other_ref = refs
    _, lower, upper = position("width")
    exists = jnp.where(on_right(), upper, lower)
    for lane in range(0, own_ref.shape[1], LANES):
        span = slice(lane, lane + LANES)
        totals = [jnp.zeros((rows, LANES), F32)] * (2 * frames)
        for d, ref in enumerate(arrived):
            column = later(d, ref[:, span].astype(F32))
            base = 2 * frames + 2 * d * frames
            for t in range(2 * frames):
                for s in range(2 * frames):
                    lag = t % frames - s % frames
                    if t // frames == s // frames:
                        if d == 0 and lag < 0:
                            continue
                    else:
                        lag = lag + (shift(frames) if t < frames else -shift(frames))
                    totals[t] = totals[t] + table_ref[base + lag, :, span] * column[s * rows : (s + 1) * rows]
        totals = [jnp.where(exists, total, jnp.zeros_like(total)) for total in totals]
        own_ref[:, span] = jnp.concatenate(totals[:frames])
        other_ref[:, span] = jnp.concatenate(totals[frames:]).astype(BF16)


def border_kernel(frames, rows, cols, chips, mine_ref, own_ref, other_ref, *refs):
    arrived, (low_ref, high_ref, *outs) = refs[: chips - 1], refs[chips - 1 :]
    sites = rows * cols
    odd, _, _ = position("height")
    right, own, other = on_right(), own_ref[...], other_ref[...].astype(F32)
    low, high = jnp.where(right, other, own), jnp.where(right, own, other)
    low_ref[...] = low
    high_ref[...] = high
    size = frames * cols
    lines, corners = [], []
    for r in (0, rows - 1):
        lines.append(jnp.concatenate([mine_ref[t * sites + r * cols : t * sites + (r + 1) * cols] for t in range(frames)]))
        ends = [side[t * rows + r : t * rows + r + 1] for side in (low, high) for t in range(frames)]
        corners.append(jnp.concatenate(ends))
    for k, out in enumerate(outs):
        line = jnp.where(odd, *(lines[::-1] if k else lines))
        for d, ref in enumerate(arrived, 1):
            if len(outs) > 1:
                ends = [ref[i * size : (i + 1) * size].astype(F32) for i in range(2)]
                more = jnp.where(odd, *(ends[::-1] if k else ends))
            else:
                more = ref[:size].astype(F32)
            line = line + later(d, more)
        out[...] = jnp.concatenate([line, jnp.where(odd, *(corners[::-1] if k else corners))]).astype(BF16)


def shifted(line, left, right):
    cols = line.shape[0]
    place = lax.broadcasted_iota(jnp.int32, line.shape, 0)
    before = jnp.where(place == 0, left, pltpu.roll(line, 1, 0))
    after = jnp.where(place == cols - 1, right, pltpu.roll(line, cols - 1, 0))
    return before, line, after


def projected(mixed, gate, wv_ref, wo_ref):
    value = jnp.dot(mixed, wv_ref[...], preferred_element_type=F32)
    hidden = (value * gate).astype(BF16)
    return jnp.dot(hidden, wo_ref[...], preferred_element_type=F32).astype(BF16)


def filtered(lines, lefts, rights, taps):
    totals = [None] * len(lines)
    for r, line in enumerate(lines):
        near = shifted(line, lefts[r], rights[r])
        for a in range(3):
            to = r + 1 - a
            if 0 <= to < len(lines):
                term = near[0] * taps[a][0] + near[1] * taps[a][1] + near[2] * taps[a][2]
                totals[to] = term if totals[to] is None else totals[to] + term
    return totals


def taps_of(taps_ref, span):
    return [[taps_ref[a, b : b + 1, span] for b in range(3)] for a in range(3)]


def inner_kernel(
    frames, rows, cols, mine_ref, low_ref, high_ref, taps_ref, gate_ref, wv_ref, wo_ref, out_ref, totals_ref, mixed
):
    sites = rows * cols
    for lane in range(0, mine_ref.shape[1], LANES):
        span = slice(lane, lane + LANES)
        taps = taps_of(taps_ref, span)
        low, high = low_ref[:, span], high_ref[:, span]
        for t in range(frames):
            at = t * sites
            lines = [mine_ref[at + r * cols : at + (r + 1) * cols, span] for r in range(rows)]
            lefts = [low[t * rows + r : t * rows + r + 1] for r in range(rows)]
            rights = [high[t * rows + r : t * rows + r + 1] for r in range(rows)]
            total = jnp.concatenate(filtered(lines, lefts, rights, taps))
            totals_ref[at : at + sites, span] = total
            mixed[at : at + sites, span] = total.astype(BF16)
    out_ref[...] = projected(mixed[...], gate_ref[...], wv_ref, wo_ref)


def last_kernel(frames, rows, cols, chips, inner_ref, totals_ref, taps_ref, gate_ref, wv_ref, wo_ref, *refs):
    *parts, out_ref, mixed = refs
    firsts, rests, ends = parts[: chips - 1], parts[chips - 1 : 2 * chips - 2], parts[2 * chips - 2 :]
    rounds_h = len(ends)
    chans = out_ref.shape[1]
    sites = rows * cols
    size = frames * cols
    odd, lower, upper = position("height")
    earlier = lax.div(lax.axis_index("tm"), 2) > 0
    none = jnp.zeros((cols, chans), F32)
    above, below = [none] * frames, [none] * frames
    for k, end in enumerate(ends):
        end = end[...].astype(F32)
        first = jnp.logical_not(odd) if k else odd
        lefts, rights = end[size : size + frames], end[size + frames : size + 2 * frames]
        exists = jnp.where(first, lower, upper)
        tap = jnp.where(first, taps_ref[0], taps_ref[2])
        for t in range(frames):
            near = shifted(end[t * cols : (t + 1) * cols], lefts[t : t + 1], rights[t : t + 1])
            more = near[0] * tap[0:1] + near[1] * tap[1:2] + near[2] * tap[2:3]
            more = jnp.where(exists, more, none)
            above[t] = above[t] + jnp.where(first, more, none)
            below[t] = below[t] + jnp.where(first, none, more)

    @pl.when(jnp.logical_not(earlier))
    def _():
        out_ref[...] = inner_ref[...]
        rows_at = [t * sites for t in range(frames)], [(t + 1) * sites - cols for t in range(frames)]
        added = above, below
        if rounds_h > 1:
            change, gate = [], []
            for at, more in zip(rows_at, added):
                change += [totals_ref[i : i + cols] + m for i, m in zip(at, more)]
                gate += [gate_ref[i : i + cols] for i in at]
        else:
            change = [
                jnp.where(odd, totals_ref[i : i + cols] + m, totals_ref[j : j + cols] + n)
                for i, j, m, n in zip(*rows_at, *added)
            ]
            gate = [jnp.where(odd, gate_ref[i : i + cols], gate_ref[j : j + cols]) for i, j in zip(*rows_at)]
        new = projected(jnp.concatenate(change).astype(BF16), jnp.concatenate(gate), wv_ref, wo_ref)
        for t in range(frames):
            i, j = rows_at[0][t], rows_at[1][t]
            line = new[t * cols : (t + 1) * cols]
            if rounds_h > 1:
                out_ref[i : i + cols] = line
                out_ref[j : j + cols] = new[size + t * cols : size + (t + 1) * cols]
            else:
                out_ref[i : i + cols] = jnp.where(odd, line, inner_ref[i : i + cols])
                out_ref[j : j + cols] = jnp.where(odd, inner_ref[j : j + cols], line)

    @pl.when(earlier)
    def _():
        for lane in range(0, chans, LANES):
            span = slice(lane, lane + LANES)
            taps = taps_of(taps_ref, span)
            lines = [jnp.zeros((size, LANES), F32)] * rows
            for d, (first, rest) in enumerate(zip(firsts, rests), 1):
                more = [first[i * size : (i + 1) * size, span].astype(F32) for i in range(rounds_h)]
                more += [rest[i * size : (i + 1) * size, span].astype(F32) for i in range(rows - rounds_h)]
                more = reordered(more, rounds_h, back=True)
                lines = [line + later(d, other) for line, other in zip(lines, more)]
            zero = [jnp.zeros((1, LANES), F32)] * rows
            for t in range(frames):
                at = t * sites
                total = filtered([line[t * cols : (t + 1) * cols] for line in lines], zero, zero, taps)
                total[0] = total[0] + above[t][:, span]
                total[rows - 1] = total[rows - 1] + below[t][:, span]
                total = jnp.concatenate(total) + totals_ref[at : at + sites, span]
                mixed[at : at + sites, span] = total.astype(BF16)
        out_ref[...] = projected(mixed[...], gate_ref[...], wv_ref, wo_ref)


def body(latents, spatial_taps, kernel_taps, skip_gain, gate_weight, value_weight, out_weight):
    frames, rows, cols, chans = latents.shape
    lags = kernel_taps.shape[0]
    n_t, n_h, n_w = lax.axis_size("tm"), lax.axis_size("height"), lax.axis_size("width")
    chips = n_t // 2
    block = frames * rows * cols
    shape = jax.ShapeDtypeStruct
    x = latents.reshape(block, chans)

    partner = lax.ppermute(x, "tm", [(i, i ^ 1) for i in range(n_t)])
    lines = frames * rows
    field = shape((block, chans), F32)
    inputs = [kernel_taps, skip_gain.reshape(1, chans), x, gate_weight, spatial_taps, value_weight, out_weight]
    near_x, near_gate, taps, value_weight, out_weight, table, side, *fields = call(
        functools.partial(early_kernel, frames, rows, cols, len(inputs)),
        "early",
        [shape(a.shape, a.dtype) for a in inputs[2:]]
        + [shape((lags + 2 * frames, cols, chans), F32), shape((lines, chans), F32)]
        + [field] * chips,
        [pltpu.VMEM(a.shape, a.dtype) for a in inputs[:2]]
        + [pltpu.SemaphoreType.DMA((len(inputs),)), pltpu.VMEM((block, LANES), F32)],
        inputs,
        far=len(inputs),
    )
    (gate,) = call(gate_kernel, "gate", [field], [], [near_x, near_gate])

    h_rounds = swaps("height")
    (column,) = call(
        functools.partial(column_kernel, frames, rows, cols),
        "column",
        [shape((2 * lines, chans), BF16)],
        [pltpu.VMEM((block, LANES), F32)],
        [partner, side],
    )
    parts = [shape((n * frames * cols, chans), BF16) for n in (len(h_rounds), rows - len(h_rounds))]
    sent = call(
        functools.partial(later_kernel, frames, rows, cols, len(h_rounds)),
        "later",
        parts * (chips - 1),
        [],
        [partner, table] + fields[1:],
        2 * (chips - 1) * frames * x.size,
    )
    (mine,) = call(
        functools.partial(own_kernel, frames, rows, cols),
        "own",
        [field],
        [],
        [partner, table, fields[0]],
        2 * frames * x.size,
    )
    columns, firsts, rests = [], [], []
    for d in range(chips):
        route = []
        for i in range(n_t):
            for h in range(n_h):
                for j in range(n_w):
                    to, beside = facing(i % 2, j, n_w), h
                    if i // 2 + d >= chips:
                        to = j
                    elif to == j and n_h % 2 == 0:
                        beside = h ^ 1
                    source = (i * n_h + h) * n_w + j
                    route.append((source, ((i + 2 * d) % n_t * n_h + beside) * n_w + to))
        columns.append(lax.ppermute(column, ("tm", "height", "width"), route))
    for d in range(1, chips):
        route = [(i, (i + 2 * d) % n_t) for i in range(n_t)]
        firsts.append(lax.ppermute(sent[2 * d - 2], "tm", route))
        rests.append(lax.ppermute(sent[2 * d - 1], "tm", route))

    own, other = call(
        functools.partial(side_kernel, frames, rows),
        "side",
        [shape((lines, chans), F32), shape((lines, chans), BF16)],
        [],
        [table] + columns,
        LATER,
    )
    other = lax.ppermute(other, "tm", [(i, i ^ 1) for i in range(n_t)])
    size = frames * cols + 2 * frames
    low, high, *ends = call(
        functools.partial(border_kernel, frames, rows, cols, chips),
        "border",
        [shape((lines, chans), F32)] * 2 + [shape((size, chans), BF16)] * len(h_rounds),
        [],
        [mine, own, other] + firsts,
    )
    ends = [lax.ppermute(e, "height", pairs) for e, pairs in zip(ends, h_rounds)]

    inner, totals = call(
        functools.partial(inner_kernel, frames, rows, cols),
        "inner",
        [shape((block, chans), BF16), field],
        [pltpu.VMEM((block, chans), BF16)],
        [mine, low, high, taps, gate, value_weight, out_weight],
        4 * block * chans * chans,
    )
    (out,) = call(
        functools.partial(last_kernel, frames, rows, cols, chips),
        "last",
        [shape((block, chans), BF16)],
        [pltpu.VMEM((block, chans), BF16)],
        [inner, totals, taps, gate, value_weight, out_weight] + firsts + rests + ends,
        4 * block * chans * chans,
    )
    return out.reshape(latents.shape)


def solution(mesh):
    in_specs = (P("tm", "height", "width", None), P(), P(), P(), P(), P(), P())
    out_specs = P("tm", "height", "width", None)
    return jax.shard_map(body, mesh=mesh, in_specs=in_specs, out_specs=out_specs, check_vma=False)
```

```python
import functools

import jax
import jax.numpy as jnp
from jax import lax
from jax.experimental import pallas as pl
from jax.experimental.pallas import tpu as pltpu
from jax.sharding import PartitionSpec as P

LANES = 128
SIDE = 4 * 10**9
PAD = 16
F32, BF16 = jnp.float32, jnp.bfloat16
VMEM = pl.BlockSpec(memory_space=pltpu.VMEM)
HBM = pl.BlockSpec(memory_space=pltpu.HBM)


def call(kernel, name, outs, scratch, operands, far=0, far_outs=0, aliases={}, flops=0):
    operands = [pltpu.with_memory_space_constraint(a, pltpu.HBM) for a in operands[:far]] + list(operands[far:])
    return pl.pallas_call(
        kernel,
        out_shape=tuple(outs),
        in_specs=[HBM] * far + [VMEM] * (len(operands) - far),
        out_specs=(HBM,) * far_outs + (VMEM,) * (len(outs) - far_outs),
        scratch_shapes=scratch,
        input_output_aliases=aliases,
        compiler_params=pltpu.CompilerParams(vmem_limit_bytes=24 * 1024 * 1024),
        cost_estimate=pl.CostEstimate(flops=flops, bytes_accessed=0, transcendentals=0),
        name=name,
    )(*operands)


def swaps(axis):
    n = lax.axis_size(axis)
    rounds = []
    for first in range(2 if n > 2 else 1):
        to = list(range(n))
        for i in range(first, n - 1, 2):
            to[i], to[i + 1] = i + 1, i
        rounds.append(list(enumerate(to)))
    return rounds


def position(axis):
    i, n = lax.axis_index(axis), lax.axis_size(axis)
    return lax.rem(i, 2) == 1, i > 0, i < n - 1


def second():
    return lax.rem(lax.axis_index("tm"), 2) == 1


def on_right():
    return lax.rem(lax.axis_index("tm") + lax.axis_index("width"), 2) == 0


def facing(core, column, columns):
    to = column + (1 if (core + column) % 2 == 0 else -1)
    return to if 0 <= to < columns else column


def outer_column(ref, lines, cols):
    return jnp.where(on_right(), ref[pl.ds(cols - 1, lines, stride=cols), :], ref[pl.ds(0, lines, stride=cols), :])


def gate_kernel(x_ref, w_ref, gate_ref):
    v = jnp.dot(x_ref[...], w_ref[...], preferred_element_type=F32)
    gate_ref[...] = v / (1.0 + jnp.exp(-v))


def early_kernel(frames, rows, cols, count, *refs):
    far, kept, rest = refs[:count], refs[count : 2 * count - 2], refs[2 * count - 2 :]
    table_ref, side_ref, *fields, taps_ref, skip_ref, arrived, held = rest
    near = (taps_ref, skip_ref) + kept
    x_ref = near[2]
    copies = [pltpu.make_async_copy(a, b, arrived.at[i]) for i, (a, b) in enumerate(zip(far, near))]
    for copy in copies:
        copy.start()
    lags, chans = taps_ref.shape
    copies[0].wait()
    copies[1].wait()
    pad = 2 * frames
    taps = taps_ref[...].astype(F32)
    table_ref[0:pad] = jnp.zeros((pad, cols, chans), F32)
    for lag in range(lags):
        tap = taps[lag : lag + 1] + (skip_ref[...] if lag == 0 else 0.0)
        table_ref[pad + lag] = jnp.broadcast_to(tap, (cols, chans))
    sites = rows * cols
    copies[2].wait()
    for lane in range(0, chans, LANES):
        span = slice(lane, lane + LANES)
        held[...] = x_ref[:, span].astype(F32)
        side_ref[:, span] = outer_column(held, frames * rows, cols)
        for d, field in enumerate(fields):
            totals = [None] * frames
            for s in range(frames):
                x = x_ref[s * sites : (s + 1) * sites, span].astype(F32).reshape(rows, cols, LANES)
                for t in range(s if d == 0 else 0, frames):
                    term = table_ref[pad + 2 * d * frames + t - s, :, span] * x
                    totals[t] = term if totals[t] is None else totals[t] + term
            for t in range(frames):
                field[t * sites : (t + 1) * sites, span] = totals[t].reshape(sites, LANES)
    for copy in copies[3:]:
        copy.wait()


def column_kernel(frames, rows, cols, partner_ref, side_ref, out_ref, held):
    for lane in range(0, out_ref.shape[1], LANES):
        span = slice(lane, lane + LANES)
        held[...] = partner_ref[:, span].astype(F32)
        column = jnp.concatenate([side_ref[:, span], outer_column(held, frames * rows, cols)])
        out_ref[:, span] = column.astype(BF16)


def shift(frames):
    return jnp.where(second(), frames, -frames)


def with_partner(frames, rows, cols, d, field_ref, partner_ref, table_ref, span):
    sites = rows * cols
    base = 2 * frames + 2 * d * frames + shift(frames)
    totals = [field_ref[t * sites : (t + 1) * sites, span].reshape(rows, cols, LANES) for t in range(frames)]
    for s in range(frames):
        x = partner_ref[s * sites : (s + 1) * sites, span].astype(F32).reshape(rows, cols, LANES)
        for t in range(frames):
            totals[t] = totals[t] + table_ref[base + t - s, :, span] * x
    return totals


def later_kernel(frames, rows, cols, rounds_h, partner_ref, table_ref, *refs):
    n = len(refs) // (2 + rounds_h)
    fields, outs = refs[:n], refs[n:]
    odd = position("height")[0]
    for d, field in enumerate(fields, 1):
        whole, *lines = outs[(d - 1) * (1 + rounds_h) : d * (1 + rounds_h)]
        for lane in range(0, field.shape[1], LANES):
            span = slice(lane, lane + LANES)
            totals = with_partner(frames, rows, cols, d, field, partner_ref, table_ref, span)
            whole[:, span] = jnp.concatenate(totals).reshape(whole.shape[0], LANES).astype(BF16)
            ends = [jnp.concatenate([t[r] for t in totals]) for r in (0, rows - 1)]
            for k, line in enumerate(lines):
                line[:, span] = jnp.where(odd, *(ends[::-1] if k else ends)).astype(BF16)


def own_kernel(frames, rows, cols, partner_ref, table_ref, field_ref, mine_ref):
    for lane in range(0, mine_ref.shape[1], LANES):
        span = slice(lane, lane + LANES)
        totals = with_partner(frames, rows, cols, 0, field_ref, partner_ref, table_ref, span)
        mine_ref[:, span] = jnp.concatenate(totals).reshape(mine_ref.shape[0], LANES)


def later(d, value):
    return jnp.where(lax.div(lax.axis_index("tm"), 2) >= d, value, jnp.zeros_like(value))


def mixed_columns(frames, rows, d, column, table_ref, span):
    base = 2 * frames + 2 * d * frames
    totals = [jnp.zeros((rows, column.shape[1]), F32)] * (2 * frames)
    for t in range(2 * frames):
        for s in range(2 * frames):
            lag = t % frames - s % frames
            if t // frames == s // frames:
                if d == 0 and lag < 0:
                    continue
            else:
                lag = lag + (shift(frames) if t < frames else -shift(frames))
            tap = table_ref[base + lag, :, span][:rows]
            totals[t] = totals[t] + tap * column[s * rows : (s + 1) * rows]
    return totals


def beside(totals):
    _, lower, upper = position("width")
    exists = jnp.where(on_right(), upper, lower)
    return [jnp.where(exists, total, jnp.zeros_like(total)) for total in totals]


def side_kernel(frames, rows, rounds_h, table_ref, arrived_ref, *refs):
    n = (len(refs) - 2) // 2
    lines, (own_ref, other_ref, *outs) = refs[:n], refs[n:]
    odd = position("height")[0]
    other_ref[frames * rows :] = jnp.zeros((PAD, other_ref.shape[1]), BF16)
    for lane in range(0, own_ref.shape[1], LANES):
        span = slice(lane, lane + LANES)
        column = arrived_ref[:, span].astype(F32)
        totals = beside(mixed_columns(frames, rows, 0, column, table_ref, span))
        own_ref[:, span] = jnp.concatenate(totals[:frames])
        other_ref[: frames * rows, span] = jnp.concatenate(totals[frames:]).astype(BF16)
        if n:
            ends = [jnp.concatenate([column[s + r : s + r + 1] for s in range(0, column.shape[0], rows)]) for r in (0, rows - 1)]
        for i, (line, out) in enumerate(zip(lines, outs)):
            d, k = i // rounds_h + 1, i % rounds_h
            pixels = jnp.where(odd, *(ends[::-1] if k else ends))
            corners = beside(mixed_columns(frames, 1, d, pixels, table_ref, span))
            out[:, span] = jnp.concatenate([line[:, span].astype(F32)] + corners).astype(BF16)


def before_kernel(frames, rows, cols, rounds_h, after_ref, table_ref, *refs):
    *arrived, own_ref, other_ref, line_ref = refs
    per = 1 + rounds_h
    size = frames * cols
    for lane in range(0, own_ref.shape[1], LANES):
        span = slice(lane, lane + LANES)
        own = other = lines = 0.0
        for d in range(1, len(arrived) // per + 1):
            column, *ends = arrived[(d - 1) * per : d * per]
            column = later(d, column[:, span].astype(F32))
            totals = beside(mixed_columns(frames, rows, d, column, table_ref, span))
            ends = [later(d, end[:, span].astype(F32)) for end in ends]
            own = own + jnp.concatenate(totals[:frames] + [end[size : size + frames] for end in ends])
            other = other + jnp.concatenate(totals[frames:] + [end[size + frames :] for end in ends])
            lines = lines + jnp.concatenate([end[:size] for end in ends])
        own_ref[:, span] = own
        other_ref[: other.shape[0], span] = other.astype(BF16)
        line_ref[:, span] = lines


def both_sides(own, other):
    right = on_right()
    return jnp.where(right, other, own), jnp.where(right, own, other)


def border_kernel(frames, rows, cols, mine_ref, own_ref, other_ref, *outs):
    sites = rows * cols
    odd, _, _ = position("height")
    sides = both_sides(own_ref[...], other_ref[: own_ref.shape[0]].astype(F32))
    ends = []
    for r in (0, rows - 1):
        line = [mine_ref[t * sites + r * cols : t * sites + (r + 1) * cols] for t in range(frames)]
        corners = [side[t * rows + r : t * rows + r + 1] for side in sides for t in range(frames)]
        ends.append(jnp.concatenate(line + corners))
    for k, out in enumerate(outs):
        out[...] = jnp.where(odd, *(ends[::-1] if k else ends)).astype(BF16)


def shifted(line, left, right):
    cols = line.shape[0]
    place = lax.broadcasted_iota(jnp.int32, line.shape, 0)
    before = jnp.where(place == 0, left, pltpu.roll(line, 1, 0))
    after = jnp.where(place == cols - 1, right, pltpu.roll(line, cols - 1, 0))
    return before, line, after


def projected(mixed, gate, wv_ref, wo_ref):
    value = jnp.dot(mixed, wv_ref[...], preferred_element_type=F32)
    hidden = (value * gate).astype(BF16)
    return jnp.dot(hidden, wo_ref[...], preferred_element_type=F32).astype(BF16)


def filtered(lines, lefts, rights, taps):
    totals = [None] * len(lines)
    for r, line in enumerate(lines):
        near = shifted(line, lefts[r], rights[r])
        for a in range(3):
            to = r + 1 - a
            if 0 <= to < len(lines):
                term = near[0] * taps[a][0] + near[1] * taps[a][1] + near[2] * taps[a][2]
                totals[to] = term if totals[to] is None else totals[to] + term
    return totals


def taps_of(taps_ref, span):
    return [[taps_ref[a, b : b + 1, span] for b in range(3)] for a in range(3)]


def inner_kernel(
    frames, rows, cols, mine_ref, own_ref, other_ref, taps_ref, gate_ref, wv_ref, wo_ref, out_ref, totals_ref, mixed
):
    sites = rows * cols
    for lane in range(0, mine_ref.shape[1], LANES):
        span = slice(lane, lane + LANES)
        taps = taps_of(taps_ref, span)
        low, high = both_sides(own_ref[:, span], other_ref[: own_ref.shape[0], span].astype(F32))
        for t in range(frames):
            at = t * sites
            lines = [mine_ref[at + r * cols : at + (r + 1) * cols, span] for r in range(rows)]
            lefts = [low[t * rows + r : t * rows + r + 1] for r in range(rows)]
            rights = [high[t * rows + r : t * rows + r + 1] for r in range(rows)]
            total = jnp.concatenate(filtered(lines, lefts, rights, taps))
            totals_ref[at : at + sites, span] = total
            mixed[at : at + sites, span] = total.astype(BF16)
    out_ref[...] = projected(mixed[...], gate_ref[...], wv_ref, wo_ref)


def from_ends(frames, cols, ends, taps_ref, sides):
    size = frames * cols
    odd, lower, upper = position("height")
    none = jnp.zeros((cols, taps_ref.shape[2]), F32)
    above, below = [none] * frames, [none] * frames
    for k, end in enumerate(ends):
        end = end[...].astype(F32)
        first = jnp.logical_not(odd) if k else odd
        line, lefts, rights = end[:size], end[size : size + frames], end[size + frames : size + 2 * frames]
        if sides:
            low, high, lines = sides
            at = low.shape[0] - (len(ends) - k) * frames
            line = line + lines[k * size : (k + 1) * size]
            lefts, rights = lefts + low[at : at + frames], rights + high[at : at + frames]
        exists = jnp.where(first, lower, upper)
        tap = jnp.where(first, taps_ref[0], taps_ref[2])
        for t in range(frames):
            near = shifted(line[t * cols : (t + 1) * cols], lefts[t : t + 1], rights[t : t + 1])
            more = near[0] * tap[0:1] + near[1] * tap[1:2] + near[2] * tap[2:3]
            more = jnp.where(exists, more, none)
            above[t] = above[t] + jnp.where(first, more, none)
            below[t] = below[t] + jnp.where(first, none, more)
    return above, below


def has_earlier():
    return lax.div(lax.axis_index("tm"), 2) > 0


def edge_kernel(frames, rows, cols, inner_ref, totals_ref, taps_ref, gate_ref, wv_ref, wo_ref, *refs):
    *ends, out_ref, held, done = refs
    rounds_h = len(ends)
    sites = rows * cols
    size = frames * cols
    odd = position("height")[0]

    @pl.when(jnp.logical_not(has_earlier()))
    def _():
        above, below = from_ends(frames, cols, ends, taps_ref, None)
        held[...] = inner_ref[...]
        rows_at = [t * sites for t in range(frames)], [(t + 1) * sites - cols for t in range(frames)]
        added = above, below
        if rounds_h > 1:
            change, gate = [], []
            for at, more in zip(rows_at, added):
                change += [totals_ref[i : i + cols] + m for i, m in zip(at, more)]
                gate += [gate_ref[i : i + cols] for i in at]
        else:
            change = [
                jnp.where(odd, totals_ref[i : i + cols] + m, totals_ref[j : j + cols] + n)
                for i, j, m, n in zip(*rows_at, *added)
            ]
            gate = [jnp.where(odd, gate_ref[i : i + cols], gate_ref[j : j + cols]) for i, j in zip(*rows_at)]
        new = projected(jnp.concatenate(change).astype(BF16), jnp.concatenate(gate), wv_ref, wo_ref)
        for t in range(frames):
            i, j = rows_at[0][t], rows_at[1][t]
            line = new[t * cols : (t + 1) * cols]
            if rounds_h > 1:
                held[i : i + cols] = line
                held[j : j + cols] = new[size + t * cols : size + (t + 1) * cols]
            else:
                held[i : i + cols] = jnp.where(odd, line, inner_ref[i : i + cols])
                held[j : j + cols] = jnp.where(odd, inner_ref[j : j + cols], line)
        copy = pltpu.make_async_copy(held, out_ref, done)
        copy.start()
        copy.wait()


def last_kernel(
    frames, rows, cols, rounds_h, before_ref, totals_ref, taps_ref, gate_ref, wv_ref, wo_ref, *refs
):
    *parts, out_ref, mixed, held, done = refs
    ends, wholes, (own_ref, other_ref, line_ref) = parts[:rounds_h], parts[rounds_h:-3], parts[-3:]
    chans = held.shape[1]
    sites = rows * cols

    @pl.when(has_earlier())
    def _():
        low, high = both_sides(own_ref[...], other_ref[: own_ref.shape[0]].astype(F32))
        above, below = from_ends(frames, cols, ends, taps_ref, (low, high, line_ref[...]))
        for lane in range(0, chans, LANES):
            span = slice(lane, lane + LANES)
            taps = taps_of(taps_ref, span)
            for t in range(frames):
                at = t * sites
                tile = 0.0
                for d, ref in enumerate(wholes, 1):
                    tile = tile + later(d, ref[at : at + sites, span].astype(F32))
                lines = [tile[r * cols : (r + 1) * cols] for r in range(rows)]
                lefts = [low[t * rows + r : t * rows + r + 1, span] for r in range(rows)]
                rights = [high[t * rows + r : t * rows + r + 1, span] for r in range(rows)]
                total = filtered(lines, lefts, rights, taps)
                total[0] = total[0] + above[t][:, span]
                total[rows - 1] = total[rows - 1] + below[t][:, span]
                total = jnp.concatenate(total) + totals_ref[at : at + sites, span]
                mixed[at : at + sites, span] = total.astype(BF16)
        held[...] = projected(mixed[...], gate_ref[...], wv_ref, wo_ref)
        copy = pltpu.make_async_copy(held, out_ref, done)
        copy.start()
        copy.wait()


def body(latents, spatial_taps, kernel_taps, skip_gain, gate_weight, value_weight, out_weight):
    frames, rows, cols, chans = latents.shape
    lags = kernel_taps.shape[0]
    n_t, n_h, n_w = lax.axis_size("tm"), lax.axis_size("height"), lax.axis_size("width")
    chips = n_t // 2
    block = frames * rows * cols
    shape = jax.ShapeDtypeStruct
    x = latents.reshape(block, chans)

    partner = lax.ppermute(x, "tm", [(i, i ^ 1) for i in range(n_t)])
    lines = frames * rows
    field = shape((block, chans), F32)
    inputs = [kernel_taps, skip_gain.reshape(1, chans), x, gate_weight, spatial_taps, value_weight, out_weight]
    near_x, near_gate, taps, value_weight, out_weight, table, side, *fields = call(
        functools.partial(early_kernel, frames, rows, cols, len(inputs)),
        "early",
        [shape(a.shape, a.dtype) for a in inputs[2:]]
        + [shape((lags + 2 * frames, cols, chans), F32), shape((lines, chans), F32)]
        + [field] * chips,
        [pltpu.VMEM(a.shape, a.dtype) for a in inputs[:2]]
        + [pltpu.SemaphoreType.DMA((len(inputs),)), pltpu.VMEM((block, LANES), F32)],
        inputs,
        far=len(inputs),
    )
    (gate,) = call(gate_kernel, "gate", [field], [], [near_x, near_gate])

    h_rounds = swaps("height")
    rounds = len(h_rounds)
    (column,) = call(
        functools.partial(column_kernel, frames, rows, cols),
        "column",
        [shape((2 * lines, chans), BF16)],
        [pltpu.VMEM((block, LANES), F32)],
        [partner, side],
    )
    sent = call(
        functools.partial(later_kernel, frames, rows, cols, rounds),
        "later",
        ([shape((block, chans), BF16)] + [shape((frames * cols, chans), BF16)] * rounds) * (chips - 1),
        [],
        [partner, table] + fields[1:],
    )
    (mine,) = call(
        functools.partial(own_kernel, frames, rows, cols),
        "own",
        [field],
        [],
        [partner, table, fields[0]],
    )

    def move(data, d, across_w, pairs=None):
        route = []
        for i in range(n_t):
            for h in range(n_h):
                for j in range(n_w):
                    real = i // 2 + d < chips
                    to = facing(i % 2, j, n_w) if across_w and real else j
                    at = pairs[h][1] if pairs and real else h
                    if d == 0 and to == j and n_h % 2 == 0:
                        at = h ^ 1
                    route.append(((i * n_h + h) * n_w + j, ((i + 2 * d) % n_t * n_h + at) * n_w + to))
        return lax.ppermute(data, ("tm", "height", "width"), route)

    wholes, before, edges = [], [], []
    for d in range(1, chips):
        whole, *lines_later = sent[(d - 1) * (1 + rounds) : d * (1 + rounds)]
        wholes.append(move(whole, d, False))
        before.append([move(column, d, True)])
        edges += lines_later
    swap = [(i, i ^ 1) for i in range(n_t)]
    with_corners = shape((frames * cols + 2 * frames, chans), BF16)
    own, other, *edges = call(
        functools.partial(side_kernel, frames, rows, rounds),
        "side",
        [shape((lines, chans), F32), shape((lines + PAD, chans), BF16)] + [with_corners] * len(edges),
        [],
        [table, move(column, 0, True)] + edges,
        flops=SIDE,
    )
    other = lax.ppermute(other, "tm", swap)
    size = frames * cols + 2 * frames
    ends = call(
        functools.partial(border_kernel, frames, rows, cols),
        "border",
        [shape((size, chans), BF16)] * rounds,
        [],
        [mine, own, other],
    )
    ends = [lax.ppermute(e, "height", pairs) for e, pairs in zip(ends, h_rounds)]

    inner, totals = call(
        functools.partial(inner_kernel, frames, rows, cols),
        "inner",
        [shape((block, chans), BF16), field],
        [pltpu.VMEM((block, chans), BF16)],
        [mine, own, other, taps, gate, value_weight, out_weight],
    )
    sides = []
    if chips > 1:
        for i, edge in enumerate(edges):
            before[i // rounds].append(move(edge, i // rounds + 1, False, h_rounds[i % rounds]))
        many = lines + rounds * frames
        mine_before, other_before, line = call(
            functools.partial(before_kernel, frames, rows, cols, rounds),
            "before",
            [shape((many, chans), F32), shape((many, chans), BF16), shape((rounds * frames * cols, chans), F32)],
            [],
            [totals, table] + sum(before, []),
        )
        sides = [mine_before, lax.ppermute(other_before, "tm", swap), line]
    (out,) = call(
        functools.partial(edge_kernel, frames, rows, cols),
        "edge",
        [shape((block, chans), BF16)],
        [pltpu.VMEM((block, chans), BF16), pltpu.SemaphoreType.DMA],
        [inner, totals, taps, gate, value_weight, out_weight] + ends,
        far_outs=1,
    )
    if chips > 1:
        (out,) = call(
            functools.partial(last_kernel, frames, rows, cols, rounds),
            "last",
            [shape((block, chans), BF16)],
            [pltpu.VMEM((block, chans), BF16), pltpu.VMEM((block, chans), BF16), pltpu.SemaphoreType.DMA],
            [out, totals, taps, gate, value_weight, out_weight] + ends + wholes + sides,
            far=1,
            far_outs=1,
            aliases={0: 0},
        )
    return out.reshape(latents.shape)


def solution(mesh):
    in_specs = (P("tm", "height", "width", None), P(), P(), P(), P(), P(), P())
    out_specs = P("tm", "height", "width", None)
    return jax.shard_map(body, mesh=mesh, in_specs=in_specs, out_specs=out_specs, check_vma=False)
```

```python
import functools

import jax
import jax.numpy as jnp
from jax import lax
from jax.experimental import pallas as pl
from jax.experimental.pallas import tpu as pltpu
from jax.sharding import PartitionSpec as P

LANES = 128
LATER = 8 * 10**9
F32, BF16 = jnp.float32, jnp.bfloat16
VMEM = pl.BlockSpec(memory_space=pltpu.VMEM)
HBM = pl.BlockSpec(memory_space=pltpu.HBM)


def call(kernel, name, outs, scratch, operands, flops=0, exps=0, far=0, aliases={}):
    operands = [pltpu.with_memory_space_constraint(a, pltpu.HBM) for a in operands[:far]] + list(operands[far:])
    moved = sum(a.size * a.dtype.itemsize for a in operands) + sum(a.size * a.dtype.itemsize for a in outs)
    return pl.pallas_call(
        kernel,
        out_shape=tuple(outs),
        in_specs=[HBM] * far + [VMEM] * (len(operands) - far),
        out_specs=(VMEM,) * len(outs),
        scratch_shapes=scratch,
        input_output_aliases=aliases,
        compiler_params=pltpu.CompilerParams(vmem_limit_bytes=24 * 1024 * 1024),
        cost_estimate=pl.CostEstimate(flops=flops, bytes_accessed=moved, transcendentals=exps),
        name=name,
    )(*operands)


def swaps(axis):
    n = lax.axis_size(axis)
    rounds = []
    for first in range(2 if n > 2 else 1):
        to = list(range(n))
        for i in range(first, n - 1, 2):
            to[i], to[i + 1] = i + 1, i
        rounds.append(list(enumerate(to)))
    return rounds


def position(axis):
    i, n = lax.axis_index(axis), lax.axis_size(axis)
    return lax.rem(i, 2) == 1, i > 0, i < n - 1


def second():
    return lax.rem(lax.axis_index("tm"), 2) == 1


def on_right():
    return lax.rem(lax.axis_index("tm") + lax.axis_index("width"), 2) == 0


def facing(core, column, columns):
    to = column + (1 if (core + column) % 2 == 0 else -1)
    return to if 0 <= to < columns else column


def outer_column(ref, lines, cols):
    return jnp.where(on_right(), ref[pl.ds(cols - 1, lines, stride=cols), :], ref[pl.ds(0, lines, stride=cols), :])


def gate_kernel(x_ref, w_ref, gate_ref):
    v = jnp.dot(x_ref[...], w_ref[...], preferred_element_type=F32)
    gate_ref[...] = v / (1.0 + jnp.exp(-v))


def early_kernel(frames, rows, cols, count, *refs):
    far, kept, rest = refs[:count], refs[count : 2 * count - 2], refs[2 * count - 2 :]
    table_ref, side_ref, *fields, taps_ref, skip_ref, arrived, held = rest
    near = (taps_ref, skip_ref) + kept
    x_ref = near[2]
    copies = [pltpu.make_async_copy(a, b, arrived.at[i]) for i, (a, b) in enumerate(zip(far, near))]
    for copy in copies:
        copy.start()
    lags, chans = taps_ref.shape
    copies[0].wait()
    copies[1].wait()
    pad = 2 * frames
    taps = taps_ref[...].astype(F32)
    table_ref[0:pad] = jnp.zeros((pad, cols, chans), F32)
    for lag in range(lags):
        tap = taps[lag : lag + 1] + (skip_ref[...] if lag == 0 else 0.0)
        table_ref[pad + lag] = jnp.broadcast_to(tap, (cols, chans))
    sites = rows * cols
    copies[2].wait()
    for lane in range(0, chans, LANES):
        span = slice(lane, lane + LANES)
        held[...] = x_ref[:, span].astype(F32)
        side_ref[:, span] = outer_column(held, frames * rows, cols)
        for d, field in enumerate(fields):
            totals = [None] * frames
            for s in range(frames):
                x = x_ref[s * sites : (s + 1) * sites, span].astype(F32).reshape(rows, cols, LANES)
                for t in range(s if d == 0 else 0, frames):
                    term = table_ref[pad + 2 * d * frames + t - s, :, span] * x
                    totals[t] = term if totals[t] is None else totals[t] + term
            for t in range(frames):
                field[t * sites : (t + 1) * sites, span] = totals[t].reshape(sites, LANES)
    for copy in copies[3:]:
        copy.wait()


def reordered(lines, rounds_h, back=False):
    if rounds_h > 1:
        return lines[:1] + lines[2:] + lines[1:2] if back else lines[:1] + lines[-1:] + lines[1:-1]
    odd = position("height")[0]
    return [jnp.where(odd, a, b) for a, b in zip(lines, lines[::-1])]


def column_kernel(frames, rows, cols, partner_ref, side_ref, out_ref, held):
    lines = frames * rows
    for lane in range(0, out_ref.shape[1], LANES):
        span = slice(lane, lane + LANES)
        held[...] = partner_ref[:, span].astype(F32)
        out_ref[:, span] = jnp.concatenate([side_ref[:, span], outer_column(held, lines, cols)]).astype(BF16)


def shift(frames):
    return jnp.where(second(), frames, -frames)


def with_partner(frames, rows, cols, d, field_ref, partner_ref, table_ref, span):
    sites = rows * cols
    base = 2 * frames + 2 * d * frames + shift(frames)
    totals = [field_ref[t * sites : (t + 1) * sites, span].reshape(rows, cols, LANES) for t in range(frames)]
    for s in range(frames):
        x = partner_ref[s * sites : (s + 1) * sites, span].astype(F32).reshape(rows, cols, LANES)
        for t in range(frames):
            totals[t] = totals[t] + table_ref[base + t - s, :, span] * x
    return totals


def later_kernel(frames, rows, cols, rounds_h, partner_ref, table_ref, *refs):
    fields, outs = refs[: len(refs) // 3], refs[len(refs) // 3 :]
    for d, field in enumerate(fields, 1):
        for lane in range(0, field.shape[1], LANES):
            span = slice(lane, lane + LANES)
            totals = with_partner(frames, rows, cols, d, field, partner_ref, table_ref, span)
            tiles = reordered([jnp.concatenate([t[r] for t in totals]) for r in range(rows)], rounds_h)
            outs[2 * d - 2][:, span] = jnp.concatenate(tiles[:rounds_h]).astype(BF16)
            outs[2 * d - 1][:, span] = jnp.concatenate(tiles[rounds_h:]).astype(BF16)


def own_kernel(frames, rows, cols, partner_ref, table_ref, field_ref, mine_ref):
    for lane in range(0, mine_ref.shape[1], LANES):
        span = slice(lane, lane + LANES)
        totals = with_partner(frames, rows, cols, 0, field_ref, partner_ref, table_ref, span)
        mine_ref[:, span] = jnp.concatenate(totals).reshape(mine_ref.shape[0], LANES)


def later(d, value):
    return jnp.where(lax.div(lax.axis_index("tm"), 2) >= d, value, jnp.zeros_like(value))


def side_kernel(frames, rows, table_ref, *refs):
    *arrived, own_ref, other_ref = refs
    _, lower, upper = position("width")
    exists = jnp.where(on_right(), upper, lower)
    for lane in range(0, own_ref.shape[1], LANES):
        span = slice(lane, lane + LANES)
        totals = [jnp.zeros((rows, LANES), F32)] * (2 * frames)
        for d, ref in enumerate(arrived):
            column = later(d, ref[:, span].astype(F32))
            base = 2 * frames + 2 * d * frames
            for t in range(2 * frames):
                for s in range(2 * frames):
                    lag = t % frames - s % frames
                    if t // frames == s // frames:
                        if d == 0 and lag < 0:
                            continue
                    else:
                        lag = lag + (shift(frames) if t < frames else -shift(frames))
                    totals[t] = totals[t] + table_ref[base + lag, :, span] * column[s * rows : (s + 1) * rows]
        totals = [jnp.where(exists, total, jnp.zeros_like(total)) for total in totals]
        own_ref[:, span] = jnp.concatenate(totals[:frames])
        other_ref[:, span] = jnp.concatenate(totals[frames:]).astype(BF16)


def border_kernel(frames, rows, cols, chips, mine_ref, own_ref, other_ref, *refs):
    arrived, (low_ref, high_ref, *outs) = refs[: chips - 1], refs[chips - 1 :]
    sites = rows * cols
    odd, _, _ = position("height")
    right, own, other = on_right(), own_ref[...], other_ref[...].astype(F32)
    low, high = jnp.where(right, other, own), jnp.where(right, own, other)
    low_ref[...] = low
    high_ref[...] = high
    size = frames * cols
    lines, corners = [], []
    for r in (0, rows - 1):
        lines.append(jnp.concatenate([mine_ref[t * sites + r * cols : t * sites + (r + 1) * cols] for t in range(frames)]))
        ends = [side[t * rows + r : t * rows + r + 1] for side in (low, high) for t in range(frames)]
        corners.append(jnp.concatenate(ends))
    for k, out in enumerate(outs):
        line = jnp.where(odd, *(lines[::-1] if k else lines))
        for d, ref in enumerate(arrived, 1):
            if len(outs) > 1:
                ends = [ref[i * size : (i + 1) * size].astype(F32) for i in range(2)]
                more = jnp.where(odd, *(ends[::-1] if k else ends))
            else:
                more = ref[:size].astype(F32)
            line = line + later(d, more)
        out[...] = jnp.concatenate([line, jnp.where(odd, *(corners[::-1] if k else corners))]).astype(BF16)


def shifted(line, left, right):
    cols = line.shape[0]
    place = lax.broadcasted_iota(jnp.int32, line.shape, 0)
    before = jnp.where(place == 0, left, pltpu.roll(line, 1, 0))
    after = jnp.where(place == cols - 1, right, pltpu.roll(line, cols - 1, 0))
    return before, line, after


def projected(mixed, gate, wv_ref, wo_ref):
    value = jnp.dot(mixed, wv_ref[...], preferred_element_type=F32)
    hidden = (value * gate).astype(BF16)
    return jnp.dot(hidden, wo_ref[...], preferred_element_type=F32).astype(BF16)


def filtered(lines, lefts, rights, taps):
    totals = [None] * len(lines)
    for r, line in enumerate(lines):
        near = shifted(line, lefts[r], rights[r])
        for a in range(3):
            to = r + 1 - a
            if 0 <= to < len(lines):
                term = near[0] * taps[a][0] + near[1] * taps[a][1] + near[2] * taps[a][2]
                totals[to] = term if totals[to] is None else totals[to] + term
    return totals


def taps_of(taps_ref, span):
    return [[taps_ref[a, b : b + 1, span] for b in range(3)] for a in range(3)]


def inner_kernel(
    frames, rows, cols, mine_ref, low_ref, high_ref, taps_ref, gate_ref, wv_ref, wo_ref, out_ref, totals_ref, mixed
):
    sites = rows * cols
    for lane in range(0, mine_ref.shape[1], LANES):
        span = slice(lane, lane + LANES)
        taps = taps_of(taps_ref, span)
        low, high = low_ref[:, span], high_ref[:, span]
        for t in range(frames):
            at = t * sites
            lines = [mine_ref[at + r * cols : at + (r + 1) * cols, span] for r in range(rows)]
            lefts = [low[t * rows + r : t * rows + r + 1] for r in range(rows)]
            rights = [high[t * rows + r : t * rows + r + 1] for r in range(rows)]
            total = jnp.concatenate(filtered(lines, lefts, rights, taps))
            totals_ref[at : at + sites, span] = total
            mixed[at : at + sites, span] = total.astype(BF16)
    out_ref[...] = projected(mixed[...], gate_ref[...], wv_ref, wo_ref)


def block_kernel(frames, rows, cols, rounds_h, inner_ref, totals_ref, taps_ref, gate_ref, wv_ref, wo_ref, *refs):
    *parts, out_ref, sums_ref, mixed = refs
    firsts, rests = parts[: len(parts) // 2], parts[len(parts) // 2 :]
    sites = rows * cols
    size = frames * cols

    @pl.when(lax.div(lax.axis_index("tm"), 2) > 0)
    def _():
        for lane in range(0, out_ref.shape[1], LANES):
            span = slice(lane, lane + LANES)
            taps = taps_of(taps_ref, span)
            lines = [jnp.zeros((size, LANES), F32)] * rows
            for d, (first, rest) in enumerate(zip(firsts, rests), 1):
                more = [first[i * size : (i + 1) * size, span].astype(F32) for i in range(rounds_h)]
                more += [rest[i * size : (i + 1) * size, span].astype(F32) for i in range(rows - rounds_h)]
                more = reordered(more, rounds_h, back=True)
                lines = [line + later(d, other) for line, other in zip(lines, more)]
            zero = [jnp.zeros((1, LANES), F32)] * rows
            for t in range(frames):
                at = t * sites
                total = filtered([line[t * cols : (t + 1) * cols] for line in lines], zero, zero, taps)
                total = jnp.concatenate(total) + totals_ref[at : at + sites, span]
                sums_ref[at : at + sites, span] = total
                mixed[at : at + sites, span] = total.astype(BF16)
        out_ref[...] = projected(mixed[...], gate_ref[...], wv_ref, wo_ref)


def last_kernel(frames, rows, cols, inner_ref, totals_ref, taps_ref, gate_ref, wv_ref, wo_ref, *refs):
    *ends, out_ref = refs
    sites = rows * cols
    size = frames * cols
    odd, lower, upper = position("height")
    out_ref[...] = inner_ref[...]
    mixed, gate = [], []
    for k, end in enumerate(ends):
        end = end[...].astype(F32)
        first = jnp.logical_not(odd) if k else odd
        lefts, rights = end[size : size + frames], end[size + frames : size + 2 * frames]
        exists = jnp.where(first, lower, upper)
        tap = jnp.where(first, taps_ref[0], taps_ref[2])
        for t in range(frames):
            near = shifted(end[t * cols : (t + 1) * cols], lefts[t : t + 1], rights[t : t + 1])
            more = near[0] * tap[0:1] + near[1] * tap[1:2] + near[2] * tap[2:3]
            i, j = t * sites, (t + 1) * sites - cols
            total = jnp.where(first, totals_ref[i : i + cols], totals_ref[j : j + cols])
            mixed.append(total + jnp.where(exists, more, jnp.zeros_like(more)))
            gate.append(jnp.where(first, gate_ref[i : i + cols], gate_ref[j : j + cols]))
    out = projected(jnp.concatenate(mixed).astype(BF16), jnp.concatenate(gate), wv_ref, wo_ref)
    for t in range(frames):
        new = [out[k * size + t * cols : k * size + (t + 1) * cols] for k in range(len(ends))]
        for at, is_last in ((t * sites, False), ((t + 1) * sites - cols, True)):
            kept = new[1] if len(new) > 1 else inner_ref[at : at + cols]
            out_ref[at : at + cols] = jnp.where(odd, kept, new[0]) if is_last else jnp.where(odd, new[0], kept)


def body(latents, spatial_taps, kernel_taps, skip_gain, gate_weight, value_weight, out_weight):
    frames, rows, cols, chans = latents.shape
    lags = kernel_taps.shape[0]
    n_t, n_h, n_w = lax.axis_size("tm"), lax.axis_size("height"), lax.axis_size("width")
    chips = n_t // 2
    block = frames * rows * cols
    shape = jax.ShapeDtypeStruct
    x = latents.reshape(block, chans)

    partner = lax.ppermute(x, "tm", [(i, i ^ 1) for i in range(n_t)])
    lines = frames * rows
    field = shape((block, chans), F32)
    inputs = [kernel_taps, skip_gain.reshape(1, chans), x, gate_weight, spatial_taps, value_weight, out_weight]
    near_x, near_gate, taps, value_weight, out_weight, table, side, *fields = call(
        functools.partial(early_kernel, frames, rows, cols, len(inputs)),
        "early",
        [shape(a.shape, a.dtype) for a in inputs[2:]]
        + [shape((lags + 2 * frames, cols, chans), F32), shape((lines, chans), F32)]
        + [field] * chips,
        [pltpu.VMEM(a.shape, a.dtype) for a in inputs[:2]]
        + [pltpu.SemaphoreType.DMA((len(inputs),)), pltpu.VMEM((block, LANES), F32)],
        inputs,
        far=len(inputs),
    )
    (gate,) = call(gate_kernel, "gate", [field], [], [near_x, near_gate])

    h_rounds = swaps("height")
    (column,) = call(
        functools.partial(column_kernel, frames, rows, cols),
        "column",
        [shape((2 * lines, chans), BF16)],
        [pltpu.VMEM((block, LANES), F32)],
        [partner, side],
    )
    parts = [shape((n * frames * cols, chans), BF16) for n in (len(h_rounds), rows - len(h_rounds))]
    sent = call(
        functools.partial(later_kernel, frames, rows, cols, len(h_rounds)),
        "later",
        parts * (chips - 1),
        [],
        [partner, table] + fields[1:],
        2 * (chips - 1) * frames * x.size,
    )
    (mine,) = call(
        functools.partial(own_kernel, frames, rows, cols),
        "own",
        [field],
        [],
        [partner, table, fields[0]],
        2 * frames * x.size,
    )
    columns, firsts, rests = [], [], []
    for d in range(chips):
        route = []
        for i in range(n_t):
            for h in range(n_h):
                for j in range(n_w):
                    to, beside = facing(i % 2, j, n_w), h
                    if i // 2 + d >= chips:
                        to = j
                    elif to == j and n_h % 2 == 0:
                        beside = h ^ 1
                    source = (i * n_h + h) * n_w + j
                    route.append((source, ((i + 2 * d) % n_t * n_h + beside) * n_w + to))
        columns.append(lax.ppermute(column, ("tm", "height", "width"), route))
    for d in range(1, chips):
        route = [(i, (i + 2 * d) % n_t) for i in range(n_t)]
        firsts.append(lax.ppermute(sent[2 * d - 2], "tm", route))
        rests.append(lax.ppermute(sent[2 * d - 1], "tm", route))

    own, other = call(
        functools.partial(side_kernel, frames, rows),
        "side",
        [shape((lines, chans), F32), shape((lines, chans), BF16)],
        [],
        [table] + columns,
        LATER,
    )
    other = lax.ppermute(other, "tm", [(i, i ^ 1) for i in range(n_t)])
    size = frames * cols + 2 * frames
    low, high, *ends = call(
        functools.partial(border_kernel, frames, rows, cols, chips),
        "border",
        [shape((lines, chans), F32)] * 2 + [shape((size, chans), BF16)] * len(h_rounds),
        [],
        [mine, own, other] + firsts,
    )
    ends = [lax.ppermute(e, "height", pairs) for e, pairs in zip(ends, h_rounds)]

    inner, totals = call(
        functools.partial(inner_kernel, frames, rows, cols),
        "inner",
        [shape((block, chans), BF16), field],
        [pltpu.VMEM((block, chans), BF16)],
        [mine, low, high, taps, gate, value_weight, out_weight],
        4 * block * chans * chans,
    )
    if chips > 1:
        inner, totals = call(
            functools.partial(block_kernel, frames, rows, cols, len(h_rounds)),
            "block",
            [shape((block, chans), BF16), field],
            [pltpu.VMEM((block, chans), BF16)],
            [inner, totals, taps, gate, value_weight, out_weight] + firsts + rests,
            aliases={0: 0, 1: 1},
        )
    (out,) = call(
        functools.partial(last_kernel, frames, rows, cols),
        "last",
        [shape((block, chans), BF16)],
        [],
        [inner, totals, taps, gate, value_weight, out_weight] + ends,
    )
    return out.reshape(latents.shape)


def solution(mesh):
    in_specs = (P("tm", "height", "width", None), P(), P(), P(), P(), P(), P())
    out_specs = P("tm", "height", "width", None)
    return jax.shard_map(body, mesh=mesh, in_specs=in_specs, out_specs=out_specs, check_vma=False)
```

```python
import functools

import jax
import jax.numpy as jnp
from jax import lax
from jax.experimental import pallas as pl
from jax.experimental.pallas import tpu as pltpu
from jax.sharding import PartitionSpec as P

LANES = 128
LATER = 8 * 10**9
F32, BF16 = jnp.float32, jnp.bfloat16
VMEM = pl.BlockSpec(memory_space=pltpu.VMEM)
HBM = pl.BlockSpec(memory_space=pltpu.HBM)


def call(kernel, name, outs, scratch, operands, flops=0, exps=0, far=0, aliases={}):
    operands = [pltpu.with_memory_space_constraint(a, pltpu.HBM) for a in operands[:far]] + list(operands[far:])
    moved = sum(a.size * a.dtype.itemsize for a in operands) + sum(a.size * a.dtype.itemsize for a in outs)
    return pl.pallas_call(
        kernel,
        out_shape=tuple(outs),
        in_specs=[HBM] * far + [VMEM] * (len(operands) - far),
        out_specs=(VMEM,) * len(outs),
        scratch_shapes=scratch,
        input_output_aliases=aliases,
        compiler_params=pltpu.CompilerParams(vmem_limit_bytes=24 * 1024 * 1024),
        cost_estimate=pl.CostEstimate(flops=flops, bytes_accessed=moved, transcendentals=exps),
        name=name,
    )(*operands)


def swaps(axis):
    n = lax.axis_size(axis)
    rounds = []
    for first in range(2 if n > 2 else 1):
        to = list(range(n))
        for i in range(first, n - 1, 2):
            to[i], to[i + 1] = i + 1, i
        rounds.append(list(enumerate(to)))
    return rounds


def position(axis):
    i, n = lax.axis_index(axis), lax.axis_size(axis)
    return lax.rem(i, 2) == 1, i > 0, i < n - 1


def second():
    return lax.rem(lax.axis_index("tm"), 2) == 1


def on_right():
    return lax.rem(lax.axis_index("tm") + lax.axis_index("width"), 2) == 0


def facing(core, column, columns):
    to = column + (1 if (core + column) % 2 == 0 else -1)
    return to if 0 <= to < columns else column


def outer_column(ref, lines, cols):
    return jnp.where(on_right(), ref[pl.ds(cols - 1, lines, stride=cols), :], ref[pl.ds(0, lines, stride=cols), :])


def gate_kernel(x_ref, w_ref, gate_ref):
    v = jnp.dot(x_ref[...], w_ref[...], preferred_element_type=F32)
    gate_ref[...] = v / (1.0 + jnp.exp(-v))


def early_kernel(frames, rows, cols, count, *refs):
    far, kept, rest = refs[:count], refs[count : 2 * count - 2], refs[2 * count - 2 :]
    table_ref, side_ref, *fields, taps_ref, skip_ref, arrived, held = rest
    near = (taps_ref, skip_ref) + kept
    x_ref = near[2]
    copies = [pltpu.make_async_copy(a, b, arrived.at[i]) for i, (a, b) in enumerate(zip(far, near))]
    for copy in copies:
        copy.start()
    lags, chans = taps_ref.shape
    copies[0].wait()
    copies[1].wait()
    pad = 2 * frames
    taps = taps_ref[...].astype(F32)
    table_ref[0:pad] = jnp.zeros((pad, cols, chans), F32)
    for lag in range(lags):
        tap = taps[lag : lag + 1] + (skip_ref[...] if lag == 0 else 0.0)
        table_ref[pad + lag] = jnp.broadcast_to(tap, (cols, chans))
    sites = rows * cols
    copies[2].wait()
    for lane in range(0, chans, LANES):
        span = slice(lane, lane + LANES)
        held[...] = x_ref[:, span].astype(F32)
        side_ref[:, span] = outer_column(held, frames * rows, cols)
        for d, field in enumerate(fields):
            totals = [None] * frames
            for s in range(frames):
                x = x_ref[s * sites : (s + 1) * sites, span].astype(F32).reshape(rows, cols, LANES)
                for t in range(s if d == 0 else 0, frames):
                    term = table_ref[pad + 2 * d * frames + t - s, :, span] * x
                    totals[t] = term if totals[t] is None else totals[t] + term
            for t in range(frames):
                field[t * sites : (t + 1) * sites, span] = totals[t].reshape(sites, LANES)
    for copy in copies[3:]:
        copy.wait()


def reordered(lines, rounds_h, back=False):
    if rounds_h > 1:
        return lines[:1] + lines[2:] + lines[1:2] if back else lines[:1] + lines[-1:] + lines[1:-1]
    odd = position("height")[0]
    return [jnp.where(odd, a, b) for a, b in zip(lines, lines[::-1])]


def column_kernel(frames, rows, cols, partner_ref, side_ref, out_ref, held):
    lines = frames * rows
    for lane in range(0, out_ref.shape[1], LANES):
        span = slice(lane, lane + LANES)
        held[...] = partner_ref[:, span].astype(F32)
        out_ref[:, span] = jnp.concatenate([side_ref[:, span], outer_column(held, lines, cols)]).astype(BF16)


def shift(frames):
    return jnp.where(second(), frames, -frames)


def with_partner(frames, rows, cols, d, field_ref, partner_ref, table_ref, span):
    sites = rows * cols
    base = 2 * frames + 2 * d * frames + shift(frames)
    totals = [field_ref[t * sites : (t + 1) * sites, span].reshape(rows, cols, LANES) for t in range(frames)]
    for s in range(frames):
        x = partner_ref[s * sites : (s + 1) * sites, span].astype(F32).reshape(rows, cols, LANES)
        for t in range(frames):
            totals[t] = totals[t] + table_ref[base + t - s, :, span] * x
    return totals


def later_kernel(frames, rows, cols, rounds_h, partner_ref, table_ref, *refs):
    fields, outs = refs[: len(refs) // 3], refs[len(refs) // 3 :]
    for d, field in enumerate(fields, 1):
        for lane in range(0, field.shape[1], LANES):
            span = slice(lane, lane + LANES)
            totals = with_partner(frames, rows, cols, d, field, partner_ref, table_ref, span)
            tiles = reordered([jnp.concatenate([t[r] for t in totals]) for r in range(rows)], rounds_h)
            outs[2 * d - 2][:, span] = jnp.concatenate(tiles[:rounds_h]).astype(BF16)
            outs[2 * d - 1][:, span] = jnp.concatenate(tiles[rounds_h:]).astype(BF16)


def own_kernel(frames, rows, cols, partner_ref, table_ref, field_ref, mine_ref):
    for lane in range(0, mine_ref.shape[1], LANES):
        span = slice(lane, lane + LANES)
        totals = with_partner(frames, rows, cols, 0, field_ref, partner_ref, table_ref, span)
        mine_ref[:, span] = jnp.concatenate(totals).reshape(mine_ref.shape[0], LANES)


def later(d, value):
    return jnp.where(lax.div(lax.axis_index("tm"), 2) >= d, value, jnp.zeros_like(value))


def add_column(frames, rows, d, totals, column, table_ref, span):
    base = 2 * frames + 2 * d * frames
    for t in range(2 * frames):
        for s in range(2 * frames):
            lag = t % frames - s % frames
            if t // frames == s // frames:
                if d == 0 and lag < 0:
                    continue
            else:
                lag = lag + (shift(frames) if t < frames else -shift(frames))
            totals[t] = totals[t] + table_ref[base + lag, :, span] * column[s * rows : (s + 1) * rows]
    return totals


def width_kernel(frames, rows, table_ref, arrived_ref, sums_ref):
    for lane in range(0, sums_ref.shape[1], LANES):
        span = slice(lane, lane + LANES)
        totals = [jnp.zeros((rows, LANES), F32)] * (2 * frames)
        totals = add_column(frames, rows, 0, totals, arrived_ref[:, span].astype(F32), table_ref, span)
        sums_ref[:, span] = jnp.concatenate(totals)


def side_kernel(frames, rows, table_ref, sums_ref, *refs):
    *arrived, own_ref, other_ref = refs
    _, lower, upper = position("width")
    exists = jnp.where(on_right(), upper, lower)
    for lane in range(0, own_ref.shape[1], LANES):
        span = slice(lane, lane + LANES)
        totals = [sums_ref[t * rows : (t + 1) * rows, span] for t in range(2 * frames)]
        for d, ref in enumerate(arrived, 1):
            totals = add_column(frames, rows, d, totals, later(d, ref[:, span].astype(F32)), table_ref, span)
        totals = [jnp.where(exists, total, jnp.zeros_like(total)) for total in totals]
        own_ref[:, span] = jnp.concatenate(totals[:frames])
        other_ref[:, span] = jnp.concatenate(totals[frames:]).astype(BF16)


def border_kernel(frames, rows, cols, chips, mine_ref, own_ref, other_ref, *refs):
    arrived, (low_ref, high_ref, *outs) = refs[: chips - 1], refs[chips - 1 :]
    sites = rows * cols
    odd, _, _ = position("height")
    right, own, other = on_right(), own_ref[...], other_ref[...].astype(F32)
    low, high = jnp.where(right, other, own), jnp.where(right, own, other)
    low_ref[...] = low
    high_ref[...] = high
    size = frames * cols
    lines, corners = [], []
    for r in (0, rows - 1):
        lines.append(jnp.concatenate([mine_ref[t * sites + r * cols : t * sites + (r + 1) * cols] for t in range(frames)]))
        ends = [side[t * rows + r : t * rows + r + 1] for side in (low, high) for t in range(frames)]
        corners.append(jnp.concatenate(ends))
    for k, out in enumerate(outs):
        line = jnp.where(odd, *(lines[::-1] if k else lines))
        for d, ref in enumerate(arrived, 1):
            if len(outs) > 1:
                ends = [ref[i * size : (i + 1) * size].astype(F32) for i in range(2)]
                more = jnp.where(odd, *(ends[::-1] if k else ends))
            else:
                more = ref[:size].astype(F32)
            line = line + later(d, more)
        out[...] = jnp.concatenate([line, jnp.where(odd, *(corners[::-1] if k else corners))]).astype(BF16)


def shifted(line, left, right):
    cols = line.shape[0]
    place = lax.broadcasted_iota(jnp.int32, line.shape, 0)
    before = jnp.where(place == 0, left, pltpu.roll(line, 1, 0))
    after = jnp.where(place == cols - 1, right, pltpu.roll(line, cols - 1, 0))
    return before, line, after


def projected(mixed, gate, wv_ref, wo_ref):
    value = jnp.dot(mixed, wv_ref[...], preferred_element_type=F32)
    hidden = (value * gate).astype(BF16)
    return jnp.dot(hidden, wo_ref[...], preferred_element_type=F32).astype(BF16)


def filtered(lines, lefts, rights, taps):
    totals = [None] * len(lines)
    for r, line in enumerate(lines):
        near = shifted(line, lefts[r], rights[r])
        for a in range(3):
            to = r + 1 - a
            if 0 <= to < len(lines):
                term = near[0] * taps[a][0] + near[1] * taps[a][1] + near[2] * taps[a][2]
                totals[to] = term if totals[to] is None else totals[to] + term
    return totals


def taps_of(taps_ref, span):
    return [[taps_ref[a, b : b + 1, span] for b in range(3)] for a in range(3)]


def inner_kernel(
    frames, rows, cols, mine_ref, low_ref, high_ref, taps_ref, gate_ref, wv_ref, wo_ref, out_ref, totals_ref, mixed
):
    sites = rows * cols
    for lane in range(0, mine_ref.shape[1], LANES):
        span = slice(lane, lane + LANES)
        taps = taps_of(taps_ref, span)
        low, high = low_ref[:, span], high_ref[:, span]
        for t in range(frames):
            at = t * sites
            lines = [mine_ref[at + r * cols : at + (r + 1) * cols, span] for r in range(rows)]
            lefts = [low[t * rows + r : t * rows + r + 1] for r in range(rows)]
            rights = [high[t * rows + r : t * rows + r + 1] for r in range(rows)]
            total = jnp.concatenate(filtered(lines, lefts, rights, taps))
            totals_ref[at : at + sites, span] = total
            mixed[at : at + sites, span] = total.astype(BF16)
    out_ref[...] = projected(mixed[...], gate_ref[...], wv_ref, wo_ref)


def block_kernel(frames, rows, cols, rounds_h, inner_ref, totals_ref, taps_ref, gate_ref, wv_ref, wo_ref, *refs):
    *parts, out_ref, sums_ref, mixed = refs
    firsts, rests = parts[: len(parts) // 2], parts[len(parts) // 2 :]
    sites = rows * cols
    size = frames * cols

    @pl.when(lax.div(lax.axis_index("tm"), 2) > 0)
    def _():
        for lane in range(0, out_ref.shape[1], LANES):
            span = slice(lane, lane + LANES)
            taps = taps_of(taps_ref, span)
            lines = [jnp.zeros((size, LANES), F32)] * rows
            for d, (first, rest) in enumerate(zip(firsts, rests), 1):
                more = [first[i * size : (i + 1) * size, span].astype(F32) for i in range(rounds_h)]
                more += [rest[i * size : (i + 1) * size, span].astype(F32) for i in range(rows - rounds_h)]
                more = reordered(more, rounds_h, back=True)
                lines = [line + later(d, other) for line, other in zip(lines, more)]
            zero = [jnp.zeros((1, LANES), F32)] * rows
            for t in range(frames):
                at = t * sites
                total = filtered([line[t * cols : (t + 1) * cols] for line in lines], zero, zero, taps)
                total = jnp.concatenate(total) + totals_ref[at : at + sites, span]
                sums_ref[at : at + sites, span] = total
                mixed[at : at + sites, span] = total.astype(BF16)
        out_ref[...] = projected(mixed[...], gate_ref[...], wv_ref, wo_ref)


def last_kernel(frames, rows, cols, inner_ref, totals_ref, taps_ref, gate_ref, wv_ref, wo_ref, *refs):
    *ends, out_ref = refs
    sites = rows * cols
    size = frames * cols
    odd, lower, upper = position("height")
    out_ref[...] = inner_ref[...]
    mixed, gate = [], []
    for k, end in enumerate(ends):
        end = end[...].astype(F32)
        first = jnp.logical_not(odd) if k else odd
        lefts, rights = end[size : size + frames], end[size + frames : size + 2 * frames]
        exists = jnp.where(first, lower, upper)
        tap = jnp.where(first, taps_ref[0], taps_ref[2])
        for t in range(frames):
            near = shifted(end[t * cols : (t + 1) * cols], lefts[t : t + 1], rights[t : t + 1])
            more = near[0] * tap[0:1] + near[1] * tap[1:2] + near[2] * tap[2:3]
            i, j = t * sites, (t + 1) * sites - cols
            total = jnp.where(first, totals_ref[i : i + cols], totals_ref[j : j + cols])
            mixed.append(total + jnp.where(exists, more, jnp.zeros_like(more)))
            gate.append(jnp.where(first, gate_ref[i : i + cols], gate_ref[j : j + cols]))
    out = projected(jnp.concatenate(mixed).astype(BF16), jnp.concatenate(gate), wv_ref, wo_ref)
    for t in range(frames):
        new = [out[k * size + t * cols : k * size + (t + 1) * cols].astype(F32) for k in range(len(ends))]
        first, final = t * sites, (t + 1) * sites - 2 * cols
        top = inner_ref[first : first + 2 * cols].astype(F32)
        bottom = inner_ref[final : final + 2 * cols].astype(F32)
        other = new[1] if len(new) > 1 else None
        row = jnp.where(odd, new[0], top[:cols] if other is None else other)
        out_ref[first : first + 2 * cols] = jnp.concatenate([row, top[cols:]]).astype(BF16)
        row = jnp.where(odd, bottom[cols:] if other is None else other, new[0])
        out_ref[final : final + 2 * cols] = jnp.concatenate([bottom[:cols], row]).astype(BF16)


def body(latents, spatial_taps, kernel_taps, skip_gain, gate_weight, value_weight, out_weight):
    frames, rows, cols, chans = latents.shape
    lags = kernel_taps.shape[0]
    n_t, n_h, n_w = lax.axis_size("tm"), lax.axis_size("height"), lax.axis_size("width")
    chips = n_t // 2
    block = frames * rows * cols
    shape = jax.ShapeDtypeStruct
    x = latents.reshape(block, chans)

    partner = lax.ppermute(x, "tm", [(i, i ^ 1) for i in range(n_t)])
    lines = frames * rows
    field = shape((block, chans), F32)
    inputs = [kernel_taps, skip_gain.reshape(1, chans), x, gate_weight, spatial_taps, value_weight, out_weight]
    near_x, near_gate, taps, value_weight, out_weight, table, side, *fields = call(
        functools.partial(early_kernel, frames, rows, cols, len(inputs)),
        "early",
        [shape(a.shape, a.dtype) for a in inputs[2:]]
        + [shape((lags + 2 * frames, cols, chans), F32), shape((lines, chans), F32)]
        + [field] * chips,
        [pltpu.VMEM(a.shape, a.dtype) for a in inputs[:2]]
        + [pltpu.SemaphoreType.DMA((len(inputs),)), pltpu.VMEM((block, LANES), F32)],
        inputs,
        far=len(inputs),
    )
    (gate,) = call(gate_kernel, "gate", [field], [], [near_x, near_gate])

    h_rounds = swaps("height")
    (column,) = call(
        functools.partial(column_kernel, frames, rows, cols),
        "column",
        [shape((2 * lines, chans), BF16)],
        [pltpu.VMEM((block, LANES), F32)],
        [partner, side],
    )
    parts = [shape((n * frames * cols, chans), BF16) for n in (len(h_rounds), rows - len(h_rounds))]
    sent = call(
        functools.partial(later_kernel, frames, rows, cols, len(h_rounds)),
        "later",
        parts * (chips - 1),
        [],
        [partner, table] + fields[1:],
        2 * (chips - 1) * frames * x.size,
    )
    (mine,) = call(
        functools.partial(own_kernel, frames, rows, cols),
        "own",
        [field],
        [],
        [partner, table, fields[0]],
        2 * frames * x.size,
    )
    columns, firsts, rests = [], [], []
    for d in range(chips):
        route = []
        for i in range(n_t):
            for h in range(n_h):
                for j in range(n_w):
                    to, beside = facing(i % 2, j, n_w), h
                    if i // 2 + d >= chips:
                        to = j
                    elif to == j and n_h % 2 == 0:
                        beside = h ^ 1
                    source = (i * n_h + h) * n_w + j
                    route.append((source, ((i + 2 * d) % n_t * n_h + beside) * n_w + to))
        columns.append(lax.ppermute(column, ("tm", "height", "width"), route))
    for d in range(1, chips):
        route = [(i, (i + 2 * d) % n_t) for i in range(n_t)]
        firsts.append(lax.ppermute(sent[2 * d - 2], "tm", route))
        rests.append(lax.ppermute(sent[2 * d - 1], "tm", route))

    (sums,) = call(
        functools.partial(width_kernel, frames, rows),
        "width",
        [shape((2 * lines, chans), F32)],
        [],
        [table, columns[0]],
    )
    own, other = call(
        functools.partial(side_kernel, frames, rows),
        "side",
        [shape((lines, chans), F32), shape((lines, chans), BF16)],
        [],
        [table, sums] + columns[1:],
        LATER,
    )
    other = lax.ppermute(other, "tm", [(i, i ^ 1) for i in range(n_t)])
    size = frames * cols + 2 * frames
    low, high, *ends = call(
        functools.partial(border_kernel, frames, rows, cols, chips),
        "border",
        [shape((lines, chans), F32)] * 2 + [shape((size, chans), BF16)] * len(h_rounds),
        [],
        [mine, own, other] + firsts,
    )
    ends = [lax.ppermute(e, "height", pairs) for e, pairs in zip(ends, h_rounds)]

    inner, totals = call(
        functools.partial(inner_kernel, frames, rows, cols),
        "inner",
        [shape((block, chans), BF16), field],
        [pltpu.VMEM((block, chans), BF16)],
        [mine, low, high, taps, gate, value_weight, out_weight],
        4 * block * chans * chans,
    )
    if chips > 1:
        inner, totals = call(
            functools.partial(block_kernel, frames, rows, cols, len(h_rounds)),
            "block",
            [shape((block, chans), BF16), field],
            [pltpu.VMEM((block, chans), BF16)],
            [inner, totals, taps, gate, value_weight, out_weight] + firsts + rests,
            aliases={0: 0, 1: 1},
        )
    (out,) = call(
        functools.partial(last_kernel, frames, rows, cols),
        "last",
        [shape((block, chans), BF16)],
        [],
        [inner, totals, taps, gate, value_weight, out_weight] + ends,
    )
    return out.reshape(latents.shape)


def solution(mesh):
    in_specs = (P("tm", "height", "width", None), P(), P(), P(), P(), P(), P())
    out_specs = P("tm", "height", "width", None)
    return jax.shard_map(body, mesh=mesh, in_specs=in_specs, out_specs=out_specs, check_vma=False)
```

```python
import functools

import jax
import jax.numpy as jnp
from jax import lax
from jax.experimental import pallas as pl
from jax.experimental.pallas import tpu as pltpu
from jax.sharding import PartitionSpec as P

LANES = 128
LATER = 8 * 10**9
F32, BF16 = jnp.float32, jnp.bfloat16
VMEM = pl.BlockSpec(memory_space=pltpu.VMEM)
HBM = pl.BlockSpec(memory_space=pltpu.HBM)


def call(kernel, name, outs, scratch, operands, flops=0, exps=0, far=0, far_outs=0, aliases={}):
    operands = [pltpu.with_memory_space_constraint(a, pltpu.HBM) for a in operands[:far]] + list(operands[far:])
    moved = sum(a.size * a.dtype.itemsize for a in operands) + sum(a.size * a.dtype.itemsize for a in outs)
    return pl.pallas_call(
        kernel,
        out_shape=tuple(outs),
        in_specs=[HBM] * far + [VMEM] * (len(operands) - far),
        out_specs=(HBM,) * far_outs + (VMEM,) * (len(outs) - far_outs),
        scratch_shapes=scratch,
        input_output_aliases=aliases,
        compiler_params=pltpu.CompilerParams(vmem_limit_bytes=24 * 1024 * 1024),
        cost_estimate=pl.CostEstimate(flops=flops, bytes_accessed=moved, transcendentals=exps),
        name=name,
    )(*operands)


def swaps(axis):
    n = lax.axis_size(axis)
    rounds = []
    for first in range(2 if n > 2 else 1):
        to = list(range(n))
        for i in range(first, n - 1, 2):
            to[i], to[i + 1] = i + 1, i
        rounds.append(list(enumerate(to)))
    return rounds


def position(axis):
    i, n = lax.axis_index(axis), lax.axis_size(axis)
    return lax.rem(i, 2) == 1, i > 0, i < n - 1


def second():
    return lax.rem(lax.axis_index("tm"), 2) == 1


def on_right():
    return lax.rem(lax.axis_index("tm") + lax.axis_index("width"), 2) == 0


def facing(core, column, columns):
    to = column + (1 if (core + column) % 2 == 0 else -1)
    return to if 0 <= to < columns else column


def outer_column(ref, lines, cols):
    return jnp.where(on_right(), ref[pl.ds(cols - 1, lines, stride=cols), :], ref[pl.ds(0, lines, stride=cols), :])


def gate_kernel(x_ref, w_ref, gate_ref):
    v = jnp.dot(x_ref[...], w_ref[...], preferred_element_type=F32)
    gate_ref[...] = v / (1.0 + jnp.exp(-v))


def early_kernel(frames, rows, cols, count, *refs):
    far, kept, rest = refs[:count], refs[count : 2 * count - 2], refs[2 * count - 2 :]
    table_ref, side_ref, *fields, taps_ref, skip_ref, arrived, held = rest
    near = (taps_ref, skip_ref) + kept
    x_ref = near[2]
    copies = [pltpu.make_async_copy(a, b, arrived.at[i]) for i, (a, b) in enumerate(zip(far, near))]
    for copy in copies:
        copy.start()
    lags, chans = taps_ref.shape
    copies[0].wait()
    copies[1].wait()
    pad = 2 * frames
    taps = taps_ref[...].astype(F32)
    table_ref[0:pad] = jnp.zeros((pad, cols, chans), F32)
    for lag in range(lags):
        tap = taps[lag : lag + 1] + (skip_ref[...] if lag == 0 else 0.0)
        table_ref[pad + lag] = jnp.broadcast_to(tap, (cols, chans))
    sites = rows * cols
    copies[2].wait()
    for lane in range(0, chans, LANES):
        span = slice(lane, lane + LANES)
        held[...] = x_ref[:, span].astype(F32)
        side_ref[:, span] = outer_column(held, frames * rows, cols)
        for d, field in enumerate(fields):
            totals = [None] * frames
            for s in range(frames):
                x = x_ref[s * sites : (s + 1) * sites, span].astype(F32).reshape(rows, cols, LANES)
                for t in range(s if d == 0 else 0, frames):
                    term = table_ref[pad + 2 * d * frames + t - s, :, span] * x
                    totals[t] = term if totals[t] is None else totals[t] + term
            for t in range(frames):
                field[t * sites : (t + 1) * sites, span] = totals[t].reshape(sites, LANES)
    for copy in copies[3:]:
        copy.wait()


def reordered(lines, rounds_h, back=False):
    if rounds_h > 1:
        return lines[:1] + lines[2:] + lines[1:2] if back else lines[:1] + lines[-1:] + lines[1:-1]
    odd = position("height")[0]
    return [jnp.where(odd, a, b) for a, b in zip(lines, lines[::-1])]


def column_kernel(frames, rows, cols, partner_ref, side_ref, out_ref, held):
    lines = frames * rows
    for lane in range(0, out_ref.shape[1], LANES):
        span = slice(lane, lane + LANES)
        held[...] = partner_ref[:, span].astype(F32)
        out_ref[:, span] = jnp.concatenate([side_ref[:, span], outer_column(held, lines, cols)]).astype(BF16)


def shift(frames):
    return jnp.where(second(), frames, -frames)


def with_partner(frames, rows, cols, d, field_ref, partner_ref, table_ref, span):
    sites = rows * cols
    base = 2 * frames + 2 * d * frames + shift(frames)
    totals = [field_ref[t * sites : (t + 1) * sites, span].reshape(rows, cols, LANES) for t in range(frames)]
    for s in range(frames):
        x = partner_ref[s * sites : (s + 1) * sites, span].astype(F32).reshape(rows, cols, LANES)
        for t in range(frames):
            totals[t] = totals[t] + table_ref[base + t - s, :, span] * x
    return totals


def later_kernel(frames, rows, cols, rounds_h, partner_ref, table_ref, *refs):
    fields, outs = refs[: len(refs) // 3], refs[len(refs) // 3 :]
    for d, field in enumerate(fields, 1):
        for lane in range(0, field.shape[1], LANES):
            span = slice(lane, lane + LANES)
            totals = with_partner(frames, rows, cols, d, field, partner_ref, table_ref, span)
            tiles = reordered([jnp.concatenate([t[r] for t in totals]) for r in range(rows)], rounds_h)
            outs[2 * d - 2][:, span] = jnp.concatenate(tiles[:rounds_h]).astype(BF16)
            outs[2 * d - 1][:, span] = jnp.concatenate(tiles[rounds_h:]).astype(BF16)


def own_kernel(frames, rows, cols, partner_ref, table_ref, field_ref, mine_ref):
    for lane in range(0, mine_ref.shape[1], LANES):
        span = slice(lane, lane + LANES)
        totals = with_partner(frames, rows, cols, 0, field_ref, partner_ref, table_ref, span)
        mine_ref[:, span] = jnp.concatenate(totals).reshape(mine_ref.shape[0], LANES)


def later(d, value):
    return jnp.where(lax.div(lax.axis_index("tm"), 2) >= d, value, jnp.zeros_like(value))


def add_column(frames, rows, d, totals, column, table_ref, span):
    base = 2 * frames + 2 * d * frames
    for t in range(2 * frames):
        for s in range(2 * frames):
            lag = t % frames - s % frames
            if t // frames == s // frames:
                if d == 0 and lag < 0:
                    continue
            else:
                lag = lag + (shift(frames) if t < frames else -shift(frames))
            totals[t] = totals[t] + table_ref[base + lag, :, span] * column[s * rows : (s + 1) * rows]
    return totals


def side_kernel(frames, rows, first, table_ref, *refs):
    *arrived, own_ref, other_ref = refs
    _, lower, upper = position("width")
    exists = jnp.where(on_right(), upper, lower)
    for lane in range(0, own_ref.shape[1], LANES):
        span = slice(lane, lane + LANES)
        totals = [jnp.zeros((rows, LANES), F32)] * (2 * frames)
        for d, ref in enumerate(arrived, first):
            totals = add_column(frames, rows, d, totals, later(d, ref[:, span].astype(F32)), table_ref, span)
        totals = [jnp.where(exists, total, jnp.zeros_like(total)) for total in totals]
        own_ref[:, span] = jnp.concatenate(totals[:frames])
        other_ref[:, span] = jnp.concatenate(totals[frames:]).astype(BF16)


def both_sides(own, other):
    right = on_right()
    return jnp.where(right, other, own), jnp.where(right, own, other)


def end_corners(frames, rows, own_ref, other_ref):
    sides = both_sides(own_ref[...], other_ref[...].astype(F32))
    pick = lambda r: [side[t * rows + r : t * rows + r + 1] for side in sides for t in range(frames)]
    return [jnp.concatenate(pick(r)) for r in (0, rows - 1)]


def border_kernel(frames, rows, cols, mine_ref, own_ref, other_ref, *outs):
    sites = rows * cols
    odd, _, _ = position("height")
    corners = end_corners(frames, rows, own_ref, other_ref)
    lines = []
    for r in (0, rows - 1):
        lines.append(jnp.concatenate([mine_ref[t * sites + r * cols : t * sites + (r + 1) * cols] for t in range(frames)]))
    ends = [jnp.concatenate(pair) for pair in zip(lines, corners)]
    for k, out in enumerate(outs):
        out[...] = jnp.where(odd, *(ends[::-1] if k else ends)).astype(BF16)


def before_kernel(frames, rows, cols, own_ref, other_ref, *refs):
    rounds_h = refs[0].shape[0] // (frames * cols)
    firsts, outs = refs[:-rounds_h], refs[-rounds_h:]
    size = frames * cols
    odd, _, _ = position("height")
    corners = end_corners(frames, rows, own_ref, other_ref)
    line = 0.0
    for d, ref in enumerate(firsts, 1):
        line = line + later(d, ref[...].astype(F32))
    for k, out in enumerate(outs):
        if rounds_h > 1:
            pair = line[:size], line[size:]
            row = jnp.where(odd, *(pair[::-1] if k else pair))
        else:
            row = line
        out[...] = jnp.concatenate([row, jnp.where(odd, *(corners[::-1] if k else corners))]).astype(BF16)


def shifted(line, left, right):
    cols = line.shape[0]
    place = lax.broadcasted_iota(jnp.int32, line.shape, 0)
    before = jnp.where(place == 0, left, pltpu.roll(line, 1, 0))
    after = jnp.where(place == cols - 1, right, pltpu.roll(line, cols - 1, 0))
    return before, line, after


def projected(mixed, gate, wv_ref, wo_ref):
    value = jnp.dot(mixed, wv_ref[...], preferred_element_type=F32)
    hidden = (value * gate).astype(BF16)
    return jnp.dot(hidden, wo_ref[...], preferred_element_type=F32).astype(BF16)


def filtered(lines, lefts, rights, taps):
    totals = [None] * len(lines)
    for r, line in enumerate(lines):
        near = shifted(line, lefts[r], rights[r])
        for a in range(3):
            to = r + 1 - a
            if 0 <= to < len(lines):
                term = near[0] * taps[a][0] + near[1] * taps[a][1] + near[2] * taps[a][2]
                totals[to] = term if totals[to] is None else totals[to] + term
    return totals


def taps_of(taps_ref, span):
    return [[taps_ref[a, b : b + 1, span] for b in range(3)] for a in range(3)]


def inner_kernel(
    frames, rows, cols, mine_ref, own_ref, other_ref, taps_ref, gate_ref, wv_ref, wo_ref, out_ref, totals_ref, mixed
):
    sites = rows * cols
    for lane in range(0, mine_ref.shape[1], LANES):
        span = slice(lane, lane + LANES)
        taps = taps_of(taps_ref, span)
        low, high = both_sides(own_ref[:, span], other_ref[:, span].astype(F32))
        for t in range(frames):
            at = t * sites
            lines = [mine_ref[at + r * cols : at + (r + 1) * cols, span] for r in range(rows)]
            lefts = [low[t * rows + r : t * rows + r + 1] for r in range(rows)]
            rights = [high[t * rows + r : t * rows + r + 1] for r in range(rows)]
            total = jnp.concatenate(filtered(lines, lefts, rights, taps))
            totals_ref[at : at + sites, span] = total
            mixed[at : at + sites, span] = total.astype(BF16)
    out_ref[...] = projected(mixed[...], gate_ref[...], wv_ref, wo_ref)


def has_earlier():
    return lax.div(lax.axis_index("tm"), 2) > 0


def block_kernel(frames, rows, cols, rounds_h, inner_ref, totals_ref, taps_ref, gate_ref, wv_ref, wo_ref, *refs):
    own_ref, other_ref, *parts, out_ref, sums_ref, mixed = refs
    firsts, rests = parts[: len(parts) // 2], parts[len(parts) // 2 :]
    sites = rows * cols
    size = frames * cols

    @pl.when(has_earlier())
    def _():
        for lane in range(0, out_ref.shape[1], LANES):
            span = slice(lane, lane + LANES)
            taps = taps_of(taps_ref, span)
            low, high = both_sides(own_ref[:, span], other_ref[:, span].astype(F32))
            lines = [jnp.zeros((size, LANES), F32)] * rows
            for d, (first, rest) in enumerate(zip(firsts, rests), 1):
                more = [first[i * size : (i + 1) * size, span].astype(F32) for i in range(rounds_h)]
                more += [rest[i * size : (i + 1) * size, span].astype(F32) for i in range(rows - rounds_h)]
                more = reordered(more, rounds_h, back=True)
                lines = [line + later(d, other) for line, other in zip(lines, more)]
            for t in range(frames):
                at = t * sites
                lefts = [low[t * rows + r : t * rows + r + 1] for r in range(rows)]
                rights = [high[t * rows + r : t * rows + r + 1] for r in range(rows)]
                total = filtered([line[t * cols : (t + 1) * cols] for line in lines], lefts, rights, taps)
                total = jnp.concatenate(total) + totals_ref[at : at + sites, span]
                sums_ref[at : at + sites, span] = total
                mixed[at : at + sites, span] = total.astype(BF16)
        out_ref[...] = projected(mixed[...], gate_ref[...], wv_ref, wo_ref)


def complete(frames, rows, cols, inner_ref, totals_ref, taps_ref, gate_ref, wv_ref, wo_ref, ends, out_ref, held, done):
    sites = rows * cols
    size = frames * cols
    odd, lower, upper = position("height")
    held[...] = inner_ref[...]
    mixed, gate = [], []
    for k, end in enumerate(ends):
        first = jnp.logical_not(odd) if k else odd
        lefts, rights = end[size : size + frames], end[size + frames : size + 2 * frames]
        exists = jnp.where(first, lower, upper)
        tap = jnp.where(first, taps_ref[0], taps_ref[2])
        for t in range(frames):
            near = shifted(end[t * cols : (t + 1) * cols], lefts[t : t + 1], rights[t : t + 1])
            more = near[0] * tap[0:1] + near[1] * tap[1:2] + near[2] * tap[2:3]
            i, j = t * sites, (t + 1) * sites - cols
            total = jnp.where(first, totals_ref[i : i + cols], totals_ref[j : j + cols])
            mixed.append(total + jnp.where(exists, more, jnp.zeros_like(more)))
            gate.append(jnp.where(first, gate_ref[i : i + cols], gate_ref[j : j + cols]))
    out = projected(jnp.concatenate(mixed).astype(BF16), jnp.concatenate(gate), wv_ref, wo_ref)
    for t in range(frames):
        new = [out[k * size + t * cols : k * size + (t + 1) * cols].astype(F32) for k in range(len(ends))]
        first, final = t * sites, (t + 1) * sites - 2 * cols
        top = inner_ref[first : first + 2 * cols].astype(F32)
        bottom = inner_ref[final : final + 2 * cols].astype(F32)
        other = new[1] if len(new) > 1 else None
        row = jnp.where(odd, new[0], top[:cols] if other is None else other)
        held[first : first + 2 * cols] = jnp.concatenate([row, top[cols:]]).astype(BF16)
        row = jnp.where(odd, bottom[cols:] if other is None else other, new[0])
        held[final : final + 2 * cols] = jnp.concatenate([bottom[:cols], row]).astype(BF16)
    copy = pltpu.make_async_copy(held, out_ref, done)
    copy.start()
    copy.wait()


def first_kernel(frames, rows, cols, inner_ref, totals_ref, taps_ref, gate_ref, wv_ref, wo_ref, *refs):
    *ends, out_ref, held, done = refs

    @pl.when(jnp.logical_not(has_earlier()))
    def _():
        values = [end[...].astype(F32) for end in ends]
        complete(
            frames, rows, cols, inner_ref, totals_ref, taps_ref, gate_ref, wv_ref, wo_ref, values, out_ref, held, done
        )


def last_kernel(frames, rows, cols, before_ref, inner_ref, totals_ref, taps_ref, gate_ref, wv_ref, wo_ref, *refs):
    *ends, out_ref, held, done = refs
    own, earlier = ends[: len(ends) // 2], ends[len(ends) // 2 :]

    @pl.when(has_earlier())
    def _():
        values = [a[...].astype(F32) + b[...].astype(F32) for a, b in zip(own, earlier)]
        complete(
            frames, rows, cols, inner_ref, totals_ref, taps_ref, gate_ref, wv_ref, wo_ref, values, out_ref, held, done
        )


def body(latents, spatial_taps, kernel_taps, skip_gain, gate_weight, value_weight, out_weight):
    frames, rows, cols, chans = latents.shape
    lags = kernel_taps.shape[0]
    n_t, n_h, n_w = lax.axis_size("tm"), lax.axis_size("height"), lax.axis_size("width")
    chips = n_t // 2
    block = frames * rows * cols
    shape = jax.ShapeDtypeStruct
    x = latents.reshape(block, chans)

    partner = lax.ppermute(x, "tm", [(i, i ^ 1) for i in range(n_t)])
    lines = frames * rows
    field = shape((block, chans), F32)
    inputs = [kernel_taps, skip_gain.reshape(1, chans), x, gate_weight, spatial_taps, value_weight, out_weight]
    near_x, near_gate, taps, value_weight, out_weight, table, side, *fields = call(
        functools.partial(early_kernel, frames, rows, cols, len(inputs)),
        "early",
        [shape(a.shape, a.dtype) for a in inputs[2:]]
        + [shape((lags + 2 * frames, cols, chans), F32), shape((lines, chans), F32)]
        + [field] * chips,
        [pltpu.VMEM(a.shape, a.dtype) for a in inputs[:2]]
        + [pltpu.SemaphoreType.DMA((len(inputs),)), pltpu.VMEM((block, LANES), F32)],
        inputs,
        far=len(inputs),
    )
    (gate,) = call(gate_kernel, "gate", [field], [], [near_x, near_gate])

    h_rounds = swaps("height")
    (column,) = call(
        functools.partial(column_kernel, frames, rows, cols),
        "column",
        [shape((2 * lines, chans), BF16)],
        [pltpu.VMEM((block, LANES), F32)],
        [partner, side],
    )
    parts = [shape((n * frames * cols, chans), BF16) for n in (len(h_rounds), rows - len(h_rounds))]
    sent = call(
        functools.partial(later_kernel, frames, rows, cols, len(h_rounds)),
        "later",
        parts * (chips - 1),
        [],
        [partner, table] + fields[1:],
        2 * (chips - 1) * frames * x.size,
    )
    (mine,) = call(
        functools.partial(own_kernel, frames, rows, cols),
        "own",
        [field],
        [],
        [partner, table, fields[0]],
        2 * frames * x.size,
    )
    columns, firsts, rests = [], [], []
    for d in range(chips):
        route = []
        for i in range(n_t):
            for h in range(n_h):
                for j in range(n_w):
                    to, beside = facing(i % 2, j, n_w), h
                    if i // 2 + d >= chips:
                        to = j
                    elif to == j and n_h % 2 == 0:
                        beside = h ^ 1
                    source = (i * n_h + h) * n_w + j
                    route.append((source, ((i + 2 * d) % n_t * n_h + beside) * n_w + to))
        columns.append(lax.ppermute(column, ("tm", "height", "width"), route))
    for d in range(1, chips):
        route = [(i, (i + 2 * d) % n_t) for i in range(n_t)]
        firsts.append(lax.ppermute(sent[2 * d - 2], "tm", route))
        rests.append(lax.ppermute(sent[2 * d - 1], "tm", route))

    swap = [(i, i ^ 1) for i in range(n_t)]
    both = [shape((lines, chans), F32), shape((lines, chans), BF16)]
    own, other = call(functools.partial(side_kernel, frames, rows, 0), "side", both, [], [table, columns[0]], LATER)
    other = lax.ppermute(other, "tm", swap)
    end = [shape((frames * cols + 2 * frames, chans), BF16)] * len(h_rounds)
    ends = call(functools.partial(border_kernel, frames, rows, cols), "border", end, [], [mine, own, other])
    ends = [lax.ppermute(e, "height", pairs) for e, pairs in zip(ends, h_rounds)]
    if chips > 1:
        own_d, other_d = call(
            functools.partial(side_kernel, frames, rows, 1), "beside", both, [], [table] + columns[1:], LATER
        )
        other_d = lax.ppermute(other_d, "tm", swap)
        earlier = call(functools.partial(before_kernel, frames, rows, cols), "before", end, [], [own_d, other_d] + firsts)
        earlier = [lax.ppermute(e, "height", pairs) for e, pairs in zip(earlier, h_rounds)]

    inner, totals = call(
        functools.partial(inner_kernel, frames, rows, cols),
        "inner",
        [shape((block, chans), BF16), field],
        [pltpu.VMEM((block, chans), BF16)],
        [mine, own, other, taps, gate, value_weight, out_weight],
        4 * block * chans * chans,
    )
    held = [pltpu.VMEM((block, chans), BF16), pltpu.SemaphoreType.DMA]
    weights = [taps, gate, value_weight, out_weight]
    out = shape((block, chans), BF16)
    (first,) = call(
        functools.partial(first_kernel, frames, rows, cols),
        "first",
        [out],
        held,
        [inner, totals] + weights + ends,
        far_outs=1,
    )
    if chips > 1:
        inner, totals = call(
            functools.partial(block_kernel, frames, rows, cols, len(h_rounds)),
            "block",
            [out, field],
            held[:1],
            [inner, totals] + weights + [own_d, other_d] + firsts + rests,
            aliases={0: 0, 1: 1},
        )
        (first,) = call(
            functools.partial(last_kernel, frames, rows, cols),
            "last",
            [out],
            held,
            [first, inner, totals] + weights + ends + earlier,
            far=1,
            far_outs=1,
            aliases={0: 0},
        )
    return first.reshape(latents.shape)


def solution(mesh):
    in_specs = (P("tm", "height", "width", None), P(), P(), P(), P(), P(), P())
    out_specs = P("tm", "height", "width", None)
    return jax.shard_map(body, mesh=mesh, in_specs=in_specs, out_specs=out_specs, check_vma=False)
```

```python
import functools

import jax
import jax.numpy as jnp
from jax import lax
from jax.experimental import pallas as pl
from jax.experimental.pallas import tpu as pltpu
from jax.sharding import PartitionSpec as P

LANES = 128
LATER = 8 * 10**9
F32, BF16 = jnp.float32, jnp.bfloat16
VMEM = pl.BlockSpec(memory_space=pltpu.VMEM)
HBM = pl.BlockSpec(memory_space=pltpu.HBM)


def call(kernel, name, outs, scratch, operands, flops=0, exps=0, far=0, far_outs=0, aliases={}):
    operands = [pltpu.with_memory_space_constraint(a, pltpu.HBM) for a in operands[:far]] + list(operands[far:])
    moved = sum(a.size * a.dtype.itemsize for a in operands) + sum(a.size * a.dtype.itemsize for a in outs)
    return pl.pallas_call(
        kernel,
        out_shape=tuple(outs),
        in_specs=[HBM] * far + [VMEM] * (len(operands) - far),
        out_specs=(HBM,) * far_outs + (VMEM,) * (len(outs) - far_outs),
        scratch_shapes=scratch,
        input_output_aliases=aliases,
        compiler_params=pltpu.CompilerParams(vmem_limit_bytes=24 * 1024 * 1024),
        cost_estimate=pl.CostEstimate(flops=flops, bytes_accessed=moved, transcendentals=exps),
        name=name,
    )(*operands)


def swaps(axis):
    n = lax.axis_size(axis)
    rounds = []
    for first in range(2 if n > 2 else 1):
        to = list(range(n))
        for i in range(first, n - 1, 2):
            to[i], to[i + 1] = i + 1, i
        rounds.append(list(enumerate(to)))
    return rounds


def position(axis):
    i, n = lax.axis_index(axis), lax.axis_size(axis)
    return lax.rem(i, 2) == 1, i > 0, i < n - 1


def second():
    return lax.rem(lax.axis_index("tm"), 2) == 1


def on_right():
    return lax.rem(lax.axis_index("tm") + lax.axis_index("width"), 2) == 0


def facing(core, column, columns):
    to = column + (1 if (core + column) % 2 == 0 else -1)
    return to if 0 <= to < columns else column


def outer_column(ref, lines, cols):
    return jnp.where(on_right(), ref[pl.ds(cols - 1, lines, stride=cols), :], ref[pl.ds(0, lines, stride=cols), :])


def gate_kernel(x_ref, w_ref, gate_ref):
    v = jnp.dot(x_ref[...], w_ref[...], preferred_element_type=F32)
    gate_ref[...] = v / (1.0 + jnp.exp(-v))


def early_kernel(frames, rows, cols, count, *refs):
    far, kept, rest = refs[:count], refs[count : 2 * count - 2], refs[2 * count - 2 :]
    table_ref, side_ref, *fields, taps_ref, skip_ref, arrived, held = rest
    near = (taps_ref, skip_ref) + kept
    x_ref = near[2]
    copies = [pltpu.make_async_copy(a, b, arrived.at[i]) for i, (a, b) in enumerate(zip(far, near))]
    for copy in copies:
        copy.start()
    lags, chans = taps_ref.shape
    copies[0].wait()
    copies[1].wait()
    pad = 2 * frames
    taps = taps_ref[...].astype(F32)
    table_ref[0:pad] = jnp.zeros((pad, cols, chans), F32)
    for lag in range(lags):
        tap = taps[lag : lag + 1] + (skip_ref[...] if lag == 0 else 0.0)
        table_ref[pad + lag] = jnp.broadcast_to(tap, (cols, chans))
    sites = rows * cols
    copies[2].wait()
    for lane in range(0, chans, LANES):
        span = slice(lane, lane + LANES)
        held[...] = x_ref[:, span].astype(F32)
        side_ref[:, span] = outer_column(held, frames * rows, cols)
        for d, field in enumerate(fields):
            totals = [None] * frames
            for s in range(frames):
                x = x_ref[s * sites : (s + 1) * sites, span].astype(F32).reshape(rows, cols, LANES)
                for t in range(s if d == 0 else 0, frames):
                    term = table_ref[pad + 2 * d * frames + t - s, :, span] * x
                    totals[t] = term if totals[t] is None else totals[t] + term
            for t in range(frames):
                field[t * sites : (t + 1) * sites, span] = totals[t].reshape(sites, LANES)
    for copy in copies[3:]:
        copy.wait()


def reordered(lines, rounds_h, back=False):
    if rounds_h > 1:
        return lines[:1] + lines[2:] + lines[1:2] if back else lines[:1] + lines[-1:] + lines[1:-1]
    odd = position("height")[0]
    return [jnp.where(odd, a, b) for a, b in zip(lines, lines[::-1])]


def column_kernel(frames, rows, cols, partner_ref, side_ref, out_ref, held):
    lines = frames * rows
    for lane in range(0, out_ref.shape[1], LANES):
        span = slice(lane, lane + LANES)
        held[...] = partner_ref[:, span].astype(F32)
        out_ref[:, span] = jnp.concatenate([side_ref[:, span], outer_column(held, lines, cols)]).astype(BF16)


def shift(frames):
    return jnp.where(second(), frames, -frames)


def with_partner(frames, rows, cols, d, field_ref, partner_ref, table_ref, span):
    sites = rows * cols
    base = 2 * frames + 2 * d * frames + shift(frames)
    totals = [field_ref[t * sites : (t + 1) * sites, span].reshape(rows, cols, LANES) for t in range(frames)]
    for s in range(frames):
        x = partner_ref[s * sites : (s + 1) * sites, span].astype(F32).reshape(rows, cols, LANES)
        for t in range(frames):
            totals[t] = totals[t] + table_ref[base + t - s, :, span] * x
    return totals


def later_kernel(frames, rows, cols, rounds_h, partner_ref, table_ref, *refs):
    fields, outs = refs[: len(refs) // 3], refs[len(refs) // 3 :]
    for d, field in enumerate(fields, 1):
        for lane in range(0, field.shape[1], LANES):
            span = slice(lane, lane + LANES)
            totals = with_partner(frames, rows, cols, d, field, partner_ref, table_ref, span)
            tiles = reordered([jnp.concatenate([t[r] for t in totals]) for r in range(rows)], rounds_h)
            outs[2 * d - 2][:, span] = jnp.concatenate(tiles[:rounds_h]).astype(BF16)
            outs[2 * d - 1][:, span] = jnp.concatenate(tiles[rounds_h:]).astype(BF16)


def own_kernel(frames, rows, cols, after_ref, partner_ref, table_ref, field_ref, mine_ref):
    for lane in range(0, mine_ref.shape[1], LANES):
        span = slice(lane, lane + LANES)
        totals = with_partner(frames, rows, cols, 0, field_ref, partner_ref, table_ref, span)
        mine_ref[:, span] = jnp.concatenate(totals).reshape(mine_ref.shape[0], LANES)


def later(d, value):
    return jnp.where(lax.div(lax.axis_index("tm"), 2) >= d, value, jnp.zeros_like(value))


def add_column(frames, rows, d, totals, column, table_ref, span):
    base = 2 * frames + 2 * d * frames
    for t in range(2 * frames):
        for s in range(2 * frames):
            lag = t % frames - s % frames
            if t // frames == s // frames:
                if d == 0 and lag < 0:
                    continue
            else:
                lag = lag + (shift(frames) if t < frames else -shift(frames))
            totals[t] = totals[t] + table_ref[base + lag, :, span] * column[s * rows : (s + 1) * rows]
    return totals


def side_kernel(frames, rows, first, count, table_ref, *refs):
    arrived, (own_ref, other_ref) = refs[:count], refs[-2:]
    _, lower, upper = position("width")
    exists = jnp.where(on_right(), upper, lower)
    for lane in range(0, own_ref.shape[1], LANES):
        span = slice(lane, lane + LANES)
        totals = [jnp.zeros((rows, LANES), F32)] * (2 * frames)
        for d, ref in enumerate(arrived, first):
            totals = add_column(frames, rows, d, totals, later(d, ref[:, span].astype(F32)), table_ref, span)
        totals = [jnp.where(exists, total, jnp.zeros_like(total)) for total in totals]
        own_ref[:, span] = jnp.concatenate(totals[:frames])
        other_ref[:, span] = jnp.concatenate(totals[frames:]).astype(BF16)


def both_sides(own, other):
    right = on_right()
    return jnp.where(right, other, own), jnp.where(right, own, other)


def end_corners(frames, rows, own_ref, other_ref):
    sides = both_sides(own_ref[...], other_ref[...].astype(F32))
    pick = lambda r: [side[t * rows + r : t * rows + r + 1] for side in sides for t in range(frames)]
    return [jnp.concatenate(pick(r)) for r in (0, rows - 1)]


def border_kernel(frames, rows, cols, mine_ref, own_ref, other_ref, *outs):
    sites = rows * cols
    odd, _, _ = position("height")
    corners = end_corners(frames, rows, own_ref, other_ref)
    lines = []
    for r in (0, rows - 1):
        lines.append(jnp.concatenate([mine_ref[t * sites + r * cols : t * sites + (r + 1) * cols] for t in range(frames)]))
    ends = [jnp.concatenate(pair) for pair in zip(lines, corners)]
    for k, out in enumerate(outs):
        out[...] = jnp.where(odd, *(ends[::-1] if k else ends)).astype(BF16)


def before_kernel(frames, rows, cols, own_ref, other_ref, *refs):
    rounds_h = refs[0].shape[0] // (frames * cols)
    firsts, outs = refs[:-rounds_h], refs[-rounds_h:]
    size = frames * cols
    odd, _, _ = position("height")
    corners = end_corners(frames, rows, own_ref, other_ref)
    line = 0.0
    for d, ref in enumerate(firsts, 1):
        line = line + later(d, ref[...].astype(F32))
    for k, out in enumerate(outs):
        if rounds_h > 1:
            pair = line[:size], line[size:]
            row = jnp.where(odd, *(pair[::-1] if k else pair))
        else:
            row = line
        out[...] = jnp.concatenate([row, jnp.where(odd, *(corners[::-1] if k else corners))]).astype(BF16)


def shifted(line, left, right):
    cols = line.shape[0]
    place = lax.broadcasted_iota(jnp.int32, line.shape, 0)
    before = jnp.where(place == 0, left, pltpu.roll(line, 1, 0))
    after = jnp.where(place == cols - 1, right, pltpu.roll(line, cols - 1, 0))
    return before, line, after


def projected(mixed, gate, wv_ref, wo_ref):
    value = jnp.dot(mixed, wv_ref[...], preferred_element_type=F32)
    hidden = (value * gate).astype(BF16)
    return jnp.dot(hidden, wo_ref[...], preferred_element_type=F32).astype(BF16)


def filtered(lines, lefts, rights, taps):
    totals = [None] * len(lines)
    for r, line in enumerate(lines):
        near = shifted(line, lefts[r], rights[r])
        for a in range(3):
            to = r + 1 - a
            if 0 <= to < len(lines):
                term = near[0] * taps[a][0] + near[1] * taps[a][1] + near[2] * taps[a][2]
                totals[to] = term if totals[to] is None else totals[to] + term
    return totals


def taps_of(taps_ref, span):
    return [[taps_ref[a, b : b + 1, span] for b in range(3)] for a in range(3)]


def inner_kernel(
    frames, rows, cols, mine_ref, own_ref, other_ref, taps_ref, gate_ref, wv_ref, wo_ref, out_ref, totals_ref, mixed
):
    sites = rows * cols
    for lane in range(0, mine_ref.shape[1], LANES):
        span = slice(lane, lane + LANES)
        taps = taps_of(taps_ref, span)
        low, high = both_sides(own_ref[:, span], other_ref[:, span].astype(F32))
        for t in range(frames):
            at = t * sites
            lines = [mine_ref[at + r * cols : at + (r + 1) * cols, span] for r in range(rows)]
            lefts = [low[t * rows + r : t * rows + r + 1] for r in range(rows)]
            rights = [high[t * rows + r : t * rows + r + 1] for r in range(rows)]
            total = jnp.concatenate(filtered(lines, lefts, rights, taps))
            totals_ref[at : at + sites, span] = total
            mixed[at : at + sites, span] = total.astype(BF16)
    out_ref[...] = projected(mixed[...], gate_ref[...], wv_ref, wo_ref)


def has_earlier():
    return lax.div(lax.axis_index("tm"), 2) > 0


def block_kernel(frames, rows, cols, rounds_h, inner_ref, totals_ref, taps_ref, gate_ref, wv_ref, wo_ref, *refs):
    own_ref, other_ref, *parts, out_ref, sums_ref, mixed = refs
    firsts, rests = parts[: len(parts) // 2], parts[len(parts) // 2 :]
    sites = rows * cols
    size = frames * cols

    @pl.when(has_earlier())
    def _():
        for lane in range(0, out_ref.shape[1], LANES):
            span = slice(lane, lane + LANES)
            taps = taps_of(taps_ref, span)
            low, high = both_sides(own_ref[:, span], other_ref[:, span].astype(F32))
            lines = [jnp.zeros((size, LANES), F32)] * rows
            for d, (first, rest) in enumerate(zip(firsts, rests), 1):
                more = [first[i * size : (i + 1) * size, span].astype(F32) for i in range(rounds_h)]
                more += [rest[i * size : (i + 1) * size, span].astype(F32) for i in range(rows - rounds_h)]
                more = reordered(more, rounds_h, back=True)
                lines = [line + later(d, other) for line, other in zip(lines, more)]
            for t in range(frames):
                at = t * sites
                lefts = [low[t * rows + r : t * rows + r + 1] for r in range(rows)]
                rights = [high[t * rows + r : t * rows + r + 1] for r in range(rows)]
                total = filtered([line[t * cols : (t + 1) * cols] for line in lines], lefts, rights, taps)
                total = jnp.concatenate(total) + totals_ref[at : at + sites, span]
                sums_ref[at : at + sites, span] = total
                mixed[at : at + sites, span] = total.astype(BF16)
        out_ref[...] = projected(mixed[...], gate_ref[...], wv_ref, wo_ref)


def complete(frames, rows, cols, inner_ref, totals_ref, taps_ref, gate_ref, wv_ref, wo_ref, ends, out_ref, held, done):
    sites = rows * cols
    size = frames * cols
    odd, lower, upper = position("height")
    held[...] = inner_ref[...]
    mixed, gate = [], []
    for k, end in enumerate(ends):
        first = jnp.logical_not(odd) if k else odd
        lefts, rights = end[size : size + frames], end[size + frames : size + 2 * frames]
        exists = jnp.where(first, lower, upper)
        tap = jnp.where(first, taps_ref[0], taps_ref[2])
        for t in range(frames):
            near = shifted(end[t * cols : (t + 1) * cols], lefts[t : t + 1], rights[t : t + 1])
            more = near[0] * tap[0:1] + near[1] * tap[1:2] + near[2] * tap[2:3]
            i, j = t * sites, (t + 1) * sites - cols
            total = jnp.where(first, totals_ref[i : i + cols], totals_ref[j : j + cols])
            mixed.append(total + jnp.where(exists, more, jnp.zeros_like(more)))
            gate.append(jnp.where(first, gate_ref[i : i + cols], gate_ref[j : j + cols]))
    out = projected(jnp.concatenate(mixed).astype(BF16), jnp.concatenate(gate), wv_ref, wo_ref)
    for t in range(frames):
        new = [out[k * size + t * cols : k * size + (t + 1) * cols].astype(F32) for k in range(len(ends))]
        first, final = t * sites, (t + 1) * sites - 2 * cols
        top = inner_ref[first : first + 2 * cols].astype(F32)
        bottom = inner_ref[final : final + 2 * cols].astype(F32)
        other = new[1] if len(new) > 1 else None
        row = jnp.where(odd, new[0], top[:cols] if other is None else other)
        held[first : first + 2 * cols] = jnp.concatenate([row, top[cols:]]).astype(BF16)
        row = jnp.where(odd, bottom[cols:] if other is None else other, new[0])
        held[final : final + 2 * cols] = jnp.concatenate([bottom[:cols], row]).astype(BF16)
    copy = pltpu.make_async_copy(held, out_ref, done)
    copy.start()
    copy.wait()


def first_kernel(frames, rows, cols, inner_ref, totals_ref, taps_ref, gate_ref, wv_ref, wo_ref, *refs):
    *ends, out_ref, held, done = refs

    @pl.when(jnp.logical_not(has_earlier()))
    def _():
        values = [end[...].astype(F32) for end in ends]
        complete(
            frames, rows, cols, inner_ref, totals_ref, taps_ref, gate_ref, wv_ref, wo_ref, values, out_ref, held, done
        )


def last_kernel(frames, rows, cols, before_ref, inner_ref, totals_ref, taps_ref, gate_ref, wv_ref, wo_ref, *refs):
    *ends, out_ref, held, done = refs
    own, earlier = ends[: len(ends) // 2], ends[len(ends) // 2 :]

    @pl.when(has_earlier())
    def _():
        values = [a[...].astype(F32) + b[...].astype(F32) for a, b in zip(own, earlier)]
        complete(
            frames, rows, cols, inner_ref, totals_ref, taps_ref, gate_ref, wv_ref, wo_ref, values, out_ref, held, done
        )


def body(latents, spatial_taps, kernel_taps, skip_gain, gate_weight, value_weight, out_weight):
    frames, rows, cols, chans = latents.shape
    lags = kernel_taps.shape[0]
    n_t, n_h, n_w = lax.axis_size("tm"), lax.axis_size("height"), lax.axis_size("width")
    chips = n_t // 2
    block = frames * rows * cols
    shape = jax.ShapeDtypeStruct
    x = latents.reshape(block, chans)

    partner = lax.ppermute(x, "tm", [(i, i ^ 1) for i in range(n_t)])
    lines = frames * rows
    field = shape((block, chans), F32)
    inputs = [kernel_taps, skip_gain.reshape(1, chans), x, gate_weight, spatial_taps, value_weight, out_weight]
    near_x, near_gate, taps, value_weight, out_weight, table, side, *fields = call(
        functools.partial(early_kernel, frames, rows, cols, len(inputs)),
        "early",
        [shape(a.shape, a.dtype) for a in inputs[2:]]
        + [shape((lags + 2 * frames, cols, chans), F32), shape((lines, chans), F32)]
        + [field] * chips,
        [pltpu.VMEM(a.shape, a.dtype) for a in inputs[:2]]
        + [pltpu.SemaphoreType.DMA((len(inputs),)), pltpu.VMEM((block, LANES), F32)],
        inputs,
        far=len(inputs),
    )
    (gate,) = call(gate_kernel, "gate", [field], [], [near_x, near_gate])

    h_rounds = swaps("height")
    (column,) = call(
        functools.partial(column_kernel, frames, rows, cols),
        "column",
        [shape((2 * lines, chans), BF16)],
        [pltpu.VMEM((block, LANES), F32)],
        [partner, side],
    )
    parts = [shape((n * frames * cols, chans), BF16) for n in (len(h_rounds), rows - len(h_rounds))]
    sent = call(
        functools.partial(later_kernel, frames, rows, cols, len(h_rounds)),
        "later",
        parts * (chips - 1),
        [],
        [partner, table] + fields[1:],
        2 * (chips - 1) * frames * x.size,
    )
    columns, firsts, rests = [], [], []
    for d in range(chips):
        route = []
        for i in range(n_t):
            for h in range(n_h):
                for j in range(n_w):
                    to, beside = facing(i % 2, j, n_w), h
                    if i // 2 + d >= chips:
                        to = j
                    elif to == j and n_h % 2 == 0:
                        beside = h ^ 1
                    source = (i * n_h + h) * n_w + j
                    route.append((source, ((i + 2 * d) % n_t * n_h + beside) * n_w + to))
        columns.append(lax.ppermute(column, ("tm", "height", "width"), route))
    for d in range(1, chips):
        route = [(i, (i + 2 * d) % n_t) for i in range(n_t)]
        firsts.append(lax.ppermute(sent[2 * d - 2], "tm", route))
        rests.append(lax.ppermute(sent[2 * d - 1], "tm", route))

    swap = [(i, i ^ 1) for i in range(n_t)]
    both = [shape((lines, chans), F32), shape((lines, chans), BF16)]
    own, other = call(functools.partial(side_kernel, frames, rows, 0, 1), "side", both, [], [table, columns[0]], LATER)
    (mine,) = call(
        functools.partial(own_kernel, frames, rows, cols),
        "own",
        [field],
        [],
        [own, partner, table, fields[0]],
        2 * frames * x.size,
    )
    other = lax.ppermute(other, "tm", swap)
    end = [shape((frames * cols + 2 * frames, chans), BF16)] * len(h_rounds)
    ends = call(functools.partial(border_kernel, frames, rows, cols), "border", end, [], [mine, own, other])
    ends = [lax.ppermute(e, "height", pairs) for e, pairs in zip(ends, h_rounds)]
    if chips > 1:
        own_d, other_d = call(
            functools.partial(side_kernel, frames, rows, 1, chips - 1),
            "beside",
            both,
            [],
            [table] + columns[1:] + [mine],
            LATER,
        )
        other_d = lax.ppermute(other_d, "tm", swap)
        earlier = call(functools.partial(before_kernel, frames, rows, cols), "before", end, [], [own_d, other_d] + firsts)
        earlier = [lax.ppermute(e, "height", pairs) for e, pairs in zip(earlier, h_rounds)]

    inner, totals = call(
        functools.partial(inner_kernel, frames, rows, cols),
        "inner",
        [shape((block, chans), BF16), field],
        [pltpu.VMEM((block, chans), BF16)],
        [mine, own, other, taps, gate, value_weight, out_weight],
        4 * block * chans * chans,
    )
    held = [pltpu.VMEM((block, chans), BF16), pltpu.SemaphoreType.DMA]
    weights = [taps, gate, value_weight, out_weight]
    out = shape((block, chans), BF16)
    (first,) = call(
        functools.partial(first_kernel, frames, rows, cols),
        "first",
        [out],
        held,
        [inner, totals] + weights + ends,
        far_outs=1,
    )
    if chips > 1:
        inner, totals = call(
            functools.partial(block_kernel, frames, rows, cols, len(h_rounds)),
            "block",
            [out, field],
            held[:1],
            [inner, totals] + weights + [own_d, other_d] + firsts + rests,
            aliases={0: 0, 1: 1},
        )
        (first,) = call(
            functools.partial(last_kernel, frames, rows, cols),
            "last",
            [out],
            held,
            [first, inner, totals] + weights + ends + earlier,
            far=1,
            far_outs=1,
            aliases={0: 0},
        )
    return first.reshape(latents.shape)


def solution(mesh):
    in_specs = (P("tm", "height", "width", None), P(), P(), P(), P(), P(), P())
    out_specs = P("tm", "height", "width", None)
    return jax.shard_map(body, mesh=mesh, in_specs=in_specs, out_specs=out_specs, check_vma=False)
```

```python
import functools

import jax
import jax.numpy as jnp
from jax import lax
from jax.experimental import pallas as pl
from jax.experimental.pallas import tpu as pltpu
from jax.sharding import PartitionSpec as P

LANES = 128
LATER = 8 * 10**9
F32, BF16 = jnp.float32, jnp.bfloat16
VMEM = pl.BlockSpec(memory_space=pltpu.VMEM)
HBM = pl.BlockSpec(memory_space=pltpu.HBM)


def call(kernel, name, outs, scratch, operands, flops=0, exps=0, far=0, far_outs=0, aliases={}):
    operands = [pltpu.with_memory_space_constraint(a, pltpu.HBM) for a in operands[:far]] + list(operands[far:])
    moved = sum(a.size * a.dtype.itemsize for a in operands) + sum(a.size * a.dtype.itemsize for a in outs)
    return pl.pallas_call(
        kernel,
        out_shape=tuple(outs),
        in_specs=[HBM] * far + [VMEM] * (len(operands) - far),
        out_specs=(HBM,) * far_outs + (VMEM,) * (len(outs) - far_outs),
        scratch_shapes=scratch,
        input_output_aliases=aliases,
        compiler_params=pltpu.CompilerParams(vmem_limit_bytes=24 * 1024 * 1024),
        cost_estimate=pl.CostEstimate(flops=flops, bytes_accessed=moved, transcendentals=exps),
        name=name,
    )(*operands)


def swaps(axis):
    n = lax.axis_size(axis)
    rounds = []
    for first in range(2 if n > 2 else 1):
        to = list(range(n))
        for i in range(first, n - 1, 2):
            to[i], to[i + 1] = i + 1, i
        rounds.append(list(enumerate(to)))
    return rounds


def position(axis):
    i, n = lax.axis_index(axis), lax.axis_size(axis)
    return lax.rem(i, 2) == 1, i > 0, i < n - 1


def second():
    return lax.rem(lax.axis_index("tm"), 2) == 1


def on_right():
    return lax.rem(lax.axis_index("tm") + lax.axis_index("width"), 2) == 0


def facing(core, column, columns):
    to = column + (1 if (core + column) % 2 == 0 else -1)
    return to if 0 <= to < columns else column


def outer_column(ref, lines, cols):
    return jnp.where(on_right(), ref[pl.ds(cols - 1, lines, stride=cols), :], ref[pl.ds(0, lines, stride=cols), :])


def gate_kernel(x_ref, w_ref, gate_ref):
    v = jnp.dot(x_ref[...], w_ref[...], preferred_element_type=F32)
    gate_ref[...] = v / (1.0 + jnp.exp(-v))


def early_kernel(frames, rows, cols, count, *refs):
    far, kept, rest = refs[:count], refs[count : 2 * count - 2], refs[2 * count - 2 :]
    table_ref, side_ref, *fields, taps_ref, skip_ref, arrived, held = rest
    near = (taps_ref, skip_ref) + kept
    x_ref = near[2]
    copies = [pltpu.make_async_copy(a, b, arrived.at[i]) for i, (a, b) in enumerate(zip(far, near))]
    for copy in copies:
        copy.start()
    lags, chans = taps_ref.shape
    copies[0].wait()
    copies[1].wait()
    pad = 2 * frames
    taps = taps_ref[...].astype(F32)
    table_ref[0:pad] = jnp.zeros((pad, cols, chans), F32)
    for lag in range(lags):
        tap = taps[lag : lag + 1] + (skip_ref[...] if lag == 0 else 0.0)
        table_ref[pad + lag] = jnp.broadcast_to(tap, (cols, chans))
    sites = rows * cols
    copies[2].wait()
    for lane in range(0, chans, LANES):
        span = slice(lane, lane + LANES)
        held[...] = x_ref[:, span].astype(F32)
        side_ref[:, span] = outer_column(held, frames * rows, cols)
        for d, field in enumerate(fields):
            totals = [None] * frames
            for s in range(frames):
                x = x_ref[s * sites : (s + 1) * sites, span].astype(F32).reshape(rows, cols, LANES)
                for t in range(s if d == 0 else 0, frames):
                    term = table_ref[pad + 2 * d * frames + t - s, :, span] * x
                    totals[t] = term if totals[t] is None else totals[t] + term
            for t in range(frames):
                field[t * sites : (t + 1) * sites, span] = totals[t].reshape(sites, LANES)
    for copy in copies[3:]:
        copy.wait()


def reordered(lines, rounds_h, back=False):
    if rounds_h > 1:
        return lines[:1] + lines[2:] + lines[1:2] if back else lines[:1] + lines[-1:] + lines[1:-1]
    odd = position("height")[0]
    return [jnp.where(odd, a, b) for a, b in zip(lines, lines[::-1])]


def column_kernel(frames, rows, cols, partner_ref, side_ref, out_ref, held):
    lines = frames * rows
    for lane in range(0, out_ref.shape[1], LANES):
        span = slice(lane, lane + LANES)
        held[...] = partner_ref[:, span].astype(F32)
        out_ref[:, span] = jnp.concatenate([side_ref[:, span], outer_column(held, lines, cols)]).astype(BF16)


def shift(frames):
    return jnp.where(second(), frames, -frames)


def with_partner(frames, rows, cols, d, field_ref, partner_ref, table_ref, span):
    sites = rows * cols
    base = 2 * frames + 2 * d * frames + shift(frames)
    totals = [field_ref[t * sites : (t + 1) * sites, span].reshape(rows, cols, LANES) for t in range(frames)]
    for s in range(frames):
        x = partner_ref[s * sites : (s + 1) * sites, span].astype(F32).reshape(rows, cols, LANES)
        for t in range(frames):
            totals[t] = totals[t] + table_ref[base + t - s, :, span] * x
    return totals


def later_kernel(frames, rows, cols, rounds_h, partner_ref, table_ref, *refs):
    fields, outs = refs[: len(refs) // 3], refs[len(refs) // 3 :]
    for d, field in enumerate(fields, 1):
        for lane in range(0, field.shape[1], LANES):
            span = slice(lane, lane + LANES)
            totals = with_partner(frames, rows, cols, d, field, partner_ref, table_ref, span)
            tiles = reordered([jnp.concatenate([t[r] for t in totals]) for r in range(rows)], rounds_h)
            outs[2 * d - 2][:, span] = jnp.concatenate(tiles[: rounds_h + 1]).astype(BF16)
            outs[2 * d - 1][:, span] = jnp.concatenate(tiles[rounds_h + 1 :]).astype(BF16)


def own_kernel(frames, rows, cols, after_ref, partner_ref, table_ref, field_ref, mine_ref):
    for lane in range(0, mine_ref.shape[1], LANES):
        span = slice(lane, lane + LANES)
        totals = with_partner(frames, rows, cols, 0, field_ref, partner_ref, table_ref, span)
        mine_ref[:, span] = jnp.concatenate(totals).reshape(mine_ref.shape[0], LANES)


def later(d, value):
    return jnp.where(lax.div(lax.axis_index("tm"), 2) >= d, value, jnp.zeros_like(value))


def add_column(frames, rows, d, totals, column, table_ref, span):
    base = 2 * frames + 2 * d * frames
    for t in range(2 * frames):
        for s in range(2 * frames):
            lag = t % frames - s % frames
            if t // frames == s // frames:
                if d == 0 and lag < 0:
                    continue
            else:
                lag = lag + (shift(frames) if t < frames else -shift(frames))
            totals[t] = totals[t] + table_ref[base + lag, :, span] * column[s * rows : (s + 1) * rows]
    return totals


def side_kernel(frames, rows, first, count, table_ref, *refs):
    arrived, (own_ref, other_ref) = refs[:count], refs[-2:]
    _, lower, upper = position("width")
    exists = jnp.where(on_right(), upper, lower)
    for lane in range(0, own_ref.shape[1], LANES):
        span = slice(lane, lane + LANES)
        totals = [jnp.zeros((rows, LANES), F32)] * (2 * frames)
        for d, ref in enumerate(arrived, first):
            totals = add_column(frames, rows, d, totals, later(d, ref[:, span].astype(F32)), table_ref, span)
        totals = [jnp.where(exists, total, jnp.zeros_like(total)) for total in totals]
        own_ref[:, span] = jnp.concatenate(totals[:frames])
        other_ref[:, span] = jnp.concatenate(totals[frames:]).astype(BF16)


def both_sides(own, other):
    right = on_right()
    return jnp.where(right, other, own), jnp.where(right, own, other)


def end_corners(frames, rows, own_ref, other_ref):
    sides = both_sides(own_ref[...], other_ref[...].astype(F32))
    pick = lambda r: [side[t * rows + r : t * rows + r + 1] for side in sides for t in range(frames)]
    return [jnp.concatenate(pick(r)) for r in (0, rows - 1)]


def border_kernel(frames, rows, cols, mine_ref, own_ref, other_ref, *outs):
    sites = rows * cols
    odd, _, _ = position("height")
    corners = end_corners(frames, rows, own_ref, other_ref)
    lines = []
    for r in (0, rows - 1):
        lines.append(jnp.concatenate([mine_ref[t * sites + r * cols : t * sites + (r + 1) * cols] for t in range(frames)]))
    ends = [jnp.concatenate(pair) for pair in zip(lines, corners)]
    for k, out in enumerate(outs):
        out[...] = jnp.where(odd, *(ends[::-1] if k else ends)).astype(BF16)


def before_kernel(frames, rows, cols, own_ref, other_ref, *refs):
    rounds_h = refs[0].shape[0] // (frames * cols) - 1
    firsts, outs = refs[:-rounds_h], refs[-rounds_h:]
    size = frames * cols
    odd, _, _ = position("height")
    corners = end_corners(frames, rows, own_ref, other_ref)
    line = 0.0
    for d, ref in enumerate(firsts, 1):
        line = line + later(d, ref[: rounds_h * size].astype(F32))
    for k, out in enumerate(outs):
        if rounds_h > 1:
            pair = line[:size], line[size:]
            row = jnp.where(odd, *(pair[::-1] if k else pair))
        else:
            row = line
        out[...] = jnp.concatenate([row, jnp.where(odd, *(corners[::-1] if k else corners))]).astype(BF16)


def shifted(line, left, right):
    cols = line.shape[0]
    place = lax.broadcasted_iota(jnp.int32, line.shape, 0)
    before = jnp.where(place == 0, left, pltpu.roll(line, 1, 0))
    after = jnp.where(place == cols - 1, right, pltpu.roll(line, cols - 1, 0))
    return before, line, after


def projected(mixed, gate, wv_ref, wo_ref):
    value = jnp.dot(mixed, wv_ref[...], preferred_element_type=F32)
    hidden = (value * gate).astype(BF16)
    return jnp.dot(hidden, wo_ref[...], preferred_element_type=F32).astype(BF16)


def filtered(lines, lefts, rights, taps):
    totals = [None] * len(lines)
    for r, line in enumerate(lines):
        near = shifted(line, lefts[r], rights[r])
        for a in range(3):
            to = r + 1 - a
            if 0 <= to < len(lines):
                term = near[0] * taps[a][0] + near[1] * taps[a][1] + near[2] * taps[a][2]
                totals[to] = term if totals[to] is None else totals[to] + term
    return totals


def taps_of(taps_ref, span):
    return [[taps_ref[a, b : b + 1, span] for b in range(3)] for a in range(3)]


def inner_kernel(
    frames, rows, cols, mine_ref, own_ref, other_ref, taps_ref, gate_ref, wv_ref, wo_ref, out_ref, totals_ref, mixed
):
    sites = rows * cols
    for lane in range(0, mine_ref.shape[1], LANES):
        span = slice(lane, lane + LANES)
        taps = taps_of(taps_ref, span)
        low, high = both_sides(own_ref[:, span], other_ref[:, span].astype(F32))
        for t in range(frames):
            at = t * sites
            lines = [mine_ref[at + r * cols : at + (r + 1) * cols, span] for r in range(rows)]
            lefts = [low[t * rows + r : t * rows + r + 1] for r in range(rows)]
            rights = [high[t * rows + r : t * rows + r + 1] for r in range(rows)]
            total = jnp.concatenate(filtered(lines, lefts, rights, taps))
            totals_ref[at : at + sites, span] = total
            mixed[at : at + sites, span] = total.astype(BF16)
    out_ref[...] = projected(mixed[...], gate_ref[...], wv_ref, wo_ref)


def has_earlier():
    return lax.div(lax.axis_index("tm"), 2) > 0


def block_kernel(frames, rows, cols, rounds_h, inner_ref, totals_ref, taps_ref, gate_ref, wv_ref, wo_ref, *refs):
    own_ref, other_ref, *parts, out_ref, sums_ref, mixed = refs
    firsts, rests = parts[: len(parts) // 2], parts[len(parts) // 2 :]
    sites = rows * cols
    size = frames * cols

    @pl.when(has_earlier())
    def _():
        for lane in range(0, out_ref.shape[1], LANES):
            span = slice(lane, lane + LANES)
            taps = taps_of(taps_ref, span)
            low, high = both_sides(own_ref[:, span], other_ref[:, span].astype(F32))
            lines = [jnp.zeros((size, LANES), F32)] * rows
            for d, (first, rest) in enumerate(zip(firsts, rests), 1):
                more = [first[i * size : (i + 1) * size, span].astype(F32) for i in range(rounds_h + 1)]
                more += [rest[i * size : (i + 1) * size, span].astype(F32) for i in range(rows - rounds_h - 1)]
                more = reordered(more, rounds_h, back=True)
                lines = [line + later(d, other) for line, other in zip(lines, more)]
            for t in range(frames):
                at = t * sites
                lefts = [low[t * rows + r : t * rows + r + 1] for r in range(rows)]
                rights = [high[t * rows + r : t * rows + r + 1] for r in range(rows)]
                total = filtered([line[t * cols : (t + 1) * cols] for line in lines], lefts, rights, taps)
                total = jnp.concatenate(total) + totals_ref[at : at + sites, span]
                sums_ref[at : at + sites, span] = total
                mixed[at : at + sites, span] = total.astype(BF16)
        out_ref[...] = projected(mixed[...], gate_ref[...], wv_ref, wo_ref)


def complete(frames, rows, cols, inner_ref, totals_ref, taps_ref, gate_ref, wv_ref, wo_ref, ends, out_ref, held, done):
    sites = rows * cols
    size = frames * cols
    odd, lower, upper = position("height")
    held[...] = inner_ref[...]
    mixed, gate = [], []
    for k, end in enumerate(ends):
        first = jnp.logical_not(odd) if k else odd
        lefts, rights = end[size : size + frames], end[size + frames : size + 2 * frames]
        exists = jnp.where(first, lower, upper)
        tap = jnp.where(first, taps_ref[0], taps_ref[2])
        for t in range(frames):
            near = shifted(end[t * cols : (t + 1) * cols], lefts[t : t + 1], rights[t : t + 1])
            more = near[0] * tap[0:1] + near[1] * tap[1:2] + near[2] * tap[2:3]
            i, j = t * sites, (t + 1) * sites - cols
            total = jnp.where(first, totals_ref[i : i + cols], totals_ref[j : j + cols])
            mixed.append(total + jnp.where(exists, more, jnp.zeros_like(more)))
            gate.append(jnp.where(first, gate_ref[i : i + cols], gate_ref[j : j + cols]))
    out = projected(jnp.concatenate(mixed).astype(BF16), jnp.concatenate(gate), wv_ref, wo_ref)
    for t in range(frames):
        new = [out[k * size + t * cols : k * size + (t + 1) * cols].astype(F32) for k in range(len(ends))]
        first, final = t * sites, (t + 1) * sites - 2 * cols
        top = inner_ref[first : first + 2 * cols].astype(F32)
        bottom = inner_ref[final : final + 2 * cols].astype(F32)
        other = new[1] if len(new) > 1 else None
        row = jnp.where(odd, new[0], top[:cols] if other is None else other)
        held[first : first + 2 * cols] = jnp.concatenate([row, top[cols:]]).astype(BF16)
        row = jnp.where(odd, bottom[cols:] if other is None else other, new[0])
        held[final : final + 2 * cols] = jnp.concatenate([bottom[:cols], row]).astype(BF16)
    copy = pltpu.make_async_copy(held, out_ref, done)
    copy.start()
    copy.wait()


def first_kernel(frames, rows, cols, inner_ref, totals_ref, taps_ref, gate_ref, wv_ref, wo_ref, *refs):
    *ends, out_ref, held, done = refs

    @pl.when(jnp.logical_not(has_earlier()))
    def _():
        values = [end[...].astype(F32) for end in ends]
        complete(
            frames, rows, cols, inner_ref, totals_ref, taps_ref, gate_ref, wv_ref, wo_ref, values, out_ref, held, done
        )


def last_kernel(frames, rows, cols, before_ref, inner_ref, totals_ref, taps_ref, gate_ref, wv_ref, wo_ref, *refs):
    *ends, out_ref, held, done = refs
    own, earlier = ends[: len(ends) // 2], ends[len(ends) // 2 :]

    @pl.when(has_earlier())
    def _():
        values = [a[...].astype(F32) + b[...].astype(F32) for a, b in zip(own, earlier)]
        complete(
            frames, rows, cols, inner_ref, totals_ref, taps_ref, gate_ref, wv_ref, wo_ref, values, out_ref, held, done
        )


def body(latents, spatial_taps, kernel_taps, skip_gain, gate_weight, value_weight, out_weight):
    frames, rows, cols, chans = latents.shape
    lags = kernel_taps.shape[0]
    n_t, n_h, n_w = lax.axis_size("tm"), lax.axis_size("height"), lax.axis_size("width")
    chips = n_t // 2
    block = frames * rows * cols
    shape = jax.ShapeDtypeStruct
    x = latents.reshape(block, chans)

    partner = lax.ppermute(x, "tm", [(i, i ^ 1) for i in range(n_t)])
    lines = frames * rows
    field = shape((block, chans), F32)
    inputs = [kernel_taps, skip_gain.reshape(1, chans), x, gate_weight, spatial_taps, value_weight, out_weight]
    near_x, near_gate, taps, value_weight, out_weight, table, side, *fields = call(
        functools.partial(early_kernel, frames, rows, cols, len(inputs)),
        "early",
        [shape(a.shape, a.dtype) for a in inputs[2:]]
        + [shape((lags + 2 * frames, cols, chans), F32), shape((lines, chans), F32)]
        + [field] * chips,
        [pltpu.VMEM(a.shape, a.dtype) for a in inputs[:2]]
        + [pltpu.SemaphoreType.DMA((len(inputs),)), pltpu.VMEM((block, LANES), F32)],
        inputs,
        far=len(inputs),
    )
    (gate,) = call(gate_kernel, "gate", [field], [], [near_x, near_gate])

    h_rounds = swaps("height")
    (column,) = call(
        functools.partial(column_kernel, frames, rows, cols),
        "column",
        [shape((2 * lines, chans), BF16)],
        [pltpu.VMEM((block, LANES), F32)],
        [partner, side],
    )
    parts = [shape((n * frames * cols, chans), BF16) for n in (len(h_rounds) + 1, rows - len(h_rounds) - 1)]
    sent = call(
        functools.partial(later_kernel, frames, rows, cols, len(h_rounds)),
        "later",
        parts * (chips - 1),
        [],
        [partner, table] + fields[1:],
        2 * (chips - 1) * frames * x.size,
    )
    columns, firsts, rests = [], [], []
    for d in range(chips):
        route = []
        for i in range(n_t):
            for h in range(n_h):
                for j in range(n_w):
                    to, beside = facing(i % 2, j, n_w), h
                    if i // 2 + d >= chips:
                        to = j
                    elif to == j and n_h % 2 == 0:
                        beside = h ^ 1
                    source = (i * n_h + h) * n_w + j
                    route.append((source, ((i + 2 * d) % n_t * n_h + beside) * n_w + to))
        columns.append(lax.ppermute(column, ("tm", "height", "width"), route))
    for d in range(1, chips):
        route = [(i, (i + 2 * d) % n_t) for i in range(n_t)]
        firsts.append(lax.ppermute(sent[2 * d - 2], "tm", route))
        rests.append(lax.ppermute(sent[2 * d - 1], "tm", route))

    swap = [(i, i ^ 1) for i in range(n_t)]
    both = [shape((lines, chans), F32), shape((lines, chans), BF16)]
    own, other = call(functools.partial(side_kernel, frames, rows, 0, 1), "side", both, [], [table, columns[0]], LATER)
    (mine,) = call(
        functools.partial(own_kernel, frames, rows, cols),
        "own",
        [field],
        [],
        [own, partner, table, fields[0]],
        2 * frames * x.size,
    )
    other = lax.ppermute(other, "tm", swap)
    end = [shape((frames * cols + 2 * frames, chans), BF16)] * len(h_rounds)
    ends = call(functools.partial(border_kernel, frames, rows, cols), "border", end, [], [mine, own, other])
    ends = [lax.ppermute(e, "height", pairs) for e, pairs in zip(ends, h_rounds)]
    if chips > 1:
        own_d, other_d = call(
            functools.partial(side_kernel, frames, rows, 1, chips - 1),
            "beside",
            both,
            [],
            [table] + columns[1:] + [mine],
            LATER,
        )
        other_d = lax.ppermute(other_d, "tm", swap)
        earlier = call(functools.partial(before_kernel, frames, rows, cols), "before", end, [], [own_d, other_d] + firsts)
        earlier = [lax.ppermute(e, "height", pairs) for e, pairs in zip(earlier, h_rounds)]

    inner, totals = call(
        functools.partial(inner_kernel, frames, rows, cols),
        "inner",
        [shape((block, chans), BF16), field],
        [pltpu.VMEM((block, chans), BF16)],
        [mine, own, other, taps, gate, value_weight, out_weight],
        4 * block * chans * chans,
    )
    held = [pltpu.VMEM((block, chans), BF16), pltpu.SemaphoreType.DMA]
    weights = [taps, gate, value_weight, out_weight]
    out = shape((block, chans), BF16)
    (first,) = call(
        functools.partial(first_kernel, frames, rows, cols),
        "first",
        [out],
        held,
        [inner, totals] + weights + ends,
        far_outs=1,
    )
    if chips > 1:
        inner, totals = call(
            functools.partial(block_kernel, frames, rows, cols, len(h_rounds)),
            "block",
            [out, field],
            held[:1],
            [inner, totals] + weights + [own_d, other_d] + firsts + rests,
            aliases={0: 0, 1: 1},
        )
        (first,) = call(
            functools.partial(last_kernel, frames, rows, cols),
            "last",
            [out],
            held,
            [first, inner, totals] + weights + ends + earlier,
            far=1,
            far_outs=1,
            aliases={0: 0},
        )
    return first.reshape(latents.shape)


def solution(mesh):
    in_specs = (P("tm", "height", "width", None), P(), P(), P(), P(), P(), P())
    out_specs = P("tm", "height", "width", None)
    return jax.shard_map(body, mesh=mesh, in_specs=in_specs, out_specs=out_specs, check_vma=False)
```

```python
import functools

import jax
import jax.numpy as jnp
from jax import lax
from jax.experimental import pallas as pl
from jax.experimental.pallas import tpu as pltpu
from jax.sharding import PartitionSpec as P

LANES = 128
LATER = 8 * 10**9
F32, BF16 = jnp.float32, jnp.bfloat16
VMEM = pl.BlockSpec(memory_space=pltpu.VMEM)
HBM = pl.BlockSpec(memory_space=pltpu.HBM)


def call(kernel, name, outs, scratch, operands, flops=0, exps=0, far=0, far_outs=0, aliases={}):
    operands = [pltpu.with_memory_space_constraint(a, pltpu.HBM) for a in operands[:far]] + list(operands[far:])
    moved = sum(a.size * a.dtype.itemsize for a in operands) + sum(a.size * a.dtype.itemsize for a in outs)
    return pl.pallas_call(
        kernel,
        out_shape=tuple(outs),
        in_specs=[HBM] * far + [VMEM] * (len(operands) - far),
        out_specs=(HBM,) * far_outs + (VMEM,) * (len(outs) - far_outs),
        scratch_shapes=scratch,
        input_output_aliases=aliases,
        compiler_params=pltpu.CompilerParams(vmem_limit_bytes=24 * 1024 * 1024),
        cost_estimate=pl.CostEstimate(flops=flops, bytes_accessed=moved, transcendentals=exps),
        name=name,
    )(*operands)


def swaps(axis):
    n = lax.axis_size(axis)
    rounds = []
    for first in range(2 if n > 2 else 1):
        to = list(range(n))
        for i in range(first, n - 1, 2):
            to[i], to[i + 1] = i + 1, i
        rounds.append(list(enumerate(to)))
    return rounds


def position(axis):
    i, n = lax.axis_index(axis), lax.axis_size(axis)
    return lax.rem(i, 2) == 1, i > 0, i < n - 1


def second():
    return lax.rem(lax.axis_index("tm"), 2) == 1


def on_right():
    return lax.rem(lax.axis_index("tm") + lax.axis_index("width"), 2) == 0


def facing(core, column, columns):
    to = column + (1 if (core + column) % 2 == 0 else -1)
    return to if 0 <= to < columns else column


def outer_column(ref, lines, cols):
    return jnp.where(on_right(), ref[pl.ds(cols - 1, lines, stride=cols), :], ref[pl.ds(0, lines, stride=cols), :])


def gate_kernel(after_ref, x_ref, w_ref, gate_ref):
    v = jnp.dot(x_ref[...], w_ref[...], preferred_element_type=F32)
    gate_ref[...] = v / (1.0 + jnp.exp(-v))


def early_kernel(frames, rows, cols, count, *refs):
    far, kept, rest = refs[:count], refs[count : 2 * count - 2], refs[2 * count - 2 :]
    table_ref, side_ref, *fields, taps_ref, skip_ref, arrived, held = rest
    near = (taps_ref, skip_ref) + kept
    x_ref = near[2]
    copies = [pltpu.make_async_copy(a, b, arrived.at[i]) for i, (a, b) in enumerate(zip(far, near))]
    for copy in copies:
        copy.start()
    lags, chans = taps_ref.shape
    copies[0].wait()
    copies[1].wait()
    pad = 2 * frames
    taps = taps_ref[...].astype(F32)
    table_ref[0:pad] = jnp.zeros((pad, cols, chans), F32)
    for lag in range(lags):
        tap = taps[lag : lag + 1] + (skip_ref[...] if lag == 0 else 0.0)
        table_ref[pad + lag] = jnp.broadcast_to(tap, (cols, chans))
    sites = rows * cols
    copies[2].wait()
    for lane in range(0, chans, LANES):
        span = slice(lane, lane + LANES)
        held[...] = x_ref[:, span].astype(F32)
        side_ref[:, span] = outer_column(held, frames * rows, cols)
        for d, field in enumerate(fields):
            totals = [None] * frames
            for s in range(frames):
                x = x_ref[s * sites : (s + 1) * sites, span].astype(F32).reshape(rows, cols, LANES)
                for t in range(s if d == 0 else 0, frames):
                    term = table_ref[pad + 2 * d * frames + t - s, :, span] * x
                    totals[t] = term if totals[t] is None else totals[t] + term
            for t in range(frames):
                field[t * sites : (t + 1) * sites, span] = totals[t].reshape(sites, LANES)
    for copy in copies[3:]:
        copy.wait()


def reordered(lines, rounds_h, back=False):
    if rounds_h > 1:
        return lines[:1] + lines[2:] + lines[1:2] if back else lines[:1] + lines[-1:] + lines[1:-1]
    odd = position("height")[0]
    return [jnp.where(odd, a, b) for a, b in zip(lines, lines[::-1])]


def column_kernel(frames, rows, cols, partner_ref, side_ref, out_ref, held):
    lines = frames * rows
    for lane in range(0, out_ref.shape[1], LANES):
        span = slice(lane, lane + LANES)
        held[...] = partner_ref[:, span].astype(F32)
        out_ref[:, span] = jnp.concatenate([side_ref[:, span], outer_column(held, lines, cols)]).astype(BF16)


def shift(frames):
    return jnp.where(second(), frames, -frames)


def with_partner(frames, rows, cols, d, field_ref, partner_ref, table_ref, span):
    sites = rows * cols
    base = 2 * frames + 2 * d * frames + shift(frames)
    totals = [field_ref[t * sites : (t + 1) * sites, span].reshape(rows, cols, LANES) for t in range(frames)]
    for s in range(frames):
        x = partner_ref[s * sites : (s + 1) * sites, span].astype(F32).reshape(rows, cols, LANES)
        for t in range(frames):
            totals[t] = totals[t] + table_ref[base + t - s, :, span] * x
    return totals


def later_kernel(frames, rows, cols, rounds_h, partner_ref, table_ref, *refs):
    fields, outs = refs[: len(refs) // 3], refs[len(refs) // 3 :]
    for d, field in enumerate(fields, 1):
        for lane in range(0, field.shape[1], LANES):
            span = slice(lane, lane + LANES)
            totals = with_partner(frames, rows, cols, d, field, partner_ref, table_ref, span)
            tiles = reordered([jnp.concatenate([t[r] for t in totals]) for r in range(rows)], rounds_h)
            outs[2 * d - 2][:, span] = jnp.concatenate(tiles[: rounds_h + 1]).astype(BF16)
            outs[2 * d - 1][:, span] = jnp.concatenate(tiles[rounds_h + 1 :]).astype(BF16)


def own_kernel(frames, rows, cols, after_ref, partner_ref, table_ref, field_ref, mine_ref):
    for lane in range(0, mine_ref.shape[1], LANES):
        span = slice(lane, lane + LANES)
        totals = with_partner(frames, rows, cols, 0, field_ref, partner_ref, table_ref, span)
        mine_ref[:, span] = jnp.concatenate(totals).reshape(mine_ref.shape[0], LANES)


def later(d, value):
    return jnp.where(lax.div(lax.axis_index("tm"), 2) >= d, value, jnp.zeros_like(value))


def add_column(frames, rows, d, totals, column, table_ref, span):
    base = 2 * frames + 2 * d * frames
    for t in range(2 * frames):
        for s in range(2 * frames):
            lag = t % frames - s % frames
            if t // frames == s // frames:
                if d == 0 and lag < 0:
                    continue
            else:
                lag = lag + (shift(frames) if t < frames else -shift(frames))
            totals[t] = totals[t] + table_ref[base + lag, :, span] * column[s * rows : (s + 1) * rows]
    return totals


def side_kernel(frames, rows, first, count, table_ref, *refs):
    arrived, (own_ref, other_ref) = refs[:count], refs[-2:]
    _, lower, upper = position("width")
    exists = jnp.where(on_right(), upper, lower)
    for lane in range(0, own_ref.shape[1], LANES):
        span = slice(lane, lane + LANES)
        totals = [jnp.zeros((rows, LANES), F32)] * (2 * frames)
        for d, ref in enumerate(arrived, first):
            totals = add_column(frames, rows, d, totals, later(d, ref[:, span].astype(F32)), table_ref, span)
        totals = [jnp.where(exists, total, jnp.zeros_like(total)) for total in totals]
        own_ref[:, span] = jnp.concatenate(totals[:frames])
        other_ref[:, span] = jnp.concatenate(totals[frames:]).astype(BF16)


def both_sides(own, other):
    right = on_right()
    return jnp.where(right, other, own), jnp.where(right, own, other)


def end_corners(frames, rows, own_ref, other_ref):
    sides = both_sides(own_ref[...], other_ref[...].astype(F32))
    pick = lambda r: [side[t * rows + r : t * rows + r + 1] for side in sides for t in range(frames)]
    return [jnp.concatenate(pick(r)) for r in (0, rows - 1)]


def border_kernel(frames, rows, cols, mine_ref, own_ref, other_ref, *outs):
    sites = rows * cols
    odd, _, _ = position("height")
    corners = end_corners(frames, rows, own_ref, other_ref)
    lines = []
    for r in (0, rows - 1):
        lines.append(jnp.concatenate([mine_ref[t * sites + r * cols : t * sites + (r + 1) * cols] for t in range(frames)]))
    ends = [jnp.concatenate(pair) for pair in zip(lines, corners)]
    for k, out in enumerate(outs):
        out[...] = jnp.where(odd, *(ends[::-1] if k else ends)).astype(BF16)


def before_kernel(frames, rows, cols, own_ref, other_ref, *refs):
    rounds_h = refs[0].shape[0] // (frames * cols) - 1
    firsts, outs = refs[:-rounds_h], refs[-rounds_h:]
    size = frames * cols
    odd, _, _ = position("height")
    corners = end_corners(frames, rows, own_ref, other_ref)
    line = 0.0
    for d, ref in enumerate(firsts, 1):
        line = line + later(d, ref[: rounds_h * size].astype(F32))
    for k, out in enumerate(outs):
        if rounds_h > 1:
            pair = line[:size], line[size:]
            row = jnp.where(odd, *(pair[::-1] if k else pair))
        else:
            row = line
        out[...] = jnp.concatenate([row, jnp.where(odd, *(corners[::-1] if k else corners))]).astype(BF16)


def shifted(line, left, right):
    cols = line.shape[0]
    place = lax.broadcasted_iota(jnp.int32, line.shape, 0)
    before = jnp.where(place == 0, left, pltpu.roll(line, 1, 0))
    after = jnp.where(place == cols - 1, right, pltpu.roll(line, cols - 1, 0))
    return before, line, after


def projected(mixed, gate, wv_ref, wo_ref):
    value = jnp.dot(mixed, wv_ref[...], preferred_element_type=F32)
    hidden = (value * gate).astype(BF16)
    return jnp.dot(hidden, wo_ref[...], preferred_element_type=F32).astype(BF16)


def filtered(lines, lefts, rights, taps):
    totals = [None] * len(lines)
    for r, line in enumerate(lines):
        near = shifted(line, lefts[r], rights[r])
        for a in range(3):
            to = r + 1 - a
            if 0 <= to < len(lines):
                term = near[0] * taps[a][0] + near[1] * taps[a][1] + near[2] * taps[a][2]
                totals[to] = term if totals[to] is None else totals[to] + term
    return totals


def taps_of(taps_ref, span):
    return [[taps_ref[a, b : b + 1, span] for b in range(3)] for a in range(3)]


def inner_kernel(
    frames, rows, cols, mine_ref, own_ref, other_ref, taps_ref, gate_ref, wv_ref, wo_ref, out_ref, totals_ref, mixed
):
    sites = rows * cols
    for lane in range(0, mine_ref.shape[1], LANES):
        span = slice(lane, lane + LANES)
        taps = taps_of(taps_ref, span)
        low, high = both_sides(own_ref[:, span], other_ref[:, span].astype(F32))
        for t in range(frames):
            at = t * sites
            lines = [mine_ref[at + r * cols : at + (r + 1) * cols, span] for r in range(rows)]
            lefts = [low[t * rows + r : t * rows + r + 1] for r in range(rows)]
            rights = [high[t * rows + r : t * rows + r + 1] for r in range(rows)]
            total = jnp.concatenate(filtered(lines, lefts, rights, taps))
            totals_ref[at : at + sites, span] = total
            mixed[at : at + sites, span] = total.astype(BF16)
    out_ref[...] = projected(mixed[...], gate_ref[...], wv_ref, wo_ref)


def has_earlier():
    return lax.div(lax.axis_index("tm"), 2) > 0


def block_kernel(frames, rows, cols, rounds_h, inner_ref, totals_ref, taps_ref, gate_ref, wv_ref, wo_ref, *refs):
    own_ref, other_ref, *parts, out_ref, sums_ref, mixed = refs
    firsts, rests = parts[: len(parts) // 2], parts[len(parts) // 2 :]
    sites = rows * cols
    size = frames * cols

    @pl.when(has_earlier())
    def _():
        for lane in range(0, out_ref.shape[1], LANES):
            span = slice(lane, lane + LANES)
            taps = taps_of(taps_ref, span)
            low, high = both_sides(own_ref[:, span], other_ref[:, span].astype(F32))
            lines = [jnp.zeros((size, LANES), F32)] * rows
            for d, (first, rest) in enumerate(zip(firsts, rests), 1):
                more = [first[i * size : (i + 1) * size, span].astype(F32) for i in range(rounds_h + 1)]
                more += [rest[i * size : (i + 1) * size, span].astype(F32) for i in range(rows - rounds_h - 1)]
                more = reordered(more, rounds_h, back=True)
                lines = [line + later(d, other) for line, other in zip(lines, more)]
            for t in range(frames):
                at = t * sites
                lefts = [low[t * rows + r : t * rows + r + 1] for r in range(rows)]
                rights = [high[t * rows + r : t * rows + r + 1] for r in range(rows)]
                total = filtered([line[t * cols : (t + 1) * cols] for line in lines], lefts, rights, taps)
                total = jnp.concatenate(total) + totals_ref[at : at + sites, span]
                sums_ref[at : at + sites, span] = total
                mixed[at : at + sites, span] = total.astype(BF16)
        out_ref[...] = projected(mixed[...], gate_ref[...], wv_ref, wo_ref)


def complete(frames, rows, cols, inner_ref, totals_ref, taps_ref, gate_ref, wv_ref, wo_ref, ends, out_ref, held, done):
    sites = rows * cols
    size = frames * cols
    group = 2 * cols
    odd, lower, upper = position("height")
    copies = []

    def send(source, start, count):
        copy = pltpu.make_async_copy(source, out_ref.at[pl.ds(start, count)], done.at[len(copies)])
        copy.start()
        copies.append(copy)

    for t in range(frames):
        inside = t * sites + group
        send(inner_ref.at[pl.ds(inside, sites - 2 * group)], inside, sites - 2 * group)
        if len(ends) == 1:
            kept = pl.multiple_of(t * sites + jnp.where(odd, sites - group, 0), group)
            send(inner_ref.at[pl.ds(kept, group)], kept, group)
    mixed, gate = [], []
    for k, end in enumerate(ends):
        first = jnp.logical_not(odd) if k else odd
        lefts, rights = end[size : size + frames], end[size + frames : size + 2 * frames]
        exists = jnp.where(first, lower, upper)
        tap = jnp.where(first, taps_ref[0], taps_ref[2])
        for t in range(frames):
            near = shifted(end[t * cols : (t + 1) * cols], lefts[t : t + 1], rights[t : t + 1])
            more = near[0] * tap[0:1] + near[1] * tap[1:2] + near[2] * tap[2:3]
            i, j = t * sites, (t + 1) * sites - cols
            total = jnp.where(first, totals_ref[i : i + cols], totals_ref[j : j + cols])
            mixed.append(total + jnp.where(exists, more, jnp.zeros_like(more)))
            gate.append(jnp.where(first, gate_ref[i : i + cols], gate_ref[j : j + cols]))
    out = projected(jnp.concatenate(mixed).astype(BF16), jnp.concatenate(gate), wv_ref, wo_ref)
    for k in range(len(ends)):
        first = jnp.logical_not(odd) if k else odd
        for t in range(frames):
            row = k * size + t * cols
            new = out[row : row + cols].astype(F32)
            top = inner_ref[t * sites : t * sites + group].astype(F32)
            bottom = inner_ref[(t + 1) * sites - group : (t + 1) * sites].astype(F32)
            lines = jnp.where(first, new, bottom[:cols]), jnp.where(first, top[cols:], new)
            held[2 * row : 2 * row + group] = jnp.concatenate(lines).astype(BF16)
            start = pl.multiple_of(t * sites + jnp.where(first, 0, sites - group), group)
            send(held.at[pl.ds(2 * row, group)], start, group)
    for copy in copies:
        copy.wait()


def first_kernel(frames, rows, cols, inner_ref, totals_ref, taps_ref, gate_ref, wv_ref, wo_ref, *refs):
    *ends, out_ref, held, done = refs

    @pl.when(jnp.logical_not(has_earlier()))
    def _():
        values = [end[...].astype(F32) for end in ends]
        complete(
            frames, rows, cols, inner_ref, totals_ref, taps_ref, gate_ref, wv_ref, wo_ref, values, out_ref, held, done
        )


def last_kernel(frames, rows, cols, before_ref, inner_ref, totals_ref, taps_ref, gate_ref, wv_ref, wo_ref, *refs):
    *ends, out_ref, held, done = refs
    own, earlier = ends[: len(ends) // 2], ends[len(ends) // 2 :]

    @pl.when(has_earlier())
    def _():
        values = [a[...].astype(F32) + b[...].astype(F32) for a, b in zip(own, earlier)]
        complete(
            frames, rows, cols, inner_ref, totals_ref, taps_ref, gate_ref, wv_ref, wo_ref, values, out_ref, held, done
        )


def body(latents, spatial_taps, kernel_taps, skip_gain, gate_weight, value_weight, out_weight):
    frames, rows, cols, chans = latents.shape
    lags = kernel_taps.shape[0]
    n_t, n_h, n_w = lax.axis_size("tm"), lax.axis_size("height"), lax.axis_size("width")
    chips = n_t // 2
    block = frames * rows * cols
    shape = jax.ShapeDtypeStruct
    x = latents.reshape(block, chans)

    partner = lax.ppermute(x, "tm", [(i, i ^ 1) for i in range(n_t)])
    lines = frames * rows
    field = shape((block, chans), F32)
    inputs = [kernel_taps, skip_gain.reshape(1, chans), x, gate_weight, spatial_taps, value_weight, out_weight]
    near_x, near_gate, taps, value_weight, out_weight, table, side, *fields = call(
        functools.partial(early_kernel, frames, rows, cols, len(inputs)),
        "early",
        [shape(a.shape, a.dtype) for a in inputs[2:]]
        + [shape((lags + 2 * frames, cols, chans), F32), shape((lines, chans), F32)]
        + [field] * chips,
        [pltpu.VMEM(a.shape, a.dtype) for a in inputs[:2]]
        + [pltpu.SemaphoreType.DMA((len(inputs),)), pltpu.VMEM((block, LANES), F32)],
        inputs,
        far=len(inputs),
    )
    h_rounds = swaps("height")
    (column,) = call(
        functools.partial(column_kernel, frames, rows, cols),
        "column",
        [shape((2 * lines, chans), BF16)],
        [pltpu.VMEM((block, LANES), F32)],
        [partner, side],
    )
    parts = [shape((n * frames * cols, chans), BF16) for n in (len(h_rounds) + 1, rows - len(h_rounds) - 1)]
    sent = call(
        functools.partial(later_kernel, frames, rows, cols, len(h_rounds)),
        "later",
        parts * (chips - 1),
        [],
        [partner, table] + fields[1:],
        2 * (chips - 1) * frames * x.size,
    )
    columns, firsts, rests = [], [], []
    for d in range(chips):
        route = []
        for i in range(n_t):
            for h in range(n_h):
                for j in range(n_w):
                    to, beside = facing(i % 2, j, n_w), h
                    if i // 2 + d >= chips:
                        to = j
                    elif to == j and n_h % 2 == 0:
                        beside = h ^ 1
                    source = (i * n_h + h) * n_w + j
                    route.append((source, ((i + 2 * d) % n_t * n_h + beside) * n_w + to))
        columns.append(lax.ppermute(column, ("tm", "height", "width"), route))
    for d in range(1, chips):
        route = [(i, (i + 2 * d) % n_t) for i in range(n_t)]
        firsts.append(lax.ppermute(sent[2 * d - 2], "tm", route))
        rests.append(lax.ppermute(sent[2 * d - 1], "tm", route))

    swap = [(i, i ^ 1) for i in range(n_t)]
    both = [shape((lines, chans), F32), shape((lines, chans), BF16)]
    own, other = call(functools.partial(side_kernel, frames, rows, 0, 1), "side", both, [], [table, columns[0]], LATER)
    (mine,) = call(
        functools.partial(own_kernel, frames, rows, cols),
        "own",
        [field],
        [],
        [own, partner, table, fields[0]],
        2 * frames * x.size,
    )
    (gate,) = call(gate_kernel, "gate", [field], [], [own, near_x, near_gate])
    other = lax.ppermute(other, "tm", swap)
    end = [shape((frames * cols + 2 * frames, chans), BF16)] * len(h_rounds)
    ends = call(functools.partial(border_kernel, frames, rows, cols), "border", end, [], [mine, own, other])
    ends = [lax.ppermute(e, "height", pairs) for e, pairs in zip(ends, h_rounds)]
    if chips > 1:
        own_d, other_d = call(
            functools.partial(side_kernel, frames, rows, 1, chips - 1),
            "beside",
            both,
            [],
            [table] + columns[1:] + [mine, gate],
            LATER,
        )
        other_d = lax.ppermute(other_d, "tm", swap)
        earlier = call(functools.partial(before_kernel, frames, rows, cols), "before", end, [], [own_d, other_d] + firsts)
        earlier = [lax.ppermute(e, "height", pairs) for e, pairs in zip(earlier, h_rounds)]

    inner, totals = call(
        functools.partial(inner_kernel, frames, rows, cols),
        "inner",
        [shape((block, chans), BF16), field],
        [pltpu.VMEM((block, chans), BF16)],
        [mine, own, other, taps, gate, value_weight, out_weight],
        4 * block * chans * chans,
    )
    held = [pltpu.VMEM((2 * len(h_rounds) * frames * cols, chans), BF16), pltpu.SemaphoreType.DMA((3 * frames,))]
    weights = [taps, gate, value_weight, out_weight]
    out = shape((block, chans), BF16)
    (first,) = call(
        functools.partial(first_kernel, frames, rows, cols),
        "first",
        [out],
        held,
        [inner, totals] + weights + ends,
        far_outs=1,
    )
    if chips > 1:
        inner, totals = call(
            functools.partial(block_kernel, frames, rows, cols, len(h_rounds)),
            "block",
            [out, field],
            [pltpu.VMEM((block, chans), BF16)],
            [inner, totals] + weights + [own_d, other_d] + firsts + rests,
            aliases={0: 0, 1: 1},
        )
        (first,) = call(
            functools.partial(last_kernel, frames, rows, cols),
            "last",
            [out],
            held,
            [first, inner, totals] + weights + ends + earlier,
            far=1,
            far_outs=1,
            aliases={0: 0},
        )
    return first.reshape(latents.shape)


def solution(mesh):
    in_specs = (P("tm", "height", "width", None), P(), P(), P(), P(), P(), P())
    out_specs = P("tm", "height", "width", None)
    return jax.shard_map(body, mesh=mesh, in_specs=in_specs, out_specs=out_specs, check_vma=False)
```

```python
import functools

import jax
import jax.numpy as jnp
from jax import lax
from jax.experimental import pallas as pl
from jax.experimental.pallas import tpu as pltpu
from jax.sharding import PartitionSpec as P

LANES = 128
LATER = 8 * 10**9
F32, BF16 = jnp.float32, jnp.bfloat16
VMEM = pl.BlockSpec(memory_space=pltpu.VMEM)
HBM = pl.BlockSpec(memory_space=pltpu.HBM)


def call(kernel, name, outs, scratch, operands, flops=0, exps=0, far=0, far_outs=0, aliases={}):
    operands = [pltpu.with_memory_space_constraint(a, pltpu.HBM) for a in operands[:far]] + list(operands[far:])
    moved = sum(a.size * a.dtype.itemsize for a in operands) + sum(a.size * a.dtype.itemsize for a in outs)
    return pl.pallas_call(
        kernel,
        out_shape=tuple(outs),
        in_specs=[HBM] * far + [VMEM] * (len(operands) - far),
        out_specs=(HBM,) * far_outs + (VMEM,) * (len(outs) - far_outs),
        scratch_shapes=scratch,
        input_output_aliases=aliases,
        compiler_params=pltpu.CompilerParams(vmem_limit_bytes=24 * 1024 * 1024),
        cost_estimate=pl.CostEstimate(flops=flops, bytes_accessed=moved, transcendentals=exps),
        name=name,
    )(*operands)


def swaps(axis):
    n = lax.axis_size(axis)
    rounds = []
    for first in range(2 if n > 2 else 1):
        to = list(range(n))
        for i in range(first, n - 1, 2):
            to[i], to[i + 1] = i + 1, i
        rounds.append(list(enumerate(to)))
    return rounds


def position(axis):
    i, n = lax.axis_index(axis), lax.axis_size(axis)
    return lax.rem(i, 2) == 1, i > 0, i < n - 1


def second():
    return lax.rem(lax.axis_index("tm"), 2) == 1


def on_right():
    return lax.rem(lax.axis_index("tm") + lax.axis_index("width"), 2) == 0


def facing(core, column, columns):
    to = column + (1 if (core + column) % 2 == 0 else -1)
    return to if 0 <= to < columns else column


def outer_column(ref, lines, cols):
    return jnp.where(on_right(), ref[pl.ds(cols - 1, lines, stride=cols), :], ref[pl.ds(0, lines, stride=cols), :])


def gate_kernel(after_ref, x_ref, w_ref, gate_ref):
    v = jnp.dot(x_ref[...], w_ref[...], preferred_element_type=F32)
    gate_ref[...] = v / (1.0 + jnp.exp(-v))


def early_kernel(frames, rows, cols, count, *refs):
    far, kept, rest = refs[:count], refs[count : 2 * count - 2], refs[2 * count - 2 :]
    table_ref, side_ref, *fields, taps_ref, skip_ref, arrived, held = rest
    near = (taps_ref, skip_ref) + kept
    x_ref = near[2]
    copies = [pltpu.make_async_copy(a, b, arrived.at[i]) for i, (a, b) in enumerate(zip(far, near))]
    for copy in copies:
        copy.start()
    lags, chans = taps_ref.shape
    copies[0].wait()
    copies[1].wait()
    pad = 2 * frames
    taps = taps_ref[...].astype(F32)
    table_ref[0:pad] = jnp.zeros((pad, cols, chans), F32)
    for lag in range(lags):
        tap = taps[lag : lag + 1] + (skip_ref[...] if lag == 0 else 0.0)
        table_ref[pad + lag] = jnp.broadcast_to(tap, (cols, chans))
    sites = rows * cols
    copies[2].wait()
    for lane in range(0, chans, LANES):
        span = slice(lane, lane + LANES)
        held[...] = x_ref[:, span].astype(F32)
        side_ref[:, span] = outer_column(held, frames * rows, cols)
        for d, field in enumerate(fields):
            totals = [None] * frames
            for s in range(frames):
                x = x_ref[s * sites : (s + 1) * sites, span].astype(F32).reshape(rows, cols, LANES)
                for t in range(s if d == 0 else 0, frames):
                    term = table_ref[pad + 2 * d * frames + t - s, :, span] * x
                    totals[t] = term if totals[t] is None else totals[t] + term
            for t in range(frames):
                field[t * sites : (t + 1) * sites, span] = totals[t].reshape(sites, LANES)
    for copy in copies[3:]:
        copy.wait()


def reordered(lines, rounds_h, back=False):
    if rounds_h > 1:
        return lines[:1] + lines[2:] + lines[1:2] if back else lines[:1] + lines[-1:] + lines[1:-1]
    odd = position("height")[0]
    return [jnp.where(odd, a, b) for a, b in zip(lines, lines[::-1])]


def column_kernel(frames, rows, cols, partner_ref, side_ref, out_ref, held):
    lines = frames * rows
    for lane in range(0, out_ref.shape[1], LANES):
        span = slice(lane, lane + LANES)
        held[...] = partner_ref[:, span].astype(F32)
        out_ref[:, span] = jnp.concatenate([side_ref[:, span], outer_column(held, lines, cols)]).astype(BF16)


def shift(frames):
    return jnp.where(second(), frames, -frames)


def with_partner(frames, rows, cols, d, field_ref, partner_ref, table_ref, span):
    sites = rows * cols
    base = 2 * frames + 2 * d * frames + shift(frames)
    totals = [field_ref[t * sites : (t + 1) * sites, span].reshape(rows, cols, LANES) for t in range(frames)]
    for s in range(frames):
        x = partner_ref[s * sites : (s + 1) * sites, span].astype(F32).reshape(rows, cols, LANES)
        for t in range(frames):
            totals[t] = totals[t] + table_ref[base + t - s, :, span] * x
    return totals


def later_kernel(frames, rows, cols, rounds_h, partner_ref, table_ref, *refs):
    fields, outs = refs[: len(refs) // 3], refs[len(refs) // 3 :]
    for d, field in enumerate(fields, 1):
        for lane in range(0, field.shape[1], LANES):
            span = slice(lane, lane + LANES)
            totals = with_partner(frames, rows, cols, d, field, partner_ref, table_ref, span)
            tiles = reordered([jnp.concatenate([t[r] for t in totals]) for r in range(rows)], rounds_h)
            outs[2 * d - 2][:, span] = jnp.concatenate(tiles[: rounds_h + 1]).astype(BF16)
            outs[2 * d - 1][:, span] = jnp.concatenate(tiles[rounds_h + 1 :]).astype(BF16)


def own_kernel(frames, rows, cols, after_ref, partner_ref, table_ref, field_ref, mine_ref):
    for lane in range(0, mine_ref.shape[1], LANES):
        span = slice(lane, lane + LANES)
        totals = with_partner(frames, rows, cols, 0, field_ref, partner_ref, table_ref, span)
        mine_ref[:, span] = jnp.concatenate(totals).reshape(mine_ref.shape[0], LANES)


def later(d, value):
    return jnp.where(lax.div(lax.axis_index("tm"), 2) >= d, value, jnp.zeros_like(value))


def add_column(frames, rows, d, totals, column, table_ref, span):
    base = 2 * frames + 2 * d * frames
    for t in range(2 * frames):
        for s in range(2 * frames):
            lag = t % frames - s % frames
            if t // frames == s // frames:
                if d == 0 and lag < 0:
                    continue
            else:
                lag = lag + (shift(frames) if t < frames else -shift(frames))
            totals[t] = totals[t] + table_ref[base + lag, :, span] * column[s * rows : (s + 1) * rows]
    return totals


def side_kernel(frames, rows, first, count, table_ref, *refs):
    arrived, (own_ref, other_ref) = refs[:count], refs[-2:]
    _, lower, upper = position("width")
    exists = jnp.where(on_right(), upper, lower)
    for lane in range(0, own_ref.shape[1], LANES):
        span = slice(lane, lane + LANES)
        totals = [jnp.zeros((rows, LANES), F32)] * (2 * frames)
        for d, ref in enumerate(arrived, first):
            totals = add_column(frames, rows, d, totals, later(d, ref[:, span].astype(F32)), table_ref, span)
        totals = [jnp.where(exists, total, jnp.zeros_like(total)) for total in totals]
        own_ref[:, span] = jnp.concatenate(totals[:frames])
        other_ref[:, span] = jnp.concatenate(totals[frames:]).astype(BF16)


def both_sides(own, other):
    right = on_right()
    return jnp.where(right, other, own), jnp.where(right, own, other)


def end_corners(frames, rows, own_ref, other_ref):
    sides = both_sides(own_ref[...], other_ref[...].astype(F32))
    pick = lambda r: [side[t * rows + r : t * rows + r + 1] for side in sides for t in range(frames)]
    return [jnp.concatenate(pick(r)) for r in (0, rows - 1)]


def border_kernel(frames, rows, cols, mine_ref, own_ref, other_ref, *outs):
    sites = rows * cols
    odd, _, _ = position("height")
    corners = end_corners(frames, rows, own_ref, other_ref)
    lines = []
    for r in (0, rows - 1):
        lines.append(jnp.concatenate([mine_ref[t * sites + r * cols : t * sites + (r + 1) * cols] for t in range(frames)]))
    ends = [jnp.concatenate(pair) for pair in zip(lines, corners)]
    for k, out in enumerate(outs):
        out[...] = jnp.where(odd, *(ends[::-1] if k else ends)).astype(BF16)


def before_kernel(frames, rows, cols, own_ref, other_ref, *refs):
    rounds_h = refs[0].shape[0] // (frames * cols) - 1
    firsts, outs = refs[:-rounds_h], refs[-rounds_h:]
    size = frames * cols
    odd, _, _ = position("height")
    corners = end_corners(frames, rows, own_ref, other_ref)
    line = 0.0
    for d, ref in enumerate(firsts, 1):
        line = line + later(d, ref[: rounds_h * size].astype(F32))
    for k, out in enumerate(outs):
        if rounds_h > 1:
            pair = line[:size], line[size:]
            row = jnp.where(odd, *(pair[::-1] if k else pair))
        else:
            row = line
        out[...] = jnp.concatenate([row, jnp.where(odd, *(corners[::-1] if k else corners))]).astype(BF16)


def shifted(line, left, right):
    cols = line.shape[0]
    place = lax.broadcasted_iota(jnp.int32, line.shape, 0)
    before = jnp.where(place == 0, left, pltpu.roll(line, 1, 0))
    after = jnp.where(place == cols - 1, right, pltpu.roll(line, cols - 1, 0))
    return before, line, after


def projected(mixed, gate, wv_ref, wo_ref):
    value = jnp.dot(mixed, wv_ref[...], preferred_element_type=F32)
    hidden = (value * gate).astype(BF16)
    return jnp.dot(hidden, wo_ref[...], preferred_element_type=F32).astype(BF16)


def filtered(lines, lefts, rights, taps):
    totals = [None] * len(lines)
    for r, line in enumerate(lines):
        near = shifted(line, lefts[r], rights[r])
        for a in range(3):
            to = r + 1 - a
            if 0 <= to < len(lines):
                term = near[0] * taps[a][0] + near[1] * taps[a][1] + near[2] * taps[a][2]
                totals[to] = term if totals[to] is None else totals[to] + term
    return totals


def taps_of(taps_ref, span):
    return [[taps_ref[a, b : b + 1, span] for b in range(3)] for a in range(3)]


def inner_kernel(
    frames, rows, cols, mine_ref, own_ref, other_ref, taps_ref, gate_ref, wv_ref, wo_ref, out_ref, totals_ref, mixed
):
    sites = rows * cols
    for lane in range(0, mine_ref.shape[1], LANES):
        span = slice(lane, lane + LANES)
        taps = taps_of(taps_ref, span)
        low, high = both_sides(own_ref[:, span], other_ref[:, span].astype(F32))
        for t in range(frames):
            at = t * sites
            lines = [mine_ref[at + r * cols : at + (r + 1) * cols, span] for r in range(rows)]
            lefts = [low[t * rows + r : t * rows + r + 1] for r in range(rows)]
            rights = [high[t * rows + r : t * rows + r + 1] for r in range(rows)]
            total = jnp.concatenate(filtered(lines, lefts, rights, taps))
            totals_ref[at : at + sites, span] = total
            mixed[at : at + sites, span] = total.astype(BF16)
    out_ref[...] = projected(mixed[...], gate_ref[...], wv_ref, wo_ref)


def has_earlier():
    return lax.div(lax.axis_index("tm"), 2) > 0


def block_kernel(frames, rows, cols, rounds_h, inner_ref, totals_ref, taps_ref, gate_ref, wv_ref, wo_ref, *refs):
    own_ref, other_ref, *parts, out_ref, sums_ref, mixed = refs
    firsts, rests = parts[: len(parts) // 2], parts[len(parts) // 2 :]
    sites = rows * cols
    size = frames * cols

    @pl.when(has_earlier())
    def _():
        for lane in range(0, out_ref.shape[1], LANES):
            span = slice(lane, lane + LANES)
            taps = taps_of(taps_ref, span)
            low, high = both_sides(own_ref[:, span], other_ref[:, span].astype(F32))
            lines = [jnp.zeros((size, LANES), F32)] * rows
            for d, (first, rest) in enumerate(zip(firsts, rests), 1):
                more = [first[i * size : (i + 1) * size, span].astype(F32) for i in range(rounds_h + 1)]
                more += [rest[i * size : (i + 1) * size, span].astype(F32) for i in range(rows - rounds_h - 1)]
                more = reordered(more, rounds_h, back=True)
                lines = [line + later(d, other) for line, other in zip(lines, more)]
            for t in range(frames):
                at = t * sites
                lefts = [low[t * rows + r : t * rows + r + 1] for r in range(rows)]
                rights = [high[t * rows + r : t * rows + r + 1] for r in range(rows)]
                total = filtered([line[t * cols : (t + 1) * cols] for line in lines], lefts, rights, taps)
                total = jnp.concatenate(total) + totals_ref[at : at + sites, span]
                sums_ref[at : at + sites, span] = total
                mixed[at : at + sites, span] = total.astype(BF16)
        out_ref[...] = projected(mixed[...], gate_ref[...], wv_ref, wo_ref)


def complete(frames, rows, cols, inner_ref, totals_ref, taps_ref, gate_ref, wv_ref, wo_ref, ends, out_ref, held, done):
    sites = rows * cols
    size = frames * cols
    odd, lower, upper = position("height")
    held[...] = inner_ref[...]
    mixed, gate = [], []
    for k, end in enumerate(ends):
        first = jnp.logical_not(odd) if k else odd
        lefts, rights = end[size : size + frames], end[size + frames : size + 2 * frames]
        exists = jnp.where(first, lower, upper)
        tap = jnp.where(first, taps_ref[0], taps_ref[2])
        for t in range(frames):
            near = shifted(end[t * cols : (t + 1) * cols], lefts[t : t + 1], rights[t : t + 1])
            more = near[0] * tap[0:1] + near[1] * tap[1:2] + near[2] * tap[2:3]
            i, j = t * sites, (t + 1) * sites - cols
            total = jnp.where(first, totals_ref[i : i + cols], totals_ref[j : j + cols])
            mixed.append(total + jnp.where(exists, more, jnp.zeros_like(more)))
            gate.append(jnp.where(first, gate_ref[i : i + cols], gate_ref[j : j + cols]))
    out = projected(jnp.concatenate(mixed).astype(BF16), jnp.concatenate(gate), wv_ref, wo_ref)
    for t in range(frames):
        new = [out[k * size + t * cols : k * size + (t + 1) * cols].astype(F32) for k in range(len(ends))]
        first, final = t * sites, (t + 1) * sites - 2 * cols
        top = inner_ref[first : first + 2 * cols].astype(F32)
        bottom = inner_ref[final : final + 2 * cols].astype(F32)
        other = new[1] if len(new) > 1 else None
        row = jnp.where(odd, new[0], top[:cols] if other is None else other)
        held[first : first + 2 * cols] = jnp.concatenate([row, top[cols:]]).astype(BF16)
        row = jnp.where(odd, bottom[cols:] if other is None else other, new[0])
        held[final : final + 2 * cols] = jnp.concatenate([bottom[:cols], row]).astype(BF16)
    copy = pltpu.make_async_copy(held, out_ref, done)
    copy.start()
    copy.wait()


def first_kernel(frames, rows, cols, inner_ref, totals_ref, taps_ref, gate_ref, wv_ref, wo_ref, *refs):
    *ends, out_ref, held, done = refs

    @pl.when(jnp.logical_not(has_earlier()))
    def _():
        values = [end[...].astype(F32) for end in ends]
        complete(
            frames, rows, cols, inner_ref, totals_ref, taps_ref, gate_ref, wv_ref, wo_ref, values, out_ref, held, done
        )


def last_kernel(frames, rows, cols, before_ref, inner_ref, totals_ref, taps_ref, gate_ref, wv_ref, wo_ref, *refs):
    *ends, out_ref, held, done = refs
    own, earlier = ends[: len(ends) // 2], ends[len(ends) // 2 :]

    @pl.when(has_earlier())
    def _():
        values = [a[...].astype(F32) + b[...].astype(F32) for a, b in zip(own, earlier)]
        complete(
            frames, rows, cols, inner_ref, totals_ref, taps_ref, gate_ref, wv_ref, wo_ref, values, out_ref, held, done
        )


def body(latents, spatial_taps, kernel_taps, skip_gain, gate_weight, value_weight, out_weight):
    frames, rows, cols, chans = latents.shape
    lags = kernel_taps.shape[0]
    n_t, n_h, n_w = lax.axis_size("tm"), lax.axis_size("height"), lax.axis_size("width")
    chips = n_t // 2
    block = frames * rows * cols
    shape = jax.ShapeDtypeStruct
    x = latents.reshape(block, chans)

    partner = lax.ppermute(x, "tm", [(i, i ^ 1) for i in range(n_t)])
    lines = frames * rows
    field = shape((block, chans), F32)
    inputs = [kernel_taps, skip_gain.reshape(1, chans), x, gate_weight, spatial_taps, value_weight, out_weight]
    near_x, near_gate, taps, value_weight, out_weight, table, side, *fields = call(
        functools.partial(early_kernel, frames, rows, cols, len(inputs)),
        "early",
        [shape(a.shape, a.dtype) for a in inputs[2:]]
        + [shape((lags + 2 * frames, cols, chans), F32), shape((lines, chans), F32)]
        + [field] * chips,
        [pltpu.VMEM(a.shape, a.dtype) for a in inputs[:2]]
        + [pltpu.SemaphoreType.DMA((len(inputs),)), pltpu.VMEM((block, LANES), F32)],
        inputs,
        far=len(inputs),
    )
    h_rounds = swaps("height")
    (column,) = call(
        functools.partial(column_kernel, frames, rows, cols),
        "column",
        [shape((2 * lines, chans), BF16)],
        [pltpu.VMEM((block, LANES), F32)],
        [partner, side],
    )
    parts = [shape((n * frames * cols, chans), BF16) for n in (len(h_rounds) + 1, rows - len(h_rounds) - 1)]
    sent = call(
        functools.partial(later_kernel, frames, rows, cols, len(h_rounds)),
        "later",
        parts * (chips - 1),
        [],
        [partner, table] + fields[1:],
        2 * (chips - 1) * frames * x.size,
    )
    columns, firsts, rests = [], [], []
    for d in range(chips):
        route = []
        for i in range(n_t):
            for h in range(n_h):
                for j in range(n_w):
                    to, beside = facing(i % 2, j, n_w), h
                    if i // 2 + d >= chips:
                        to = j
                    elif to == j and n_h % 2 == 0:
                        beside = h ^ 1
                    source = (i * n_h + h) * n_w + j
                    route.append((source, ((i + 2 * d) % n_t * n_h + beside) * n_w + to))
        columns.append(lax.ppermute(column, ("tm", "height", "width"), route))
    for d in range(1, chips):
        route = [(i, (i + 2 * d) % n_t) for i in range(n_t)]
        firsts.append(lax.ppermute(sent[2 * d - 2], "tm", route))
        rests.append(lax.ppermute(sent[2 * d - 1], "tm", route))

    swap = [(i, i ^ 1) for i in range(n_t)]
    both = [shape((lines, chans), F32), shape((lines, chans), BF16)]
    own, other = call(functools.partial(side_kernel, frames, rows, 0, 1), "side", both, [], [table, columns[0]], LATER)
    (mine,) = call(
        functools.partial(own_kernel, frames, rows, cols),
        "own",
        [field],
        [],
        [own, partner, table, fields[0]],
        2 * frames * x.size,
    )
    (gate,) = call(gate_kernel, "gate", [field], [], [own, near_x, near_gate])
    other = lax.ppermute(other, "tm", swap)
    end = [shape((frames * cols + 2 * frames, chans), BF16)] * len(h_rounds)
    ends = call(functools.partial(border_kernel, frames, rows, cols), "border", end, [], [mine, own, other])
    ends = [lax.ppermute(e, "height", pairs) for e, pairs in zip(ends, h_rounds)]
    if chips > 1:
        own_d, other_d = call(
            functools.partial(side_kernel, frames, rows, 1, chips - 1),
            "beside",
            both,
            [],
            [table] + columns[1:] + [mine, gate],
            LATER,
        )
        other_d = lax.ppermute(other_d, "tm", swap)
        earlier = call(functools.partial(before_kernel, frames, rows, cols), "before", end, [], [own_d, other_d] + firsts)
        earlier = [lax.ppermute(e, "height", pairs) for e, pairs in zip(earlier, h_rounds)]

    inner, totals = call(
        functools.partial(inner_kernel, frames, rows, cols),
        "inner",
        [shape((block, chans), BF16), field],
        [pltpu.VMEM((block, chans), BF16)],
        [mine, own, other, taps, gate, value_weight, out_weight],
        4 * block * chans * chans,
    )
    held = [pltpu.VMEM((block, chans), BF16), pltpu.SemaphoreType.DMA]
    weights = [taps, gate, value_weight, out_weight]
    out = shape((block, chans), BF16)
    (first,) = call(
        functools.partial(first_kernel, frames, rows, cols),
        "first",
        [out],
        held,
        [inner, totals] + weights + ends,
        far_outs=1,
    )
    if chips > 1:
        inner, totals = call(
            functools.partial(block_kernel, frames, rows, cols, len(h_rounds)),
            "block",
            [out, field],
            held[:1],
            [inner, totals] + weights + [own_d, other_d] + firsts + rests,
            aliases={0: 0, 1: 1},
        )
        (first,) = call(
            functools.partial(last_kernel, frames, rows, cols),
            "last",
            [out],
            held,
            [first, inner, totals] + weights + ends + earlier,
            far=1,
            far_outs=1,
            aliases={0: 0},
        )
    return first.reshape(latents.shape)


def solution(mesh):
    in_specs = (P("tm", "height", "width", None), P(), P(), P(), P(), P(), P())
    out_specs = P("tm", "height", "width", None)
    return jax.shard_map(body, mesh=mesh, in_specs=in_specs, out_specs=out_specs, check_vma=False)
```

```python
import functools

import jax
import jax.numpy as jnp
from jax import lax
from jax.experimental import pallas as pl
from jax.experimental.pallas import tpu as pltpu
from jax.sharding import PartitionSpec as P

LANES = 128
LATER = 8 * 10**9
F32, BF16 = jnp.float32, jnp.bfloat16
VMEM = pl.BlockSpec(memory_space=pltpu.VMEM)
HBM = pl.BlockSpec(memory_space=pltpu.HBM)


def call(kernel, name, outs, scratch, operands, flops=0, exps=0, far=0, far_outs=0, aliases={}):
    operands = [pltpu.with_memory_space_constraint(a, pltpu.HBM) for a in operands[:far]] + list(operands[far:])
    moved = sum(a.size * a.dtype.itemsize for a in operands) + sum(a.size * a.dtype.itemsize for a in outs)
    return pl.pallas_call(
        kernel,
        out_shape=tuple(outs),
        in_specs=[HBM] * far + [VMEM] * (len(operands) - far),
        out_specs=(HBM,) * far_outs + (VMEM,) * (len(outs) - far_outs),
        scratch_shapes=scratch,
        input_output_aliases=aliases,
        compiler_params=pltpu.CompilerParams(vmem_limit_bytes=24 * 1024 * 1024),
        cost_estimate=pl.CostEstimate(flops=flops, bytes_accessed=moved, transcendentals=exps),
        name=name,
    )(*operands)


def swaps(axis):
    n = lax.axis_size(axis)
    rounds = []
    for first in range(2 if n > 2 else 1):
        to = list(range(n))
        for i in range(first, n - 1, 2):
            to[i], to[i + 1] = i + 1, i
        rounds.append(list(enumerate(to)))
    return rounds


def position(axis):
    i, n = lax.axis_index(axis), lax.axis_size(axis)
    return lax.rem(i, 2) == 1, i > 0, i < n - 1


def second():
    return lax.rem(lax.axis_index("tm"), 2) == 1


def on_right():
    return lax.rem(lax.axis_index("tm") + lax.axis_index("width"), 2) == 0


def facing(core, column, columns):
    to = column + (1 if (core + column) % 2 == 0 else -1)
    return to if 0 <= to < columns else column


def outer_column(ref, lines, cols):
    return jnp.where(on_right(), ref[pl.ds(cols - 1, lines, stride=cols), :], ref[pl.ds(0, lines, stride=cols), :])


def gate_kernel(x_ref, w_ref, gate_ref):
    v = jnp.dot(x_ref[...], w_ref[...], preferred_element_type=F32)
    gate_ref[...] = v / (1.0 + jnp.exp(-v))


def early_kernel(frames, rows, cols, count, *refs):
    far, kept, rest = refs[:count], refs[count : 2 * count - 2], refs[2 * count - 2 :]
    table_ref, side_ref, *fields, taps_ref, skip_ref, arrived, held = rest
    near = (taps_ref, skip_ref) + kept
    x_ref = near[2]
    copies = [pltpu.make_async_copy(a, b, arrived.at[i]) for i, (a, b) in enumerate(zip(far, near))]
    for copy in copies:
        copy.start()
    lags, chans = taps_ref.shape
    copies[0].wait()
    copies[1].wait()
    pad = 2 * frames
    taps = taps_ref[...].astype(F32)
    table_ref[0:pad] = jnp.zeros((pad, cols, chans), F32)
    for lag in range(lags):
        tap = taps[lag : lag + 1] + (skip_ref[...] if lag == 0 else 0.0)
        table_ref[pad + lag] = jnp.broadcast_to(tap, (cols, chans))
    sites = rows * cols
    copies[2].wait()
    for lane in range(0, chans, LANES):
        span = slice(lane, lane + LANES)
        held[...] = x_ref[:, span].astype(F32)
        side_ref[:, span] = outer_column(held, frames * rows, cols)
        for d, field in enumerate(fields):
            totals = [None] * frames
            for s in range(frames):
                x = x_ref[s * sites : (s + 1) * sites, span].astype(F32).reshape(rows, cols, LANES)
                for t in range(s if d == 0 else 0, frames):
                    term = table_ref[pad + 2 * d * frames + t - s, :, span] * x
                    totals[t] = term if totals[t] is None else totals[t] + term
            for t in range(frames):
                field[t * sites : (t + 1) * sites, span] = totals[t].reshape(sites, LANES)
    for copy in copies[3:]:
        copy.wait()


def reordered(lines, rounds_h, back=False):
    if rounds_h > 1:
        return lines[:1] + lines[2:] + lines[1:2] if back else lines[:1] + lines[-1:] + lines[1:-1]
    odd = position("height")[0]
    return [jnp.where(odd, a, b) for a, b in zip(lines, lines[::-1])]


def column_kernel(frames, rows, cols, partner_ref, side_ref, out_ref, held):
    lines = frames * rows
    for lane in range(0, out_ref.shape[1], LANES):
        span = slice(lane, lane + LANES)
        held[...] = partner_ref[:, span].astype(F32)
        out_ref[:, span] = jnp.concatenate([side_ref[:, span], outer_column(held, lines, cols)]).astype(BF16)


def shift(frames):
    return jnp.where(second(), frames, -frames)


def with_partner(frames, rows, cols, d, field_ref, partner_ref, table_ref, span):
    sites = rows * cols
    base = 2 * frames + 2 * d * frames + shift(frames)
    totals = [field_ref[t * sites : (t + 1) * sites, span].reshape(rows, cols, LANES) for t in range(frames)]
    for s in range(frames):
        x = partner_ref[s * sites : (s + 1) * sites, span].astype(F32).reshape(rows, cols, LANES)
        for t in range(frames):
            totals[t] = totals[t] + table_ref[base + t - s, :, span] * x
    return totals


def later_kernel(frames, rows, cols, rounds_h, partner_ref, table_ref, *refs):
    fields, outs = refs[: len(refs) // 3], refs[len(refs) // 3 :]
    for d, field in enumerate(fields, 1):
        for lane in range(0, field.shape[1], LANES):
            span = slice(lane, lane + LANES)
            totals = with_partner(frames, rows, cols, d, field, partner_ref, table_ref, span)
            tiles = reordered([jnp.concatenate([t[r] for t in totals]) for r in range(rows)], rounds_h)
            outs[2 * d - 2][:, span] = jnp.concatenate(tiles[: rounds_h + 1]).astype(BF16)
            outs[2 * d - 1][:, span] = jnp.concatenate(tiles[rounds_h + 1 :]).astype(BF16)


def rest_kernel(after_ref, rest_ref, out_ref):
    out_ref[...] = rest_ref[...]


def own_kernel(frames, rows, cols, partner_ref, table_ref, field_ref, mine_ref):
    for lane in range(0, mine_ref.shape[1], LANES):
        span = slice(lane, lane + LANES)
        totals = with_partner(frames, rows, cols, 0, field_ref, partner_ref, table_ref, span)
        mine_ref[:, span] = jnp.concatenate(totals).reshape(mine_ref.shape[0], LANES)


def later(d, value):
    return jnp.where(lax.div(lax.axis_index("tm"), 2) >= d, value, jnp.zeros_like(value))


def add_column(frames, rows, d, totals, column, table_ref, span):
    base = 2 * frames + 2 * d * frames
    for t in range(2 * frames):
        for s in range(2 * frames):
            lag = t % frames - s % frames
            if t // frames == s // frames:
                if d == 0 and lag < 0:
                    continue
            else:
                lag = lag + (shift(frames) if t < frames else -shift(frames))
            totals[t] = totals[t] + table_ref[base + lag, :, span] * column[s * rows : (s + 1) * rows]
    return totals


def side_kernel(frames, rows, first, count, table_ref, *refs):
    arrived, (own_ref, other_ref) = refs[:count], refs[-2:]
    _, lower, upper = position("width")
    exists = jnp.where(on_right(), upper, lower)
    for lane in range(0, own_ref.shape[1], LANES):
        span = slice(lane, lane + LANES)
        totals = [jnp.zeros((rows, LANES), F32)] * (2 * frames)
        for d, ref in enumerate(arrived, first):
            totals = add_column(frames, rows, d, totals, later(d, ref[:, span].astype(F32)), table_ref, span)
        totals = [jnp.where(exists, total, jnp.zeros_like(total)) for total in totals]
        own_ref[:, span] = jnp.concatenate(totals[:frames])
        other_ref[:, span] = jnp.concatenate(totals[frames:]).astype(BF16)


def both_sides(own, other):
    right = on_right()
    return jnp.where(right, other, own), jnp.where(right, own, other)


def end_corners(frames, rows, own_ref, other_ref):
    sides = both_sides(own_ref[...], other_ref[...].astype(F32))
    pick = lambda r: [side[t * rows + r : t * rows + r + 1] for side in sides for t in range(frames)]
    return [jnp.concatenate(pick(r)) for r in (0, rows - 1)]


def border_kernel(frames, rows, cols, mine_ref, own_ref, other_ref, *outs):
    sites = rows * cols
    odd, _, _ = position("height")
    corners = end_corners(frames, rows, own_ref, other_ref)
    lines = []
    for r in (0, rows - 1):
        lines.append(jnp.concatenate([mine_ref[t * sites + r * cols : t * sites + (r + 1) * cols] for t in range(frames)]))
    ends = [jnp.concatenate(pair) for pair in zip(lines, corners)]
    for k, out in enumerate(outs):
        out[...] = jnp.where(odd, *(ends[::-1] if k else ends)).astype(BF16)


def before_kernel(frames, rows, cols, own_ref, other_ref, *refs):
    rounds_h = refs[0].shape[0] // (frames * cols) - 1
    firsts, outs = refs[:-rounds_h], refs[-rounds_h:]
    size = frames * cols
    odd, _, _ = position("height")
    corners = end_corners(frames, rows, own_ref, other_ref)
    line = 0.0
    for d, ref in enumerate(firsts, 1):
        line = line + later(d, ref[: rounds_h * size].astype(F32))
    for k, out in enumerate(outs):
        if rounds_h > 1:
            pair = line[:size], line[size:]
            row = jnp.where(odd, *(pair[::-1] if k else pair))
        else:
            row = line
        out[...] = jnp.concatenate([row, jnp.where(odd, *(corners[::-1] if k else corners))]).astype(BF16)


def shifted(line, left, right):
    cols = line.shape[0]
    place = lax.broadcasted_iota(jnp.int32, line.shape, 0)
    before = jnp.where(place == 0, left, pltpu.roll(line, 1, 0))
    after = jnp.where(place == cols - 1, right, pltpu.roll(line, cols - 1, 0))
    return before, line, after


def projected(mixed, gate, wv_ref, wo_ref):
    value = jnp.dot(mixed, wv_ref[...], preferred_element_type=F32)
    hidden = (value * gate).astype(BF16)
    return jnp.dot(hidden, wo_ref[...], preferred_element_type=F32).astype(BF16)


def filtered(lines, lefts, rights, taps):
    totals = [None] * len(lines)
    for r, line in enumerate(lines):
        near = shifted(line, lefts[r], rights[r])
        for a in range(3):
            to = r + 1 - a
            if 0 <= to < len(lines):
                term = near[0] * taps[a][0] + near[1] * taps[a][1] + near[2] * taps[a][2]
                totals[to] = term if totals[to] is None else totals[to] + term
    return totals


def taps_of(taps_ref, span):
    return [[taps_ref[a, b : b + 1, span] for b in range(3)] for a in range(3)]


def inner_kernel(
    frames, rows, cols, mine_ref, own_ref, other_ref, taps_ref, gate_ref, wv_ref, wo_ref, out_ref, totals_ref, mixed
):
    sites = rows * cols
    for lane in range(0, mine_ref.shape[1], LANES):
        span = slice(lane, lane + LANES)
        taps = taps_of(taps_ref, span)
        low, high = both_sides(own_ref[:, span], other_ref[:, span].astype(F32))
        for t in range(frames):
            at = t * sites
            lines = [mine_ref[at + r * cols : at + (r + 1) * cols, span] for r in range(rows)]
            lefts = [low[t * rows + r : t * rows + r + 1] for r in range(rows)]
            rights = [high[t * rows + r : t * rows + r + 1] for r in range(rows)]
            total = jnp.concatenate(filtered(lines, lefts, rights, taps))
            totals_ref[at : at + sites, span] = total
            mixed[at : at + sites, span] = total.astype(BF16)
    out_ref[...] = projected(mixed[...], gate_ref[...], wv_ref, wo_ref)


def has_earlier():
    return lax.div(lax.axis_index("tm"), 2) > 0


def block_kernel(frames, rows, cols, rounds_h, inner_ref, totals_ref, taps_ref, gate_ref, wv_ref, wo_ref, *refs):
    own_ref, other_ref, *parts, out_ref, sums_ref, mixed = refs
    firsts, rests = parts[: len(parts) // 2], parts[len(parts) // 2 :]
    sites = rows * cols
    size = frames * cols

    @pl.when(has_earlier())
    def _():
        for lane in range(0, out_ref.shape[1], LANES):
            span = slice(lane, lane + LANES)
            taps = taps_of(taps_ref, span)
            low, high = both_sides(own_ref[:, span], other_ref[:, span].astype(F32))
            lines = [jnp.zeros((size, LANES), F32)] * rows
            for d, (first, rest) in enumerate(zip(firsts, rests), 1):
                more = [first[i * size : (i + 1) * size, span].astype(F32) for i in range(rounds_h + 1)]
                more += [rest[i * size : (i + 1) * size, span].astype(F32) for i in range(rows - rounds_h - 1)]
                more = reordered(more, rounds_h, back=True)
                lines = [line + later(d, other) for line, other in zip(lines, more)]
            for t in range(frames):
                at = t * sites
                lefts = [low[t * rows + r : t * rows + r + 1] for r in range(rows)]
                rights = [high[t * rows + r : t * rows + r + 1] for r in range(rows)]
                total = filtered([line[t * cols : (t + 1) * cols] for line in lines], lefts, rights, taps)
                total = jnp.concatenate(total) + totals_ref[at : at + sites, span]
                sums_ref[at : at + sites, span] = total
                mixed[at : at + sites, span] = total.astype(BF16)
        out_ref[...] = projected(mixed[...], gate_ref[...], wv_ref, wo_ref)


def complete(frames, rows, cols, inner_ref, totals_ref, taps_ref, gate_ref, wv_ref, wo_ref, ends, out_ref, held, done):
    sites = rows * cols
    size = frames * cols
    odd, lower, upper = position("height")
    held[...] = inner_ref[...]
    mixed, gate = [], []
    for k, end in enumerate(ends):
        first = jnp.logical_not(odd) if k else odd
        lefts, rights = end[size : size + frames], end[size + frames : size + 2 * frames]
        exists = jnp.where(first, lower, upper)
        tap = jnp.where(first, taps_ref[0], taps_ref[2])
        for t in range(frames):
            near = shifted(end[t * cols : (t + 1) * cols], lefts[t : t + 1], rights[t : t + 1])
            more = near[0] * tap[0:1] + near[1] * tap[1:2] + near[2] * tap[2:3]
            i, j = t * sites, (t + 1) * sites - cols
            total = jnp.where(first, totals_ref[i : i + cols], totals_ref[j : j + cols])
            mixed.append(total + jnp.where(exists, more, jnp.zeros_like(more)))
            gate.append(jnp.where(first, gate_ref[i : i + cols], gate_ref[j : j + cols]))
    out = projected(jnp.concatenate(mixed).astype(BF16), jnp.concatenate(gate), wv_ref, wo_ref)
    for t in range(frames):
        new = [out[k * size + t * cols : k * size + (t + 1) * cols].astype(F32) for k in range(len(ends))]
        first, final = t * sites, (t + 1) * sites - 2 * cols
        top = inner_ref[first : first + 2 * cols].astype(F32)
        bottom = inner_ref[final : final + 2 * cols].astype(F32)
        other = new[1] if len(new) > 1 else None
        row = jnp.where(odd, new[0], top[:cols] if other is None else other)
        held[first : first + 2 * cols] = jnp.concatenate([row, top[cols:]]).astype(BF16)
        row = jnp.where(odd, bottom[cols:] if other is None else other, new[0])
        held[final : final + 2 * cols] = jnp.concatenate([bottom[:cols], row]).astype(BF16)
    copy = pltpu.make_async_copy(held, out_ref, done)
    copy.start()
    copy.wait()


def first_kernel(frames, rows, cols, inner_ref, totals_ref, taps_ref, gate_ref, wv_ref, wo_ref, *refs):
    *ends, out_ref, held, done = refs

    @pl.when(jnp.logical_not(has_earlier()))
    def _():
        values = [end[...].astype(F32) for end in ends]
        complete(
            frames, rows, cols, inner_ref, totals_ref, taps_ref, gate_ref, wv_ref, wo_ref, values, out_ref, held, done
        )


def last_kernel(frames, rows, cols, before_ref, inner_ref, totals_ref, taps_ref, gate_ref, wv_ref, wo_ref, *refs):
    *ends, out_ref, held, done = refs
    own, earlier = ends[: len(ends) // 2], ends[len(ends) // 2 :]

    @pl.when(has_earlier())
    def _():
        values = [a[...].astype(F32) + b[...].astype(F32) for a, b in zip(own, earlier)]
        complete(
            frames, rows, cols, inner_ref, totals_ref, taps_ref, gate_ref, wv_ref, wo_ref, values, out_ref, held, done
        )


def body(latents, spatial_taps, kernel_taps, skip_gain, gate_weight, value_weight, out_weight):
    frames, rows, cols, chans = latents.shape
    lags = kernel_taps.shape[0]
    n_t, n_h, n_w = lax.axis_size("tm"), lax.axis_size("height"), lax.axis_size("width")
    chips = n_t // 2
    block = frames * rows * cols
    shape = jax.ShapeDtypeStruct
    x = latents.reshape(block, chans)

    partner = lax.ppermute(x, "tm", [(i, i ^ 1) for i in range(n_t)])
    lines = frames * rows
    field = shape((block, chans), F32)
    inputs = [kernel_taps, skip_gain.reshape(1, chans), x, gate_weight, spatial_taps, value_weight, out_weight]
    near_x, near_gate, taps, value_weight, out_weight, table, side, *fields = call(
        functools.partial(early_kernel, frames, rows, cols, len(inputs)),
        "early",
        [shape(a.shape, a.dtype) for a in inputs[2:]]
        + [shape((lags + 2 * frames, cols, chans), F32), shape((lines, chans), F32)]
        + [field] * chips,
        [pltpu.VMEM(a.shape, a.dtype) for a in inputs[:2]]
        + [pltpu.SemaphoreType.DMA((len(inputs),)), pltpu.VMEM((block, LANES), F32)],
        inputs,
        far=len(inputs),
    )
    h_rounds = swaps("height")
    (column,) = call(
        functools.partial(column_kernel, frames, rows, cols),
        "column",
        [shape((2 * lines, chans), BF16)],
        [pltpu.VMEM((block, LANES), F32)],
        [partner, side],
    )
    parts = [shape((n * frames * cols, chans), BF16) for n in (len(h_rounds) + 1, rows - len(h_rounds) - 1)]
    sent = call(
        functools.partial(later_kernel, frames, rows, cols, len(h_rounds)),
        "later",
        parts * (chips - 1),
        [],
        [partner, table] + fields[1:],
        2 * (chips - 1) * frames * x.size,
    )
    columns, firsts, rests = [], [], []
    for d in range(chips):
        route = []
        for i in range(n_t):
            for h in range(n_h):
                for j in range(n_w):
                    to, beside = facing(i % 2, j, n_w), h
                    if i // 2 + d >= chips:
                        to = j
                    elif to == j and n_h % 2 == 0:
                        beside = h ^ 1
                    source = (i * n_h + h) * n_w + j
                    route.append((source, ((i + 2 * d) % n_t * n_h + beside) * n_w + to))
        columns.append(lax.ppermute(column, ("tm", "height", "width"), route))
    for d in range(1, chips):
        route = [(i, (i + 2 * d) % n_t) for i in range(n_t)]
        firsts.append(lax.ppermute(sent[2 * d - 2], "tm", route))
        rests.append((sent[2 * d - 1], route))

    swap = [(i, i ^ 1) for i in range(n_t)]
    both = [shape((lines, chans), F32), shape((lines, chans), BF16)]
    own, other = call(functools.partial(side_kernel, frames, rows, 0, 1), "side", both, [], [table, columns[0]], LATER)
    (mine,) = call(
        functools.partial(own_kernel, frames, rows, cols),
        "own",
        [field],
        [],
        [partner, table, fields[0]],
        2 * frames * x.size,
    )
    (gate,) = call(gate_kernel, "gate", [field], [], [near_x, near_gate])
    other = lax.ppermute(other, "tm", swap)
    for d, (rest, route) in enumerate(rests):
        (rest,) = call(rest_kernel, "rest", [shape(rest.shape, BF16)], [], [own, rest])
        rests[d] = lax.ppermute(rest, "tm", route)
    end = [shape((frames * cols + 2 * frames, chans), BF16)] * len(h_rounds)
    ends = call(functools.partial(border_kernel, frames, rows, cols), "border", end, [], [mine, own, other])
    ends = [lax.ppermute(e, "height", pairs) for e, pairs in zip(ends, h_rounds)]
    if chips > 1:
        own_d, other_d = call(
            functools.partial(side_kernel, frames, rows, 1, chips - 1),
            "beside",
            both,
            [],
            [table] + columns[1:] + [mine],
            LATER,
        )
        other_d = lax.ppermute(other_d, "tm", swap)
        earlier = call(functools.partial(before_kernel, frames, rows, cols), "before", end, [], [own_d, other_d] + firsts)
        earlier = [lax.ppermute(e, "height", pairs) for e, pairs in zip(earlier, h_rounds)]

    inner, totals = call(
        functools.partial(inner_kernel, frames, rows, cols),
        "inner",
        [shape((block, chans), BF16), field],
        [pltpu.VMEM((block, chans), BF16)],
        [mine, own, other, taps, gate, value_weight, out_weight],
        4 * block * chans * chans,
    )
    held = [pltpu.VMEM((block, chans), BF16), pltpu.SemaphoreType.DMA]
    weights = [taps, gate, value_weight, out_weight]
    out = shape((block, chans), BF16)
    (first,) = call(
        functools.partial(first_kernel, frames, rows, cols),
        "first",
        [out],
        held,
        [inner, totals] + weights + ends,
        far_outs=1,
    )
    if chips > 1:
        inner, totals = call(
            functools.partial(block_kernel, frames, rows, cols, len(h_rounds)),
            "block",
            [out, field],
            held[:1],
            [inner, totals] + weights + [own_d, other_d] + firsts + rests,
            aliases={0: 0, 1: 1},
        )
        (first,) = call(
            functools.partial(last_kernel, frames, rows, cols),
            "last",
            [out],
            held,
            [first, inner, totals] + weights + ends + earlier,
            far=1,
            far_outs=1,
            aliases={0: 0},
        )
    return first.reshape(latents.shape)


def solution(mesh):
    in_specs = (P("tm", "height", "width", None), P(), P(), P(), P(), P(), P())
    out_specs = P("tm", "height", "width", None)
    return jax.shard_map(body, mesh=mesh, in_specs=in_specs, out_specs=out_specs, check_vma=False)
```

```python
import functools

import jax
import jax.numpy as jnp
from jax import lax
from jax.experimental import pallas as pl
from jax.experimental.pallas import tpu as pltpu
from jax.sharding import PartitionSpec as P

LANES = 128
LATER = 8 * 10**9
F32, BF16 = jnp.float32, jnp.bfloat16
VMEM = pl.BlockSpec(memory_space=pltpu.VMEM)
HBM = pl.BlockSpec(memory_space=pltpu.HBM)


def call(kernel, name, outs, scratch, operands, flops=0, exps=0, far=0, far_outs=0, aliases={}):
    operands = [pltpu.with_memory_space_constraint(a, pltpu.HBM) for a in operands[:far]] + list(operands[far:])
    moved = sum(a.size * a.dtype.itemsize for a in operands) + sum(a.size * a.dtype.itemsize for a in outs)
    return pl.pallas_call(
        kernel,
        out_shape=tuple(outs),
        in_specs=[HBM] * far + [VMEM] * (len(operands) - far),
        out_specs=(HBM,) * far_outs + (VMEM,) * (len(outs) - far_outs),
        scratch_shapes=scratch,
        input_output_aliases=aliases,
        compiler_params=pltpu.CompilerParams(vmem_limit_bytes=24 * 1024 * 1024),
        cost_estimate=pl.CostEstimate(flops=flops, bytes_accessed=moved, transcendentals=exps),
        name=name,
    )(*operands)


def swaps(axis):
    n = lax.axis_size(axis)
    rounds = []
    for first in range(2 if n > 2 else 1):
        to = list(range(n))
        for i in range(first, n - 1, 2):
            to[i], to[i + 1] = i + 1, i
        rounds.append(list(enumerate(to)))
    return rounds


def position(axis):
    i, n = lax.axis_index(axis), lax.axis_size(axis)
    return lax.rem(i, 2) == 1, i > 0, i < n - 1


def second():
    return lax.rem(lax.axis_index("tm"), 2) == 1


def on_right():
    return lax.rem(lax.axis_index("tm") + lax.axis_index("width"), 2) == 0


def facing(core, column, columns):
    to = column + (1 if (core + column) % 2 == 0 else -1)
    return to if 0 <= to < columns else column


def outer_column(ref, lines, cols):
    return jnp.where(on_right(), ref[pl.ds(cols - 1, lines, stride=cols), :], ref[pl.ds(0, lines, stride=cols), :])


def gate_kernel(x_ref, w_ref, gate_ref):
    v = jnp.dot(x_ref[...], w_ref[...], preferred_element_type=F32)
    gate_ref[...] = v / (1.0 + jnp.exp(-v))


def early_kernel(frames, rows, cols, count, *refs):
    far, kept, rest = refs[:count], refs[count : 2 * count - 2], refs[2 * count - 2 :]
    table_ref, side_ref, *fields, taps_ref, skip_ref, arrived, held = rest
    near = (taps_ref, skip_ref) + kept
    x_ref = near[2]
    copies = [pltpu.make_async_copy(a, b, arrived.at[i]) for i, (a, b) in enumerate(zip(far, near))]
    for copy in copies:
        copy.start()
    lags, chans = taps_ref.shape
    copies[0].wait()
    copies[1].wait()
    pad = 2 * frames
    taps = taps_ref[...].astype(F32)
    table_ref[0:pad] = jnp.zeros((pad, cols, chans), F32)
    for lag in range(lags):
        tap = taps[lag : lag + 1] + (skip_ref[...] if lag == 0 else 0.0)
        table_ref[pad + lag] = jnp.broadcast_to(tap, (cols, chans))
    sites = rows * cols
    copies[2].wait()
    for lane in range(0, chans, LANES):
        span = slice(lane, lane + LANES)
        held[...] = x_ref[:, span].astype(F32)
        side_ref[:, span] = outer_column(held, frames * rows, cols)
        for d, field in enumerate(fields):
            totals = [None] * frames
            for s in range(frames):
                x = x_ref[s * sites : (s + 1) * sites, span].astype(F32).reshape(rows, cols, LANES)
                for t in range(s if d == 0 else 0, frames):
                    term = table_ref[pad + 2 * d * frames + t - s, :, span] * x
                    totals[t] = term if totals[t] is None else totals[t] + term
            for t in range(frames):
                field[t * sites : (t + 1) * sites, span] = totals[t].reshape(sites, LANES)
    for copy in copies[3:]:
        copy.wait()


def reordered(lines, rounds_h, back=False):
    if rounds_h > 1:
        return lines[:1] + lines[2:] + lines[1:2] if back else lines[:1] + lines[-1:] + lines[1:-1]
    odd = position("height")[0]
    return [jnp.where(odd, a, b) for a, b in zip(lines, lines[::-1])]


def column_kernel(frames, rows, cols, partner_ref, side_ref, out_ref, held):
    lines = frames * rows
    for lane in range(0, out_ref.shape[1], LANES):
        span = slice(lane, lane + LANES)
        held[...] = partner_ref[:, span].astype(F32)
        out_ref[:, span] = jnp.concatenate([side_ref[:, span], outer_column(held, lines, cols)]).astype(BF16)


def shift(frames):
    return jnp.where(second(), frames, -frames)


def with_partner(frames, rows, cols, d, field_ref, partner_ref, table_ref, span):
    sites = rows * cols
    base = 2 * frames + 2 * d * frames + shift(frames)
    totals = [field_ref[t * sites : (t + 1) * sites, span].reshape(rows, cols, LANES) for t in range(frames)]
    for s in range(frames):
        x = partner_ref[s * sites : (s + 1) * sites, span].astype(F32).reshape(rows, cols, LANES)
        for t in range(frames):
            totals[t] = totals[t] + table_ref[base + t - s, :, span] * x
    return totals


def later_kernel(frames, rows, cols, rounds_h, partner_ref, table_ref, *refs):
    fields, outs = refs[: len(refs) // 3], refs[len(refs) // 3 :]
    for d, field in enumerate(fields, 1):
        for lane in range(0, field.shape[1], LANES):
            span = slice(lane, lane + LANES)
            totals = with_partner(frames, rows, cols, d, field, partner_ref, table_ref, span)
            tiles = reordered([jnp.concatenate([t[r] for t in totals]) for r in range(rows)], rounds_h)
            outs[2 * d - 2][:, span] = jnp.concatenate(tiles[: rounds_h + 1]).astype(BF16)
            outs[2 * d - 1][:, span] = jnp.concatenate(tiles[rounds_h + 1 :]).astype(BF16)


def rest_kernel(after_ref, rest_ref, out_ref):
    out_ref[...] = rest_ref[...]


def own_kernel(frames, rows, cols, partner_ref, table_ref, field_ref, mine_ref):
    for lane in range(0, mine_ref.shape[1], LANES):
        span = slice(lane, lane + LANES)
        totals = with_partner(frames, rows, cols, 0, field_ref, partner_ref, table_ref, span)
        mine_ref[:, span] = jnp.concatenate(totals).reshape(mine_ref.shape[0], LANES)


def later(d, value):
    return jnp.where(lax.div(lax.axis_index("tm"), 2) >= d, value, jnp.zeros_like(value))


def add_column(frames, rows, d, totals, column, table_ref, span):
    base = 2 * frames + 2 * d * frames
    for t in range(2 * frames):
        for s in range(2 * frames):
            lag = t % frames - s % frames
            if t // frames == s // frames:
                if d == 0 and lag < 0:
                    continue
            else:
                lag = lag + (shift(frames) if t < frames else -shift(frames))
            totals[t] = totals[t] + table_ref[base + lag, :, span] * column[s * rows : (s + 1) * rows]
    return totals


def side_kernel(frames, rows, first, count, table_ref, *refs):
    arrived, (own_ref, other_ref) = refs[:count], refs[-2:]
    _, lower, upper = position("width")
    exists = jnp.where(on_right(), upper, lower)
    for lane in range(0, own_ref.shape[1], LANES):
        span = slice(lane, lane + LANES)
        totals = [jnp.zeros((rows, LANES), F32)] * (2 * frames)
        for d, ref in enumerate(arrived, first):
            totals = add_column(frames, rows, d, totals, later(d, ref[:, span].astype(F32)), table_ref, span)
        totals = [jnp.where(exists, total, jnp.zeros_like(total)) for total in totals]
        own_ref[:, span] = jnp.concatenate(totals[:frames])
        other_ref[:, span] = jnp.concatenate(totals[frames:]).astype(BF16)


def both_sides(own, other):
    right = on_right()
    return jnp.where(right, other, own), jnp.where(right, own, other)


def end_corners(frames, rows, own_ref, other_ref):
    sides = both_sides(own_ref[...], other_ref[...].astype(F32))
    pick = lambda r: [side[t * rows + r : t * rows + r + 1] for side in sides for t in range(frames)]
    return [jnp.concatenate(pick(r)) for r in (0, rows - 1)]


def border_kernel(frames, rows, cols, mine_ref, own_ref, other_ref, *outs):
    sites = rows * cols
    odd, _, _ = position("height")
    corners = end_corners(frames, rows, own_ref, other_ref)
    lines = []
    for r in (0, rows - 1):
        lines.append(jnp.concatenate([mine_ref[t * sites + r * cols : t * sites + (r + 1) * cols] for t in range(frames)]))
    ends = [jnp.concatenate(pair) for pair in zip(lines, corners)]
    for k, out in enumerate(outs):
        out[...] = jnp.where(odd, *(ends[::-1] if k else ends)).astype(BF16)


def before_kernel(frames, rows, cols, own_ref, other_ref, *refs):
    rounds_h = refs[0].shape[0] // (frames * cols) - 1
    firsts, outs = refs[:-rounds_h], refs[-rounds_h:]
    size = frames * cols
    odd, _, _ = position("height")
    corners = end_corners(frames, rows, own_ref, other_ref)
    line = 0.0
    for d, ref in enumerate(firsts, 1):
        line = line + later(d, ref[: rounds_h * size].astype(F32))
    for k, out in enumerate(outs):
        if rounds_h > 1:
            pair = line[:size], line[size:]
            row = jnp.where(odd, *(pair[::-1] if k else pair))
        else:
            row = line
        out[...] = jnp.concatenate([row, jnp.where(odd, *(corners[::-1] if k else corners))]).astype(BF16)


def shifted(line, left, right):
    cols = line.shape[0]
    place = lax.broadcasted_iota(jnp.int32, line.shape, 0)
    before = jnp.where(place == 0, left, pltpu.roll(line, 1, 0))
    after = jnp.where(place == cols - 1, right, pltpu.roll(line, cols - 1, 0))
    return before, line, after


def projected(mixed, gate, wv_ref, wo_ref):
    value = jnp.dot(mixed, wv_ref[...], preferred_element_type=F32)
    hidden = (value * gate).astype(BF16)
    return jnp.dot(hidden, wo_ref[...], preferred_element_type=F32).astype(BF16)


def filtered(lines, lefts, rights, taps):
    totals = [None] * len(lines)
    for r, line in enumerate(lines):
        near = shifted(line, lefts[r], rights[r])
        for a in range(3):
            to = r + 1 - a
            if 0 <= to < len(lines):
                term = near[0] * taps[a][0] + near[1] * taps[a][1] + near[2] * taps[a][2]
                totals[to] = term if totals[to] is None else totals[to] + term
    return totals


def taps_of(taps_ref, span):
    return [[taps_ref[a, b : b + 1, span] for b in range(3)] for a in range(3)]


def inner_kernel(
    frames, rows, cols, mine_ref, own_ref, other_ref, taps_ref, gate_ref, wv_ref, wo_ref, out_ref, totals_ref, mixed
):
    sites = rows * cols
    for lane in range(0, mine_ref.shape[1], LANES):
        span = slice(lane, lane + LANES)
        taps = taps_of(taps_ref, span)
        low, high = both_sides(own_ref[:, span], other_ref[:, span].astype(F32))
        for t in range(frames):
            at = t * sites
            lines = [mine_ref[at + r * cols : at + (r + 1) * cols, span] for r in range(rows)]
            lefts = [low[t * rows + r : t * rows + r + 1] for r in range(rows)]
            rights = [high[t * rows + r : t * rows + r + 1] for r in range(rows)]
            total = jnp.concatenate(filtered(lines, lefts, rights, taps))
            totals_ref[at : at + sites, span] = total
            mixed[at : at + sites, span] = total.astype(BF16)
    out_ref[...] = projected(mixed[...], gate_ref[...], wv_ref, wo_ref)


def has_earlier():
    return lax.div(lax.axis_index("tm"), 2) > 0


def block_kernel(frames, rows, cols, rounds_h, inner_ref, totals_ref, taps_ref, gate_ref, wv_ref, wo_ref, *refs):
    own_ref, other_ref, *parts, out_ref, sums_ref, mixed = refs
    firsts, rests = parts[: len(parts) // 2], parts[len(parts) // 2 :]
    sites = rows * cols
    size = frames * cols

    def add(lines_of):
        for lane in range(0, out_ref.shape[1], LANES):
            span = slice(lane, lane + LANES)
            taps = taps_of(taps_ref, span)
            low, high = both_sides(own_ref[:, span], other_ref[:, span].astype(F32))
            lines = None
            for d, (first, rest) in enumerate(zip(firsts, rests), 1):
                more = [first[i * size : (i + 1) * size, span].astype(F32) for i in range(rounds_h + 1)]
                more += [rest[i * size : (i + 1) * size, span].astype(F32) for i in range(rows - rounds_h - 1)]
                more = lines_of(more)
                lines = more if d == 1 else [line + later(d, other) for line, other in zip(lines, more)]
            for t in range(frames):
                at = t * sites
                lefts = [low[t * rows + r : t * rows + r + 1] for r in range(rows)]
                rights = [high[t * rows + r : t * rows + r + 1] for r in range(rows)]
                total = filtered([line[t * cols : (t + 1) * cols] for line in lines], lefts, rights, taps)
                total = jnp.concatenate(total) + totals_ref[at : at + sites, span]
                sums_ref[at : at + sites, span] = total
                mixed[at : at + sites, span] = total.astype(BF16)
        out_ref[...] = projected(mixed[...], gate_ref[...], wv_ref, wo_ref)

    odd = position("height")[0]
    if rounds_h > 1:
        pl.when(has_earlier())(lambda: add(lambda more: reordered(more, rounds_h, back=True)))
    else:
        pl.when(jnp.logical_and(has_earlier(), odd))(lambda: add(lambda more: more))
        pl.when(jnp.logical_and(has_earlier(), jnp.logical_not(odd)))(lambda: add(lambda more: more[::-1]))


def complete(frames, rows, cols, inner_ref, totals_ref, taps_ref, gate_ref, wv_ref, wo_ref, ends, out_ref, held, done):
    sites = rows * cols
    size = frames * cols
    odd, lower, upper = position("height")
    held[...] = inner_ref[...]
    mixed, gate = [], []
    for k, end in enumerate(ends):
        first = jnp.logical_not(odd) if k else odd
        lefts, rights = end[size : size + frames], end[size + frames : size + 2 * frames]
        exists = jnp.where(first, lower, upper)
        tap = jnp.where(first, taps_ref[0], taps_ref[2])
        for t in range(frames):
            near = shifted(end[t * cols : (t + 1) * cols], lefts[t : t + 1], rights[t : t + 1])
            more = near[0] * tap[0:1] + near[1] * tap[1:2] + near[2] * tap[2:3]
            i, j = t * sites, (t + 1) * sites - cols
            total = jnp.where(first, totals_ref[i : i + cols], totals_ref[j : j + cols])
            mixed.append(total + jnp.where(exists, more, jnp.zeros_like(more)))
            gate.append(jnp.where(first, gate_ref[i : i + cols], gate_ref[j : j + cols]))
    out = projected(jnp.concatenate(mixed).astype(BF16), jnp.concatenate(gate), wv_ref, wo_ref)
    for t in range(frames):
        new = [out[k * size + t * cols : k * size + (t + 1) * cols].astype(F32) for k in range(len(ends))]
        first, final = t * sites, (t + 1) * sites - 2 * cols
        top = inner_ref[first : first + 2 * cols].astype(F32)
        bottom = inner_ref[final : final + 2 * cols].astype(F32)
        other = new[1] if len(new) > 1 else None
        row = jnp.where(odd, new[0], top[:cols] if other is None else other)
        held[first : first + 2 * cols] = jnp.concatenate([row, top[cols:]]).astype(BF16)
        row = jnp.where(odd, bottom[cols:] if other is None else other, new[0])
        held[final : final + 2 * cols] = jnp.concatenate([bottom[:cols], row]).astype(BF16)
    copy = pltpu.make_async_copy(held, out_ref, done)
    copy.start()
    copy.wait()


def first_kernel(frames, rows, cols, inner_ref, totals_ref, taps_ref, gate_ref, wv_ref, wo_ref, *refs):
    *ends, out_ref, held, done = refs

    @pl.when(jnp.logical_not(has_earlier()))
    def _():
        values = [end[...].astype(F32) for end in ends]
        complete(
            frames, rows, cols, inner_ref, totals_ref, taps_ref, gate_ref, wv_ref, wo_ref, values, out_ref, held, done
        )


def last_kernel(frames, rows, cols, before_ref, inner_ref, totals_ref, taps_ref, gate_ref, wv_ref, wo_ref, *refs):
    *ends, out_ref, held, done = refs
    own, earlier = ends[: len(ends) // 2], ends[len(ends) // 2 :]

    @pl.when(has_earlier())
    def _():
        values = [a[...].astype(F32) + b[...].astype(F32) for a, b in zip(own, earlier)]
        complete(
            frames, rows, cols, inner_ref, totals_ref, taps_ref, gate_ref, wv_ref, wo_ref, values, out_ref, held, done
        )


def body(latents, spatial_taps, kernel_taps, skip_gain, gate_weight, value_weight, out_weight):
    frames, rows, cols, chans = latents.shape
    lags = kernel_taps.shape[0]
    n_t, n_h, n_w = lax.axis_size("tm"), lax.axis_size("height"), lax.axis_size("width")
    chips = n_t // 2
    block = frames * rows * cols
    shape = jax.ShapeDtypeStruct
    x = latents.reshape(block, chans)

    partner = lax.ppermute(x, "tm", [(i, i ^ 1) for i in range(n_t)])
    lines = frames * rows
    field = shape((block, chans), F32)
    inputs = [kernel_taps, skip_gain.reshape(1, chans), x, gate_weight, spatial_taps, value_weight, out_weight]
    near_x, near_gate, taps, value_weight, out_weight, table, side, *fields = call(
        functools.partial(early_kernel, frames, rows, cols, len(inputs)),
        "early",
        [shape(a.shape, a.dtype) for a in inputs[2:]]
        + [shape((lags + 2 * frames, cols, chans), F32), shape((lines, chans), F32)]
        + [field] * chips,
        [pltpu.VMEM(a.shape, a.dtype) for a in inputs[:2]]
        + [pltpu.SemaphoreType.DMA((len(inputs),)), pltpu.VMEM((block, LANES), F32)],
        inputs,
        far=len(inputs),
    )
    h_rounds = swaps("height")
    (column,) = call(
        functools.partial(column_kernel, frames, rows, cols),
        "column",
        [shape((2 * lines, chans), BF16)],
        [pltpu.VMEM((block, LANES), F32)],
        [partner, side],
    )
    parts = [shape((n * frames * cols, chans), BF16) for n in (len(h_rounds) + 1, rows - len(h_rounds) - 1)]
    sent = call(
        functools.partial(later_kernel, frames, rows, cols, len(h_rounds)),
        "later",
        parts * (chips - 1),
        [],
        [partner, table] + fields[1:],
        2 * (chips - 1) * frames * x.size,
    )
    columns, firsts, rests = [], [], []
    for d in range(chips):
        route = []
        for i in range(n_t):
            for h in range(n_h):
                for j in range(n_w):
                    to, beside = facing(i % 2, j, n_w), h
                    if i // 2 + d >= chips:
                        to = j
                    elif to == j and n_h % 2 == 0:
                        beside = h ^ 1
                    source = (i * n_h + h) * n_w + j
                    route.append((source, ((i + 2 * d) % n_t * n_h + beside) * n_w + to))
        columns.append(lax.ppermute(column, ("tm", "height", "width"), route))
    for d in range(1, chips):
        route = [(i, (i + 2 * d) % n_t) for i in range(n_t)]
        firsts.append(lax.ppermute(sent[2 * d - 2], "tm", route))
        rests.append((sent[2 * d - 1], route))

    swap = [(i, i ^ 1) for i in range(n_t)]
    both = [shape((lines, chans), F32), shape((lines, chans), BF16)]
    own, other = call(functools.partial(side_kernel, frames, rows, 0, 1), "side", both, [], [table, columns[0]], LATER)
    (mine,) = call(
        functools.partial(own_kernel, frames, rows, cols),
        "own",
        [field],
        [],
        [partner, table, fields[0]],
        2 * frames * x.size,
    )
    (gate,) = call(gate_kernel, "gate", [field], [], [near_x, near_gate])
    other = lax.ppermute(other, "tm", swap)
    for d, (rest, route) in enumerate(rests):
        (rest,) = call(rest_kernel, "rest", [shape(rest.shape, BF16)], [], [own, rest])
        rests[d] = lax.ppermute(rest, "tm", route)
    end = [shape((frames * cols + 2 * frames, chans), BF16)] * len(h_rounds)
    ends = call(functools.partial(border_kernel, frames, rows, cols), "border", end, [], [mine, own, other])
    ends = [lax.ppermute(e, "height", pairs) for e, pairs in zip(ends, h_rounds)]
    if chips > 1:
        own_d, other_d = call(
            functools.partial(side_kernel, frames, rows, 1, chips - 1),
            "beside",
            both,
            [],
            [table] + columns[1:] + [mine],
            LATER,
        )
        other_d = lax.ppermute(other_d, "tm", swap)
        earlier = call(functools.partial(before_kernel, frames, rows, cols), "before", end, [], [own_d, other_d] + firsts)
        earlier = [lax.ppermute(e, "height", pairs) for e, pairs in zip(earlier, h_rounds)]

    inner, totals = call(
        functools.partial(inner_kernel, frames, rows, cols),
        "inner",
        [shape((block, chans), BF16), field],
        [pltpu.VMEM((block, chans), BF16)],
        [mine, own, other, taps, gate, value_weight, out_weight],
        4 * block * chans * chans,
    )
    held = [pltpu.VMEM((block, chans), BF16), pltpu.SemaphoreType.DMA]
    weights = [taps, gate, value_weight, out_weight]
    out = shape((block, chans), BF16)
    (first,) = call(
        functools.partial(first_kernel, frames, rows, cols),
        "first",
        [out],
        held,
        [inner, totals] + weights + ends,
        far_outs=1,
    )
    if chips > 1:
        inner, totals = call(
            functools.partial(block_kernel, frames, rows, cols, len(h_rounds)),
            "block",
            [out, field],
            held[:1],
            [inner, totals] + weights + [own_d, other_d] + firsts + rests,
            aliases={0: 0, 1: 1},
        )
        (first,) = call(
            functools.partial(last_kernel, frames, rows, cols),
            "last",
            [out],
            held,
            [first, inner, totals] + weights + ends + earlier,
            far=1,
            far_outs=1,
            aliases={0: 0},
        )
    return first.reshape(latents.shape)


def solution(mesh):
    in_specs = (P("tm", "height", "width", None), P(), P(), P(), P(), P(), P())
    out_specs = P("tm", "height", "width", None)
    return jax.shard_map(body, mesh=mesh, in_specs=in_specs, out_specs=out_specs, check_vma=False)
```

```python
import functools

import jax
import jax.numpy as jnp
from jax import lax
from jax.experimental import pallas as pl
from jax.experimental.pallas import tpu as pltpu
from jax.sharding import PartitionSpec as P

LANES = 128
LATER = 8 * 10**9
F32, BF16 = jnp.float32, jnp.bfloat16
VMEM = pl.BlockSpec(memory_space=pltpu.VMEM)
HBM = pl.BlockSpec(memory_space=pltpu.HBM)


def call(kernel, name, outs, scratch, operands, flops=0, exps=0, far=0, far_outs=0, aliases={}):
    operands = [pltpu.with_memory_space_constraint(a, pltpu.HBM) for a in operands[:far]] + list(operands[far:])
    moved = sum(a.size * a.dtype.itemsize for a in operands) + sum(a.size * a.dtype.itemsize for a in outs)
    return pl.pallas_call(
        kernel,
        out_shape=tuple(outs),
        in_specs=[HBM] * far + [VMEM] * (len(operands) - far),
        out_specs=(HBM,) * far_outs + (VMEM,) * (len(outs) - far_outs),
        scratch_shapes=scratch,
        input_output_aliases=aliases,
        compiler_params=pltpu.CompilerParams(vmem_limit_bytes=24 * 1024 * 1024),
        cost_estimate=pl.CostEstimate(flops=flops, bytes_accessed=moved, transcendentals=exps),
        name=name,
    )(*operands)


def swaps(axis):
    n = lax.axis_size(axis)
    rounds = []
    for first in range(2 if n > 2 else 1):
        to = list(range(n))
        for i in range(first, n - 1, 2):
            to[i], to[i + 1] = i + 1, i
        rounds.append(list(enumerate(to)))
    return rounds


def position(axis):
    i, n = lax.axis_index(axis), lax.axis_size(axis)
    return lax.rem(i, 2) == 1, i > 0, i < n - 1


def second():
    return lax.rem(lax.axis_index("tm"), 2) == 1


def on_right():
    return lax.rem(lax.axis_index("tm") + lax.axis_index("width"), 2) == 1


def facing(core, column, columns):
    to = column + (1 if (core + column) % 2 == 1 else -1)
    return to if 0 <= to < columns else column


def outer_column(ref, lines, cols):
    return jnp.where(on_right(), ref[pl.ds(cols - 1, lines, stride=cols), :], ref[pl.ds(0, lines, stride=cols), :])


def gate_kernel(x_ref, w_ref, gate_ref):
    v = jnp.dot(x_ref[...], w_ref[...], preferred_element_type=F32)
    gate_ref[...] = v / (1.0 + jnp.exp(-v))


def early_kernel(frames, rows, cols, count, *refs):
    far, kept, rest = refs[:count], refs[count : 2 * count - 2], refs[2 * count - 2 :]
    table_ref, side_ref, *fields, taps_ref, skip_ref, arrived, held = rest
    near = (taps_ref, skip_ref) + kept
    x_ref = near[2]
    copies = [pltpu.make_async_copy(a, b, arrived.at[i]) for i, (a, b) in enumerate(zip(far, near))]
    for copy in copies:
        copy.start()
    lags, chans = taps_ref.shape
    copies[0].wait()
    copies[1].wait()
    pad = 2 * frames
    taps = taps_ref[...].astype(F32)
    table_ref[0:pad] = jnp.zeros((pad, cols, chans), F32)
    for lag in range(lags):
        tap = taps[lag : lag + 1] + (skip_ref[...] if lag == 0 else 0.0)
        table_ref[pad + lag] = jnp.broadcast_to(tap, (cols, chans))
    sites = rows * cols
    copies[2].wait()
    for lane in range(0, chans, LANES):
        span = slice(lane, lane + LANES)
        held[...] = x_ref[:, span].astype(F32)
        side_ref[:, span] = outer_column(held, frames * rows, cols)
        for d, field in enumerate(fields):
            totals = [None] * frames
            for s in range(frames):
                x = x_ref[s * sites : (s + 1) * sites, span].astype(F32).reshape(rows, cols, LANES)
                for t in range(s if d == 0 else 0, frames):
                    term = table_ref[pad + 2 * d * frames + t - s, :, span] * x
                    totals[t] = term if totals[t] is None else totals[t] + term
            for t in range(frames):
                field[t * sites : (t + 1) * sites, span] = totals[t].reshape(sites, LANES)
    for copy in copies[3:]:
        copy.wait()


def reordered(lines, rounds_h, back=False):
    if rounds_h > 1:
        return lines[:1] + lines[2:] + lines[1:2] if back else lines[:1] + lines[-1:] + lines[1:-1]
    odd = position("height")[0]
    return [jnp.where(odd, a, b) for a, b in zip(lines, lines[::-1])]


def column_kernel(frames, rows, cols, partner_ref, side_ref, out_ref, held):
    lines = frames * rows
    for lane in range(0, out_ref.shape[1], LANES):
        span = slice(lane, lane + LANES)
        held[...] = partner_ref[:, span].astype(F32)
        out_ref[:, span] = jnp.concatenate([side_ref[:, span], outer_column(held, lines, cols)]).astype(BF16)


def shift(frames):
    return jnp.where(second(), frames, -frames)


def with_partner(frames, rows, cols, d, field_ref, partner_ref, table_ref, span):
    sites = rows * cols
    base = 2 * frames + 2 * d * frames + shift(frames)
    totals = [field_ref[t * sites : (t + 1) * sites, span].reshape(rows, cols, LANES) for t in range(frames)]
    for s in range(frames):
        x = partner_ref[s * sites : (s + 1) * sites, span].astype(F32).reshape(rows, cols, LANES)
        for t in range(frames):
            totals[t] = totals[t] + table_ref[base + t - s, :, span] * x
    return totals


def later_kernel(frames, rows, cols, rounds_h, partner_ref, table_ref, *refs):
    fields, outs = refs[: len(refs) // 3], refs[len(refs) // 3 :]
    for d, field in enumerate(fields, 1):
        for lane in range(0, field.shape[1], LANES):
            span = slice(lane, lane + LANES)
            totals = with_partner(frames, rows, cols, d, field, partner_ref, table_ref, span)
            tiles = reordered([jnp.concatenate([t[r] for t in totals]) for r in range(rows)], rounds_h)
            outs[2 * d - 2][:, span] = jnp.concatenate(tiles[: rounds_h + 1]).astype(BF16)
            outs[2 * d - 1][:, span] = jnp.concatenate(tiles[rounds_h + 1 :]).astype(BF16)


def rest_kernel(after_ref, rest_ref, out_ref):
    out_ref[...] = rest_ref[...]


def own_kernel(frames, rows, cols, partner_ref, table_ref, field_ref, mine_ref):
    for lane in range(0, mine_ref.shape[1], LANES):
        span = slice(lane, lane + LANES)
        totals = with_partner(frames, rows, cols, 0, field_ref, partner_ref, table_ref, span)
        mine_ref[:, span] = jnp.concatenate(totals).reshape(mine_ref.shape[0], LANES)


def later(d, value):
    return jnp.where(lax.div(lax.axis_index("tm"), 2) >= d, value, jnp.zeros_like(value))


def add_column(frames, rows, d, totals, column, table_ref, span):
    base = 2 * frames + 2 * d * frames
    for t in range(2 * frames):
        for s in range(2 * frames):
            lag = t % frames - s % frames
            if t // frames == s // frames:
                if d == 0 and lag < 0:
                    continue
            else:
                lag = lag + (shift(frames) if t < frames else -shift(frames))
            totals[t] = totals[t] + table_ref[base + lag, :, span] * column[s * rows : (s + 1) * rows]
    return totals


def side_kernel(frames, rows, first, count, table_ref, *refs):
    arrived, (own_ref, other_ref) = refs[:count], refs[-2:]
    _, lower, upper = position("width")
    exists = jnp.where(on_right(), upper, lower)
    for lane in range(0, own_ref.shape[1], LANES):
        span = slice(lane, lane + LANES)
        totals = [jnp.zeros((rows, LANES), F32)] * (2 * frames)
        for d, ref in enumerate(arrived, first):
            totals = add_column(frames, rows, d, totals, later(d, ref[:, span].astype(F32)), table_ref, span)
        totals = [jnp.where(exists, total, jnp.zeros_like(total)) for total in totals]
        own_ref[:, span] = jnp.concatenate(totals[:frames])
        other_ref[:, span] = jnp.concatenate(totals[frames:]).astype(BF16)


def both_sides(own, other):
    right = on_right()
    return jnp.where(right, other, own), jnp.where(right, own, other)


def end_corners(frames, rows, own_ref, other_ref):
    sides = both_sides(own_ref[...], other_ref[...].astype(F32))
    pick = lambda r: [side[t * rows + r : t * rows + r + 1] for side in sides for t in range(frames)]
    return [jnp.concatenate(pick(r)) for r in (0, rows - 1)]


def border_kernel(frames, rows, cols, mine_ref, own_ref, other_ref, *outs):
    sites = rows * cols
    odd, _, _ = position("height")
    corners = end_corners(frames, rows, own_ref, other_ref)
    lines = []
    for r in (0, rows - 1):
        lines.append(jnp.concatenate([mine_ref[t * sites + r * cols : t * sites + (r + 1) * cols] for t in range(frames)]))
    ends = [jnp.concatenate(pair) for pair in zip(lines, corners)]
    for k, out in enumerate(outs):
        out[...] = jnp.where(odd, *(ends[::-1] if k else ends)).astype(BF16)


def before_kernel(frames, rows, cols, own_ref, other_ref, *refs):
    rounds_h = refs[0].shape[0] // (frames * cols) - 1
    firsts, outs = refs[:-rounds_h], refs[-rounds_h:]
    size = frames * cols
    odd, _, _ = position("height")
    corners = end_corners(frames, rows, own_ref, other_ref)
    line = 0.0
    for d, ref in enumerate(firsts, 1):
        line = line + later(d, ref[: rounds_h * size].astype(F32))
    for k, out in enumerate(outs):
        if rounds_h > 1:
            pair = line[:size], line[size:]
            row = jnp.where(odd, *(pair[::-1] if k else pair))
        else:
            row = line
        out[...] = jnp.concatenate([row, jnp.where(odd, *(corners[::-1] if k else corners))]).astype(BF16)


def shifted(line, left, right):
    cols = line.shape[0]
    place = lax.broadcasted_iota(jnp.int32, line.shape, 0)
    before = jnp.where(place == 0, left, pltpu.roll(line, 1, 0))
    after = jnp.where(place == cols - 1, right, pltpu.roll(line, cols - 1, 0))
    return before, line, after


def projected(mixed, gate, wv_ref, wo_ref):
    value = jnp.dot(mixed, wv_ref[...], preferred_element_type=F32)
    hidden = (value * gate).astype(BF16)
    return jnp.dot(hidden, wo_ref[...], preferred_element_type=F32).astype(BF16)


def filtered(lines, lefts, rights, taps):
    totals = [None] * len(lines)
    for r, line in enumerate(lines):
        near = shifted(line, lefts[r], rights[r])
        for a in range(3):
            to = r + 1 - a
            if 0 <= to < len(lines):
                term = near[0] * taps[a][0] + near[1] * taps[a][1] + near[2] * taps[a][2]
                totals[to] = term if totals[to] is None else totals[to] + term
    return totals


def taps_of(taps_ref, span):
    return [[taps_ref[a, b : b + 1, span] for b in range(3)] for a in range(3)]


def inner_kernel(
    frames, rows, cols, mine_ref, own_ref, other_ref, taps_ref, gate_ref, wv_ref, wo_ref, out_ref, totals_ref, mixed
):
    sites = rows * cols
    for lane in range(0, mine_ref.shape[1], LANES):
        span = slice(lane, lane + LANES)
        taps = taps_of(taps_ref, span)
        low, high = both_sides(own_ref[:, span], other_ref[:, span].astype(F32))
        for t in range(frames):
            at = t * sites
            lines = [mine_ref[at + r * cols : at + (r + 1) * cols, span] for r in range(rows)]
            lefts = [low[t * rows + r : t * rows + r + 1] for r in range(rows)]
            rights = [high[t * rows + r : t * rows + r + 1] for r in range(rows)]
            total = jnp.concatenate(filtered(lines, lefts, rights, taps))
            totals_ref[at : at + sites, span] = total
            mixed[at : at + sites, span] = total.astype(BF16)
    out_ref[...] = projected(mixed[...], gate_ref[...], wv_ref, wo_ref)


def has_earlier():
    return lax.div(lax.axis_index("tm"), 2) > 0


def block_kernel(frames, rows, cols, rounds_h, inner_ref, totals_ref, taps_ref, gate_ref, wv_ref, wo_ref, *refs):
    own_ref, other_ref, *parts, out_ref, sums_ref, mixed = refs
    firsts, rests = parts[: len(parts) // 2], parts[len(parts) // 2 :]
    sites = rows * cols
    size = frames * cols

    @pl.when(has_earlier())
    def _():
        for lane in range(0, out_ref.shape[1], LANES):
            span = slice(lane, lane + LANES)
            taps = taps_of(taps_ref, span)
            low, high = both_sides(own_ref[:, span], other_ref[:, span].astype(F32))
            lines = [jnp.zeros((size, LANES), F32)] * rows
            for d, (first, rest) in enumerate(zip(firsts, rests), 1):
                more = [first[i * size : (i + 1) * size, span].astype(F32) for i in range(rounds_h + 1)]
                more += [rest[i * size : (i + 1) * size, span].astype(F32) for i in range(rows - rounds_h - 1)]
                more = reordered(more, rounds_h, back=True)
                lines = [line + later(d, other) for line, other in zip(lines, more)]
            for t in range(frames):
                at = t * sites
                lefts = [low[t * rows + r : t * rows + r + 1] for r in range(rows)]
                rights = [high[t * rows + r : t * rows + r + 1] for r in range(rows)]
                total = filtered([line[t * cols : (t + 1) * cols] for line in lines], lefts, rights, taps)
                total = jnp.concatenate(total) + totals_ref[at : at + sites, span]
                sums_ref[at : at + sites, span] = total
                mixed[at : at + sites, span] = total.astype(BF16)
        out_ref[...] = projected(mixed[...], gate_ref[...], wv_ref, wo_ref)


def complete(frames, rows, cols, inner_ref, totals_ref, taps_ref, gate_ref, wv_ref, wo_ref, ends, out_ref, held, done):
    sites = rows * cols
    size = frames * cols
    odd, lower, upper = position("height")
    held[...] = inner_ref[...]
    mixed, gate = [], []
    for k, end in enumerate(ends):
        first = jnp.logical_not(odd) if k else odd
        lefts, rights = end[size : size + frames], end[size + frames : size + 2 * frames]
        exists = jnp.where(first, lower, upper)
        tap = jnp.where(first, taps_ref[0], taps_ref[2])
        for t in range(frames):
            near = shifted(end[t * cols : (t + 1) * cols], lefts[t : t + 1], rights[t : t + 1])
            more = near[0] * tap[0:1] + near[1] * tap[1:2] + near[2] * tap[2:3]
            i, j = t * sites, (t + 1) * sites - cols
            total = jnp.where(first, totals_ref[i : i + cols], totals_ref[j : j + cols])
            mixed.append(total + jnp.where(exists, more, jnp.zeros_like(more)))
            gate.append(jnp.where(first, gate_ref[i : i + cols], gate_ref[j : j + cols]))
    out = projected(jnp.concatenate(mixed).astype(BF16), jnp.concatenate(gate), wv_ref, wo_ref)
    for t in range(frames):
        new = [out[k * size + t * cols : k * size + (t + 1) * cols].astype(F32) for k in range(len(ends))]
        first, final = t * sites, (t + 1) * sites - 2 * cols
        top = inner_ref[first : first + 2 * cols].astype(F32)
        bottom = inner_ref[final : final + 2 * cols].astype(F32)
        other = new[1] if len(new) > 1 else None
        row = jnp.where(odd, new[0], top[:cols] if other is None else other)
        held[first : first + 2 * cols] = jnp.concatenate([row, top[cols:]]).astype(BF16)
        row = jnp.where(odd, bottom[cols:] if other is None else other, new[0])
        held[final : final + 2 * cols] = jnp.concatenate([bottom[:cols], row]).astype(BF16)
    copy = pltpu.make_async_copy(held, out_ref, done)
    copy.start()
    copy.wait()


def first_kernel(frames, rows, cols, inner_ref, totals_ref, taps_ref, gate_ref, wv_ref, wo_ref, *refs):
    *ends, out_ref, held, done = refs

    @pl.when(jnp.logical_not(has_earlier()))
    def _():
        values = [end[...].astype(F32) for end in ends]
        complete(
            frames, rows, cols, inner_ref, totals_ref, taps_ref, gate_ref, wv_ref, wo_ref, values, out_ref, held, done
        )


def last_kernel(frames, rows, cols, before_ref, inner_ref, totals_ref, taps_ref, gate_ref, wv_ref, wo_ref, *refs):
    *ends, out_ref, held, done = refs
    own, earlier = ends[: len(ends) // 2], ends[len(ends) // 2 :]

    @pl.when(has_earlier())
    def _():
        values = [a[...].astype(F32) + b[...].astype(F32) for a, b in zip(own, earlier)]
        complete(
            frames, rows, cols, inner_ref, totals_ref, taps_ref, gate_ref, wv_ref, wo_ref, values, out_ref, held, done
        )


def body(latents, spatial_taps, kernel_taps, skip_gain, gate_weight, value_weight, out_weight):
    frames, rows, cols, chans = latents.shape
    lags = kernel_taps.shape[0]
    n_t, n_h, n_w = lax.axis_size("tm"), lax.axis_size("height"), lax.axis_size("width")
    chips = n_t // 2
    block = frames * rows * cols
    shape = jax.ShapeDtypeStruct
    x = latents.reshape(block, chans)

    partner = lax.ppermute(x, "tm", [(i, i ^ 1) for i in range(n_t)])
    lines = frames * rows
    field = shape((block, chans), F32)
    inputs = [kernel_taps, skip_gain.reshape(1, chans), x, gate_weight, spatial_taps, value_weight, out_weight]
    near_x, near_gate, taps, value_weight, out_weight, table, side, *fields = call(
        functools.partial(early_kernel, frames, rows, cols, len(inputs)),
        "early",
        [shape(a.shape, a.dtype) for a in inputs[2:]]
        + [shape((lags + 2 * frames, cols, chans), F32), shape((lines, chans), F32)]
        + [field] * chips,
        [pltpu.VMEM(a.shape, a.dtype) for a in inputs[:2]]
        + [pltpu.SemaphoreType.DMA((len(inputs),)), pltpu.VMEM((block, LANES), F32)],
        inputs,
        far=len(inputs),
    )
    h_rounds = swaps("height")
    (column,) = call(
        functools.partial(column_kernel, frames, rows, cols),
        "column",
        [shape((2 * lines, chans), BF16)],
        [pltpu.VMEM((block, LANES), F32)],
        [partner, side],
    )
    parts = [shape((n * frames * cols, chans), BF16) for n in (len(h_rounds) + 1, rows - len(h_rounds) - 1)]
    sent = call(
        functools.partial(later_kernel, frames, rows, cols, len(h_rounds)),
        "later",
        parts * (chips - 1),
        [],
        [partner, table] + fields[1:],
        2 * (chips - 1) * frames * x.size,
    )
    columns, firsts, rests = [], [], []
    for d in range(chips):
        route = []
        for i in range(n_t):
            for h in range(n_h):
                for j in range(n_w):
                    to, beside = facing(i % 2, j, n_w), h
                    if i // 2 + d >= chips:
                        to = j
                    elif to == j and n_h % 2 == 0:
                        beside = h ^ 1
                    source = (i * n_h + h) * n_w + j
                    route.append((source, ((i + 2 * d) % n_t * n_h + beside) * n_w + to))
        columns.append(lax.ppermute(column, ("tm", "height", "width"), route))
    for d in range(1, chips):
        route = [(i, (i + 2 * d) % n_t) for i in range(n_t)]
        firsts.append(lax.ppermute(sent[2 * d - 2], "tm", route))
        rests.append((sent[2 * d - 1], route))

    swap = [(i, i ^ 1) for i in range(n_t)]
    both = [shape((lines, chans), F32), shape((lines, chans), BF16)]
    own, other = call(functools.partial(side_kernel, frames, rows, 0, 1), "side", both, [], [table, columns[0]], LATER)
    (mine,) = call(
        functools.partial(own_kernel, frames, rows, cols),
        "own",
        [field],
        [],
        [partner, table, fields[0]],
        2 * frames * x.size,
    )
    (gate,) = call(gate_kernel, "gate", [field], [], [near_x, near_gate])
    other = lax.ppermute(other, "tm", swap)
    for d, (rest, route) in enumerate(rests):
        (rest,) = call(rest_kernel, "rest", [shape(rest.shape, BF16)], [], [own, rest])
        rests[d] = lax.ppermute(rest, "tm", route)
    end = [shape((frames * cols + 2 * frames, chans), BF16)] * len(h_rounds)
    ends = call(functools.partial(border_kernel, frames, rows, cols), "border", end, [], [mine, own, other])
    ends = [lax.ppermute(e, "height", pairs) for e, pairs in zip(ends, h_rounds)]
    if chips > 1:
        own_d, other_d = call(
            functools.partial(side_kernel, frames, rows, 1, chips - 1),
            "beside",
            both,
            [],
            [table] + columns[1:] + [mine],
            LATER,
        )
        other_d = lax.ppermute(other_d, "tm", swap)
        earlier = call(functools.partial(before_kernel, frames, rows, cols), "before", end, [], [own_d, other_d] + firsts)
        earlier = [lax.ppermute(e, "height", pairs) for e, pairs in zip(earlier, h_rounds)]

    inner, totals = call(
        functools.partial(inner_kernel, frames, rows, cols),
        "inner",
        [shape((block, chans), BF16), field],
        [pltpu.VMEM((block, chans), BF16)],
        [mine, own, other, taps, gate, value_weight, out_weight],
        4 * block * chans * chans,
    )
    held = [pltpu.VMEM((block, chans), BF16), pltpu.SemaphoreType.DMA]
    weights = [taps, gate, value_weight, out_weight]
    out = shape((block, chans), BF16)
    (first,) = call(
        functools.partial(first_kernel, frames, rows, cols),
        "first",
        [out],
        held,
        [inner, totals] + weights + ends,
        far_outs=1,
    )
    if chips > 1:
        inner, totals = call(
            functools.partial(block_kernel, frames, rows, cols, len(h_rounds)),
            "block",
            [out, field],
            held[:1],
            [inner, totals] + weights + [own_d, other_d] + firsts + rests,
            aliases={0: 0, 1: 1},
        )
        (first,) = call(
            functools.partial(last_kernel, frames, rows, cols),
            "last",
            [out],
            held,
            [first, inner, totals] + weights + ends + earlier,
            far=1,
            far_outs=1,
            aliases={0: 0},
        )
    return first.reshape(latents.shape)


def solution(mesh):
    in_specs = (P("tm", "height", "width", None), P(), P(), P(), P(), P(), P())
    out_specs = P("tm", "height", "width", None)
    return jax.shard_map(body, mesh=mesh, in_specs=in_specs, out_specs=out_specs, check_vma=False)
```

```python
import functools

import jax
import jax.numpy as jnp
from jax import lax
from jax.experimental import pallas as pl
from jax.experimental.pallas import tpu as pltpu
from jax.sharding import PartitionSpec as P

LANES = 128
LATER = 8 * 10**9
F32, BF16 = jnp.float32, jnp.bfloat16
VMEM = pl.BlockSpec(memory_space=pltpu.VMEM)
HBM = pl.BlockSpec(memory_space=pltpu.HBM)


def call(kernel, name, outs, scratch, operands, flops=0, exps=0, far=0, far_outs=0, aliases={}):
    operands = [pltpu.with_memory_space_constraint(a, pltpu.HBM) for a in operands[:far]] + list(operands[far:])
    moved = sum(a.size * a.dtype.itemsize for a in operands) + sum(a.size * a.dtype.itemsize for a in outs)
    return pl.pallas_call(
        kernel,
        out_shape=tuple(outs),
        in_specs=[HBM] * far + [VMEM] * (len(operands) - far),
        out_specs=(HBM,) * far_outs + (VMEM,) * (len(outs) - far_outs),
        scratch_shapes=scratch,
        input_output_aliases=aliases,
        compiler_params=pltpu.CompilerParams(vmem_limit_bytes=24 * 1024 * 1024),
        cost_estimate=pl.CostEstimate(flops=flops, bytes_accessed=moved, transcendentals=exps),
        name=name,
    )(*operands)


def swaps(axis):
    n = lax.axis_size(axis)
    rounds = []
    for first in range(2 if n > 2 else 1):
        to = list(range(n))
        for i in range(first, n - 1, 2):
            to[i], to[i + 1] = i + 1, i
        rounds.append(list(enumerate(to)))
    return rounds


def position(axis):
    i, n = lax.axis_index(axis), lax.axis_size(axis)
    return lax.rem(i, 2) == 1, i > 0, i < n - 1


def second():
    return lax.rem(lax.axis_index("tm"), 2) == 1


def on_right():
    return lax.rem(lax.axis_index("tm") + lax.axis_index("width"), 2) == 1


def facing(core, column, columns):
    to = column + (1 if (core + column) % 2 == 1 else -1)
    return to if 0 <= to < columns else column


def outer_column(ref, lines, cols):
    return jnp.where(on_right(), ref[pl.ds(cols - 1, lines, stride=cols), :], ref[pl.ds(0, lines, stride=cols), :])


def gate_kernel(x_ref, w_ref, gate_ref):
    v = jnp.dot(x_ref[...], w_ref[...], preferred_element_type=F32)
    gate_ref[...] = v / (1.0 + jnp.exp(-v))


def early_kernel(frames, rows, cols, count, *refs):
    far, kept, rest = refs[:count], refs[count : 2 * count - 2], refs[2 * count - 2 :]
    table_ref, side_ref, *fields, taps_ref, skip_ref, arrived, held = rest
    near = (taps_ref, skip_ref) + kept
    x_ref = near[2]
    copies = [pltpu.make_async_copy(a, b, arrived.at[i]) for i, (a, b) in enumerate(zip(far, near))]
    for copy in copies:
        copy.start()
    lags, chans = taps_ref.shape
    copies[0].wait()
    copies[1].wait()
    pad = 2 * frames
    taps = taps_ref[...].astype(F32)
    table_ref[0:pad] = jnp.zeros((pad, cols, chans), F32)
    for lag in range(lags):
        tap = taps[lag : lag + 1] + (skip_ref[...] if lag == 0 else 0.0)
        table_ref[pad + lag] = jnp.broadcast_to(tap, (cols, chans))
    sites = rows * cols
    copies[2].wait()
    for lane in range(0, chans, LANES):
        span = slice(lane, lane + LANES)
        held[...] = x_ref[:, span].astype(F32)
        side_ref[:, span] = outer_column(held, frames * rows, cols)
        for d, field in enumerate(fields):
            totals = [None] * frames
            for s in range(frames):
                x = x_ref[s * sites : (s + 1) * sites, span].astype(F32).reshape(rows, cols, LANES)
                for t in range(s if d == 0 else 0, frames):
                    term = table_ref[pad + 2 * d * frames + t - s, :, span] * x
                    totals[t] = term if totals[t] is None else totals[t] + term
            for t in range(frames):
                field[t * sites : (t + 1) * sites, span] = totals[t].reshape(sites, LANES)
    for copy in copies[3:]:
        copy.wait()


def reordered(lines, rounds_h, back=False):
    if rounds_h > 1:
        return lines[:1] + lines[2:] + lines[1:2] if back else lines[:1] + lines[-1:] + lines[1:-1]
    odd = position("height")[0]
    return [jnp.where(odd, a, b) for a, b in zip(lines, lines[::-1])]


def column_kernel(frames, rows, cols, partner_ref, side_ref, out_ref, held):
    lines = frames * rows
    for lane in range(0, out_ref.shape[1], LANES):
        span = slice(lane, lane + LANES)
        held[...] = partner_ref[:, span].astype(F32)
        out_ref[:, span] = jnp.concatenate([side_ref[:, span], outer_column(held, lines, cols)]).astype(BF16)


def shift(frames):
    return jnp.where(second(), frames, -frames)


def with_partner(frames, rows, cols, d, field_ref, partner_ref, table_ref, span):
    sites = rows * cols
    base = 2 * frames + 2 * d * frames + shift(frames)
    totals = [field_ref[t * sites : (t + 1) * sites, span].reshape(rows, cols, LANES) for t in range(frames)]
    for s in range(frames):
        x = partner_ref[s * sites : (s + 1) * sites, span].astype(F32).reshape(rows, cols, LANES)
        for t in range(frames):
            totals[t] = totals[t] + table_ref[base + t - s, :, span] * x
    return totals


def later_kernel(frames, rows, cols, rounds_h, partner_ref, table_ref, *refs):
    fields, outs = refs[: len(refs) // 3], refs[len(refs) // 3 :]
    for d, field in enumerate(fields, 1):
        for lane in range(0, field.shape[1], LANES):
            span = slice(lane, lane + LANES)
            totals = with_partner(frames, rows, cols, d, field, partner_ref, table_ref, span)
            tiles = reordered([jnp.concatenate([t[r] for t in totals]) for r in range(rows)], rounds_h)
            outs[2 * d - 2][:, span] = jnp.concatenate(tiles[: rounds_h + 1]).astype(BF16)
            outs[2 * d - 1][:, span] = jnp.concatenate(tiles[rounds_h + 1 :]).astype(BF16)


def rest_kernel(after_ref, rest_ref, out_ref):
    out_ref[...] = rest_ref[...]


def own_kernel(frames, rows, cols, partner_ref, table_ref, field_ref, mine_ref):
    for lane in range(0, mine_ref.shape[1], LANES):
        span = slice(lane, lane + LANES)
        totals = with_partner(frames, rows, cols, 0, field_ref, partner_ref, table_ref, span)
        mine_ref[:, span] = jnp.concatenate(totals).reshape(mine_ref.shape[0], LANES)


def later(d, value):
    return jnp.where(lax.div(lax.axis_index("tm"), 2) >= d, value, jnp.zeros_like(value))


def add_column(frames, rows, d, totals, column, table_ref, span):
    base = 2 * frames + 2 * d * frames
    for t in range(2 * frames):
        for s in range(2 * frames):
            lag = t % frames - s % frames
            if t // frames == s // frames:
                if d == 0 and lag < 0:
                    continue
            else:
                lag = lag + (shift(frames) if t < frames else -shift(frames))
            totals[t] = totals[t] + table_ref[base + lag, :, span] * column[s * rows : (s + 1) * rows]
    return totals


def side_kernel(frames, rows, first, count, table_ref, *refs):
    arrived, (own_ref, other_ref) = refs[:count], refs[-2:]
    _, lower, upper = position("width")
    exists = jnp.where(on_right(), upper, lower)
    for lane in range(0, own_ref.shape[1], LANES):
        span = slice(lane, lane + LANES)
        totals = [jnp.zeros((rows, LANES), F32)] * (2 * frames)
        for d, ref in enumerate(arrived, first):
            totals = add_column(frames, rows, d, totals, later(d, ref[:, span].astype(F32)), table_ref, span)
        totals = [jnp.where(exists, total, jnp.zeros_like(total)) for total in totals]
        own_ref[:, span] = jnp.concatenate(totals[:frames])
        other_ref[:, span] = jnp.concatenate(totals[frames:]).astype(BF16)


def both_sides(own, other):
    right = on_right()
    return jnp.where(right, other, own), jnp.where(right, own, other)


def end_corners(frames, rows, own_ref, other_ref):
    sides = both_sides(own_ref[...], other_ref[...].astype(F32))
    pick = lambda r: [side[t * rows + r : t * rows + r + 1] for side in sides for t in range(frames)]
    return [jnp.concatenate(pick(r)) for r in (0, rows - 1)]


def border_kernel(frames, rows, cols, mine_ref, own_ref, other_ref, *outs):
    sites = rows * cols
    odd, _, _ = position("height")
    corners = end_corners(frames, rows, own_ref, other_ref)
    lines = []
    for r in (0, rows - 1):
        lines.append(jnp.concatenate([mine_ref[t * sites + r * cols : t * sites + (r + 1) * cols] for t in range(frames)]))
    ends = [jnp.concatenate(pair) for pair in zip(lines, corners)]
    for k, out in enumerate(outs):
        out[...] = jnp.where(odd, *(ends[::-1] if k else ends)).astype(BF16)


def before_kernel(frames, rows, cols, own_ref, other_ref, *refs):
    rounds_h = refs[0].shape[0] // (frames * cols) - 1
    firsts, outs = refs[:-rounds_h], refs[-rounds_h:]
    size = frames * cols
    odd, _, _ = position("height")
    corners = end_corners(frames, rows, own_ref, other_ref)
    line = 0.0
    for d, ref in enumerate(firsts, 1):
        line = line + later(d, ref[: rounds_h * size].astype(F32))
    for k, out in enumerate(outs):
        if rounds_h > 1:
            pair = line[:size], line[size:]
            row = jnp.where(odd, *(pair[::-1] if k else pair))
        else:
            row = line
        out[...] = jnp.concatenate([row, jnp.where(odd, *(corners[::-1] if k else corners))]).astype(BF16)


def shifted(line, left, right):
    cols = line.shape[0]
    place = lax.broadcasted_iota(jnp.int32, line.shape, 0)
    before = jnp.where(place == 0, left, pltpu.roll(line, 1, 0))
    after = jnp.where(place == cols - 1, right, pltpu.roll(line, cols - 1, 0))
    return before, line, after


def projected(mixed, gate, wv_ref, wo_ref):
    value = jnp.dot(mixed, wv_ref[...], preferred_element_type=F32)
    hidden = (value * gate).astype(BF16)
    return jnp.dot(hidden, wo_ref[...], preferred_element_type=F32).astype(BF16)


def filtered(lines, lefts, rights, taps):
    totals = [None] * len(lines)
    for r, line in enumerate(lines):
        near = shifted(line, lefts[r], rights[r])
        for a in range(3):
            to = r + 1 - a
            if 0 <= to < len(lines):
                term = near[0] * taps[a][0] + near[1] * taps[a][1] + near[2] * taps[a][2]
                totals[to] = term if totals[to] is None else totals[to] + term
    return totals


def taps_of(taps_ref, span):
    return [[taps_ref[a, b : b + 1, span] for b in range(3)] for a in range(3)]


def inner_kernel(
    frames, rows, cols, mine_ref, own_ref, other_ref, taps_ref, gate_ref, wv_ref, wo_ref, out_ref, totals_ref, mixed
):
    sites = rows * cols
    for lane in range(0, mine_ref.shape[1], LANES):
        span = slice(lane, lane + LANES)
        taps = taps_of(taps_ref, span)
        low, high = both_sides(own_ref[:, span], other_ref[:, span].astype(F32))
        for t in range(frames):
            at = t * sites
            lines = [mine_ref[at + r * cols : at + (r + 1) * cols, span] for r in range(rows)]
            lefts = [low[t * rows + r : t * rows + r + 1] for r in range(rows)]
            rights = [high[t * rows + r : t * rows + r + 1] for r in range(rows)]
            total = jnp.concatenate(filtered(lines, lefts, rights, taps))
            totals_ref[at : at + sites, span] = total
            mixed[at : at + sites, span] = total.astype(BF16)
    out_ref[...] = projected(mixed[...], gate_ref[...], wv_ref, wo_ref)


def has_earlier():
    return lax.div(lax.axis_index("tm"), 2) > 0


def block_kernel(frames, rows, cols, rounds_h, inner_ref, totals_ref, taps_ref, gate_ref, wv_ref, wo_ref, *refs):
    own_ref, other_ref, *parts, out_ref, sums_ref, mixed = refs
    firsts, rests = parts[: len(parts) // 2], parts[len(parts) // 2 :]
    sites = rows * cols
    size = frames * cols

    def add(lines_of):
        for lane in range(0, out_ref.shape[1], LANES):
            span = slice(lane, lane + LANES)
            taps = taps_of(taps_ref, span)
            low, high = both_sides(own_ref[:, span], other_ref[:, span].astype(F32))
            lines = None
            for d, (first, rest) in enumerate(zip(firsts, rests), 1):
                more = [first[i * size : (i + 1) * size, span].astype(F32) for i in range(rounds_h + 1)]
                more += [rest[i * size : (i + 1) * size, span].astype(F32) for i in range(rows - rounds_h - 1)]
                more = lines_of(more)
                lines = more if d == 1 else [line + later(d, other) for line, other in zip(lines, more)]
            for t in range(frames):
                at = t * sites
                lefts = [low[t * rows + r : t * rows + r + 1] for r in range(rows)]
                rights = [high[t * rows + r : t * rows + r + 1] for r in range(rows)]
                total = filtered([line[t * cols : (t + 1) * cols] for line in lines], lefts, rights, taps)
                total = jnp.concatenate(total) + totals_ref[at : at + sites, span]
                sums_ref[at : at + sites, span] = total
                mixed[at : at + sites, span] = total.astype(BF16)
        out_ref[...] = projected(mixed[...], gate_ref[...], wv_ref, wo_ref)

    odd = position("height")[0]
    if rounds_h > 1:
        pl.when(has_earlier())(lambda: add(lambda more: reordered(more, rounds_h, back=True)))
    else:
        pl.when(jnp.logical_and(has_earlier(), odd))(lambda: add(lambda more: more))
        pl.when(jnp.logical_and(has_earlier(), jnp.logical_not(odd)))(lambda: add(lambda more: more[::-1]))


def complete(frames, rows, cols, inner_ref, totals_ref, taps_ref, gate_ref, wv_ref, wo_ref, ends, out_ref, held, done):
    sites = rows * cols
    size = frames * cols
    odd, lower, upper = position("height")
    held[...] = inner_ref[...]
    mixed, gate = [], []
    for k, end in enumerate(ends):
        first = jnp.logical_not(odd) if k else odd
        lefts, rights = end[size : size + frames], end[size + frames : size + 2 * frames]
        exists = jnp.where(first, lower, upper)
        tap = jnp.where(first, taps_ref[0], taps_ref[2])
        for t in range(frames):
            near = shifted(end[t * cols : (t + 1) * cols], lefts[t : t + 1], rights[t : t + 1])
            more = near[0] * tap[0:1] + near[1] * tap[1:2] + near[2] * tap[2:3]
            i, j = t * sites, (t + 1) * sites - cols
            total = jnp.where(first, totals_ref[i : i + cols], totals_ref[j : j + cols])
            mixed.append(total + jnp.where(exists, more, jnp.zeros_like(more)))
            gate.append(jnp.where(first, gate_ref[i : i + cols], gate_ref[j : j + cols]))
    out = projected(jnp.concatenate(mixed).astype(BF16), jnp.concatenate(gate), wv_ref, wo_ref)
    for t in range(frames):
        new = [out[k * size + t * cols : k * size + (t + 1) * cols].astype(F32) for k in range(len(ends))]
        first, final = t * sites, (t + 1) * sites - 2 * cols
        top = inner_ref[first : first + 2 * cols].astype(F32)
        bottom = inner_ref[final : final + 2 * cols].astype(F32)
        other = new[1] if len(new) > 1 else None
        row = jnp.where(odd, new[0], top[:cols] if other is None else other)
        held[first : first + 2 * cols] = jnp.concatenate([row, top[cols:]]).astype(BF16)
        row = jnp.where(odd, bottom[cols:] if other is None else other, new[0])
        held[final : final + 2 * cols] = jnp.concatenate([bottom[:cols], row]).astype(BF16)
    copy = pltpu.make_async_copy(held, out_ref, done)
    copy.start()
    copy.wait()


def first_kernel(frames, rows, cols, inner_ref, totals_ref, taps_ref, gate_ref, wv_ref, wo_ref, *refs):
    *ends, out_ref, held, done = refs

    @pl.when(jnp.logical_not(has_earlier()))
    def _():
        values = [end[...].astype(F32) for end in ends]
        complete(
            frames, rows, cols, inner_ref, totals_ref, taps_ref, gate_ref, wv_ref, wo_ref, values, out_ref, held, done
        )


def last_kernel(frames, rows, cols, before_ref, inner_ref, totals_ref, taps_ref, gate_ref, wv_ref, wo_ref, *refs):
    *ends, out_ref, held, done = refs
    own, earlier = ends[: len(ends) // 2], ends[len(ends) // 2 :]

    @pl.when(has_earlier())
    def _():
        values = [a[...].astype(F32) + b[...].astype(F32) for a, b in zip(own, earlier)]
        complete(
            frames, rows, cols, inner_ref, totals_ref, taps_ref, gate_ref, wv_ref, wo_ref, values, out_ref, held, done
        )


def body(latents, spatial_taps, kernel_taps, skip_gain, gate_weight, value_weight, out_weight):
    frames, rows, cols, chans = latents.shape
    lags = kernel_taps.shape[0]
    n_t, n_h, n_w = lax.axis_size("tm"), lax.axis_size("height"), lax.axis_size("width")
    chips = n_t // 2
    block = frames * rows * cols
    shape = jax.ShapeDtypeStruct
    x = latents.reshape(block, chans)

    partner = lax.ppermute(x, "tm", [(i, i ^ 1) for i in range(n_t)])
    lines = frames * rows
    field = shape((block, chans), F32)
    inputs = [kernel_taps, skip_gain.reshape(1, chans), x, gate_weight, spatial_taps, value_weight, out_weight]
    near_x, near_gate, taps, value_weight, out_weight, table, side, *fields = call(
        functools.partial(early_kernel, frames, rows, cols, len(inputs)),
        "early",
        [shape(a.shape, a.dtype) for a in inputs[2:]]
        + [shape((lags + 2 * frames, cols, chans), F32), shape((lines, chans), F32)]
        + [field] * chips,
        [pltpu.VMEM(a.shape, a.dtype) for a in inputs[:2]]
        + [pltpu.SemaphoreType.DMA((len(inputs),)), pltpu.VMEM((block, LANES), F32)],
        inputs,
        far=len(inputs),
    )
    h_rounds = swaps("height")
    (column,) = call(
        functools.partial(column_kernel, frames, rows, cols),
        "column",
        [shape((2 * lines, chans), BF16)],
        [pltpu.VMEM((block, LANES), F32)],
        [partner, side],
    )
    parts = [shape((n * frames * cols, chans), BF16) for n in (len(h_rounds) + 1, rows - len(h_rounds) - 1)]
    sent = call(
        functools.partial(later_kernel, frames, rows, cols, len(h_rounds)),
        "later",
        parts * (chips - 1),
        [],
        [partner, table] + fields[1:],
        2 * (chips - 1) * frames * x.size,
    )
    columns, firsts, rests = [], [], []
    for d in range(chips):
        route = []
        for i in range(n_t):
            for h in range(n_h):
                for j in range(n_w):
                    to, beside = facing(i % 2, j, n_w), h
                    if i // 2 + d >= chips:
                        to = j
                    elif to == j and n_h % 2 == 0:
                        beside = h ^ 1
                    source = (i * n_h + h) * n_w + j
                    route.append((source, ((i + 2 * d) % n_t * n_h + beside) * n_w + to))
        columns.append(lax.ppermute(column, ("tm", "height", "width"), route))
    for d in range(1, chips):
        route = [(i, (i + 2 * d) % n_t) for i in range(n_t)]
        firsts.append(lax.ppermute(sent[2 * d - 2], "tm", route))
        rests.append((sent[2 * d - 1], route))

    swap = [(i, i ^ 1) for i in range(n_t)]
    both = [shape((lines, chans), F32), shape((lines, chans), BF16)]
    own, other = call(functools.partial(side_kernel, frames, rows, 0, 1), "side", both, [], [table, columns[0]], LATER)
    (mine,) = call(
        functools.partial(own_kernel, frames, rows, cols),
        "own",
        [field],
        [],
        [partner, table, fields[0]],
        2 * frames * x.size,
    )
    (gate,) = call(gate_kernel, "gate", [field], [], [near_x, near_gate])
    other = lax.ppermute(other, "tm", swap)
    for d, (rest, route) in enumerate(rests):
        (rest,) = call(rest_kernel, "rest", [shape(rest.shape, BF16)], [], [own, rest])
        rests[d] = lax.ppermute(rest, "tm", route)
    end = [shape((frames * cols + 2 * frames, chans), BF16)] * len(h_rounds)
    ends = call(functools.partial(border_kernel, frames, rows, cols), "border", end, [], [mine, own, other])
    ends = [lax.ppermute(e, "height", pairs) for e, pairs in zip(ends, h_rounds)]
    if chips > 1:
        own_d, other_d = call(
            functools.partial(side_kernel, frames, rows, 1, chips - 1),
            "beside",
            both,
            [],
            [table] + columns[1:] + [mine],
            LATER,
        )
        other_d = lax.ppermute(other_d, "tm", swap)
        earlier = call(functools.partial(before_kernel, frames, rows, cols), "before", end, [], [own_d, other_d] + firsts)
        earlier = [lax.ppermute(e, "height", pairs) for e, pairs in zip(earlier, h_rounds)]

    inner, totals = call(
        functools.partial(inner_kernel, frames, rows, cols),
        "inner",
        [shape((block, chans), BF16), field],
        [pltpu.VMEM((block, chans), BF16)],
        [mine, own, other, taps, gate, value_weight, out_weight],
        4 * block * chans * chans,
    )
    held = [pltpu.VMEM((block, chans), BF16), pltpu.SemaphoreType.DMA]
    weights = [taps, gate, value_weight, out_weight]
    out = shape((block, chans), BF16)
    (first,) = call(
        functools.partial(first_kernel, frames, rows, cols),
        "first",
        [out],
        held,
        [inner, totals] + weights + ends,
        far_outs=1,
    )
    if chips > 1:
        inner, totals = call(
            functools.partial(block_kernel, frames, rows, cols, len(h_rounds)),
            "block",
            [out, field],
            held[:1],
            [inner, totals] + weights + [own_d, other_d] + firsts + rests,
            aliases={0: 0, 1: 1},
        )
        (first,) = call(
            functools.partial(last_kernel, frames, rows, cols),
            "last",
            [out],
            held,
            [first, inner, totals] + weights + ends + earlier,
            far=1,
            far_outs=1,
            aliases={0: 0},
        )
    return first.reshape(latents.shape)


def solution(mesh):
    in_specs = (P("tm", "height", "width", None), P(), P(), P(), P(), P(), P())
    out_specs = P("tm", "height", "width", None)
    return jax.shard_map(body, mesh=mesh, in_specs=in_specs, out_specs=out_specs, check_vma=False)
```

```python
import functools

import jax
import jax.numpy as jnp
from jax import lax
from jax.experimental import pallas as pl
from jax.experimental.pallas import tpu as pltpu
from jax.sharding import PartitionSpec as P

LANES = 128
LATER = 8 * 10**9
F32, BF16 = jnp.float32, jnp.bfloat16
VMEM = pl.BlockSpec(memory_space=pltpu.VMEM)
HBM = pl.BlockSpec(memory_space=pltpu.HBM)


def call(kernel, name, outs, scratch, operands, flops=0, exps=0, far=0, far_outs=0, aliases={}):
    operands = [pltpu.with_memory_space_constraint(a, pltpu.HBM) for a in operands[:far]] + list(operands[far:])
    moved = sum(a.size * a.dtype.itemsize for a in operands) + sum(a.size * a.dtype.itemsize for a in outs)
    return pl.pallas_call(
        kernel,
        out_shape=tuple(outs),
        in_specs=[HBM] * far + [VMEM] * (len(operands) - far),
        out_specs=(HBM,) * far_outs + (VMEM,) * (len(outs) - far_outs),
        scratch_shapes=scratch,
        input_output_aliases=aliases,
        compiler_params=pltpu.CompilerParams(vmem_limit_bytes=24 * 1024 * 1024),
        cost_estimate=pl.CostEstimate(flops=flops, bytes_accessed=moved, transcendentals=exps),
        name=name,
    )(*operands)


def swaps(axis):
    n = lax.axis_size(axis)
    rounds = []
    for first in range(2 if n > 2 else 1):
        to = list(range(n))
        for i in range(first, n - 1, 2):
            to[i], to[i + 1] = i + 1, i
        rounds.append(list(enumerate(to)))
    return rounds


def position(axis):
    i, n = lax.axis_index(axis), lax.axis_size(axis)
    return lax.rem(i, 2) == 1, i > 0, i < n - 1


def second():
    return lax.rem(lax.axis_index("tm"), 2) == 1


def on_right():
    return lax.rem(lax.axis_index("tm") + lax.axis_index("width"), 2) == 0


def facing(core, column, columns):
    to = column + (1 if (core + column) % 2 == 0 else -1)
    return to if 0 <= to < columns else column


def outer_column(ref, lines, cols):
    return jnp.where(on_right(), ref[pl.ds(cols - 1, lines, stride=cols), :], ref[pl.ds(0, lines, stride=cols), :])


def gate_kernel(x_ref, w_ref, gate_ref):
    v = jnp.dot(x_ref[...], w_ref[...], preferred_element_type=F32)
    gate_ref[...] = v / (1.0 + jnp.exp(-v))


def early_kernel(frames, rows, cols, count, *refs):
    far, kept, rest = refs[:count], refs[count : 2 * count - 2], refs[2 * count - 2 :]
    table_ref, side_ref, *fields, taps_ref, skip_ref, arrived, held = rest
    near = (taps_ref, skip_ref) + kept
    x_ref = near[2]
    copies = [pltpu.make_async_copy(a, b, arrived.at[i]) for i, (a, b) in enumerate(zip(far, near))]
    for copy in copies:
        copy.start()
    lags, chans = taps_ref.shape
    copies[0].wait()
    copies[1].wait()
    pad = 2 * frames
    taps = taps_ref[...].astype(F32)
    table_ref[0:pad] = jnp.zeros((pad, cols, chans), F32)
    for lag in range(lags):
        tap = taps[lag : lag + 1] + (skip_ref[...] if lag == 0 else 0.0)
        table_ref[pad + lag] = jnp.broadcast_to(tap, (cols, chans))
    sites = rows * cols
    copies[2].wait()
    for lane in range(0, chans, LANES):
        span = slice(lane, lane + LANES)
        held[...] = x_ref[:, span].astype(F32)
        side_ref[:, span] = outer_column(held, frames * rows, cols)
        for d, field in enumerate(fields):
            totals = [None] * frames
            for s in range(frames):
                x = x_ref[s * sites : (s + 1) * sites, span].astype(F32).reshape(rows, cols, LANES)
                for t in range(s if d == 0 else 0, frames):
                    term = table_ref[pad + 2 * d * frames + t - s, :, span] * x
                    totals[t] = term if totals[t] is None else totals[t] + term
            for t in range(frames):
                field[t * sites : (t + 1) * sites, span] = totals[t].reshape(sites, LANES)
    for copy in copies[3:]:
        copy.wait()


def reordered(lines, rounds_h, back=False):
    if rounds_h > 1:
        return lines[:1] + lines[2:] + lines[1:2] if back else lines[:1] + lines[-1:] + lines[1:-1]
    odd = position("height")[0]
    return [jnp.where(odd, a, b) for a, b in zip(lines, lines[::-1])]


def column_kernel(frames, rows, cols, partner_ref, side_ref, out_ref, held):
    lines = frames * rows
    for lane in range(0, out_ref.shape[1], LANES):
        span = slice(lane, lane + LANES)
        held[...] = partner_ref[:, span].astype(F32)
        out_ref[:, span] = jnp.concatenate([side_ref[:, span], outer_column(held, lines, cols)]).astype(BF16)


def shift(frames):
    return jnp.where(second(), frames, -frames)


def with_partner(frames, rows, cols, d, field_ref, partner_ref, table_ref, span):
    sites = rows * cols
    base = 2 * frames + 2 * d * frames + shift(frames)
    totals = [field_ref[t * sites : (t + 1) * sites, span].reshape(rows, cols, LANES) for t in range(frames)]
    for s in range(frames):
        x = partner_ref[s * sites : (s + 1) * sites, span].astype(F32).reshape(rows, cols, LANES)
        for t in range(frames):
            totals[t] = totals[t] + table_ref[base + t - s, :, span] * x
    return totals


def later_kernel(frames, rows, cols, rounds_h, partner_ref, table_ref, *refs):
    fields, outs = refs[: len(refs) // 3], refs[len(refs) // 3 :]
    for d, field in enumerate(fields, 1):
        for lane in range(0, field.shape[1], LANES):
            span = slice(lane, lane + LANES)
            totals = with_partner(frames, rows, cols, d, field, partner_ref, table_ref, span)
            tiles = reordered([jnp.concatenate([t[r] for t in totals]) for r in range(rows)], rounds_h)
            outs[2 * d - 2][:, span] = jnp.concatenate(tiles[: rounds_h + 2]).astype(BF16)
            outs[2 * d - 1][:, span] = jnp.concatenate(tiles[rounds_h + 2 :]).astype(BF16)


def rest_kernel(after_ref, rest_ref, out_ref):
    out_ref[...] = rest_ref[...]


def own_kernel(frames, rows, cols, partner_ref, table_ref, field_ref, mine_ref):
    for lane in range(0, mine_ref.shape[1], LANES):
        span = slice(lane, lane + LANES)
        totals = with_partner(frames, rows, cols, 0, field_ref, partner_ref, table_ref, span)
        mine_ref[:, span] = jnp.concatenate(totals).reshape(mine_ref.shape[0], LANES)


def later(d, value):
    return jnp.where(lax.div(lax.axis_index("tm"), 2) >= d, value, jnp.zeros_like(value))


def add_column(frames, rows, d, totals, column, table_ref, span):
    base = 2 * frames + 2 * d * frames
    for t in range(2 * frames):
        for s in range(2 * frames):
            lag = t % frames - s % frames
            if t // frames == s // frames:
                if d == 0 and lag < 0:
                    continue
            else:
                lag = lag + (shift(frames) if t < frames else -shift(frames))
            totals[t] = totals[t] + table_ref[base + lag, :, span] * column[s * rows : (s + 1) * rows]
    return totals


def side_kernel(frames, rows, first, count, table_ref, *refs):
    arrived, (own_ref, other_ref) = refs[:count], refs[-2:]
    _, lower, upper = position("width")
    exists = jnp.where(on_right(), upper, lower)
    for lane in range(0, own_ref.shape[1], LANES):
        span = slice(lane, lane + LANES)
        totals = [jnp.zeros((rows, LANES), F32)] * (2 * frames)
        for d, ref in enumerate(arrived, first):
            totals = add_column(frames, rows, d, totals, later(d, ref[:, span].astype(F32)), table_ref, span)
        totals = [jnp.where(exists, total, jnp.zeros_like(total)) for total in totals]
        own_ref[:, span] = jnp.concatenate(totals[:frames])
        other_ref[:, span] = jnp.concatenate(totals[frames:]).astype(BF16)


def both_sides(own, other):
    right = on_right()
    return jnp.where(right, other, own), jnp.where(right, own, other)


def end_corners(frames, rows, own_ref, other_ref):
    sides = both_sides(own_ref[...], other_ref[...].astype(F32))
    pick = lambda r: [side[t * rows + r : t * rows + r + 1] for side in sides for t in range(frames)]
    return [jnp.concatenate(pick(r)) for r in (0, rows - 1)]


def border_kernel(frames, rows, cols, mine_ref, own_ref, other_ref, *outs):
    sites = rows * cols
    odd, _, _ = position("height")
    corners = end_corners(frames, rows, own_ref, other_ref)
    lines = []
    for r in (0, rows - 1):
        lines.append(jnp.concatenate([mine_ref[t * sites + r * cols : t * sites + (r + 1) * cols] for t in range(frames)]))
    ends = [jnp.concatenate(pair) for pair in zip(lines, corners)]
    for k, out in enumerate(outs):
        out[...] = jnp.where(odd, *(ends[::-1] if k else ends)).astype(BF16)


def before_kernel(frames, rows, cols, own_ref, other_ref, *refs):
    rounds_h = refs[0].shape[0] // (frames * cols) - 2
    firsts, outs = refs[:-rounds_h], refs[-rounds_h:]
    size = frames * cols
    odd, _, _ = position("height")
    corners = end_corners(frames, rows, own_ref, other_ref)
    line = 0.0
    for d, ref in enumerate(firsts, 1):
        line = line + later(d, ref[: rounds_h * size].astype(F32))
    for k, out in enumerate(outs):
        if rounds_h > 1:
            pair = line[:size], line[size:]
            row = jnp.where(odd, *(pair[::-1] if k else pair))
        else:
            row = line
        out[...] = jnp.concatenate([row, jnp.where(odd, *(corners[::-1] if k else corners))]).astype(BF16)


def shifted(line, left, right):
    cols = line.shape[0]
    place = lax.broadcasted_iota(jnp.int32, line.shape, 0)
    before = jnp.where(place == 0, left, pltpu.roll(line, 1, 0))
    after = jnp.where(place == cols - 1, right, pltpu.roll(line, cols - 1, 0))
    return before, line, after


def projected(mixed, gate, wv_ref, wo_ref):
    value = jnp.dot(mixed, wv_ref[...], preferred_element_type=F32)
    hidden = (value * gate).astype(BF16)
    return jnp.dot(hidden, wo_ref[...], preferred_element_type=F32).astype(BF16)


def filtered(lines, lefts, rights, taps):
    totals = [None] * len(lines)
    for r, line in enumerate(lines):
        near = shifted(line, lefts[r], rights[r])
        for a in range(3):
            to = r + 1 - a
            if 0 <= to < len(lines):
                term = near[0] * taps[a][0] + near[1] * taps[a][1] + near[2] * taps[a][2]
                totals[to] = term if totals[to] is None else totals[to] + term
    return totals


def taps_of(taps_ref, span):
    return [[taps_ref[a, b : b + 1, span] for b in range(3)] for a in range(3)]


def inner_kernel(
    frames, rows, cols, mine_ref, own_ref, other_ref, taps_ref, gate_ref, wv_ref, wo_ref, out_ref, totals_ref, mixed
):
    sites = rows * cols
    for lane in range(0, mine_ref.shape[1], LANES):
        span = slice(lane, lane + LANES)
        taps = taps_of(taps_ref, span)
        low, high = both_sides(own_ref[:, span], other_ref[:, span].astype(F32))
        for t in range(frames):
            at = t * sites
            lines = [mine_ref[at + r * cols : at + (r + 1) * cols, span] for r in range(rows)]
            lefts = [low[t * rows + r : t * rows + r + 1] for r in range(rows)]
            rights = [high[t * rows + r : t * rows + r + 1] for r in range(rows)]
            total = jnp.concatenate(filtered(lines, lefts, rights, taps))
            totals_ref[at : at + sites, span] = total
            mixed[at : at + sites, span] = total.astype(BF16)
    out_ref[...] = projected(mixed[...], gate_ref[...], wv_ref, wo_ref)


def has_earlier():
    return lax.div(lax.axis_index("tm"), 2) > 0


def block_kernel(frames, rows, cols, rounds_h, inner_ref, totals_ref, taps_ref, gate_ref, wv_ref, wo_ref, *refs):
    own_ref, other_ref, *parts, out_ref, sums_ref, mixed = refs
    firsts, rests = parts[: len(parts) // 2], parts[len(parts) // 2 :]
    sites = rows * cols
    size = frames * cols

    @pl.when(has_earlier())
    def _():
        for lane in range(0, out_ref.shape[1], LANES):
            span = slice(lane, lane + LANES)
            taps = taps_of(taps_ref, span)
            low, high = both_sides(own_ref[:, span], other_ref[:, span].astype(F32))
            lines = [jnp.zeros((size, LANES), F32)] * rows
            for d, (first, rest) in enumerate(zip(firsts, rests), 1):
                more = [first[i * size : (i + 1) * size, span].astype(F32) for i in range(rounds_h + 2)]
                more += [rest[i * size : (i + 1) * size, span].astype(F32) for i in range(rows - rounds_h - 2)]
                more = reordered(more, rounds_h, back=True)
                lines = [line + later(d, other) for line, other in zip(lines, more)]
            for t in range(frames):
                at = t * sites
                lefts = [low[t * rows + r : t * rows + r + 1] for r in range(rows)]
                rights = [high[t * rows + r : t * rows + r + 1] for r in range(rows)]
                total = filtered([line[t * cols : (t + 1) * cols] for line in lines], lefts, rights, taps)
                total = jnp.concatenate(total) + totals_ref[at : at + sites, span]
                sums_ref[at : at + sites, span] = total
                mixed[at : at + sites, span] = total.astype(BF16)
        out_ref[...] = projected(mixed[...], gate_ref[...], wv_ref, wo_ref)


def complete(frames, rows, cols, inner_ref, totals_ref, taps_ref, gate_ref, wv_ref, wo_ref, ends, out_ref, held, done):
    sites = rows * cols
    size = frames * cols
    odd, lower, upper = position("height")
    held[...] = inner_ref[...]
    mixed, gate = [], []
    for k, end in enumerate(ends):
        first = jnp.logical_not(odd) if k else odd
        lefts, rights = end[size : size + frames], end[size + frames : size + 2 * frames]
        exists = jnp.where(first, lower, upper)
        tap = jnp.where(first, taps_ref[0], taps_ref[2])
        for t in range(frames):
            near = shifted(end[t * cols : (t + 1) * cols], lefts[t : t + 1], rights[t : t + 1])
            more = near[0] * tap[0:1] + near[1] * tap[1:2] + near[2] * tap[2:3]
            i, j = t * sites, (t + 1) * sites - cols
            total = jnp.where(first, totals_ref[i : i + cols], totals_ref[j : j + cols])
            mixed.append(total + jnp.where(exists, more, jnp.zeros_like(more)))
            gate.append(jnp.where(first, gate_ref[i : i + cols], gate_ref[j : j + cols]))
    out = projected(jnp.concatenate(mixed).astype(BF16), jnp.concatenate(gate), wv_ref, wo_ref)
    for t in range(frames):
        new = [out[k * size + t * cols : k * size + (t + 1) * cols].astype(F32) for k in range(len(ends))]
        first, final = t * sites, (t + 1) * sites - 2 * cols
        top = inner_ref[first : first + 2 * cols].astype(F32)
        bottom = inner_ref[final : final + 2 * cols].astype(F32)
        other = new[1] if len(new) > 1 else None
        row = jnp.where(odd, new[0], top[:cols] if other is None else other)
        held[first : first + 2 * cols] = jnp.concatenate([row, top[cols:]]).astype(BF16)
        row = jnp.where(odd, bottom[cols:] if other is None else other, new[0])
        held[final : final + 2 * cols] = jnp.concatenate([bottom[:cols], row]).astype(BF16)
    copy = pltpu.make_async_copy(held, out_ref, done)
    copy.start()
    copy.wait()


def first_kernel(frames, rows, cols, inner_ref, totals_ref, taps_ref, gate_ref, wv_ref, wo_ref, *refs):
    *ends, out_ref, held, done = refs

    @pl.when(jnp.logical_not(has_earlier()))
    def _():
        values = [end[...].astype(F32) for end in ends]
        complete(
            frames, rows, cols, inner_ref, totals_ref, taps_ref, gate_ref, wv_ref, wo_ref, values, out_ref, held, done
        )


def last_kernel(frames, rows, cols, before_ref, inner_ref, totals_ref, taps_ref, gate_ref, wv_ref, wo_ref, *refs):
    *ends, out_ref, held, done = refs
    own, earlier = ends[: len(ends) // 2], ends[len(ends) // 2 :]

    @pl.when(has_earlier())
    def _():
        values = [a[...].astype(F32) + b[...].astype(F32) for a, b in zip(own, earlier)]
        complete(
            frames, rows, cols, inner_ref, totals_ref, taps_ref, gate_ref, wv_ref, wo_ref, values, out_ref, held, done
        )


def body(latents, spatial_taps, kernel_taps, skip_gain, gate_weight, value_weight, out_weight):
    frames, rows, cols, chans = latents.shape
    lags = kernel_taps.shape[0]
    n_t, n_h, n_w = lax.axis_size("tm"), lax.axis_size("height"), lax.axis_size("width")
    chips = n_t // 2
    block = frames * rows * cols
    shape = jax.ShapeDtypeStruct
    x = latents.reshape(block, chans)

    partner = lax.ppermute(x, "tm", [(i, i ^ 1) for i in range(n_t)])
    lines = frames * rows
    field = shape((block, chans), F32)
    inputs = [kernel_taps, skip_gain.reshape(1, chans), x, gate_weight, spatial_taps, value_weight, out_weight]
    near_x, near_gate, taps, value_weight, out_weight, table, side, *fields = call(
        functools.partial(early_kernel, frames, rows, cols, len(inputs)),
        "early",
        [shape(a.shape, a.dtype) for a in inputs[2:]]
        + [shape((lags + 2 * frames, cols, chans), F32), shape((lines, chans), F32)]
        + [field] * chips,
        [pltpu.VMEM(a.shape, a.dtype) for a in inputs[:2]]
        + [pltpu.SemaphoreType.DMA((len(inputs),)), pltpu.VMEM((block, LANES), F32)],
        inputs,
        far=len(inputs),
    )
    h_rounds = swaps("height")
    (column,) = call(
        functools.partial(column_kernel, frames, rows, cols),
        "column",
        [shape((2 * lines, chans), BF16)],
        [pltpu.VMEM((block, LANES), F32)],
        [partner, side],
    )
    parts = [shape((n * frames * cols, chans), BF16) for n in (len(h_rounds) + 2, rows - len(h_rounds) - 2)]
    sent = call(
        functools.partial(later_kernel, frames, rows, cols, len(h_rounds)),
        "later",
        parts * (chips - 1),
        [],
        [partner, table] + fields[1:],
        2 * (chips - 1) * frames * x.size,
    )
    columns, firsts, rests = [], [], []
    for d in range(chips):
        route = []
        for i in range(n_t):
            for h in range(n_h):
                for j in range(n_w):
                    to, beside = facing(i % 2, j, n_w), h
                    if i // 2 + d >= chips:
                        to = j
                    elif to == j and n_h % 2 == 0:
                        beside = h ^ 1
                    source = (i * n_h + h) * n_w + j
                    route.append((source, ((i + 2 * d) % n_t * n_h + beside) * n_w + to))
        columns.append(lax.ppermute(column, ("tm", "height", "width"), route))
    for d in range(1, chips):
        route = [(i, (i + 2 * d) % n_t) for i in range(n_t)]
        firsts.append(lax.ppermute(sent[2 * d - 2], "tm", route))
        rests.append((sent[2 * d - 1], route))

    swap = [(i, i ^ 1) for i in range(n_t)]
    both = [shape((lines, chans), F32), shape((lines, chans), BF16)]
    own, other = call(functools.partial(side_kernel, frames, rows, 0, 1), "side", both, [], [table, columns[0]], LATER)
    (mine,) = call(
        functools.partial(own_kernel, frames, rows, cols),
        "own",
        [field],
        [],
        [partner, table, fields[0]],
        2 * frames * x.size,
    )
    (gate,) = call(gate_kernel, "gate", [field], [], [near_x, near_gate])
    other = lax.ppermute(other, "tm", swap)
    for d, (rest, route) in enumerate(rests):
        (rest,) = call(rest_kernel, "rest", [shape(rest.shape, BF16)], [], [own, rest])
        rests[d] = lax.ppermute(rest, "tm", route)
    end = [shape((frames * cols + 2 * frames, chans), BF16)] * len(h_rounds)
    ends = call(functools.partial(border_kernel, frames, rows, cols), "border", end, [], [mine, own, other])
    ends = [lax.ppermute(e, "height", pairs) for e, pairs in zip(ends, h_rounds)]
    if chips > 1:
        own_d, other_d = call(
            functools.partial(side_kernel, frames, rows, 1, chips - 1),
            "beside",
            both,
            [],
            [table] + columns[1:] + [mine],
            LATER,
        )
        other_d = lax.ppermute(other_d, "tm", swap)
        earlier = call(functools.partial(before_kernel, frames, rows, cols), "before", end, [], [own_d, other_d] + firsts)
        earlier = [lax.ppermute(e, "height", pairs) for e, pairs in zip(earlier, h_rounds)]

    inner, totals = call(
        functools.partial(inner_kernel, frames, rows, cols),
        "inner",
        [shape((block, chans), BF16), field],
        [pltpu.VMEM((block, chans), BF16)],
        [mine, own, other, taps, gate, value_weight, out_weight],
        4 * block * chans * chans,
    )
    held = [pltpu.VMEM((block, chans), BF16), pltpu.SemaphoreType.DMA]
    weights = [taps, gate, value_weight, out_weight]
    out = shape((block, chans), BF16)
    (first,) = call(
        functools.partial(first_kernel, frames, rows, cols),
        "first",
        [out],
        held,
        [inner, totals] + weights + ends,
        far_outs=1,
    )
    if chips > 1:
        inner, totals = call(
            functools.partial(block_kernel, frames, rows, cols, len(h_rounds)),
            "block",
            [out, field],
            held[:1],
            [inner, totals] + weights + [own_d, other_d] + firsts + rests,
            aliases={0: 0, 1: 1},
        )
        (first,) = call(
            functools.partial(last_kernel, frames, rows, cols),
            "last",
            [out],
            held,
            [first, inner, totals] + weights + ends + earlier,
            far=1,
            far_outs=1,
            aliases={0: 0},
        )
    return first.reshape(latents.shape)


def solution(mesh):
    in_specs = (P("tm", "height", "width", None), P(), P(), P(), P(), P(), P())
    out_specs = P("tm", "height", "width", None)
    return jax.shard_map(body, mesh=mesh, in_specs=in_specs, out_specs=out_specs, check_vma=False)
```
